32 devices in a mesh: mem: 16 (over z, y, x), rows: 2 (over core).
Axes of the slice: x: 2, y: 2, z: 4, core: 2. Of those that a mesh axis runs over, the one named last changes fastest.
Arguments:
- sample_collection: float32 [256, 2, 16, 128], P('mem', None, 'rows'), may hold values from -6 to 6
- obs_values: float32 [2, 16, 128], P(None, 'rows', 'mem'), may hold values from -6 to 6
- obs_inverse_variance: float32 [2, 16, 128], P(None, 'rows', 'mem'), may hold values from 0.5 to 4
- obs_mask: int32 [2, 16, 128], P(None, 'rows', 'mem'), may hold values 0 or 1
Outputs:
- cycled: float32 [256, 2, 16, 128], P('mem', None, 'rows')
The draws below stay inside these ranges and needn't reach their ends.
All inputs are finite; a program needn't handle non-finite values. No bound on the sum of `obs_mask` on one device may be relied on, other than what follows from the above.
Results may differ from the reference program's by a relative error of at most 0.0051.
Values may be sent and summed in bfloat16 or wider, within the bound.
No kernel may reach another device: no remote copies, remote signals or barrier semaphores. Data moves between devices by JAX's collectives and lax.ppermute only.
A program may use at most 64 MiB of HBM per device.

```python
import math
import jax
import jax.numpy as jnp
from jax import lax

MEMBERS = 256
PATCH = 8
RADIUS = 4
FSTEPS = 4
SCHULZ_STEPS = 3
NY = 16
NX = 128


def with_ends(values, own_key, least, high):
    spot = [jax.random.randint(jax.random.fold_in(own_key, axis), (), 0, length) for axis, length in enumerate(values.shape)]
    longest = values.shape.index(max(values.shape))
    neighbour = spot[:longest] + [(spot[longest] + 1) % values.shape[longest]] + spot[longest + 1:]
    return values.at[tuple(spot)].set(least).at[tuple(neighbour)].set(high)


def steps_of(rng, shape, cuts, least, top_value):
    loudness, own = 1.0, jax.random.fold_in(rng, 6)
    for dim, parts in cuts:
        heights = jnp.exp(jax.random.uniform(jax.random.fold_in(own, dim), (parts,), jnp.float32, least / len(cuts), top_value / len(cuts)))
        loudness = loudness * jnp.repeat(heights, shape[dim] // parts).reshape([-1 if axis == dim else 1 for axis in range(len(shape))])
    return loudness


def gaussian(stream_key, extent, scale, bound, shards=(), kind=jnp.bfloat16):
    result = scale * jax.random.normal(stream_key, extent, jnp.float32)
    if shards:
        result = result * steps_of(stream_key, extent, shards, -0.22, 0.18)
    return jnp.clip(result, -bound, bound).astype(kind)


def setup_inputs(seed: int = 0) -> dict:
    streams_of = jax.random.split(jax.random.key(seed), 5)
    sample_collection = gaussian(streams_of[0], (MEMBERS, 2, NY, NX), 1.0, 6.0, ((0, 16), (2, 2)), jnp.float32)
    obs_values = gaussian(streams_of[1], (2, NY, NX), 1.0, 6.0, ((1, 2), (2, 16)), jnp.float32)
    obs_inverse_variance = jnp.clip(jnp.exp(math.log(4.0) - 2.0794415 * jax.random.uniform(streams_of[2], (2, NY, NX), jnp.float32) ** steps_of(streams_of[2], (2, NY, NX), ((1, 2), (2, 16)), -0.2, 0.2)), 0.5, 4.0)
    obs_mask = with_ends((jax.random.randint(streams_of[3], (2, NY, NX), 0, 2) < 1).astype(jnp.int32), jax.random.fold_in(streams_of[3], 1), 0, 1)
    return {"sample_collection": sample_collection, "obs_values": obs_values, "obs_inverse_variance": obs_inverse_variance, "obs_mask": obs_mask}


CADV = 0.05

def advance(dynamics_fields):
    u_field = dynamics_fields[0]
    v_field = dynamics_fields[1]

    def tendency(field):
        along_x = jnp.roll(field, -1, 1) - jnp.roll(field, 1, 1)
        along_y = jnp.roll(field, -1, 0) - jnp.roll(field, 1, 0)
        return field - CADV * (u_field * along_x + v_field * along_y)
    return jnp.stack([tendency(u_field), tendency(v_field)])

def predicted_prior(sample_fields):

    def one_member(dynamics_fields):
        for step in range(FSTEPS):
            dynamics_fields = advance(dynamics_fields)
        return dynamics_fields
    return lax.map(one_member, sample_fields)

def windows(array):
    width = array.shape[-1] - 2 * RADIUS
    count = width // PATCH
    left = array[..., :width].reshape(array.shape[:-1] + (count, PATCH))
    right = array[..., PATCH:PATCH + width].reshape(array.shape[:-1] + (count, PATCH))
    return jnp.concatenate([left, right], -1)

def taper_table():
    index = jnp.arange(2 * PATCH)
    dist = jnp.maximum(jnp.maximum(RADIUS - index, index - (RADIUS + PATCH - 1)), 0)
    far = jnp.maximum(dist[:, None], dist[None, :]).astype(jnp.float32)
    return 1.0 - far / (RADIUS + 1.0)

def analyse(dev_ext, obs_ext, mean_band):
    high = lax.Precision.HIGHEST
    region = windows(dev_ext)
    obs_region = windows(obs_ext)
    taper = taper_table()[:, None, :]
    weighted = (region.astype(jnp.float32) * (obs_region[0].astype(jnp.float32) * taper)).astype(jnp.bfloat16)
    weighted_f = weighted.astype(jnp.float32)
    gram = jnp.einsum('kvrpc,lvrpc->pkl', weighted_f, region.astype(jnp.float32), precision=high)
    projected = jnp.einsum('kvrpc,vrpc->pk', weighted_f, obs_region[1].astype(jnp.float32), precision=high)
    eye = jnp.eye(MEMBERS, dtype=jnp.float32)
    system = (MEMBERS - 1.0) * eye + gram
    scale = jnp.sqrt(lax.optimization_barrier(jnp.sum(system * system, axis=(1, 2))))[:, None, None]
    iter_y = system / scale
    iter_z = jnp.broadcast_to(eye, system.shape)
    for step in range(SCHULZ_STEPS):
        middle = 1.5 * eye - 0.5 * jnp.matmul(iter_z, iter_y, precision=high)
        iter_y = jnp.matmul(iter_y, middle, precision=high)
        iter_z = jnp.matmul(middle, iter_z, precision=high)
    root = iter_z / jnp.sqrt(scale)
    half_way = jnp.einsum('pkl,pl->pk', root, projected, precision=high)
    shift = jnp.einsum('pkl,pl->pk', root, half_way, precision=high)
    ensemble_transform = (jnp.sqrt(MEMBERS - 1.0) * root + shift[:, :, None]).astype(jnp.bfloat16)
    inner = dev_ext[:, :, RADIUS:RADIUS + PATCH, RADIUS:-RADIUS]
    inner = inner.reshape(inner.shape[:3] + (inner.shape[3] // PATCH, PATCH))
    increment = jnp.einsum('kvrpc,pkm->mvrpc', inner.astype(jnp.float32), ensemble_transform.astype(jnp.float32), precision=high)
    increment = increment.reshape(increment.shape[:3] + (-1,))
    return mean_band + increment

def wrap_columns(array):
    return jnp.concatenate([array[..., -RADIUS:], array, array[..., :RADIUS]], -1)

def reference(sample_collection, obs_values, obs_inverse_variance, obs_mask):
    leading_output = predicted_prior(sample_collection)
    mean = lax.optimization_barrier(jnp.sum(leading_output, 0)) / MEMBERS
    deviation = (leading_output - mean).astype(jnp.bfloat16)
    member_weight = (obs_mask.astype(jnp.float32) * obs_inverse_variance).astype(jnp.bfloat16)
    innovation = (obs_values - mean).astype(jnp.bfloat16)
    obs_pair = jnp.stack([member_weight, innovation])

    def band(index):
        picks = ((index * PATCH - RADIUS + jnp.arange(PATCH + 2 * RADIUS)) % NY).astype(jnp.int32)
        dev_ext = wrap_columns(jnp.take(deviation, picks, axis=2))
        obs_ext = wrap_columns(jnp.take(obs_pair, picks, axis=2))
        mean_band = lax.dynamic_slice_in_dim(mean, (index * PATCH).astype(jnp.int32), PATCH, 1)
        return analyse(dev_ext, obs_ext, mean_band)
    bands = lax.map(band, jnp.arange(NY // PATCH, dtype=jnp.int32))
    updated_estimate = jnp.transpose(bands, (1, 2, 0, 3, 4)).reshape(MEMBERS, 2, NY, NX)
    return predicted_prior(updated_estimate)
```

```python
import functools

import jax
import jax.numpy as jnp
from jax import lax
from jax.experimental import pallas as pl
from jax.experimental.pallas import tpu as pltpu
from jax.sharding import PartitionSpec as P

PATCH = 8
RADIUS = 4
FSTEPS = 4
CADV = 0.05

LOCAL = 16
FIELDS = 2
BAND = 8
WIDTH = 128
REGION = PATCH + 2 * RADIUS
HALF = FIELDS * (BAND // 2) * REGION
BLOCKS = 2 * FIELDS * (BAND // 2)

BF = jnp.bfloat16
F32 = jnp.float32


def forecast_rows(u_rows, v_rows):
    for _ in range(FSTEPS):
        new_u, new_v = [], []
        for i in range(1, len(u_rows) - 1):
            cu, cv = CADV * u_rows[i], CADV * v_rows[i]
            for rows, new in ((u_rows, new_u), (v_rows, new_v)):
                along_x = pltpu.roll(rows[i], WIDTH - 1, 1) - pltpu.roll(rows[i], 1, 1)
                along_y = rows[i + 1] - rows[i - 1]
                new.append(rows[i] - (cu * along_x + cv * along_y))
        u_rows, v_rows = new_u, new_v
    return u_rows, v_rows


def swap_blocks(parts, size):
    count = len(parts)
    lane = lax.broadcasted_iota(jnp.int32, parts[0].shape, 1) // size
    stride = 1
    while stride < count:
        upper = (lane & stride) != 0
        new = list(parts)
        for j in range(count):
            if j & stride == 0:
                a, b = parts[j], parts[j + stride]
                new[j] = jnp.where(upper, pltpu.roll(b, stride * size, 1), a)
                new[j + stride] = jnp.where(upper, b, pltpu.roll(a, WIDTH - stride * size, 1))
        parts = new
        stride *= 2
    return parts


def pack_kernel(x_ref, near_ref, obs_ref, out_ref):
    stride = FIELDS * BAND

    def row(ref, field, index):
        return ref[pl.ds(field * BAND + index, LOCAL, stride=stride), :]

    fields = []
    for field in range(FIELDS):
        before = [row(near_ref, field, r) for r in range(BAND - FSTEPS, BAND)]
        own = [row(x_ref, field, r) for r in range(BAND)]
        after = [row(near_ref, field, r) for r in range(FSTEPS)]
        fields.append(before + own + after)
    done = forecast_rows(*fields)
    stacked = []
    for half in range(2):
        for field in range(FIELDS):
            for r in range(BAND // 2):
                value = done[field][half * (BAND // 2) + r]
                mean = jnp.sum(value, 0, keepdims=True) * (1.0 / LOCAL)
                high = mean.astype(BF).astype(F32)
                low = mean - high
                index = lax.broadcasted_iota(jnp.int32, (8, WIDTH), 0)
                tail = jnp.where(index == 0, high, jnp.where(index == 1, low, 0.0))
                stacked += [value - mean, tail]
    rows = jnp.concatenate(stacked, 0).astype(BF)
    column = lax.broadcasted_iota(jnp.int32, (WIDTH, 2 * WIDTH), 0)
    lane = lax.broadcasted_iota(jnp.int32, (WIDTH, 2 * WIDTH), 1)
    wanted = ((lane // REGION) * PATCH + lane % REGION + (WIDTH - RADIUS)) % WIDTH
    widen = (column == wanted).astype(F32).astype(BF)
    wide = jnp.dot(rows, widen, preferred_element_type=F32)
    height = LOCAL + 8
    for side in range(2):
        tails = [[], []]
        for half in range(2):
            parts = [
                wide[(half * 8 + j) * height : (half * 8 + j + 1) * height, side * WIDTH : (side + 1) * WIDTH]
                for j in range(8)
            ]
            parts = swap_blocks(parts, REGION)
            for i in range(8):
                out_ref[side * 8 + i, :, half * WIDTH : (half + 1) * WIDTH] = parts[i][:LOCAL].astype(BF)
                tails[half].append(parts[i][LOCAL:])
        for i in range(8):
            tail = jnp.concatenate([tails[0][i], tails[1][i]], 0) + obs_ref[...]
            out_ref[side * 8 + i, :, 2 * WIDTH :] = tail.astype(BF)


def halves_of(ref, me, count):
    tails = [ref[s, :, 2 * WIDTH :].astype(F32) for s in range(count)]
    lane = lax.broadcasted_iota(jnp.int32, (16, WIDTH), 1) % REGION
    left = ref[lax.rem(me + count - 1, count), :, 2 * WIDTH :].astype(F32)
    own = ref[me, :, 2 * WIDTH :].astype(F32)
    right = ref[lax.rem(me + 1, count), :, 2 * WIDTH :].astype(F32)
    seen = jnp.where(
        lane < RADIUS,
        pltpu.roll(left, WIDTH - (PATCH - RADIUS), 1),
        jnp.where(lane < RADIUS + PATCH, pltpu.roll(own, RADIUS, 1), pltpu.roll(right, RADIUS + PATCH, 1)),
    )
    result = []
    for half in range(2):
        base = half * 8
        means = [t[base : base + 1] + t[base + 1 : base + 2] for t in tails]
        mean = functools.reduce(jnp.add, means) * (1.0 / count)
        deviation = jnp.concatenate(
            [
                (ref[s, :, half * WIDTH : (half + 1) * WIDTH].astype(F32) + (means[s] - mean)).astype(BF)
                for s in range(count)
            ],
            0,
        )
        weight = seen[base + 2 : base + 3]
        obs = seen[base + 3 : base + 4] + seen[base + 4 : base + 5] + seen[base + 5 : base + 6]
        innovation = (obs - mean).astype(BF).astype(F32)
        result.append((deviation, mean, weight, innovation))
    return result


def analysis_kernel(me_ref, own_ref, near_ref, out_ref):
    count = own_ref.shape[0]
    members = count * LOCAL
    me = me_ref[0]
    own = halves_of(own_ref, me, count)
    near = halves_of(near_ref, me, count)
    lane = lax.broadcasted_iota(jnp.int32, (1, WIDTH), 1)
    region_column = lane % REGION
    half_row = (lane // REGION) % (BAND // 2)
    column_distance = jnp.maximum(
        jnp.maximum(RADIUS - region_column, region_column - (RADIUS + PATCH - 1)), 0
    )
    row_distances = (0 * lane, 0 * lane, half_row + 1, RADIUS - half_row)
    weighted, deviation, innovation = [], [], []
    for (dev, _, weight, inno), row_distance in zip(own + near, row_distances):
        far = jnp.maximum(row_distance, column_distance).astype(F32)
        factor = weight * (1.0 - far / (RADIUS + 1.0))
        weighted.append((dev.astype(F32) * factor).astype(BF))
        deviation.append(dev)
        innovation.append(jnp.broadcast_to(inno, (16, WIDTH)).astype(BF))
    weighted = jnp.concatenate(weighted, 1)
    inner = jnp.concatenate(deviation[:2], 1)
    rows = jnp.concatenate([jnp.concatenate(deviation, 1), jnp.concatenate(innovation, 1)], 0)
    both = lax.dot_general(rows, weighted, (((1,), (1,)), ((), ())), preferred_element_type=F32)
    row = lax.broadcasted_iota(jnp.int32, (members, members), 0)
    col = lax.broadcasted_iota(jnp.int32, (members, members), 1)
    system = both[:members] + jnp.where(row == col, members - 1.0, 0.0)
    line = both[members:]
    scale = jnp.sqrt(jnp.sum(system * system))
    y0 = system * (1.0 / scale)

    def mul(a, b):
        return jnp.dot(a.astype(BF), b.astype(BF), preferred_element_type=F32)

    y0b = y0.astype(BF)
    inner_f = inner.astype(F32)
    x1 = 1.5 * inner_f - 0.5 * mul(y0b, inner)
    line1 = 1.5 * line - 0.5 * mul(line, y0b)
    y1 = 1.5 * y0 - 0.5 * mul(y0b, y0b)
    p1 = 1.5 * y1 - 0.5 * mul(y1, y0b)
    p1b = p1.astype(BF)
    x2 = 1.5 * x1 - 0.5 * mul(p1b, x1)
    line2 = 1.5 * line1 - 0.5 * mul(line1, p1b)
    q1 = 1.5 * p1 - 0.5 * mul(p1b, p1b)
    p2 = 1.5 * q1 - 0.5 * mul(q1, p1b)
    p2b = p2.astype(BF)
    x3 = 1.5 * x2 - 0.5 * mul(p2b, x2)
    line3 = 1.5 * line2 - 0.5 * mul(line2, p2b)
    inverse = 1.0 / jnp.sqrt(scale)
    x3 = x3 * inverse
    line3 = line3 * inverse
    xh = x3.astype(BF)
    xl = (x3 - xh.astype(F32)).astype(BF)
    lh = line3.astype(BF)
    ll = (line3 - lh.astype(F32)).astype(BF)
    shift = mul(lh, xh) + (mul(ll, xh) + mul(lh, xl))
    mean = jnp.concatenate([own[0][1], own[1][1]], 1)
    root = jnp.sqrt(jnp.full((1, 1), members - 1.0, F32))
    result = (root * x3 + (shift[:1] + mean)).astype(BF)
    lane = lax.broadcasted_iota(jnp.int32, (2 * WIDTH, WIDTH), 0)
    target = lax.broadcasted_iota(jnp.int32, (2 * WIDTH, WIDTH), 1)
    narrow = (lane == (target // PATCH) * REGION + RADIUS + target % PATCH).astype(F32).astype(BF)
    result = jnp.dot(result, narrow, preferred_element_type=F32).astype(BF)
    for s in range(count):
        out_ref[s] = result[s * LOCAL : (s + 1) * LOCAL]


def unpack_kernel(own_ref, near_ref, out_ref):
    count = own_ref.shape[0]

    def rows_of(ref):
        parts = swap_blocks([ref[p].astype(F32) for p in range(count)], PATCH)
        half = BAND // 2
        return [
            [parts[h * FIELDS * half + field * half + r] for h in range(2) for r in range(half)]
            for field in range(FIELDS)
        ]

    own, near = rows_of(own_ref), rows_of(near_ref)
    fields = [n[BAND - FSTEPS :] + o + n[:FSTEPS] for o, n in zip(own, near)]
    done = forecast_rows(*fields)
    for field in range(FIELDS):
        for r in range(BAND):
            out_ref[pl.ds(field * BAND + r, LOCAL, stride=FIELDS * BAND), :] = done[field][r]


def from_next(value):
    count = lax.axis_size("rows")
    return lax.ppermute(value, "rows", [((i + 1) % count, i) for i in range(count)])


def from_previous(value):
    count = lax.axis_size("rows")
    return lax.ppermute(value, "rows", [(i, (i + 1) % count) for i in range(count)])


def near_rows(value, join):
    if lax.axis_size("rows") == 2:
        return from_next(value)
    return join(from_next(value), from_previous(value))


def join_grid(after, before):
    return jnp.concatenate([after[:, :, : BAND // 2], before[:, :, BAND // 2 :]], 2)


def join_region(after, before):
    tail = jnp.concatenate([after[:, :8, 2 * WIDTH :], before[:, 8:, 2 * WIDTH :]], 1)
    return jnp.concatenate([after[..., :WIDTH], before[..., WIDTH : 2 * WIDTH], tail], 2)


def join_inner(after, before):
    return jnp.concatenate([after[..., : WIDTH // 2], before[..., WIDTH // 2 :]], 2)


def vmem(count):
    return [pl.BlockSpec(memory_space=pltpu.VMEM)] * count


def observation_rows(obs_values, obs_inverse_variance, obs_mask):
    weight = (obs_mask.astype(F32) * obs_inverse_variance).astype(BF).astype(F32)
    high = obs_values.astype(BF).astype(F32)
    rest = obs_values - high
    middle = rest.astype(BF).astype(F32)
    low = rest - middle
    rows = jnp.stack([weight, high, middle, low], 0)
    rows = rows.reshape(4, FIELDS, 2, BAND // 2, PATCH)
    rows = jnp.transpose(rows, (2, 0, 1, 3, 4))
    rows = jnp.pad(rows, ((0, 0), (2, 2), (0, 0), (0, 0), (0, REGION - PATCH)))
    return rows.reshape(16, WIDTH)


def local(sample_collection, obs_values, obs_inverse_variance, obs_mask):
    count = lax.axis_size("mem")
    shape = sample_collection.shape
    assert shape == (LOCAL, FIELDS, BAND, WIDTH) and count * PATCH == WIDTH
    near = near_rows(sample_collection, join_grid)
    obs = observation_rows(obs_values, obs_inverse_variance, obs_mask)
    sending = pl.pallas_call(
        pack_kernel,
        out_shape=jax.ShapeDtypeStruct((count, LOCAL, 3 * WIDTH), BF),
        in_specs=vmem(3),
        out_specs=vmem(1)[0],
        name="forecast_pack",
    )(sample_collection.reshape(-1, WIDTH), near.reshape(-1, WIDTH), obs)
    region = lax.all_to_all(sending, "mem", split_axis=0, concat_axis=0, tiled=True)
    region_near = near_rows(region, join_region)
    me = lax.axis_index("mem").astype(jnp.int32).reshape(1)
    returning = pl.pallas_call(
        analysis_kernel,
        out_shape=jax.ShapeDtypeStruct((count, LOCAL, WIDTH), BF),
        in_specs=[pl.BlockSpec(memory_space=pltpu.SMEM)] + vmem(2),
        out_specs=vmem(1)[0],
        name="analysis",
    )(me, region, region_near)
    inner = lax.all_to_all(returning, "mem", split_axis=0, concat_axis=0, tiled=True)
    inner_near = near_rows(inner, join_inner)
    cycled = pl.pallas_call(
        unpack_kernel,
        out_shape=jax.ShapeDtypeStruct((LOCAL * FIELDS * BAND, WIDTH), F32),
        in_specs=vmem(2),
        out_specs=vmem(1)[0],
        name="unpack_forecast",
    )(inner, inner_near)
    return cycled.reshape(shape)


def solution(mesh):
    return jax.shard_map(
        local,
        mesh=mesh,
        in_specs=(
            P("mem", None, "rows", None),
            P(None, "rows", "mem"),
            P(None, "rows", "mem"),
            P(None, "rows", "mem"),
        ),
        out_specs=P("mem", None, "rows", None),
        check_vma=False,
    )
```

```python
import functools

import jax
import jax.numpy as jnp
from jax import lax
from jax.experimental import pallas as pl
from jax.experimental.pallas import tpu as pltpu
from jax.sharding import PartitionSpec as P

PATCH = 8
RADIUS = 4
FSTEPS = 4
CADV = 0.05

LOCAL = 16
FIELDS = 2
BAND = 8
WIDTH = 128
REGION = PATCH + 2 * RADIUS
HALF = FIELDS * (BAND // 2) * REGION
BLOCKS = 2 * FIELDS * (BAND // 2)

BF = jnp.bfloat16
F32 = jnp.float32


def forecast_rows(u_rows, v_rows):
    for _ in range(FSTEPS):
        new_u, new_v = [], []
        for i in range(1, len(u_rows) - 1):
            cu, cv = CADV * u_rows[i], CADV * v_rows[i]
            for rows, new in ((u_rows, new_u), (v_rows, new_v)):
                along_x = pltpu.roll(rows[i], WIDTH - 1, 1) - pltpu.roll(rows[i], 1, 1)
                along_y = rows[i + 1] - rows[i - 1]
                new.append(rows[i] - (cu * along_x + cv * along_y))
        u_rows, v_rows = new_u, new_v
    return u_rows, v_rows


def swap_blocks(parts, size):
    count = len(parts)
    lane = lax.broadcasted_iota(jnp.int32, parts[0].shape, 1) // size
    stride = 1
    while stride < count:
        upper = (lane & stride) != 0
        new = list(parts)
        for j in range(count):
            if j & stride == 0:
                a, b = parts[j], parts[j + stride]
                new[j] = jnp.where(upper, pltpu.roll(b, stride * size, 1), a)
                new[j + stride] = jnp.where(upper, b, pltpu.roll(a, WIDTH - stride * size, 1))
        parts = new
        stride *= 2
    return parts


def pack_kernel(x_ref, near_ref, obs_ref, out_ref):
    stride = FIELDS * BAND

    def row(ref, field, index):
        return ref[pl.ds(field * BAND + index, LOCAL, stride=stride), :]

    fields = []
    for field in range(FIELDS):
        before = [row(near_ref, field, r) for r in range(BAND - FSTEPS, BAND)]
        own = [row(x_ref, field, r) for r in range(BAND)]
        after = [row(near_ref, field, r) for r in range(FSTEPS)]
        fields.append(before + own + after)
    done = forecast_rows(*fields)
    stacked = []
    for half in range(2):
        for field in range(FIELDS):
            for r in range(BAND // 2):
                value = done[field][half * (BAND // 2) + r]
                mean = jnp.sum(value, 0, keepdims=True) * (1.0 / LOCAL)
                high = mean.astype(BF).astype(F32)
                low = mean - high
                index = lax.broadcasted_iota(jnp.int32, (8, WIDTH), 0)
                tail = jnp.where(index == 0, high, jnp.where(index == 1, low, 0.0))
                stacked += [value - mean, tail]
    rows = jnp.concatenate(stacked, 0).astype(BF)
    column = lax.broadcasted_iota(jnp.int32, (WIDTH, 2 * WIDTH), 0)
    lane = lax.broadcasted_iota(jnp.int32, (WIDTH, 2 * WIDTH), 1)
    wanted = ((lane // REGION) * PATCH + lane % REGION + (WIDTH - RADIUS)) % WIDTH
    widen = (column == wanted).astype(F32).astype(BF)
    wide = jnp.dot(rows, widen, preferred_element_type=F32)
    height = LOCAL + 8
    for side in range(2):
        tails = [[], []]
        for half in range(2):
            parts = [
                wide[(half * 8 + j) * height : (half * 8 + j + 1) * height, side * WIDTH : (side + 1) * WIDTH]
                for j in range(8)
            ]
            parts = swap_blocks(parts, REGION)
            for i in range(8):
                out_ref[side * 8 + i, :, half * WIDTH : (half + 1) * WIDTH] = parts[i][:LOCAL].astype(BF)
                tails[half].append(parts[i][LOCAL:])
        for i in range(8):
            tail = jnp.concatenate([tails[0][i], tails[1][i]], 0) + obs_ref[...]
            out_ref[side * 8 + i, :, 2 * WIDTH :] = tail.astype(BF)


def halves_of(ref, me, count):
    tails = [ref[s, :, 2 * WIDTH :].astype(F32) for s in range(count)]
    lane = lax.broadcasted_iota(jnp.int32, (16, WIDTH), 1) % REGION
    left = ref[lax.rem(me + count - 1, count), :, 2 * WIDTH :].astype(F32)
    own = ref[me, :, 2 * WIDTH :].astype(F32)
    right = ref[lax.rem(me + 1, count), :, 2 * WIDTH :].astype(F32)
    seen = jnp.where(
        lane < RADIUS,
        pltpu.roll(left, WIDTH - (PATCH - RADIUS), 1),
        jnp.where(lane < RADIUS + PATCH, pltpu.roll(own, RADIUS, 1), pltpu.roll(right, RADIUS + PATCH, 1)),
    )
    result = []
    for half in range(2):
        base = half * 8
        means = [t[base : base + 1] + t[base + 1 : base + 2] for t in tails]
        mean = functools.reduce(jnp.add, means) * (1.0 / count)
        deviation = jnp.concatenate(
            [
                (ref[s, :, half * WIDTH : (half + 1) * WIDTH].astype(F32) + (means[s] - mean)).astype(BF)
                for s in range(count)
            ],
            0,
        )
        weight = seen[base + 2 : base + 3]
        obs = seen[base + 3 : base + 4] + seen[base + 4 : base + 5] + seen[base + 5 : base + 6]
        innovation = (obs - mean).astype(BF).astype(F32)
        result.append((deviation, mean, weight, innovation))
    return result


def analysis_kernel(me_ref, own_ref, near_ref, out_ref):
    count = own_ref.shape[0]
    members = count * LOCAL
    me = me_ref[0]
    own = halves_of(own_ref, me, count)
    near = halves_of(near_ref, me, count)
    lane = lax.broadcasted_iota(jnp.int32, (1, WIDTH), 1)
    region_column = lane % REGION
    half_row = (lane // REGION) % (BAND // 2)
    column_distance = jnp.maximum(
        jnp.maximum(RADIUS - region_column, region_column - (RADIUS + PATCH - 1)), 0
    )
    row_distances = (0 * lane, 0 * lane, half_row + 1, RADIUS - half_row)
    weighted, deviation, innovation = [], [], []
    for (dev, _, weight, inno), row_distance in zip(own + near, row_distances):
        far = jnp.maximum(row_distance, column_distance).astype(F32)
        factor = weight * (1.0 - far / (RADIUS + 1.0))
        weighted.append((dev.astype(F32) * factor).astype(BF))
        deviation.append(dev)
        innovation.append(jnp.broadcast_to(inno, (16, WIDTH)).astype(BF))
    weighted = jnp.concatenate(weighted, 1)
    inner = jnp.concatenate(deviation[:2], 1)
    rows = jnp.concatenate([jnp.concatenate(deviation, 1), jnp.concatenate(innovation, 1)], 0)
    both = lax.dot_general(rows, weighted, (((1,), (1,)), ((), ())), preferred_element_type=F32)
    row = lax.broadcasted_iota(jnp.int32, (members, members), 0)
    col = lax.broadcasted_iota(jnp.int32, (members, members), 1)
    system = both[:members] + jnp.where(row == col, members - 1.0, 0.0)
    line = both[members:]
    scale = jnp.sqrt(jnp.sum(system * system))
    y0 = system * (1.0 / scale)

    def mul(a, b):
        return jnp.dot(a.astype(BF), b.astype(BF), preferred_element_type=F32)

    y0b = y0.astype(BF)
    inner_f = inner.astype(F32)
    x1 = 1.5 * inner_f - 0.5 * mul(y0b, inner)
    line1 = 1.5 * line - 0.5 * mul(line, y0b)
    y1 = 1.5 * y0 - 0.5 * mul(y0b, y0b)
    p1 = 1.5 * y1 - 0.5 * mul(y1, y0b)
    p1b = p1.astype(BF)
    x2 = 1.5 * x1 - 0.5 * mul(p1b, x1)
    line2 = 1.5 * line1 - 0.5 * mul(line1, p1b)
    q1 = 1.5 * p1 - 0.5 * mul(p1b, p1b)
    p2 = 1.5 * q1 - 0.5 * mul(q1, p1b)
    p2b = p2.astype(BF)
    x3 = 1.5 * x2 - 0.5 * mul(p2b, x2)
    line3 = 1.5 * line2 - 0.5 * mul(line2, p2b)
    inverse = 1.0 / jnp.sqrt(scale)
    x3 = x3 * inverse
    line3 = line3 * inverse
    xh = x3.astype(BF)
    xl = (x3 - xh.astype(F32)).astype(BF)
    lh = line3.astype(BF)
    ll = (line3 - lh.astype(F32)).astype(BF)
    shift = mul(lh, xh) + (mul(ll, xh) + mul(lh, xl))
    mean = jnp.concatenate([own[0][1], own[1][1]], 1)
    root = jnp.sqrt(jnp.full((1, 1), members - 1.0, F32))
    result = (root * x3 + (shift[:1] + mean)).astype(BF)
    lane = lax.broadcasted_iota(jnp.int32, (2 * WIDTH, WIDTH), 0)
    target = lax.broadcasted_iota(jnp.int32, (2 * WIDTH, WIDTH), 1)
    narrow = (lane == (target // PATCH) * REGION + RADIUS + target % PATCH).astype(F32).astype(BF)
    result = jnp.dot(result, narrow, preferred_element_type=F32).astype(BF)
    for s in range(count):
        out_ref[s] = result[s * LOCAL : (s + 1) * LOCAL]


def unpack_kernel(own_ref, near_ref, out_ref):
    count = own_ref.shape[0]

    def rows_of(ref):
        parts = swap_blocks([ref[p].astype(F32) for p in range(count)], PATCH)
        half = BAND // 2
        return [
            [parts[h * FIELDS * half + field * half + r] for h in range(2) for r in range(half)]
            for field in range(FIELDS)
        ]

    own, near = rows_of(own_ref), rows_of(near_ref)
    fields = [n[BAND - FSTEPS :] + o + n[:FSTEPS] for o, n in zip(own, near)]
    done = forecast_rows(*fields)
    for field in range(FIELDS):
        for r in range(BAND):
            out_ref[pl.ds(field * BAND + r, LOCAL, stride=FIELDS * BAND), :] = done[field][r]


def from_next(value):
    count = lax.axis_size("rows")
    return lax.ppermute(value, "rows", [((i + 1) % count, i) for i in range(count)])


def from_previous(value):
    count = lax.axis_size("rows")
    return lax.ppermute(value, "rows", [(i, (i + 1) % count) for i in range(count)])


def near_rows(value, join):
    if lax.axis_size("rows") == 2:
        return from_next(value)
    return join(from_next(value), from_previous(value))


def join_grid(after, before):
    return jnp.concatenate([after[:, :, : BAND // 2], before[:, :, BAND // 2 :]], 2)


def join_region(after, before):
    tail = jnp.concatenate([after[:, :8, 2 * WIDTH :], before[:, 8:, 2 * WIDTH :]], 1)
    return jnp.concatenate([after[..., :WIDTH], before[..., WIDTH : 2 * WIDTH], tail], 2)


def join_inner(after, before):
    return jnp.concatenate([after[..., : WIDTH // 2], before[..., WIDTH // 2 :]], 2)


def vmem(count):
    return [pl.BlockSpec(memory_space=pltpu.VMEM)] * count


def observation_rows(obs_values, obs_inverse_variance, obs_mask):
    weight = (obs_mask.astype(F32) * obs_inverse_variance).astype(BF).astype(F32)
    high = obs_values.astype(BF).astype(F32)
    rest = obs_values - high
    middle = rest.astype(BF).astype(F32)
    low = rest - middle
    rows = jnp.stack([weight, high, middle, low], 0)
    rows = rows.reshape(4, FIELDS, 2, BAND // 2, PATCH)
    rows = jnp.transpose(rows, (2, 0, 1, 3, 4))
    rows = jnp.pad(rows, ((0, 0), (2, 2), (0, 0), (0, 0), (0, REGION - PATCH)))
    return rows.reshape(16, WIDTH)


def local(sample_collection, obs_values, obs_inverse_variance, obs_mask):
    count = lax.axis_size("mem")
    shape = sample_collection.shape
    assert shape == (LOCAL, FIELDS, BAND, WIDTH) and count * PATCH == WIDTH
    near = near_rows(sample_collection, join_grid)
    obs = observation_rows(obs_values, obs_inverse_variance, obs_mask)
    sending = pl.pallas_call(
        pack_kernel,
        out_shape=jax.ShapeDtypeStruct((count, LOCAL, 3 * WIDTH), BF),
        in_specs=vmem(3),
        out_specs=vmem(1)[0],
        compiler_params=pltpu.CompilerParams(vmem_limit_bytes=16 * 2**20),
        name="forecast_pack",
    )(sample_collection.reshape(-1, WIDTH), near.reshape(-1, WIDTH), obs)
    region = lax.all_to_all(sending, "mem", split_axis=0, concat_axis=0, tiled=True)
    region_near = near_rows(region, join_region)
    me = lax.axis_index("mem").astype(jnp.int32).reshape(1)
    returning = pl.pallas_call(
        analysis_kernel,
        out_shape=jax.ShapeDtypeStruct((count, LOCAL, WIDTH), BF),
        in_specs=[pl.BlockSpec(memory_space=pltpu.SMEM)] + vmem(2),
        out_specs=vmem(1)[0],
        compiler_params=pltpu.CompilerParams(vmem_limit_bytes=16 * 2**20),
        name="analysis",
    )(me, region, region_near)
    inner = lax.all_to_all(returning, "mem", split_axis=0, concat_axis=0, tiled=True)
    inner_near = near_rows(inner, join_inner)
    cycled = pl.pallas_call(
        unpack_kernel,
        out_shape=jax.ShapeDtypeStruct((LOCAL * FIELDS * BAND, WIDTH), F32),
        in_specs=vmem(2),
        out_specs=vmem(1)[0],
        compiler_params=pltpu.CompilerParams(vmem_limit_bytes=16 * 2**20),
        name="unpack_forecast",
    )(inner, inner_near)
    return cycled.reshape(shape)


def solution(mesh):
    return jax.shard_map(
        local,
        mesh=mesh,
        in_specs=(
            P("mem", None, "rows", None),
            P(None, "rows", "mem"),
            P(None, "rows", "mem"),
            P(None, "rows", "mem"),
        ),
        out_specs=P("mem", None, "rows", None),
        check_vma=False,
    )
```

```python
import functools

import jax
import jax.numpy as jnp
from jax import lax
from jax.experimental import pallas as pl
from jax.experimental.pallas import tpu as pltpu
from jax.sharding import PartitionSpec as P

PATCH = 8
RADIUS = 4
FSTEPS = 4
CADV = 0.05

LOCAL = 16
FIELDS = 2
BAND = 8
WIDTH = 128
REGION = PATCH + 2 * RADIUS
GROUP = 4

BF = jnp.bfloat16
F32 = jnp.float32


def forecast_rows(u_rows, v_rows):
    for _ in range(FSTEPS):
        new_u, new_v = [], []
        for i in range(1, len(u_rows) - 1):
            cu, cv = CADV * u_rows[i], CADV * v_rows[i]
            for rows, new in ((u_rows, new_u), (v_rows, new_v)):
                along_x = pltpu.roll(rows[i], WIDTH - 1, 1) - pltpu.roll(rows[i], 1, 1)
                along_y = rows[i + 1] - rows[i - 1]
                new.append(rows[i] - (cu * along_x + cv * along_y))
        u_rows, v_rows = new_u, new_v
    return u_rows, v_rows


def swap_blocks(parts, size):
    count = len(parts)
    lane = lax.broadcasted_iota(jnp.int32, parts[0].shape, 1) // size
    stride = 1
    while stride < count:
        upper = (lane & stride) != 0
        new = list(parts)
        for j in range(count):
            if j & stride == 0:
                a, b = parts[j], parts[j + stride]
                new[j] = jnp.where(upper, pltpu.roll(b, stride * size, 1), a)
                new[j + stride] = jnp.where(upper, b, pltpu.roll(a, WIDTH - stride * size, 1))
        parts = new
        stride *= 2
    return parts


def xor_blocks(me, high, low):
    return ((me // GROUP) ^ high) * GROUP + ((me % GROUP) ^ low)


def observation_rows(values_ref, inverse_ref, mask_ref):
    points = FIELDS * BAND
    weight = (mask_ref[...].astype(F32) * inverse_ref[...]).astype(BF).astype(F32).reshape(points, PATCH)
    values = values_ref[...].reshape(points, PATCH)
    high = values.astype(BF).astype(F32)
    middle = (values - high).astype(BF).astype(F32)
    low = values - high - middle
    rows = jnp.concatenate([weight, high, middle, low], 0).astype(BF)
    source = lax.broadcasted_iota(jnp.int32, (PATCH, WIDTH), 0)
    lane = lax.broadcasted_iota(jnp.int32, (PATCH, WIDTH), 1)
    spread = (lane % PATCH == source).astype(F32).astype(BF)
    wide = jnp.dot(rows, spread, preferred_element_type=F32)
    row = lax.broadcasted_iota(jnp.int32, wide.shape, 0)
    lane = lax.broadcasted_iota(jnp.int32, wide.shape, 1)
    part, field, y = row // points, (row % points) // BAND, row % BAND
    place = (field * (BAND // 2) + y % (BAND // 2)) * 2 + part % 2
    wide = jnp.where(lane // PATCH == place, wide, 0.0).astype(BF)
    target = lax.broadcasted_iota(jnp.int32, (8, 4 * points), 0)
    row = lax.broadcasted_iota(jnp.int32, (8, 4 * points), 1)
    wanted = ((row % BAND) // (BAND // 2)) * 4 + 2 + row // (2 * points)
    gather = (target == wanted).astype(F32).astype(BF)
    return jnp.dot(gather, wide, preferred_element_type=F32)


def pack_kernel(me_ref, x_ref, near_ref, values_ref, inverse_ref, mask_ref, *refs):
    outs, blocks = refs[:GROUP], refs[GROUP]
    stride = FIELDS * BAND

    def row(ref, field, index):
        return ref[pl.ds(field * BAND + index, LOCAL, stride=stride), :]

    fields = []
    for field in range(FIELDS):
        before = [row(near_ref, field, r) for r in range(BAND - FSTEPS, BAND)]
        own = [row(x_ref, field, r) for r in range(BAND)]
        after = [row(near_ref, field, r) for r in range(FSTEPS)]
        fields.append(before + own + after)
    done = forecast_rows(*fields)
    stacked = []
    index = lax.broadcasted_iota(jnp.int32, (8, WIDTH), 0)
    for half in range(2):
        for field in range(FIELDS):
            for r in range(BAND // 2):
                value = done[field][half * (BAND // 2) + r]
                mean = jnp.sum(value, 0, keepdims=True) * (1.0 / LOCAL)
                high = mean.astype(BF).astype(F32)
                low = mean - high
                tail = jnp.where(index == 4 * half, high, jnp.where(index == 4 * half + 1, low, 0.0))
                stacked += [value - mean, tail]
    rows = jnp.concatenate(stacked, 0).astype(BF)
    column = lax.broadcasted_iota(jnp.int32, (WIDTH, 2 * WIDTH), 0)
    lane = lax.broadcasted_iota(jnp.int32, (WIDTH, 2 * WIDTH), 1)
    wanted = ((lane // REGION) * PATCH + lane % REGION + (WIDTH - RADIUS)) % WIDTH
    widen = (column == wanted).astype(F32).astype(BF)
    wide = jnp.dot(rows, widen, preferred_element_type=F32)
    height = LOCAL + 8
    obs = observation_rows(values_ref, inverse_ref, mask_ref)
    for side in range(2):
        tails = [obs] * 8
        for half in range(2):
            parts = [
                wide[(half * 8 + j) * height : (half * 8 + j + 1) * height, side * WIDTH : (side + 1) * WIDTH]
                for j in range(8)
            ]
            parts = swap_blocks(parts, REGION)
            for i in range(8):
                for eight in range(2):
                    blocks[side * 8 + i, half * 2 + eight] = parts[i][eight * 8 : eight * 8 + 8].astype(BF)
                tails[i] = tails[i] + parts[i][LOCAL:]
        for i in range(8):
            blocks[side * 8 + i, 4] = tails[i].astype(BF)
    low = me_ref[0] % GROUP
    for k in range(GROUP):
        for high in range(GROUP):
            outs[k][high] = blocks[high * GROUP + (low ^ k)]


def regroup_region_kernel(me_ref, *refs):
    ins, outs = refs[:GROUP], refs[GROUP:]
    high = me_ref[0] // GROUP
    for j in range(GROUP):
        for k in range(GROUP):
            outs[j][k] = ins[k][high ^ j]


def regroup_inner_kernel(*refs):
    ins, outs = refs[:GROUP], refs[GROUP:]
    for k in range(GROUP):
        for j in range(GROUP):
            outs[k][j] = ins[j][k]


def halves_of(refs, tail_ref, me):
    count = GROUP * GROUP
    blocks = [(refs[j], k) for j in range(GROUP) for k in range(GROUP)]
    tails = [ref[k, 4].astype(F32) for ref, k in blocks]
    for s in range(count):
        tail_ref[s] = tails[s]

    def tail_of(device):
        return tail_ref[xor_blocks(me, device // GROUP, device % GROUP)]

    lane = lax.broadcasted_iota(jnp.int32, (8, WIDTH), 1) % REGION
    left = tail_of(lax.rem(me + count - 1, count))
    own = tails[0]
    right = tail_of(lax.rem(me + 1, count))

    def seen(offset):
        return jnp.where(
            lane < RADIUS,
            pltpu.roll(left, (WIDTH + RADIUS - PATCH - offset) % WIDTH, 1),
            jnp.where(
                lane < RADIUS + PATCH,
                pltpu.roll(own, (WIDTH + RADIUS - offset) % WIDTH, 1),
                pltpu.roll(right, (WIDTH + RADIUS + PATCH - offset) % WIDTH, 1),
            ),
        )

    first, second = seen(0), seen(PATCH)
    result = []
    for half in range(2):
        base = half * 4
        means = [t[base : base + 1] + t[base + 1 : base + 2] for t in tails]
        mean = functools.reduce(jnp.add, means) * (1.0 / count)
        deviation = []
        for (ref, k), own_mean in zip(blocks, means):
            value = jnp.concatenate([ref[k, half * 2 + eight].astype(F32) for eight in range(2)], 0)
            deviation.append((value + (own_mean - mean)).astype(BF))
        weight = first[base + 2 : base + 3]
        obs = second[base + 2 : base + 3] + first[base + 3 : base + 4] + second[base + 3 : base + 4]
        innovation = (obs - mean).astype(BF).astype(F32)
        result.append((jnp.concatenate(deviation, 0), mean, weight, innovation))
    return result


def analysis_kernel(me_ref, *refs):
    own_refs, near_refs, outs = refs[:GROUP], refs[GROUP : 2 * GROUP], refs[2 * GROUP : 3 * GROUP]
    tail_ref, near_tail_ref = refs[3 * GROUP :]
    members = GROUP * GROUP * LOCAL
    me = me_ref[0]
    own = halves_of(own_refs, tail_ref, me)
    near = halves_of(near_refs, near_tail_ref, me)
    lane = lax.broadcasted_iota(jnp.int32, (1, WIDTH), 1)
    region_column = lane % REGION
    half_row = (lane // REGION) % (BAND // 2)
    column_distance = jnp.maximum(
        jnp.maximum(RADIUS - region_column, region_column - (RADIUS + PATCH - 1)), 0
    )
    row_distances = (0 * lane, 0 * lane, half_row + 1, RADIUS - half_row)
    weighted, deviation, innovation = [], [], []
    for (dev, _, weight, inno), row_distance in zip(own + near, row_distances):
        far = jnp.maximum(row_distance, column_distance).astype(F32)
        factor = weight * (1.0 - far / (RADIUS + 1.0))
        weighted.append((dev.astype(F32) * factor).astype(BF))
        deviation.append(dev)
        innovation.append(jnp.broadcast_to(inno, (16, WIDTH)).astype(BF))
    weighted = jnp.concatenate(weighted, 1)
    inner = jnp.concatenate(deviation[:2], 1)
    rows = jnp.concatenate([jnp.concatenate(deviation, 1), jnp.concatenate(innovation, 1)], 0)
    both = lax.dot_general(rows, weighted, (((1,), (1,)), ((), ())), preferred_element_type=F32)
    row = lax.broadcasted_iota(jnp.int32, (members, members), 0)
    col = lax.broadcasted_iota(jnp.int32, (members, members), 1)
    system = both[:members] + jnp.where(row == col, members - 1.0, 0.0)
    line = both[members:]
    scale = jnp.sqrt(jnp.sum(system * system))
    y0 = system * (1.0 / scale)

    def mul(a, b):
        return jnp.dot(a.astype(BF), b.astype(BF), preferred_element_type=F32)

    y0b = y0.astype(BF)
    inner_f = inner.astype(F32)
    x1 = 1.5 * inner_f - 0.5 * mul(y0b, inner)
    line1 = 1.5 * line - 0.5 * mul(line, y0b)
    y1 = 1.5 * y0 - 0.5 * mul(y0b, y0b)
    p1 = 1.5 * y1 - 0.5 * mul(y1, y0b)
    p1b = p1.astype(BF)
    x2 = 1.5 * x1 - 0.5 * mul(p1b, x1)
    line2 = 1.5 * line1 - 0.5 * mul(line1, p1b)
    q1 = 1.5 * p1 - 0.5 * mul(p1b, p1b)
    p2 = 1.5 * q1 - 0.5 * mul(q1, p1b)
    p2b = p2.astype(BF)
    x3 = 1.5 * x2 - 0.5 * mul(p2b, x2)
    line3 = 1.5 * line2 - 0.5 * mul(line2, p2b)
    inverse = 1.0 / jnp.sqrt(scale)
    x3 = x3 * inverse
    line3 = line3 * inverse
    xh = x3.astype(BF)
    xl = (x3 - xh.astype(F32)).astype(BF)
    lh = line3.astype(BF)
    ll = (line3 - lh.astype(F32)).astype(BF)
    shift = mul(lh, xh) + (mul(ll, xh) + mul(lh, xl))
    mean = jnp.concatenate([own[0][1], own[1][1]], 1)
    root = jnp.sqrt(jnp.full((1, 1), members - 1.0, F32))
    result = (root * x3 + (shift[:1] + mean)).astype(BF)
    lane = lax.broadcasted_iota(jnp.int32, (2 * WIDTH, WIDTH), 0)
    target = lax.broadcasted_iota(jnp.int32, (2 * WIDTH, WIDTH), 1)
    narrow = (lane == (target // PATCH) * REGION + RADIUS + target % PATCH).astype(F32).astype(BF)
    result = jnp.dot(result, narrow, preferred_element_type=F32).astype(BF)
    for j in range(GROUP):
        for k in range(GROUP):
            start = (j * GROUP + k) * LOCAL
            outs[j][k] = result[start : start + LOCAL]


def unpack_kernel(me_ref, *refs):
    own_refs, near_refs, out_ref = refs[:GROUP], refs[GROUP : 2 * GROUP], refs[2 * GROUP]
    me = me_ref[0]

    def rows_of(ins, blocks):
        for k in range(GROUP):
            for j in range(GROUP):
                blocks[xor_blocks(me, j, k)] = ins[k][j].astype(F32)
        parts = swap_blocks([blocks[p] for p in range(GROUP * GROUP)], PATCH)
        half = BAND // 2
        return [
            [parts[h * FIELDS * half + field * half + r] for h in range(2) for r in range(half)]
            for field in range(FIELDS)
        ]

    own, near = rows_of(own_refs, refs[2 * GROUP + 1]), rows_of(near_refs, refs[2 * GROUP + 2])
    fields = [n[BAND - FSTEPS :] + o + n[:FSTEPS] for o, n in zip(own, near)]
    done = forecast_rows(*fields)
    for field in range(FIELDS):
        for r in range(BAND):
            out_ref[pl.ds(field * BAND + r, LOCAL, stride=FIELDS * BAND), :] = done[field][r]


def from_next(value):
    count = lax.axis_size("rows")
    return lax.ppermute(value, "rows", [((i + 1) % count, i) for i in range(count)])


def from_previous(value):
    count = lax.axis_size("rows")
    return lax.ppermute(value, "rows", [(i, (i + 1) % count) for i in range(count)])


def near_rows(value, join):
    if lax.axis_size("rows") == 2:
        return from_next(value)
    return join(from_next(value), from_previous(value))


def join_grid(after, before):
    return jnp.concatenate([after[:, :, : BAND // 2], before[:, :, BAND // 2 :]], 2)


def join_region(after, before):
    tail = jnp.concatenate([after[:, 4:, :4], before[:, 4:, 4:]], 2)
    return jnp.concatenate([after[:, :2], before[:, 2:4], tail], 1)


def join_inner(after, before):
    return jnp.concatenate([after[..., : WIDTH // 2], before[..., WIDTH // 2 :]], 2)


def from_partner(value, distance):
    return lax.ppermute(value, "mem", [(i, i ^ distance) for i in range(lax.axis_size("mem"))])


def exchange(values, unit):
    return [values[0]] + [from_partner(values[k], k * unit) for k in range(1, GROUP)]


def call(kernel, name, out_shape, *args, scratch=()):
    spaces = [pltpu.SMEM if arg.shape == (1,) else pltpu.VMEM for arg in args]
    return pl.pallas_call(
        kernel,
        out_shape=out_shape,
        in_specs=[pl.BlockSpec(memory_space=space) for space in spaces],
        out_specs=jax.tree.map(lambda _: pl.BlockSpec(memory_space=pltpu.VMEM), out_shape),
        scratch_shapes=scratch,
        compiler_params=pltpu.CompilerParams(vmem_limit_bytes=16 * 2**20),
        name=name,
    )(*args)


def local(sample_collection, obs_values, obs_inverse_variance, obs_mask):
    count = lax.axis_size("mem")
    shape = sample_collection.shape
    assert shape == (LOCAL, FIELDS, BAND, WIDTH) and count * PATCH == WIDTH and count == GROUP * GROUP
    me = lax.axis_index("mem").astype(jnp.int32).reshape(1)
    near = near_rows(sample_collection, join_grid)
    region_shape = [jax.ShapeDtypeStruct((GROUP, 5, 8, WIDTH), BF)] * GROUP
    inner_shape = [jax.ShapeDtypeStruct((GROUP, LOCAL, WIDTH), BF)] * GROUP
    sending = call(
        pack_kernel,
        "forecast_pack",
        region_shape,
        me,
        sample_collection.reshape(-1, WIDTH),
        near.reshape(-1, WIDTH),
        obs_values,
        obs_inverse_variance,
        obs_mask,
        scratch=[pltpu.VMEM((count, 5, 8, WIDTH), BF)],
    )
    sending = call(regroup_region_kernel, "regroup_region", region_shape, me, *exchange(sending, 1))
    region = exchange(sending, GROUP)
    region_near = [near_rows(value, join_region) for value in region]
    returning = call(
        analysis_kernel,
        "analysis",
        inner_shape,
        me,
        *region,
        *region_near,
        scratch=[pltpu.VMEM((count, 8, WIDTH), F32)] * 2,
    )
    returning = call(regroup_inner_kernel, "regroup_inner", inner_shape, *exchange(returning, GROUP))
    inner = exchange(returning, 1)
    inner_near = [near_rows(value, join_inner) for value in inner]
    cycled = call(
        unpack_kernel,
        "unpack_forecast",
        jax.ShapeDtypeStruct((LOCAL * FIELDS * BAND, WIDTH), F32),
        me,
        *inner,
        *inner_near,
        scratch=[pltpu.VMEM((count, LOCAL, WIDTH), F32)] * 2,
    )
    return cycled.reshape(shape)


def solution(mesh):
    return jax.shard_map(
        local,
        mesh=mesh,
        in_specs=(
            P("mem", None, "rows", None),
            P(None, "rows", "mem"),
            P(None, "rows", "mem"),
            P(None, "rows", "mem"),
        ),
        out_specs=P("mem", None, "rows", None),
        check_vma=False,
    )
```

```python
import functools

import jax
import jax.numpy as jnp
from jax import lax
from jax.experimental import pallas as pl
from jax.experimental.pallas import tpu as pltpu
from jax.sharding import PartitionSpec as P

PATCH = 8
RADIUS = 4
FSTEPS = 4
CADV = 0.05

LOCAL = 16
FIELDS = 2
BAND = 8
WIDTH = 128
REGION = PATCH + 2 * RADIUS
GROUP = 4

BF = jnp.bfloat16
F32 = jnp.float32


def forecast_rows(u_rows, v_rows):
    for _ in range(FSTEPS):
        new_u, new_v = [], []
        for i in range(1, len(u_rows) - 1):
            cu, cv = CADV * u_rows[i], CADV * v_rows[i]
            for rows, new in ((u_rows, new_u), (v_rows, new_v)):
                along_x = pltpu.roll(rows[i], WIDTH - 1, 1) - pltpu.roll(rows[i], 1, 1)
                along_y = rows[i + 1] - rows[i - 1]
                new.append(rows[i] - (cu * along_x + cv * along_y))
        u_rows, v_rows = new_u, new_v
    return u_rows, v_rows


def swap_blocks(parts, size):
    count = len(parts)
    lane = lax.broadcasted_iota(jnp.int32, parts[0].shape, 1) // size
    stride = 1
    while stride < count:
        upper = (lane & stride) != 0
        new = list(parts)
        for j in range(count):
            if j & stride == 0:
                a, b = parts[j], parts[j + stride]
                new[j] = jnp.where(upper, pltpu.roll(b, stride * size, 1), a)
                new[j + stride] = jnp.where(upper, b, pltpu.roll(a, WIDTH - stride * size, 1))
        parts = new
        stride *= 2
    return parts


def observation_rows(values_ref, inverse_ref, mask_ref):
    points = FIELDS * BAND
    weight = (mask_ref[...].astype(F32) * inverse_ref[...]).astype(BF).astype(F32).reshape(points, PATCH)
    values = values_ref[...].reshape(points, PATCH)
    high = values.astype(BF).astype(F32)
    middle = (values - high).astype(BF).astype(F32)
    low = values - high - middle
    rows = jnp.concatenate([weight, high, middle, low], 0).astype(BF)
    source = lax.broadcasted_iota(jnp.int32, (PATCH, WIDTH), 0)
    lane = lax.broadcasted_iota(jnp.int32, (PATCH, WIDTH), 1)
    spread = (lane % PATCH == source).astype(F32).astype(BF)
    wide = jnp.dot(rows, spread, preferred_element_type=F32)
    row = lax.broadcasted_iota(jnp.int32, wide.shape, 0)
    lane = lax.broadcasted_iota(jnp.int32, wide.shape, 1)
    part, field, y = row // points, (row % points) // BAND, row % BAND
    place = (field * (BAND // 2) + y % (BAND // 2)) * 2 + part % 2
    wide = jnp.where(lane // PATCH == place, wide, 0.0).astype(BF)
    target = lax.broadcasted_iota(jnp.int32, (8, 4 * points), 0)
    row = lax.broadcasted_iota(jnp.int32, (8, 4 * points), 1)
    wanted = ((row % BAND) // (BAND // 2)) * 4 + 2 + row // (2 * points)
    gather = (target == wanted).astype(F32).astype(BF)
    return jnp.dot(gather, wide, preferred_element_type=F32)


def prepare_kernel(*refs):
    sources, rows_ref, obs_ref, held, sems = refs[:4], refs[4], refs[5], refs[6:10], refs[10]
    points = FIELDS * BAND
    copies = [pltpu.make_async_copy(a, b, sems.at[i]) for i, (a, b) in enumerate(zip(sources, held))]
    for copy in copies:
        copy.start()
    for copy in copies:
        copy.wait()
    for i in range(points):
        rows_ref[i] = held[0][pl.ds(i, LOCAL, stride=points), :]
    obs_ref[...] = observation_rows(*held[1:])


def pack_kernel(rows_ref, near_ref, obs_ref, out_ref):
    points = FIELDS * BAND

    def near(field, index):
        return near_ref[pl.ds(field * BAND + index, LOCAL, stride=points), :]

    fields = []
    for field in range(FIELDS):
        before = [near(field, r) for r in range(BAND - FSTEPS, BAND)]
        own = [rows_ref[field * BAND + r] for r in range(BAND)]
        after = [near(field, r) for r in range(FSTEPS)]
        fields.append(before + own + after)
    done = forecast_rows(*fields)
    stacked = []
    index = lax.broadcasted_iota(jnp.int32, (8, WIDTH), 0)
    for half in range(2):
        for field in range(FIELDS):
            for r in range(BAND // 2):
                value = done[field][half * (BAND // 2) + r]
                mean = jnp.sum(value, 0, keepdims=True) * (1.0 / LOCAL)
                high = mean.astype(BF).astype(F32)
                low = mean - high
                tail = jnp.where(index == 4 * half, high, jnp.where(index == 4 * half + 1, low, 0.0))
                stacked += [value - mean, tail]
    rows = jnp.concatenate(stacked, 0).astype(BF)
    column = lax.broadcasted_iota(jnp.int32, (WIDTH, 2 * WIDTH), 0)
    lane = lax.broadcasted_iota(jnp.int32, (WIDTH, 2 * WIDTH), 1)
    wanted = ((lane // REGION) * PATCH + lane % REGION + (WIDTH - RADIUS)) % WIDTH
    widen = (column == wanted).astype(F32).astype(BF)
    wide = jnp.dot(rows, widen, preferred_element_type=F32)
    height = LOCAL + 8
    obs = obs_ref[...]
    for side in range(2):
        tails = [obs] * 8
        for half in range(2):
            parts = [
                wide[(half * 8 + j) * height : (half * 8 + j + 1) * height, side * WIDTH : (side + 1) * WIDTH]
                for j in range(8)
            ]
            parts = swap_blocks(parts, REGION)
            for i in range(8):
                for eight in range(2):
                    out_ref[i % GROUP, side * 2 + i // GROUP, half * 2 + eight] = parts[i][eight * 8 : eight * 8 + 8].astype(BF)
                tails[i] = tails[i] + parts[i][LOCAL:]
        for i in range(8):
            out_ref[i % GROUP, side * 2 + i // GROUP, 4] = tails[i].astype(BF)


def regroup_kernel(in_ref, out_ref):
    for i in range(GROUP):
        for j in range(GROUP):
            out_ref[j, i] = in_ref[i, j]


def halves_of(ref, me):
    count = GROUP * GROUP
    tails = [ref[s // GROUP, s % GROUP, 4].astype(F32) for s in range(count)]

    def tail_of(device):
        return ref[device // GROUP, device % GROUP, 4].astype(F32)

    lane = lax.broadcasted_iota(jnp.int32, (8, WIDTH), 1) % REGION
    left = tail_of(lax.rem(me + count - 1, count))
    own = tail_of(me)
    right = tail_of(lax.rem(me + 1, count))

    def seen(offset):
        return jnp.where(
            lane < RADIUS,
            pltpu.roll(left, (WIDTH + RADIUS - PATCH - offset) % WIDTH, 1),
            jnp.where(
                lane < RADIUS + PATCH,
                pltpu.roll(own, (WIDTH + RADIUS - offset) % WIDTH, 1),
                pltpu.roll(right, (WIDTH + RADIUS + PATCH - offset) % WIDTH, 1),
            ),
        )

    first, second = seen(0), seen(PATCH)
    result = []
    for half in range(2):
        base = half * 4
        means = [t[base : base + 1] + t[base + 1 : base + 2] for t in tails]
        mean = functools.reduce(jnp.add, means) * (1.0 / count)
        deviation = []
        for s, own_mean in enumerate(means):
            block = ref.at[s // GROUP, s % GROUP]
            value = jnp.concatenate([block[half * 2 + eight].astype(F32) for eight in range(2)], 0)
            deviation.append((value + (own_mean - mean)).astype(BF))
        weight = first[base + 2 : base + 3]
        obs = second[base + 2 : base + 3] + first[base + 3 : base + 4] + second[base + 3 : base + 4]
        innovation = (obs - mean).astype(BF).astype(F32)
        result.append((jnp.concatenate(deviation, 0), mean, weight, innovation))
    return result


def analysis_kernel(me_ref, own_ref, near_ref, out_ref):
    members = GROUP * GROUP * LOCAL
    me = me_ref[0]
    own = halves_of(own_ref, me)
    near = halves_of(near_ref, me)
    lane = lax.broadcasted_iota(jnp.int32, (1, WIDTH), 1)
    region_column = lane % REGION
    half_row = (lane // REGION) % (BAND // 2)
    column_distance = jnp.maximum(
        jnp.maximum(RADIUS - region_column, region_column - (RADIUS + PATCH - 1)), 0
    )
    row_distances = (0 * lane, 0 * lane, half_row + 1, RADIUS - half_row)
    weighted, deviation, innovation = [], [], []
    for (dev, _, weight, inno), row_distance in zip(own + near, row_distances):
        far = jnp.maximum(row_distance, column_distance).astype(F32)
        factor = weight * (1.0 - far / (RADIUS + 1.0))
        weighted.append((dev.astype(F32) * factor).astype(BF))
        deviation.append(dev)
        innovation.append(jnp.broadcast_to(inno, (16, WIDTH)).astype(BF))
    weighted = jnp.concatenate(weighted, 1)
    inner = jnp.concatenate(deviation[:2], 1)
    rows = jnp.concatenate([jnp.concatenate(deviation, 1), jnp.concatenate(innovation, 1)], 0)
    both = lax.dot_general(rows, weighted, (((1,), (1,)), ((), ())), preferred_element_type=F32)
    row = lax.broadcasted_iota(jnp.int32, (members, members), 0)
    col = lax.broadcasted_iota(jnp.int32, (members, members), 1)
    system = both[:members] + jnp.where(row == col, members - 1.0, 0.0)
    line = both[members:]
    scale = jnp.sqrt(jnp.sum(system * system))
    y0 = system * (1.0 / scale)

    def mul(a, b):
        return jnp.dot(a.astype(BF), b.astype(BF), preferred_element_type=F32)

    y0b = y0.astype(BF)
    inner_f = inner.astype(F32)
    x1 = 1.5 * inner_f - 0.5 * mul(y0b, inner)
    line1 = 1.5 * line - 0.5 * mul(line, y0b)
    y1 = 1.5 * y0 - 0.5 * mul(y0b, y0b)
    p1 = 1.5 * y1 - 0.5 * mul(y1, y0b)
    p1b = p1.astype(BF)
    x2 = 1.5 * x1 - 0.5 * mul(p1b, x1)
    line2 = 1.5 * line1 - 0.5 * mul(line1, p1b)
    q1 = 1.5 * p1 - 0.5 * mul(p1b, p1b)
    p2 = 1.5 * q1 - 0.5 * mul(q1, p1b)
    p2b = p2.astype(BF)
    x3 = 1.5 * x2 - 0.5 * mul(p2b, x2)
    line3 = 1.5 * line2 - 0.5 * mul(line2, p2b)
    inverse = 1.0 / jnp.sqrt(scale)
    x3 = x3 * inverse
    line3 = line3 * inverse
    xh = x3.astype(BF)
    xl = (x3 - xh.astype(F32)).astype(BF)
    lh = line3.astype(BF)
    ll = (line3 - lh.astype(F32)).astype(BF)
    shift = mul(lh, xh) + (mul(ll, xh) + mul(lh, xl))
    mean = jnp.concatenate([own[0][1], own[1][1]], 1)
    root = jnp.sqrt(jnp.full((1, 1), members - 1.0, F32))
    result = (root * x3 + (shift[:1] + mean)).astype(BF)
    lane = lax.broadcasted_iota(jnp.int32, (2 * WIDTH, WIDTH), 0)
    target = lax.broadcasted_iota(jnp.int32, (2 * WIDTH, WIDTH), 1)
    narrow = (lane == (target // PATCH) * REGION + RADIUS + target % PATCH).astype(F32).astype(BF)
    result = jnp.dot(result, narrow, preferred_element_type=F32).astype(BF)
    for j in range(GROUP):
        for k in range(GROUP):
            start = (j * GROUP + k) * LOCAL
            out_ref[j, k] = result[start : start + LOCAL]


def unpack_kernel(own_ref, near_ref, out_ref):
    def rows_of(ref):
        blocks = [ref[p % GROUP, p // GROUP].astype(F32) for p in range(GROUP * GROUP)]
        parts = swap_blocks(blocks, PATCH)
        half = BAND // 2
        return [
            [parts[h * FIELDS * half + field * half + r] for h in range(2) for r in range(half)]
            for field in range(FIELDS)
        ]

    own, near = rows_of(own_ref), rows_of(near_ref)
    fields = [n[BAND - FSTEPS :] + o + n[:FSTEPS] for o, n in zip(own, near)]
    done = forecast_rows(*fields)
    for field in range(FIELDS):
        for r in range(BAND):
            out_ref[pl.ds(field * BAND + r, LOCAL, stride=FIELDS * BAND), :] = done[field][r]


def from_next(value):
    count = lax.axis_size("rows")
    return lax.ppermute(value, "rows", [((i + 1) % count, i) for i in range(count)])


def from_previous(value):
    count = lax.axis_size("rows")
    return lax.ppermute(value, "rows", [(i, (i + 1) % count) for i in range(count)])


def near_rows(value, join):
    if lax.axis_size("rows") == 2:
        return from_next(value)
    return join(from_next(value), from_previous(value))


def join_grid(after, before):
    return jnp.concatenate([after[:, :, : BAND // 2], before[:, :, BAND // 2 :]], 2)


def join_region(after, before):
    tail = jnp.concatenate([after[:, :, 4:, :4], before[:, :, 4:, 4:]], 3)
    return jnp.concatenate([after[:, :, :2], before[:, :, 2:4], tail], 2)


def join_inner(after, before):
    return jnp.concatenate([after[..., : WIDTH // 2], before[..., WIDTH // 2 :]], 3)


def exchange(value, low):
    places = range(GROUP)
    groups = [[(i * GROUP + j) if low else (j * GROUP + i) for j in places] for i in places]
    return lax.all_to_all(value, "mem", split_axis=0, concat_axis=0, axis_index_groups=groups, tiled=True)


def call(kernel, name, out_shape, *args, space=pltpu.VMEM, scratch=()):
    spaces = [pltpu.SMEM if arg.shape == (1,) else space for arg in args]
    return pl.pallas_call(
        kernel,
        out_shape=out_shape,
        in_specs=[pl.BlockSpec(memory_space=space) for space in spaces],
        out_specs=jax.tree.map(lambda _: pl.BlockSpec(memory_space=pltpu.VMEM), out_shape),
        scratch_shapes=scratch,
        compiler_params=pltpu.CompilerParams(vmem_limit_bytes=16 * 2**20),
        name=name,
    )(*args)


def local(sample_collection, obs_values, obs_inverse_variance, obs_mask):
    count = lax.axis_size("mem")
    shape = sample_collection.shape
    assert shape == (LOCAL, FIELDS, BAND, WIDTH) and count * PATCH == WIDTH and count == GROUP * GROUP
    me = lax.axis_index("mem").astype(jnp.int32).reshape(1)
    near = near_rows(sample_collection, join_grid)
    sources = (sample_collection.reshape(-1, WIDTH), obs_values, obs_inverse_variance, obs_mask)
    rows, obs = call(
        prepare_kernel,
        "prepare",
        [jax.ShapeDtypeStruct((FIELDS * BAND, LOCAL, WIDTH), F32), jax.ShapeDtypeStruct((8, WIDTH), F32)],
        *sources,
        space=pltpu.HBM,
        scratch=[pltpu.VMEM(x.shape, x.dtype) for x in sources] + [pltpu.SemaphoreType.DMA((len(sources),))],
    )
    region_shape = jax.ShapeDtypeStruct((GROUP, GROUP, 5, 8, WIDTH), BF)
    inner_shape = jax.ShapeDtypeStruct((GROUP, GROUP, LOCAL, WIDTH), BF)
    sending = call(pack_kernel, "forecast_pack", region_shape, rows, near.reshape(-1, WIDTH), obs)
    region = exchange(call(regroup_kernel, "regroup_region", region_shape, exchange(sending, True)), False)
    region_near = near_rows(region, join_region)
    returning = call(analysis_kernel, "analysis", inner_shape, me, region, region_near)
    inner = exchange(call(regroup_kernel, "regroup_inner", inner_shape, exchange(returning, False)), True)
    inner_near = near_rows(inner, join_inner)
    cycled = call(
        unpack_kernel,
        "unpack_forecast",
        jax.ShapeDtypeStruct((LOCAL * FIELDS * BAND, WIDTH), F32),
        inner,
        inner_near,
    )
    return cycled.reshape(shape)


def solution(mesh):
    return jax.shard_map(
        local,
        mesh=mesh,
        in_specs=(
            P("mem", None, "rows", None),
            P(None, "rows", "mem"),
            P(None, "rows", "mem"),
            P(None, "rows", "mem"),
        ),
        out_specs=P("mem", None, "rows", None),
        check_vma=False,
    )
```

```python
import functools

import jax
import jax.numpy as jnp
from jax import lax
from jax.experimental import pallas as pl
from jax.experimental.pallas import tpu as pltpu
from jax.sharding import PartitionSpec as P

PATCH = 8
RADIUS = 4
FSTEPS = 4
CADV = 0.05

LOCAL = 16
FIELDS = 2
BAND = 8
WIDTH = 128
REGION = PATCH + 2 * RADIUS

BF = jnp.bfloat16
F32 = jnp.float32


def forecast_rows(u_rows, v_rows):
    for _ in range(FSTEPS):
        new_u, new_v = [], []
        for i in range(1, len(u_rows) - 1):
            cu, cv = CADV * u_rows[i], CADV * v_rows[i]
            for rows, new in ((u_rows, new_u), (v_rows, new_v)):
                along_x = pltpu.roll(rows[i], WIDTH - 1, 1) - pltpu.roll(rows[i], 1, 1)
                along_y = rows[i + 1] - rows[i - 1]
                new.append(rows[i] - (cu * along_x + cv * along_y))
        u_rows, v_rows = new_u, new_v
    return u_rows, v_rows


def swap_blocks(parts, size):
    count = len(parts)
    lane = lax.broadcasted_iota(jnp.int32, parts[0].shape, 1) // size
    stride = 1
    while stride < count:
        upper = (lane & stride) != 0
        new = list(parts)
        for j in range(count):
            if j & stride == 0:
                a, b = parts[j], parts[j + stride]
                new[j] = jnp.where(upper, pltpu.roll(b, stride * size, 1), a)
                new[j + stride] = jnp.where(upper, b, pltpu.roll(a, WIDTH - stride * size, 1))
        parts = new
        stride *= 2
    return parts


def observation_rows(stack_ref):
    points = FIELDS * BAND
    values, inverse, mask = (stack_ref[i].reshape(points, PATCH) for i in range(3))
    weight = (mask * inverse).astype(BF).astype(F32)
    high = values.astype(BF).astype(F32)
    middle = (values - high).astype(BF).astype(F32)
    low = values - high - middle
    rows = jnp.concatenate([weight, high, middle, low], 0).astype(BF)
    source = lax.broadcasted_iota(jnp.int32, (PATCH, WIDTH), 0)
    lane = lax.broadcasted_iota(jnp.int32, (PATCH, WIDTH), 1)
    spread = (lane % PATCH == source).astype(F32).astype(BF)
    wide = jnp.dot(rows, spread, preferred_element_type=F32)
    row = lax.broadcasted_iota(jnp.int32, wide.shape, 0)
    lane = lax.broadcasted_iota(jnp.int32, wide.shape, 1)
    part, field, y = row // points, (row % points) // BAND, row % BAND
    place = (field * (BAND // 2) + y % (BAND // 2)) * 2 + part % 2
    wide = jnp.where(lane // PATCH == place, wide, 0.0).astype(BF)
    target = lax.broadcasted_iota(jnp.int32, (8, 4 * points), 0)
    row = lax.broadcasted_iota(jnp.int32, (8, 4 * points), 1)
    wanted = ((row % BAND) // (BAND // 2)) * 4 + 2 + row // (2 * points)
    gather = (target == wanted).astype(F32).astype(BF)
    return jnp.dot(gather, wide, preferred_element_type=F32)


def pack_kernel(rows_ref, near_ref, stack_ref, out_ref):
    points = FIELDS * BAND

    def near(field, index):
        return near_ref[pl.ds(field * BAND + index, LOCAL, stride=points), :]

    fields = []
    for field in range(FIELDS):
        before = [near(field, r) for r in range(BAND - FSTEPS, BAND)]
        own = [rows_ref[field * BAND + r] for r in range(BAND)]
        after = [near(field, r) for r in range(FSTEPS)]
        fields.append(before + own + after)
    done = forecast_rows(*fields)
    stacked = []
    index = lax.broadcasted_iota(jnp.int32, (8, WIDTH), 0)
    for half in range(2):
        for field in range(FIELDS):
            for r in range(BAND // 2):
                value = done[field][half * (BAND // 2) + r]
                mean = jnp.sum(value, 0, keepdims=True) * (1.0 / LOCAL)
                high = mean.astype(BF).astype(F32)
                low = mean - high
                tail = jnp.where(index == 4 * half, high, jnp.where(index == 4 * half + 1, low, 0.0))
                stacked += [value - mean, tail]
    rows = jnp.concatenate(stacked, 0).astype(BF)
    column = lax.broadcasted_iota(jnp.int32, (WIDTH, 2 * WIDTH), 0)
    lane = lax.broadcasted_iota(jnp.int32, (WIDTH, 2 * WIDTH), 1)
    wanted = ((lane // REGION) * PATCH + lane % REGION + (WIDTH - RADIUS)) % WIDTH
    widen = (column == wanted).astype(F32).astype(BF)
    wide = jnp.dot(rows, widen, preferred_element_type=F32)
    height = LOCAL + 8
    obs = observation_rows(stack_ref)
    for side in range(2):
        tails = [obs] * 8
        for half in range(2):
            parts = [
                wide[(half * 8 + j) * height : (half * 8 + j + 1) * height, side * WIDTH : (side + 1) * WIDTH]
                for j in range(8)
            ]
            parts = swap_blocks(parts, REGION)
            for i in range(8):
                for eight in range(2):
                    out_ref[side * 8 + i, half * 2 + eight] = parts[i][eight * 8 : eight * 8 + 8].astype(BF)
                tails[i] = tails[i] + parts[i][LOCAL:]
        for i in range(8):
            out_ref[side * 8 + i, 4] = tails[i].astype(BF)


def halves_of(ref, me):
    count = ref.shape[0]
    tails = [ref[s, 4].astype(F32) for s in range(count)]

    def tail_of(device):
        return ref[device, 4].astype(F32)

    lane = lax.broadcasted_iota(jnp.int32, (8, WIDTH), 1) % REGION
    left = tail_of(lax.rem(me + count - 1, count))
    own = tail_of(me)
    right = tail_of(lax.rem(me + 1, count))

    def seen(offset):
        return jnp.where(
            lane < RADIUS,
            pltpu.roll(left, (WIDTH + RADIUS - PATCH - offset) % WIDTH, 1),
            jnp.where(
                lane < RADIUS + PATCH,
                pltpu.roll(own, (WIDTH + RADIUS - offset) % WIDTH, 1),
                pltpu.roll(right, (WIDTH + RADIUS + PATCH - offset) % WIDTH, 1),
            ),
        )

    first, second = seen(0), seen(PATCH)
    result = []
    for half in range(2):
        base = half * 4
        means = [t[base : base + 1] + t[base + 1 : base + 2] for t in tails]
        mean = functools.reduce(jnp.add, means) * (1.0 / count)
        deviation = []
        for s, own_mean in enumerate(means):
            value = jnp.concatenate([ref[s, half * 2 + eight].astype(F32) for eight in range(2)], 0)
            deviation.append((value + (own_mean - mean)).astype(BF))
        weight = first[base + 2 : base + 3]
        obs = second[base + 2 : base + 3] + first[base + 3 : base + 4] + second[base + 3 : base + 4]
        innovation = (obs - mean).astype(BF).astype(F32)
        result.append((jnp.concatenate(deviation, 0), mean, weight, innovation))
    return result


def analysis_kernel(me_ref, own_ref, near_ref, out_ref):
    count = own_ref.shape[0]
    members = count * LOCAL
    me = me_ref[0]
    own = halves_of(own_ref, me)
    near = halves_of(near_ref, me)
    lane = lax.broadcasted_iota(jnp.int32, (1, WIDTH), 1)
    region_column = lane % REGION
    half_row = (lane // REGION) % (BAND // 2)
    column_distance = jnp.maximum(
        jnp.maximum(RADIUS - region_column, region_column - (RADIUS + PATCH - 1)), 0
    )
    row_distances = (0 * lane, 0 * lane, half_row + 1, RADIUS - half_row)
    weighted, deviation, innovation = [], [], []
    for (dev, _, weight, inno), row_distance in zip(own + near, row_distances):
        far = jnp.maximum(row_distance, column_distance).astype(F32)
        factor = weight * (1.0 - far / (RADIUS + 1.0))
        weighted.append((dev.astype(F32) * factor).astype(BF))
        deviation.append(dev)
        innovation.append(jnp.broadcast_to(inno, (16, WIDTH)).astype(BF))
    weighted = jnp.concatenate(weighted, 1)
    inner = jnp.concatenate(deviation[:2], 1)
    rows = jnp.concatenate([jnp.concatenate(deviation, 1), jnp.concatenate(innovation, 1)], 0)
    both = lax.dot_general(rows, weighted, (((1,), (1,)), ((), ())), preferred_element_type=F32)
    row = lax.broadcasted_iota(jnp.int32, (members, members), 0)
    col = lax.broadcasted_iota(jnp.int32, (members, members), 1)
    system = both[:members] + jnp.where(row == col, members - 1.0, 0.0)
    line = both[members:]
    scale = jnp.sqrt(jnp.sum(system * system))
    y0 = system * (1.0 / scale)

    def mul(a, b):
        return jnp.dot(a.astype(BF), b.astype(BF), preferred_element_type=F32)

    y0b = y0.astype(BF)
    inner_f = inner.astype(F32)
    x1 = 1.5 * inner_f - 0.5 * mul(y0b, inner)
    line1 = 1.5 * line - 0.5 * mul(line, y0b)
    y1 = 1.5 * y0 - 0.5 * mul(y0b, y0b)
    p1 = 1.5 * y1 - 0.5 * mul(y1, y0b)
    p1b = p1.astype(BF)
    x2 = 1.5 * x1 - 0.5 * mul(p1b, x1)
    line2 = 1.5 * line1 - 0.5 * mul(line1, p1b)
    q1 = 1.5 * p1 - 0.5 * mul(p1b, p1b)
    p2 = 1.5 * q1 - 0.5 * mul(q1, p1b)
    p2b = p2.astype(BF)
    x3 = 1.5 * x2 - 0.5 * mul(p2b, x2)
    line3 = 1.5 * line2 - 0.5 * mul(line2, p2b)
    inverse = 1.0 / jnp.sqrt(scale)
    x3 = x3 * inverse
    line3 = line3 * inverse
    xh = x3.astype(BF)
    xl = (x3 - xh.astype(F32)).astype(BF)
    lh = line3.astype(BF)
    ll = (line3 - lh.astype(F32)).astype(BF)
    shift = mul(lh, xh) + (mul(ll, xh) + mul(lh, xl))
    mean = jnp.concatenate([own[0][1], own[1][1]], 1)
    root = jnp.sqrt(jnp.full((1, 1), members - 1.0, F32))
    result = (root * x3 + (shift[:1] + mean)).astype(BF)
    lane = lax.broadcasted_iota(jnp.int32, (2 * WIDTH, WIDTH), 0)
    target = lax.broadcasted_iota(jnp.int32, (2 * WIDTH, WIDTH), 1)
    narrow = (lane == (target // PATCH) * REGION + RADIUS + target % PATCH).astype(F32).astype(BF)
    result = jnp.dot(result, narrow, preferred_element_type=F32).astype(BF)
    for s in range(count):
        out_ref[s] = result[s * LOCAL : (s + 1) * LOCAL]


def unpack_kernel(own_ref, near_ref, out_ref):
    def rows_of(ref):
        parts = swap_blocks([ref[p].astype(F32) for p in range(ref.shape[0])], PATCH)
        half = BAND // 2
        return [
            [parts[h * FIELDS * half + field * half + r] for h in range(2) for r in range(half)]
            for field in range(FIELDS)
        ]

    own, near = rows_of(own_ref), rows_of(near_ref)
    fields = [n[BAND - FSTEPS :] + o + n[:FSTEPS] for o, n in zip(own, near)]
    done = forecast_rows(*fields)
    for field in range(FIELDS):
        for r in range(BAND):
            out_ref[pl.ds(field * BAND + r, LOCAL, stride=FIELDS * BAND), :] = done[field][r]


def from_next(value):
    count = lax.axis_size("rows")
    return lax.ppermute(value, "rows", [((i + 1) % count, i) for i in range(count)])


def from_previous(value):
    count = lax.axis_size("rows")
    return lax.ppermute(value, "rows", [(i, (i + 1) % count) for i in range(count)])


def near_rows(value, join):
    if lax.axis_size("rows") == 2:
        return from_next(value)
    return join(from_next(value), from_previous(value))


def join_grid(after, before):
    return jnp.concatenate([after[:, :, : BAND // 2], before[:, :, BAND // 2 :]], 2)


def join_region(after, before):
    tail = jnp.concatenate([after[:, 4:, :4], before[:, 4:, 4:]], 2)
    return jnp.concatenate([after[:, :2], before[:, 2:4], tail], 1)


def join_inner(after, before):
    return jnp.concatenate([after[..., : WIDTH // 2], before[..., WIDTH // 2 :]], 2)


def exchange(value):
    return lax.all_to_all(value, "mem", split_axis=0, concat_axis=0, tiled=True)


def call(kernel, name, out_shape, *args):
    spaces = [pltpu.SMEM if arg.shape == (1,) else pltpu.VMEM for arg in args]
    return pl.pallas_call(
        kernel,
        out_shape=out_shape,
        in_specs=[pl.BlockSpec(memory_space=space) for space in spaces],
        out_specs=jax.tree.map(lambda _: pl.BlockSpec(memory_space=pltpu.VMEM), out_shape),
        compiler_params=pltpu.CompilerParams(vmem_limit_bytes=16 * 2**20),
        name=name,
    )(*args)


def local(sample_collection, obs_values, obs_inverse_variance, obs_mask):
    count = lax.axis_size("mem")
    shape = sample_collection.shape
    assert shape == (LOCAL, FIELDS, BAND, WIDTH) and count * PATCH == WIDTH
    me = lax.axis_index("mem").astype(jnp.int32).reshape(1)
    near = near_rows(sample_collection, join_grid)
    rows = jnp.transpose(sample_collection.reshape(LOCAL, FIELDS * BAND, WIDTH), (1, 0, 2))
    stack = jnp.stack([obs_values, obs_inverse_variance, obs_mask.astype(F32)])
    region_shape = jax.ShapeDtypeStruct((count, 5, 8, WIDTH), BF)
    inner_shape = jax.ShapeDtypeStruct((count, LOCAL, WIDTH), BF)
    region = exchange(call(pack_kernel, "forecast_pack", region_shape, rows, near.reshape(-1, WIDTH), stack))
    region_near = near_rows(region, join_region)
    inner = exchange(call(analysis_kernel, "analysis", inner_shape, me, region, region_near))
    inner_near = near_rows(inner, join_inner)
    cycled = call(
        unpack_kernel,
        "unpack_forecast",
        jax.ShapeDtypeStruct((LOCAL * FIELDS * BAND, WIDTH), F32),
        inner,
        inner_near,
    )
    return cycled.reshape(shape)


def solution(mesh):
    return jax.shard_map(
        local,
        mesh=mesh,
        in_specs=(
            P("mem", None, "rows", None),
            P(None, "rows", "mem"),
            P(None, "rows", "mem"),
            P(None, "rows", "mem"),
        ),
        out_specs=P("mem", None, "rows", None),
        check_vma=False,
    )
```

```python
import functools

import jax
import jax.numpy as jnp
from jax import lax
from jax.experimental import pallas as pl
from jax.experimental.pallas import tpu as pltpu
from jax.sharding import PartitionSpec as P

PATCH = 8
RADIUS = 4
FSTEPS = 4
CADV = 0.05

LOCAL = 16
FIELDS = 2
BAND = 8
WIDTH = 128
REGION = PATCH + 2 * RADIUS

BF = jnp.bfloat16
F32 = jnp.float32


def forecast_rows(u_rows, v_rows):
    for _ in range(FSTEPS):
        new_u, new_v = [], []
        for i in range(1, len(u_rows) - 1):
            cu, cv = CADV * u_rows[i], CADV * v_rows[i]
            for rows, new in ((u_rows, new_u), (v_rows, new_v)):
                along_x = pltpu.roll(rows[i], WIDTH - 1, 1) - pltpu.roll(rows[i], 1, 1)
                along_y = rows[i + 1] - rows[i - 1]
                new.append(rows[i] - (cu * along_x + cv * along_y))
        u_rows, v_rows = new_u, new_v
    return u_rows, v_rows


def swap_blocks(parts, size):
    count = len(parts)
    lane = lax.broadcasted_iota(jnp.int32, parts[0].shape, 1) // size
    stride = 1
    while stride < count:
        upper = (lane & stride) != 0
        new = list(parts)
        for j in range(count):
            if j & stride == 0:
                a, b = parts[j], parts[j + stride]
                new[j] = jnp.where(upper, pltpu.roll(b, stride * size, 1), a)
                new[j + stride] = jnp.where(upper, b, pltpu.roll(a, WIDTH - stride * size, 1))
        parts = new
        stride *= 2
    return parts


def observation_rows(stack_ref):
    points = FIELDS * BAND
    values, inverse, mask = (stack_ref[i].reshape(points, PATCH) for i in range(3))
    weight = (mask * inverse).astype(BF).astype(F32)
    high = values.astype(BF).astype(F32)
    middle = (values - high).astype(BF).astype(F32)
    low = values - high - middle
    rows = jnp.concatenate([weight, high, middle, low], 0).astype(BF)
    source = lax.broadcasted_iota(jnp.int32, (PATCH, WIDTH), 0)
    lane = lax.broadcasted_iota(jnp.int32, (PATCH, WIDTH), 1)
    spread = (lane % PATCH == source).astype(F32).astype(BF)
    wide = jnp.dot(rows, spread, preferred_element_type=F32)
    row = lax.broadcasted_iota(jnp.int32, wide.shape, 0)
    lane = lax.broadcasted_iota(jnp.int32, wide.shape, 1)
    part, field, y = row // points, (row % points) // BAND, row % BAND
    place = (field * (BAND // 2) + y % (BAND // 2)) * 2 + part % 2
    wide = jnp.where(lane // PATCH == place, wide, 0.0).astype(BF)
    target = lax.broadcasted_iota(jnp.int32, (8, 4 * points), 0)
    row = lax.broadcasted_iota(jnp.int32, (8, 4 * points), 1)
    wanted = ((row % BAND) // (BAND // 2)) * 4 + 2 + row // (2 * points)
    gather = (target == wanted).astype(F32).astype(BF)
    return jnp.dot(gather, wide, preferred_element_type=F32)


def pack_kernel(rows_ref, near_ref, stack_ref, out_ref):
    points = FIELDS * BAND

    def near(field, index):
        return near_ref[pl.ds(field * BAND + index, LOCAL, stride=points), :]

    fields = []
    for field in range(FIELDS):
        before = [near(field, r) for r in range(BAND - FSTEPS, BAND)]
        own = [rows_ref[field * BAND + r] for r in range(BAND)]
        after = [near(field, r) for r in range(FSTEPS)]
        fields.append(before + own + after)
    done = forecast_rows(*fields)
    stacked = []
    index = lax.broadcasted_iota(jnp.int32, (8, WIDTH), 0)
    for half in range(2):
        for field in range(FIELDS):
            for r in range(BAND // 2):
                value = done[field][half * (BAND // 2) + r]
                mean = jnp.sum(value, 0, keepdims=True) * (1.0 / LOCAL)
                high = mean.astype(BF).astype(F32)
                low = mean - high
                tail = jnp.where(index == 4 * half, high, jnp.where(index == 4 * half + 1, low, 0.0))
                stacked += [value - mean, tail]
    rows = jnp.concatenate(stacked, 0).astype(BF)
    column = lax.broadcasted_iota(jnp.int32, (WIDTH, 2 * WIDTH), 0)
    lane = lax.broadcasted_iota(jnp.int32, (WIDTH, 2 * WIDTH), 1)
    wanted = ((lane // REGION) * PATCH + lane % REGION + (WIDTH - RADIUS)) % WIDTH
    widen = (column == wanted).astype(F32).astype(BF)
    wide = jnp.dot(rows, widen, preferred_element_type=F32)
    height = LOCAL + 8
    obs = observation_rows(stack_ref)
    for side in range(2):
        tails = [obs] * 8
        for half in range(2):
            parts = [
                wide[(half * 8 + j) * height : (half * 8 + j + 1) * height, side * WIDTH : (side + 1) * WIDTH]
                for j in range(8)
            ]
            parts = swap_blocks(parts, REGION)
            for i in range(8):
                for eight in range(2):
                    out_ref[side * 8 + i, half * 2 + eight] = parts[i][eight * 8 : eight * 8 + 8].astype(BF)
                tails[i] = tails[i] + parts[i][LOCAL:]
        for i in range(8):
            out_ref[side * 8 + i, 4] = tails[i].astype(BF)


def halves_of(ref, me):
    count = ref.shape[0]
    tails = [ref[s, 4].astype(F32) for s in range(count)]

    def tail_of(device):
        return ref[device, 4].astype(F32)

    lane = lax.broadcasted_iota(jnp.int32, (8, WIDTH), 1) % REGION
    left = tail_of(lax.rem(me + count - 1, count))
    own = tail_of(me)
    right = tail_of(lax.rem(me + 1, count))

    def seen(offset):
        return jnp.where(
            lane < RADIUS,
            pltpu.roll(left, (WIDTH + RADIUS - PATCH - offset) % WIDTH, 1),
            jnp.where(
                lane < RADIUS + PATCH,
                pltpu.roll(own, (WIDTH + RADIUS - offset) % WIDTH, 1),
                pltpu.roll(right, (WIDTH + RADIUS + PATCH - offset) % WIDTH, 1),
            ),
        )

    first, second = seen(0), seen(PATCH)
    result = []
    for half in range(2):
        base = half * 4
        means = [t[base : base + 1] + t[base + 1 : base + 2] for t in tails]
        mean = functools.reduce(jnp.add, means) * (1.0 / count)
        deviation = []
        for s, own_mean in enumerate(means):
            value = jnp.concatenate([ref[s, half * 2 + eight].astype(F32) for eight in range(2)], 0)
            deviation.append((value + (own_mean - mean)).astype(BF))
        weight = first[base + 2 : base + 3]
        obs = second[base + 2 : base + 3] + first[base + 3 : base + 4] + second[base + 3 : base + 4]
        innovation = (obs - mean).astype(BF).astype(F32)
        result.append((jnp.concatenate(deviation, 0), mean, weight, innovation))
    return result


def analysis_kernel(me_ref, own_ref, near_ref, out_ref):
    count = own_ref.shape[0]
    members = count * LOCAL
    me = me_ref[0]
    own = halves_of(own_ref, me)
    near = halves_of(near_ref, me)
    lane = lax.broadcasted_iota(jnp.int32, (1, WIDTH), 1)
    region_column = lane % REGION
    half_row = (lane // REGION) % (BAND // 2)
    column_distance = jnp.maximum(
        jnp.maximum(RADIUS - region_column, region_column - (RADIUS + PATCH - 1)), 0
    )
    row_distances = (0 * lane, 0 * lane, half_row + 1, RADIUS - half_row)
    weighted, deviation, innovation = [], [], []
    for (dev, _, weight, inno), row_distance in zip(own + near, row_distances):
        far = jnp.maximum(row_distance, column_distance).astype(F32)
        factor = weight * (1.0 - far / (RADIUS + 1.0))
        weighted.append((dev.astype(F32) * factor).astype(BF))
        deviation.append(dev)
        innovation.append(jnp.broadcast_to(inno, (16, WIDTH)).astype(BF))
    weighted = jnp.concatenate(weighted, 1)
    inner = jnp.concatenate(deviation[:2], 1)
    rows = jnp.concatenate([jnp.concatenate(deviation, 1), jnp.concatenate(innovation, 1)], 0)
    both = lax.dot_general(rows, weighted, (((1,), (1,)), ((), ())), preferred_element_type=F32)
    row = lax.broadcasted_iota(jnp.int32, (members, members), 0)
    col = lax.broadcasted_iota(jnp.int32, (members, members), 1)
    system = both[:members] + jnp.where(row == col, members - 1.0, 0.0)
    line = both[members:]
    scale = jnp.sqrt(jnp.sum(system * system))
    y0 = system * (1.0 / scale)

    def mul(a, b):
        return jnp.dot(a.astype(BF), b.astype(BF), preferred_element_type=F32)

    y0b = y0.astype(BF)
    inner_f = inner.astype(F32)
    x1 = 1.5 * inner_f - 0.5 * mul(y0b, inner)
    line1 = 1.5 * line - 0.5 * mul(line, y0b)
    y1 = 1.5 * y0 - 0.5 * mul(y0b, y0b)
    p1 = 1.5 * y1 - 0.5 * mul(y1, y0b)
    p1b = p1.astype(BF)
    x2 = 1.5 * x1 - 0.5 * mul(p1b, x1)
    line2 = 1.5 * line1 - 0.5 * mul(line1, p1b)
    q1 = 1.5 * p1 - 0.5 * mul(p1b, p1b)
    p2 = 1.5 * q1 - 0.5 * mul(q1, p1b)
    p2b = p2.astype(BF)
    x3 = 1.5 * x2 - 0.5 * mul(p2b, x2)
    line3 = 1.5 * line2 - 0.5 * mul(line2, p2b)
    inverse = 1.0 / jnp.sqrt(scale)
    x3 = x3 * inverse
    line3 = line3 * inverse
    xh = x3.astype(BF)
    xl = (x3 - xh.astype(F32)).astype(BF)
    lh = line3.astype(BF)
    ll = (line3 - lh.astype(F32)).astype(BF)
    shift = mul(lh, xh) + (mul(ll, xh) + mul(lh, xl))
    mean = jnp.concatenate([own[0][1], own[1][1]], 1)
    root = jnp.sqrt(jnp.full((1, 1), members - 1.0, F32))
    result = (root * x3 + (shift[:1] + mean)).astype(BF)
    lane = lax.broadcasted_iota(jnp.int32, (2 * WIDTH, WIDTH), 0)
    target = lax.broadcasted_iota(jnp.int32, (2 * WIDTH, WIDTH), 1)
    narrow = (lane == (target // PATCH) * REGION + RADIUS + target % PATCH).astype(F32).astype(BF)
    result = jnp.dot(result, narrow, preferred_element_type=F32).astype(BF)
    for s in range(count):
        out_ref[s] = result[s * LOCAL : (s + 1) * LOCAL]


def unpack_kernel(own_ref, near_ref, out_ref):
    def rows_of(ref):
        parts = swap_blocks([ref[p].astype(F32) for p in range(ref.shape[0])], PATCH)
        half = BAND // 2
        return [
            [parts[h * FIELDS * half + field * half + r] for h in range(2) for r in range(half)]
            for field in range(FIELDS)
        ]

    own, near = rows_of(own_ref), rows_of(near_ref)
    fields = [n[BAND - FSTEPS :] + o + n[:FSTEPS] for o, n in zip(own, near)]
    done = forecast_rows(*fields)
    for field in range(FIELDS):
        for r in range(BAND):
            out_ref[pl.ds(field * BAND + r, LOCAL, stride=FIELDS * BAND), :] = done[field][r]


def from_next(value):
    count = lax.axis_size("rows")
    return lax.ppermute(value, "rows", [((i + 1) % count, i) for i in range(count)])


def from_previous(value):
    count = lax.axis_size("rows")
    return lax.ppermute(value, "rows", [(i, (i + 1) % count) for i in range(count)])


def near_rows(value, join):
    if lax.axis_size("rows") == 2:
        return from_next(value)
    return join(from_next(value), from_previous(value))


def join_grid(after, before):
    return jnp.concatenate([after[:, :, : BAND // 2], before[:, :, BAND // 2 :]], 2)


def join_region(after, before):
    tail = jnp.concatenate([after[:, 4:, :4], before[:, 4:, 4:]], 2)
    return jnp.concatenate([after[:, :2], before[:, 2:4], tail], 1)


def join_inner(after, before):
    return jnp.concatenate([after[..., : WIDTH // 2], before[..., WIDTH // 2 :]], 2)


def exchange(value):
    return lax.all_to_all(value, "mem", split_axis=0, concat_axis=0, tiled=True)


def call(kernel, name, out_shape, *args):
    spaces = [pltpu.SMEM if arg.shape == (1,) else pltpu.VMEM for arg in args]
    return pl.pallas_call(
        kernel,
        out_shape=out_shape,
        in_specs=[pl.BlockSpec(memory_space=space) for space in spaces],
        out_specs=jax.tree.map(lambda _: pl.BlockSpec(memory_space=pltpu.VMEM), out_shape),
        compiler_params=pltpu.CompilerParams(vmem_limit_bytes=16 * 2**20),
        name=name,
    )(*args)


def local(sample_collection, obs_values, obs_inverse_variance, obs_mask):
    count = lax.axis_size("mem")
    shape = sample_collection.shape
    assert shape == (LOCAL, FIELDS, BAND, WIDTH) and count * PATCH == WIDTH
    me = lax.axis_index("mem").astype(jnp.int32).reshape(1)
    near = near_rows(sample_collection, join_grid)
    rows = jnp.transpose(sample_collection.reshape(LOCAL, FIELDS * BAND, WIDTH), (1, 0, 2))
    stack = jnp.stack([obs_values, obs_inverse_variance, obs_mask.astype(F32)])
    region_shape = jax.ShapeDtypeStruct((count, 5, 8, WIDTH), BF)
    inner_shape = jax.ShapeDtypeStruct((count, LOCAL, WIDTH), BF)
    region = exchange(call(pack_kernel, "forecast_pack", region_shape, rows, near.reshape(-1, WIDTH), stack))
    region_near = near_rows(region, join_region)
    analysed = call(analysis_kernel, "analysis", inner_shape, me, region, region_near)
    everyone = lax.all_gather(analysed, "mem", axis=0)
    inner = lax.dynamic_index_in_dim(everyone, me[0], 1, keepdims=False)
    inner_near = near_rows(inner, join_inner)
    cycled = call(
        unpack_kernel,
        "unpack_forecast",
        jax.ShapeDtypeStruct((LOCAL * FIELDS * BAND, WIDTH), F32),
        inner,
        inner_near,
    )
    return cycled.reshape(shape)


def solution(mesh):
    return jax.shard_map(
        local,
        mesh=mesh,
        in_specs=(
            P("mem", None, "rows", None),
            P(None, "rows", "mem"),
            P(None, "rows", "mem"),
            P(None, "rows", "mem"),
        ),
        out_specs=P("mem", None, "rows", None),
        check_vma=False,
    )
```

```python
import functools

import jax
import jax.numpy as jnp
from jax import lax
from jax.experimental import pallas as pl
from jax.experimental.pallas import tpu as pltpu
from jax.sharding import PartitionSpec as P

PATCH = 8
RADIUS = 4
FSTEPS = 4
CADV = 0.05

LOCAL = 16
FIELDS = 2
BAND = 8
WIDTH = 128
REGION = PATCH + 2 * RADIUS

BF = jnp.bfloat16
F32 = jnp.float32


def forecast_rows(u_rows, v_rows):
    for _ in range(FSTEPS):
        new_u, new_v = [], []
        for i in range(1, len(u_rows) - 1):
            cu, cv = CADV * u_rows[i], CADV * v_rows[i]
            for rows, new in ((u_rows, new_u), (v_rows, new_v)):
                along_x = pltpu.roll(rows[i], WIDTH - 1, 1) - pltpu.roll(rows[i], 1, 1)
                along_y = rows[i + 1] - rows[i - 1]
                new.append(rows[i] - (cu * along_x + cv * along_y))
        u_rows, v_rows = new_u, new_v
    return u_rows, v_rows


def swap_blocks(parts, size):
    count = len(parts)
    lane = lax.broadcasted_iota(jnp.int32, parts[0].shape, 1) // size
    stride = 1
    while stride < count:
        upper = (lane & stride) != 0
        new = list(parts)
        for j in range(count):
            if j & stride == 0:
                a, b = parts[j], parts[j + stride]
                new[j] = jnp.where(upper, pltpu.roll(b, stride * size, 1), a)
                new[j + stride] = jnp.where(upper, b, pltpu.roll(a, WIDTH - stride * size, 1))
        parts = new
        stride *= 2
    return parts


def observation_rows(values_ref, inverse_ref, mask_ref):
    points = FIELDS * BAND
    weight = (mask_ref[...].astype(F32) * inverse_ref[...]).astype(BF).astype(F32).reshape(points, PATCH)
    values = values_ref[...].reshape(points, PATCH)
    high = values.astype(BF).astype(F32)
    middle = (values - high).astype(BF).astype(F32)
    low = values - high - middle
    rows = jnp.concatenate([weight, high, middle, low], 0).astype(BF)
    source = lax.broadcasted_iota(jnp.int32, (PATCH, WIDTH), 0)
    lane = lax.broadcasted_iota(jnp.int32, (PATCH, WIDTH), 1)
    spread = (lane % PATCH == source).astype(F32).astype(BF)
    wide = jnp.dot(rows, spread, preferred_element_type=F32)
    row = lax.broadcasted_iota(jnp.int32, wide.shape, 0)
    lane = lax.broadcasted_iota(jnp.int32, wide.shape, 1)
    part, field, y = row // points, (row % points) // BAND, row % BAND
    place = (field * (BAND // 2) + y % (BAND // 2)) * 2 + part % 2
    wide = jnp.where(lane // PATCH == place, wide, 0.0).astype(BF)
    target = lax.broadcasted_iota(jnp.int32, (8, 4 * points), 0)
    row = lax.broadcasted_iota(jnp.int32, (8, 4 * points), 1)
    wanted = ((row % BAND) // (BAND // 2)) * 4 + 2 + row // (2 * points)
    gather = (target == wanted).astype(F32).astype(BF)
    return jnp.dot(gather, wide, preferred_element_type=F32)


def pack_kernel(rows_ref, near_ref, values_ref, inverse_ref, mask_ref, out_ref):
    points = FIELDS * BAND

    def near(field, index):
        return near_ref[pl.ds(field * BAND + index, LOCAL, stride=points), :]

    fields = []
    for field in range(FIELDS):
        before = [near(field, r) for r in range(BAND - FSTEPS, BAND)]
        own = [rows_ref[field * BAND + r] for r in range(BAND)]
        after = [near(field, r) for r in range(FSTEPS)]
        fields.append(before + own + after)
    done = forecast_rows(*fields)
    half_rows = BAND // 2
    index = lax.broadcasted_iota(jnp.int32, (8, WIDTH), 0)
    values, means = [], [jnp.zeros((8, WIDTH), F32)] * (FIELDS * half_rows)
    for half in range(2):
        for j in range(FIELDS * half_rows):
            value = done[j // half_rows][half * half_rows + j % half_rows]
            mean = jnp.sum(value, 0, keepdims=True) * (1.0 / LOCAL)
            high = mean.astype(BF).astype(F32)
            means[j] = jnp.where(index == 4 * half, high, jnp.where(index == 4 * half + 1, mean - high, means[j]))
            values.append(value - mean)
    obs = observation_rows(values_ref, inverse_ref, mask_ref)
    is_mean = index & 2 == 0
    means = [
        jnp.where(is_mean, pltpu.roll(m, RADIUS, 1), pltpu.roll(pltpu.roll(m, WIDTH + RADIUS - PATCH, 1), 2, 0))
        for m in means
    ]
    means = swap_blocks(means, REGION)
    for parity in range(2):
        for i in range(8):
            mean = pltpu.roll(means[i], 6, 0) if parity else means[i]
            out_ref[2 * i + parity, 4] = jnp.where(is_mean, mean, obs).astype(BF)
        for half in range(2):
            shift = (WIDTH + RADIUS - parity * PATCH) % WIDTH
            parts = swap_blocks([pltpu.roll(v, shift, 1) for v in values[half * 8 : half * 8 + 8]], REGION)
            for i in range(8):
                for eight in range(2):
                    out_ref[2 * i + parity, half * 2 + eight] = parts[i][eight * 8 : eight * 8 + 8].astype(BF)


def halves_of(ref, me):
    count = ref.shape[0]
    tails = [ref[s, 4].astype(F32) for s in range(count)]

    def tail_of(device):
        return ref[device, 4].astype(F32)

    lane = lax.broadcasted_iota(jnp.int32, (8, WIDTH), 1) % REGION
    left = tail_of(lax.rem(me + count - 1, count))
    own = tail_of(me)
    right = tail_of(lax.rem(me + 1, count))

    def seen(offset):
        return jnp.where(
            lane < RADIUS,
            pltpu.roll(left, (WIDTH + RADIUS - PATCH - offset) % WIDTH, 1),
            jnp.where(
                lane < RADIUS + PATCH,
                pltpu.roll(own, (WIDTH + RADIUS - offset) % WIDTH, 1),
                pltpu.roll(right, (WIDTH + RADIUS + PATCH - offset) % WIDTH, 1),
            ),
        )

    first, second = seen(0), seen(PATCH)
    result = []
    for half in range(2):
        base = half * 4
        means = [t[base : base + 1] + t[base + 1 : base + 2] for t in tails]
        mean = functools.reduce(jnp.add, means) * (1.0 / count)
        deviation = []
        for s, own_mean in enumerate(means):
            value = jnp.concatenate([ref[s, half * 2 + eight].astype(F32) for eight in range(2)], 0)
            deviation.append((value + (own_mean - mean)).astype(BF))
        weight = first[base + 2 : base + 3]
        obs = second[base + 2 : base + 3] + first[base + 3 : base + 4] + second[base + 3 : base + 4]
        innovation = (obs - mean).astype(BF).astype(F32)
        result.append((jnp.concatenate(deviation, 0), mean, weight, innovation))
    return result


def half_sums(halves, row_distances):
    lane = lax.broadcasted_iota(jnp.int32, (1, WIDTH), 1)
    region_column = lane % REGION
    half_row = (lane // REGION) % (BAND // 2)
    column_distance = jnp.maximum(
        jnp.maximum(RADIUS - region_column, region_column - (RADIUS + PATCH - 1)), 0
    )
    weighted, deviation, innovation = [], [], []
    for (dev, _, weight, inno), row_distance in zip(halves, row_distances):
        far = jnp.maximum(row_distance(half_row), column_distance).astype(F32)
        factor = weight * (1.0 - far / (RADIUS + 1.0))
        weighted.append((dev.astype(F32) * factor).astype(BF))
        deviation.append(dev)
        innovation.append(jnp.broadcast_to(inno, (16, WIDTH)).astype(BF))
    deviation = jnp.concatenate(deviation, 1)
    rows = jnp.concatenate([deviation, jnp.concatenate(innovation, 1)], 0)
    weighted = jnp.concatenate(weighted, 1)
    return deviation, lax.dot_general(rows, weighted, (((1,), (1,)), ((), ())), preferred_element_type=F32)


def own_kernel(me_ref, own_ref, inner_ref, sums_ref, mean_ref):
    halves = halves_of(own_ref, me_ref[0])
    deviation, sums_ref[...] = half_sums(halves, [jnp.zeros_like] * 2)
    lane = lax.broadcasted_iota(jnp.int32, (2 * WIDTH, WIDTH), 0)
    target = lax.broadcasted_iota(jnp.int32, (2 * WIDTH, WIDTH), 1)
    narrow = (lane == (target // PATCH) * REGION + RADIUS + target % PATCH).astype(F32).astype(BF)
    inner_ref[...] = jnp.dot(deviation, narrow, preferred_element_type=F32).astype(BF)
    mean = jnp.broadcast_to(jnp.concatenate([halves[0][1], halves[1][1]], 1), (16, 2 * WIDTH))
    high = mean.astype(BF)
    middle = (mean - high.astype(F32)).astype(BF)
    low = (mean - high.astype(F32) - middle.astype(F32)).astype(BF)
    parts = jnp.dot(jnp.concatenate([high, middle, low], 0), narrow, preferred_element_type=F32)
    mean_ref[...] = parts[:8] + (parts[16:24] + parts[32:40])


def analysis_kernel(me_ref, near_ref, inner_ref, sums_ref, mean_ref, out_ref):
    count = near_ref.shape[0]
    members = count * LOCAL
    halves = halves_of(near_ref, me_ref[0])
    both = sums_ref[...] + half_sums(halves, [lambda r: r + 1, lambda r: RADIUS - r])[1]
    row = lax.broadcasted_iota(jnp.int32, (members, members), 0)
    col = lax.broadcasted_iota(jnp.int32, (members, members), 1)
    system = both[:members] + jnp.where(row == col, members - 1.0, 0.0)
    def mul(a, b):
        return jnp.dot(a.astype(BF), b.astype(BF), preferred_element_type=F32)

    def with_line(a, line):
        return jnp.concatenate([a.astype(BF), line.astype(BF)], 0)

    inner, line = inner_ref[...], both[members:]
    system_b = system.astype(BF)
    first = mul(with_line(system_b, line), system_b)
    system_x = mul(system_b, inner)
    scale = jnp.sqrt(jnp.sum(system * system))
    inverse = 1.0 / scale
    x1 = 1.5 * inner.astype(F32) - (0.5 * inverse) * system_x
    line1 = 1.5 * line - (0.5 * inverse) * first[members:]
    y1 = inverse * (1.5 * system - (0.5 * inverse) * first[:members])
    p1 = 1.5 * y1 - (0.5 * inverse) * mul(y1, system_b)
    p1b = p1.astype(BF)
    second = mul(with_line(p1b, line1), p1b)
    x2 = 1.5 * x1 - 0.5 * mul(p1b, x1)
    line2 = 1.5 * line1 - 0.5 * second[members:]
    q1 = 1.5 * p1 - 0.5 * second[:members]
    p2 = 1.5 * q1 - 0.5 * mul(q1, p1b)
    p2b = p2.astype(BF)
    factor = 1.0 / jnp.sqrt(scale)
    x3 = (1.5 * x2 - 0.5 * mul(p2b, x2)) * factor
    line3 = (1.5 * line2 - 0.5 * mul(line2, p2b)) * factor
    line_b = line3.astype(BF)
    lines = with_line(line_b, line3 - line_b.astype(F32))
    shift = mul(lines, x3)
    shift = shift[:1] + shift[16:17]
    root = jnp.sqrt(jnp.full((1, 1), members - 1.0, F32))
    result = (root * x3 + (shift + mean_ref[:1])).astype(BF)
    for s in range(count):
        for eight in range(2):
            out_ref[s, eight] = result[s * LOCAL + eight * 8 : s * LOCAL + eight * 8 + 8]


def unpacked(ref, eight):
    return swap_blocks([ref[p, eight].astype(F32) for p in range(ref.shape[0])], PATCH)


def unpack_kernel(in_ref, out_ref):
    @pl.loop(0, 2)
    def _(eight):
        for i, row in enumerate(unpacked(in_ref, eight)):
            out_ref[eight, i] = row


def forecast_kernel(own_ref, near_ref, out_ref):
    def by_field(rows):
        half = BAND // 2
        return [
            [rows[h * FIELDS * half + field * half + r] for h in range(2) for r in range(half)]
            for field in range(FIELDS)
        ]

    @pl.loop(0, 2)
    def _(eight):
        own, near = by_field(own_ref.at[eight]), by_field(unpacked(near_ref, eight))
        fields = [n[BAND - FSTEPS :] + o + n[:FSTEPS] for o, n in zip(own, near)]
        done = forecast_rows(*fields)
        points = FIELDS * BAND
        for field in range(FIELDS):
            for r in range(BAND):
                out_ref[pl.ds(eight * 8 * points + field * BAND + r, 8, stride=points), :] = done[field][r]


def from_next(value):
    count = lax.axis_size("rows")
    return lax.ppermute(value, "rows", [((i + 1) % count, i) for i in range(count)])


def from_previous(value):
    count = lax.axis_size("rows")
    return lax.ppermute(value, "rows", [(i, (i + 1) % count) for i in range(count)])


def near_rows(value, join):
    if lax.axis_size("rows") == 2:
        return from_next(value)
    return join(from_next(value), from_previous(value))


def join_grid(after, before):
    return jnp.concatenate([after[:, :, : BAND // 2], before[:, :, BAND // 2 :]], 2)


def join_region(after, before):
    tail = jnp.concatenate([after[:, 4:, :4], before[:, 4:, 4:]], 2)
    return jnp.concatenate([after[:, :2], before[:, 2:4], tail], 1)


def join_inner(after, before):
    return jnp.concatenate([after[..., : WIDTH // 2], before[..., WIDTH // 2 :]], 3)


def exchange(value):
    return lax.all_to_all(value, "mem", split_axis=0, concat_axis=0, tiled=True)


def call(kernel, name, out_shape, *args, flops=0):
    spaces = [pltpu.SMEM if arg.shape == (1,) else pltpu.VMEM for arg in args]
    moved = sum(x.size * x.dtype.itemsize for x in [*args, *jax.tree.leaves(out_shape)])
    return pl.pallas_call(
        kernel,
        out_shape=out_shape,
        in_specs=[pl.BlockSpec(memory_space=space) for space in spaces],
        out_specs=jax.tree.map(lambda _: pl.BlockSpec(memory_space=pltpu.VMEM), out_shape),
        compiler_params=pltpu.CompilerParams(vmem_limit_bytes=16 * 2**20),
        cost_estimate=pl.CostEstimate(flops=flops, bytes_accessed=moved, transcendentals=0),
        name=name,
    )(*args)


def local(sample_collection, obs_values, obs_inverse_variance, obs_mask):
    count = lax.axis_size("mem")
    shape = sample_collection.shape
    assert shape == (LOCAL, FIELDS, BAND, WIDTH) and count * PATCH == WIDTH
    me = lax.axis_index("mem").astype(jnp.int32).reshape(1)
    near = near_rows(sample_collection, join_grid)
    rows = jnp.transpose(sample_collection.reshape(LOCAL, FIELDS * BAND, WIDTH), (1, 0, 2))
    region_shape = jax.ShapeDtypeStruct((count, 5, 8, WIDTH), BF)
    inner_shape = jax.ShapeDtypeStruct((count, 2, 8, WIDTH), BF)
    observations = (obs_values, obs_inverse_variance, obs_mask)
    region = exchange(call(pack_kernel, "forecast_pack", region_shape, rows, near.reshape(-1, WIDTH), *observations))
    members, points = count * LOCAL, 2 * WIDTH
    own_shapes = [
        jax.ShapeDtypeStruct((members, WIDTH), BF),
        jax.ShapeDtypeStruct((members + 16, members), F32),
        jax.ShapeDtypeStruct((8, WIDTH), F32),
    ]
    flops = 2 * members * members * points
    region_near = near_rows(region, join_region)
    own = call(own_kernel, "own_half", own_shapes, me, region, flops=flops)
    inner = exchange(call(analysis_kernel, "analysis", inner_shape, me, region_near, *own, flops=8 * flops))
    inner_near = near_rows(inner, join_inner)
    rows_shape = jax.ShapeDtypeStruct((2, FIELDS * BAND, 8, WIDTH), F32)
    inner = call(unpack_kernel, "unpack_own", rows_shape, inner)
    out_shape = jax.ShapeDtypeStruct((LOCAL * FIELDS * BAND, WIDTH), F32)
    cycled = call(forecast_kernel, "unpack_forecast", out_shape, inner, inner_near)
    return cycled.reshape(shape)


def solution(mesh):
    return jax.shard_map(
        local,
        mesh=mesh,
        in_specs=(
            P("mem", None, "rows", None),
            P(None, "rows", "mem"),
            P(None, "rows", "mem"),
            P(None, "rows", "mem"),
        ),
        out_specs=P("mem", None, "rows", None),
        check_vma=False,
    )
```

```python
import functools

import jax
import jax.numpy as jnp
from jax import lax
from jax.experimental import pallas as pl
from jax.experimental.pallas import tpu as pltpu
from jax.sharding import PartitionSpec as P

PATCH = 8
RADIUS = 4
FSTEPS = 4
CADV = 0.05

LOCAL = 16
FIELDS = 2
BAND = 8
WIDTH = 128
REGION = PATCH + 2 * RADIUS

BF = jnp.bfloat16
F32 = jnp.float32


def forecast_rows(u_rows, v_rows):
    for _ in range(FSTEPS):
        new_u, new_v = [], []
        for i in range(1, len(u_rows) - 1):
            cu, cv = CADV * u_rows[i], CADV * v_rows[i]
            for rows, new in ((u_rows, new_u), (v_rows, new_v)):
                along_x = pltpu.roll(rows[i], WIDTH - 1, 1) - pltpu.roll(rows[i], 1, 1)
                along_y = rows[i + 1] - rows[i - 1]
                new.append(rows[i] - (cu * along_x + cv * along_y))
        u_rows, v_rows = new_u, new_v
    return u_rows, v_rows


def swap_blocks(parts, size):
    count = len(parts)
    lane = lax.broadcasted_iota(jnp.int32, parts[0].shape, 1) // size
    stride = 1
    while stride < count:
        upper = (lane & stride) != 0
        new = list(parts)
        for j in range(count):
            if j & stride == 0:
                a, b = parts[j], parts[j + stride]
                new[j] = jnp.where(upper, pltpu.roll(b, stride * size, 1), a)
                new[j + stride] = jnp.where(upper, b, pltpu.roll(a, WIDTH - stride * size, 1))
        parts = new
        stride *= 2
    return parts


def observation_rows(values_ref, inverse_ref, mask_ref):
    points = FIELDS * BAND
    weight = (mask_ref[...].astype(F32) * inverse_ref[...]).astype(BF).astype(F32).reshape(points, PATCH)
    values = values_ref[...].reshape(points, PATCH)
    high = values.astype(BF).astype(F32)
    middle = (values - high).astype(BF).astype(F32)
    low = values - high - middle
    rows = jnp.concatenate([weight, high, middle, low], 0).astype(BF)
    source = lax.broadcasted_iota(jnp.int32, (PATCH, WIDTH), 0)
    lane = lax.broadcasted_iota(jnp.int32, (PATCH, WIDTH), 1)
    spread = (lane % PATCH == source).astype(F32).astype(BF)
    wide = jnp.dot(rows, spread, preferred_element_type=F32)
    row = lax.broadcasted_iota(jnp.int32, wide.shape, 0)
    lane = lax.broadcasted_iota(jnp.int32, wide.shape, 1)
    part, field, y = row // points, (row % points) // BAND, row % BAND
    place = (field * (BAND // 2) + y % (BAND // 2)) * 2 + part % 2
    wide = jnp.where(lane // PATCH == place, wide, 0.0).astype(BF)
    target = lax.broadcasted_iota(jnp.int32, (8, 4 * points), 0)
    row = lax.broadcasted_iota(jnp.int32, (8, 4 * points), 1)
    wanted = ((row % BAND) // (BAND // 2)) * 4 + 2 + row // (2 * points)
    gather = (target == wanted).astype(F32).astype(BF)
    return jnp.dot(gather, wide, preferred_element_type=F32)


def pack_kernel(rows_ref, near_ref, values_ref, inverse_ref, mask_ref, out_ref):
    points = FIELDS * BAND

    def near(field, index):
        return near_ref[pl.ds(field * BAND + index, LOCAL, stride=points), :]

    fields = []
    for field in range(FIELDS):
        before = [near(field, r) for r in range(BAND - FSTEPS, BAND)]
        own = [rows_ref[field * BAND + r] for r in range(BAND)]
        after = [near(field, r) for r in range(FSTEPS)]
        fields.append(before + own + after)
    done = forecast_rows(*fields)
    half_rows = BAND // 2
    index = lax.broadcasted_iota(jnp.int32, (8, WIDTH), 0)
    values, means = [], [jnp.zeros((8, WIDTH), F32)] * (FIELDS * half_rows)
    for half in range(2):
        for j in range(FIELDS * half_rows):
            value = done[j // half_rows][half * half_rows + j % half_rows]
            mean = jnp.sum(value, 0, keepdims=True) * (1.0 / LOCAL)
            high = mean.astype(BF).astype(F32)
            means[j] = jnp.where(index == 4 * half, high, jnp.where(index == 4 * half + 1, mean - high, means[j]))
            values.append(value - mean)
    rows = jnp.concatenate(values + means, 0).astype(BF)
    column = lax.broadcasted_iota(jnp.int32, (WIDTH, 2 * WIDTH), 0)
    lane = lax.broadcasted_iota(jnp.int32, (WIDTH, 2 * WIDTH), 1)
    wanted = ((lane // REGION) * PATCH + lane % REGION + (WIDTH - RADIUS)) % WIDTH
    widen = (column == wanted).astype(F32).astype(BF)
    wide = jnp.dot(rows, widen, preferred_element_type=F32)
    obs = observation_rows(values_ref, inverse_ref, mask_ref)
    start = len(values) * LOCAL
    is_mean = index & 2 == 0
    means = []
    for j in range(8):
        part = wide[start + j * 8 : start + j * 8 + 8]
        means.append(jnp.where(is_mean, part[:, :WIDTH], pltpu.roll(part[:, WIDTH:], 2, 0)))
    means = swap_blocks(means, REGION)
    for side in range(2):
        for half in range(2):
            parts = [
                wide[(half * 8 + j) * LOCAL : (half * 8 + j + 1) * LOCAL, side * WIDTH : (side + 1) * WIDTH].astype(BF)
                for j in range(8)
            ]
            parts = swap_blocks(parts, REGION)
            for i in range(8):
                out_ref[side * 8 + i, half * LOCAL : (half + 1) * LOCAL] = parts[i]
        for i in range(8):
            mean = means[i] if side == 0 else pltpu.roll(means[i], 6, 0)
            out_ref[side * 8 + i, 2 * LOCAL :] = jnp.where(is_mean, mean, obs).astype(BF)


def halves_of(ref, me):
    count = ref.shape[0]
    tails = [ref[s, 2 * LOCAL :].astype(F32) for s in range(count)]

    def tail_of(device):
        return ref[device, 2 * LOCAL :].astype(F32)

    lane = lax.broadcasted_iota(jnp.int32, (8, WIDTH), 1) % REGION
    left = tail_of(lax.rem(me + count - 1, count))
    own = tail_of(me)
    right = tail_of(lax.rem(me + 1, count))

    def seen(offset):
        return jnp.where(
            lane < RADIUS,
            pltpu.roll(left, (WIDTH + RADIUS - PATCH - offset) % WIDTH, 1),
            jnp.where(
                lane < RADIUS + PATCH,
                pltpu.roll(own, (WIDTH + RADIUS - offset) % WIDTH, 1),
                pltpu.roll(right, (WIDTH + RADIUS + PATCH - offset) % WIDTH, 1),
            ),
        )

    first, second = seen(0), seen(PATCH)
    result = []
    for half in range(2):
        base = half * 4
        means = [t[base : base + 1] + t[base + 1 : base + 2] for t in tails]
        mean = functools.reduce(jnp.add, means) * (1.0 / count)
        deviation = []
        for s, own_mean in enumerate(means):
            value = ref[s, half * LOCAL : (half + 1) * LOCAL].astype(F32)
            deviation.append((value + (own_mean - mean)).astype(BF))
        weight = first[base + 2 : base + 3]
        obs = second[base + 2 : base + 3] + first[base + 3 : base + 4] + second[base + 3 : base + 4]
        innovation = (obs - mean).astype(BF).astype(F32)
        result.append((jnp.concatenate(deviation, 0), mean, weight, innovation))
    return result


def half_sums(halves, row_distances):
    lane = lax.broadcasted_iota(jnp.int32, (1, WIDTH), 1)
    region_column = lane % REGION
    half_row = (lane // REGION) % (BAND // 2)
    column_distance = jnp.maximum(
        jnp.maximum(RADIUS - region_column, region_column - (RADIUS + PATCH - 1)), 0
    )
    weighted, deviation, innovation = [], [], []
    for (dev, _, weight, inno), row_distance in zip(halves, row_distances):
        far = jnp.maximum(row_distance(half_row), column_distance).astype(F32)
        factor = weight * (1.0 - far / (RADIUS + 1.0))
        weighted.append((dev.astype(F32) * factor).astype(BF))
        deviation.append(dev)
        innovation.append(jnp.broadcast_to(inno, (16, WIDTH)).astype(BF))
    deviation = jnp.concatenate(deviation, 1)
    rows = jnp.concatenate([deviation, jnp.concatenate(innovation, 1)], 0)
    weighted = jnp.concatenate(weighted, 1)
    return deviation, lax.dot_general(rows, weighted, (((1,), (1,)), ((), ())), preferred_element_type=F32)


def own_kernel(me_ref, own_ref, inner_ref, sums_ref, mean_ref):
    halves = halves_of(own_ref, me_ref[0])
    deviation, sums_ref[...] = half_sums(halves, [jnp.zeros_like] * 2)
    lane = lax.broadcasted_iota(jnp.int32, (2 * WIDTH, WIDTH), 0)
    target = lax.broadcasted_iota(jnp.int32, (2 * WIDTH, WIDTH), 1)
    narrow = (lane == (target // PATCH) * REGION + RADIUS + target % PATCH).astype(F32).astype(BF)
    inner_ref[...] = jnp.dot(deviation, narrow, preferred_element_type=F32).astype(BF)
    mean = jnp.broadcast_to(jnp.concatenate([halves[0][1], halves[1][1]], 1), (16, 2 * WIDTH))
    high = mean.astype(BF)
    middle = (mean - high.astype(F32)).astype(BF)
    low = (mean - high.astype(F32) - middle.astype(F32)).astype(BF)
    parts = jnp.dot(jnp.concatenate([high, middle, low], 0), narrow, preferred_element_type=F32)
    mean_ref[...] = parts[:8] + (parts[16:24] + parts[32:40])


def analysis_kernel(me_ref, near_ref, inner_ref, sums_ref, mean_ref, out_ref):
    count = near_ref.shape[0]
    members = count * LOCAL
    halves = halves_of(near_ref, me_ref[0])
    both = sums_ref[...] + half_sums(halves, [lambda r: r + 1, lambda r: RADIUS - r])[1]
    row = lax.broadcasted_iota(jnp.int32, (members, members), 0)
    col = lax.broadcasted_iota(jnp.int32, (members, members), 1)
    system = both[:members] + jnp.where(row == col, members - 1.0, 0.0)
    def mul(a, b):
        return jnp.dot(a.astype(BF), b.astype(BF), preferred_element_type=F32)

    def with_line(a, line):
        return jnp.concatenate([a.astype(BF), line.astype(BF)], 0)

    inner, line = inner_ref[...], both[members:]
    system_b = system.astype(BF)
    first = mul(with_line(system_b, line), system_b)
    system_x = mul(system_b, inner)
    scale = jnp.sqrt(jnp.sum(system * system))
    inverse = 1.0 / scale
    x1 = 1.5 * inner.astype(F32) - (0.5 * inverse) * system_x
    line1 = 1.5 * line - (0.5 * inverse) * first[members:]
    y1 = inverse * (1.5 * system - (0.5 * inverse) * first[:members])
    p1 = 1.5 * y1 - (0.5 * inverse) * mul(y1, system_b)
    p1b = p1.astype(BF)
    second = mul(with_line(p1b, line1), p1b)
    x2 = 1.5 * x1 - 0.5 * mul(p1b, x1)
    line2 = 1.5 * line1 - 0.5 * second[members:]
    q1 = 1.5 * p1 - 0.5 * second[:members]
    p2 = 1.5 * q1 - 0.5 * mul(q1, p1b)
    p2b = p2.astype(BF)
    factor = 1.0 / jnp.sqrt(scale)
    x3 = (1.5 * x2 - 0.5 * mul(p2b, x2)) * factor
    line3 = (1.5 * line2 - 0.5 * mul(line2, p2b)) * factor
    line_b = line3.astype(BF)
    lines = with_line(line_b, line3 - line_b.astype(F32))
    shift = mul(lines, x3)
    shift = shift[:1] + shift[16:17]
    root = jnp.sqrt(jnp.full((1, 1), members - 1.0, F32))
    result = (root * x3 + (shift + mean_ref[:1])).astype(BF)
    for s in range(count):
        out_ref[s] = result[s * LOCAL : (s + 1) * LOCAL]


def unpacked(ref):
    return [row.astype(F32) for row in swap_blocks([ref[p] for p in range(ref.shape[0])], PATCH)]


def unpack_kernel(in_ref, out_ref):
    for i, row in enumerate(unpacked(in_ref)):
        out_ref[i] = row


def forecast_kernel(own_ref, near_ref, out_ref):
    def by_field(rows):
        half = BAND // 2
        return [
            [rows[h * FIELDS * half + field * half + r] for h in range(2) for r in range(half)]
            for field in range(FIELDS)
        ]

    own, near = by_field(own_ref), by_field(unpacked(near_ref))
    fields = [n[BAND - FSTEPS :] + o + n[:FSTEPS] for o, n in zip(own, near)]
    done = forecast_rows(*fields)
    for field in range(FIELDS):
        for r in range(BAND):
            out_ref[pl.ds(field * BAND + r, LOCAL, stride=FIELDS * BAND), :] = done[field][r]


def from_next(value):
    count = lax.axis_size("rows")
    return lax.ppermute(value, "rows", [((i + 1) % count, i) for i in range(count)])


def from_previous(value):
    count = lax.axis_size("rows")
    return lax.ppermute(value, "rows", [(i, (i + 1) % count) for i in range(count)])


def near_rows(value, join):
    if lax.axis_size("rows") == 2:
        return from_next(value)
    return join(from_next(value), from_previous(value))


def join_grid(after, before):
    return jnp.concatenate([after[:, :, : BAND // 2], before[:, :, BAND // 2 :]], 2)


def join_region(after, before):
    after, before = (x.reshape(x.shape[0], -1, 4, WIDTH) for x in (after, before))
    near = jnp.concatenate([after[:, :4], before[:, 4:8], after[:, 8:9], before[:, 9:]], 1)
    return near.reshape(near.shape[0], -1, WIDTH)


def join_inner(after, before):
    return jnp.concatenate([after[..., : WIDTH // 2], before[..., WIDTH // 2 :]], 2)


def exchange(value):
    return lax.all_to_all(value, "mem", split_axis=0, concat_axis=0, tiled=True)


def call(kernel, name, out_shape, *args, flops=0):
    spaces = [pltpu.SMEM if arg.shape == (1,) else pltpu.VMEM for arg in args]
    moved = sum(x.size * x.dtype.itemsize for x in [*args, *jax.tree.leaves(out_shape)])
    return pl.pallas_call(
        kernel,
        out_shape=out_shape,
        in_specs=[pl.BlockSpec(memory_space=space) for space in spaces],
        out_specs=jax.tree.map(lambda _: pl.BlockSpec(memory_space=pltpu.VMEM), out_shape),
        compiler_params=pltpu.CompilerParams(vmem_limit_bytes=16 * 2**20),
        cost_estimate=pl.CostEstimate(flops=flops, bytes_accessed=moved, transcendentals=0),
        name=name,
    )(*args)


def local(sample_collection, obs_values, obs_inverse_variance, obs_mask):
    count = lax.axis_size("mem")
    shape = sample_collection.shape
    assert shape == (LOCAL, FIELDS, BAND, WIDTH) and count * PATCH == WIDTH
    me = lax.axis_index("mem").astype(jnp.int32).reshape(1)
    near = near_rows(sample_collection, join_grid)
    rows = jnp.transpose(sample_collection.reshape(LOCAL, FIELDS * BAND, WIDTH), (1, 0, 2))
    region_shape = jax.ShapeDtypeStruct((count, 2 * LOCAL + 8, WIDTH), BF)
    inner_shape = jax.ShapeDtypeStruct((count, LOCAL, WIDTH), BF)
    observations = (obs_values, obs_inverse_variance, obs_mask)
    region = exchange(call(pack_kernel, "forecast_pack", region_shape, rows, near.reshape(-1, WIDTH), *observations))
    members, points = count * LOCAL, 2 * WIDTH
    own_shapes = [
        jax.ShapeDtypeStruct((members, WIDTH), BF),
        jax.ShapeDtypeStruct((members + 16, members), F32),
        jax.ShapeDtypeStruct((8, WIDTH), F32),
    ]
    flops = 2 * members * members * points
    region_near = near_rows(region, join_region)
    own = call(own_kernel, "own_half", own_shapes, me, region, flops=flops)
    inner = exchange(call(analysis_kernel, "analysis", inner_shape, me, region_near, *own, flops=8 * flops))
    inner_near = near_rows(inner, join_inner)
    rows_shape = jax.ShapeDtypeStruct((FIELDS * BAND, LOCAL, WIDTH), F32)
    inner = call(unpack_kernel, "unpack_own", rows_shape, inner)
    out_shape = jax.ShapeDtypeStruct((LOCAL * FIELDS * BAND, WIDTH), F32)
    cycled = call(forecast_kernel, "unpack_forecast", out_shape, inner, inner_near)
    return cycled.reshape(shape)


def solution(mesh):
    return jax.shard_map(
        local,
        mesh=mesh,
        in_specs=(
            P("mem", None, "rows", None),
            P(None, "rows", "mem"),
            P(None, "rows", "mem"),
            P(None, "rows", "mem"),
        ),
        out_specs=P("mem", None, "rows", None),
        check_vma=False,
    )
```

```python
import functools

import jax
import jax.numpy as jnp
from jax import lax
from jax.experimental import pallas as pl
from jax.experimental.pallas import tpu as pltpu
from jax.sharding import PartitionSpec as P

PATCH = 8
RADIUS = 4
FSTEPS = 4
CADV = 0.05

LOCAL = 16
FIELDS = 2
BAND = 8
WIDTH = 128
REGION = PATCH + 2 * RADIUS

BF = jnp.bfloat16
F32 = jnp.float32


def forecast_rows(u_rows, v_rows):
    for _ in range(FSTEPS):
        new_u, new_v = [], []
        for i in range(1, len(u_rows) - 1):
            cu, cv = CADV * u_rows[i], CADV * v_rows[i]
            for rows, new in ((u_rows, new_u), (v_rows, new_v)):
                along_x = pltpu.roll(rows[i], WIDTH - 1, 1) - pltpu.roll(rows[i], 1, 1)
                along_y = rows[i + 1] - rows[i - 1]
                new.append(rows[i] - (cu * along_x + cv * along_y))
        u_rows, v_rows = new_u, new_v
    return u_rows, v_rows


def swap_blocks(parts, size):
    count = len(parts)
    block = lax.broadcasted_iota(jnp.int32, parts[0].shape, 1) // size
    stride = 1
    while stride < count:
        base = min(4, count // stride)
        here = [(block // stride) % base == digit for digit in range(base)]
        new = []
        for j in range(count):
            own = (j // stride) % base
            value = parts[j]
            for digit in range(base):
                if digit != own:
                    move = (digit - own) * stride
                    value = jnp.where(here[digit], pltpu.roll(parts[j + move], (move * size) % WIDTH, 1), value)
            new.append(value)
        parts = new
        stride *= base
    return parts


def observation_rows(values_ref, inverse_ref, mask_ref):
    points = FIELDS * BAND
    weight = (mask_ref[...].astype(F32) * inverse_ref[...]).astype(BF).astype(F32).reshape(points, PATCH)
    values = values_ref[...].reshape(points, PATCH)
    high = values.astype(BF).astype(F32)
    middle = (values - high).astype(BF).astype(F32)
    low = values - high - middle
    rows = jnp.concatenate([weight, high, middle, low], 0).astype(BF)
    source = lax.broadcasted_iota(jnp.int32, (PATCH, WIDTH), 0)
    lane = lax.broadcasted_iota(jnp.int32, (PATCH, WIDTH), 1)
    spread = (lane % PATCH == source).astype(F32).astype(BF)
    wide = jnp.dot(rows, spread, preferred_element_type=F32)
    row = lax.broadcasted_iota(jnp.int32, wide.shape, 0)
    lane = lax.broadcasted_iota(jnp.int32, wide.shape, 1)
    part, field, y = row // points, (row % points) // BAND, row % BAND
    place = (field * (BAND // 2) + y % (BAND // 2)) * 2 + part % 2
    wide = jnp.where(lane // PATCH == place, wide, 0.0).astype(BF)
    target = lax.broadcasted_iota(jnp.int32, (8, 4 * points), 0)
    row = lax.broadcasted_iota(jnp.int32, (8, 4 * points), 1)
    wanted = ((row % BAND) // (BAND // 2)) * 4 + 2 + row // (2 * points)
    gather = (target == wanted).astype(F32).astype(BF)
    return jnp.dot(gather, wide, preferred_element_type=F32)


def pack_kernel(rows_ref, near_ref, values_ref, inverse_ref, mask_ref, out_ref):
    points = FIELDS * BAND

    def near(field, index):
        return near_ref[pl.ds(field * BAND + index, LOCAL, stride=points), :]

    fields = []
    for field in range(FIELDS):
        before = [near(field, r) for r in range(BAND - FSTEPS, BAND)]
        own = [rows_ref[field * BAND + r] for r in range(BAND)]
        after = [near(field, r) for r in range(FSTEPS)]
        fields.append(before + own + after)
    done = forecast_rows(*fields)
    half_rows = BAND // 2
    index = lax.broadcasted_iota(jnp.int32, (8, WIDTH), 0)
    values, means = [], [jnp.zeros((8, WIDTH), F32)] * (FIELDS * half_rows)
    for half in range(2):
        for j in range(FIELDS * half_rows):
            value = done[j // half_rows][half * half_rows + j % half_rows]
            mean = jnp.sum(value, 0, keepdims=True) * (1.0 / LOCAL)
            high = mean.astype(BF).astype(F32)
            means[j] = jnp.where(index == 4 * half, high, jnp.where(index == 4 * half + 1, mean - high, means[j]))
            values.append(value - mean)
    rows = jnp.concatenate(values + means, 0).astype(BF)
    column = lax.broadcasted_iota(jnp.int32, (WIDTH, 2 * WIDTH), 0)
    lane = lax.broadcasted_iota(jnp.int32, (WIDTH, 2 * WIDTH), 1)
    wanted = ((lane // REGION) * PATCH + lane % REGION + (WIDTH - RADIUS)) % WIDTH
    widen = (column == wanted).astype(F32).astype(BF)
    wide = jnp.dot(rows, widen, preferred_element_type=F32)
    obs = observation_rows(values_ref, inverse_ref, mask_ref)
    start = len(values) * LOCAL
    is_mean = index & 2 == 0
    for side in range(2):
        means = [wide[start + j * 8 : start + j * 8 + 8, side * WIDTH : (side + 1) * WIDTH] for j in range(8)]
        for i, mean in enumerate(swap_blocks(means, REGION)):
            out_ref[side * 8 + i, 2 * LOCAL :] = jnp.where(is_mean, mean, obs).astype(BF)
        for half in range(2):
            parts = [
                wide[(half * 8 + j) * LOCAL : (half * 8 + j + 1) * LOCAL, side * WIDTH : (side + 1) * WIDTH].astype(BF)
                for j in range(8)
            ]
            parts = swap_blocks(parts, REGION)
            for i in range(8):
                out_ref[side * 8 + i, half * LOCAL : (half + 1) * LOCAL] = parts[i]


def halves_of(ref, me):
    count = ref.shape[0]
    tails = [ref[s, 2 * LOCAL :].astype(F32) for s in range(count)]

    def tail_of(device):
        return ref[device, 2 * LOCAL :].astype(F32)

    lane = lax.broadcasted_iota(jnp.int32, (8, WIDTH), 1) % REGION
    left = tail_of(lax.rem(me + count - 1, count))
    own = tail_of(me)
    right = tail_of(lax.rem(me + 1, count))

    def seen(offset):
        return jnp.where(
            lane < RADIUS,
            pltpu.roll(left, (WIDTH + RADIUS - PATCH - offset) % WIDTH, 1),
            jnp.where(
                lane < RADIUS + PATCH,
                pltpu.roll(own, (WIDTH + RADIUS - offset) % WIDTH, 1),
                pltpu.roll(right, (WIDTH + RADIUS + PATCH - offset) % WIDTH, 1),
            ),
        )

    first, second = seen(0), seen(PATCH)
    result = []
    for half in range(2):
        base = half * 4
        means = [t[base : base + 1] + t[base + 1 : base + 2] for t in tails]
        mean = functools.reduce(jnp.add, means) * (1.0 / count)
        deviation = []
        for s, own_mean in enumerate(means):
            value = ref[s, half * LOCAL : (half + 1) * LOCAL].astype(F32)
            deviation.append((value + (own_mean - mean)).astype(BF))
        weight = first[base + 2 : base + 3]
        obs = second[base + 2 : base + 3] + first[base + 3 : base + 4] + second[base + 3 : base + 4]
        innovation = (obs - mean).astype(BF).astype(F32)
        result.append((jnp.concatenate(deviation, 0), mean, weight, innovation))
    return result


def half_sums(halves, row_distances):
    lane = lax.broadcasted_iota(jnp.int32, (1, WIDTH), 1)
    region_column = lane % REGION
    half_row = (lane // REGION) % (BAND // 2)
    column_distance = jnp.maximum(
        jnp.maximum(RADIUS - region_column, region_column - (RADIUS + PATCH - 1)), 0
    )
    weighted, deviation, innovation = [], [], []
    for (dev, _, weight, inno), row_distance in zip(halves, row_distances):
        far = jnp.maximum(row_distance(half_row), column_distance).astype(F32)
        factor = weight * (1.0 - far / (RADIUS + 1.0))
        weighted.append((dev.astype(F32) * factor).astype(BF))
        deviation.append(dev)
        innovation.append(jnp.broadcast_to(inno, (16, WIDTH)).astype(BF))
    deviation = jnp.concatenate(deviation, 1)
    rows = jnp.concatenate([deviation, jnp.concatenate(innovation, 1)], 0)
    weighted = jnp.concatenate(weighted, 1)
    return deviation, lax.dot_general(rows, weighted, (((1,), (1,)), ((), ())), preferred_element_type=F32)


def own_kernel(me_ref, own_ref, inner_ref, sums_ref, mean_ref):
    halves = halves_of(own_ref, me_ref[0])
    deviation, sums_ref[...] = half_sums(halves, [jnp.zeros_like] * 2)
    lane = lax.broadcasted_iota(jnp.int32, (2 * WIDTH, WIDTH), 0)
    target = lax.broadcasted_iota(jnp.int32, (2 * WIDTH, WIDTH), 1)
    narrow = (lane == (target // PATCH) * REGION + RADIUS + target % PATCH).astype(F32).astype(BF)
    inner_ref[...] = jnp.dot(deviation, narrow, preferred_element_type=F32).astype(BF)
    mean = jnp.broadcast_to(jnp.concatenate([halves[0][1], halves[1][1]], 1), (16, 2 * WIDTH))
    high = mean.astype(BF)
    middle = (mean - high.astype(F32)).astype(BF)
    low = (mean - high.astype(F32) - middle.astype(F32)).astype(BF)
    parts = jnp.dot(jnp.concatenate([high, middle, low], 0), narrow, preferred_element_type=F32)
    mean_ref[...] = parts[:8] + (parts[16:24] + parts[32:40])


def analysis_kernel(me_ref, near_ref, inner_ref, sums_ref, mean_ref, out_ref):
    count = near_ref.shape[0]
    members = count * LOCAL
    halves = halves_of(near_ref, me_ref[0])
    both = sums_ref[...] + half_sums(halves, [lambda r: r + 1, lambda r: RADIUS - r])[1]
    row = lax.broadcasted_iota(jnp.int32, (members, members), 0)
    col = lax.broadcasted_iota(jnp.int32, (members, members), 1)
    system = both[:members] + jnp.where(row == col, members - 1.0, 0.0)
    def mul(a, b):
        return jnp.dot(a.astype(BF), b.astype(BF), preferred_element_type=F32)

    def with_line(a, line):
        return jnp.concatenate([a.astype(BF), line.astype(BF)], 0)

    inner, line = inner_ref[...], both[members:]
    system_b = system.astype(BF)
    first = mul(with_line(system_b, line), system_b)
    system_x = mul(system_b, inner)
    scale = jnp.sqrt(jnp.sum(system * system))
    inverse = 1.0 / scale
    x1 = 1.5 * inner.astype(F32) - (0.5 * inverse) * system_x
    line1 = 1.5 * line - (0.5 * inverse) * first[members:]
    y1 = inverse * (1.5 * system - (0.5 * inverse) * first[:members])
    p1 = 1.5 * y1 - (0.5 * inverse) * mul(y1, system_b)
    p1b = p1.astype(BF)
    second = mul(with_line(p1b, line1), p1b)
    x2 = 1.5 * x1 - 0.5 * mul(p1b, x1)
    line2 = 1.5 * line1 - 0.5 * second[members:]
    q1 = 1.5 * p1 - 0.5 * second[:members]
    p2 = 1.5 * q1 - 0.5 * mul(q1, p1b)
    p2b = p2.astype(BF)
    factor = 1.0 / jnp.sqrt(scale)
    x3 = (1.5 * x2 - 0.5 * mul(p2b, x2)) * factor
    line3 = (1.5 * line2 - 0.5 * mul(line2, p2b)) * factor
    line_b = line3.astype(BF)
    lines = with_line(line_b, line3 - line_b.astype(F32))
    shift = mul(lines, x3)
    shift = shift[:1] + shift[16:17]
    root = jnp.sqrt(jnp.full((1, 1), members - 1.0, F32))
    result = (root * x3 + (shift + mean_ref[:1])).astype(BF)
    for s in range(count):
        out_ref[s] = result[s * LOCAL : (s + 1) * LOCAL]


def unpacked(ref):
    return [row.astype(F32) for row in swap_blocks([ref[p] for p in range(ref.shape[0])], PATCH)]


def unpack_kernel(in_ref, out_ref):
    for i, row in enumerate(unpacked(in_ref)):
        out_ref[i] = row


def forecast_kernel(own_ref, near_ref, out_ref):
    def by_field(rows):
        half = BAND // 2
        return [
            [rows[h * FIELDS * half + field * half + r] for h in range(2) for r in range(half)]
            for field in range(FIELDS)
        ]

    own, near = by_field(own_ref), by_field(unpacked(near_ref))
    fields = [n[BAND - FSTEPS :] + o + n[:FSTEPS] for o, n in zip(own, near)]
    done = forecast_rows(*fields)
    for field in range(FIELDS):
        for r in range(BAND):
            out_ref[pl.ds(field * BAND + r, LOCAL, stride=FIELDS * BAND), :] = done[field][r]


def from_next(value):
    count = lax.axis_size("rows")
    return lax.ppermute(value, "rows", [((i + 1) % count, i) for i in range(count)])


def from_previous(value):
    count = lax.axis_size("rows")
    return lax.ppermute(value, "rows", [(i, (i + 1) % count) for i in range(count)])


def near_rows(value, join):
    if lax.axis_size("rows") == 2:
        return from_next(value)
    return join(from_next(value), from_previous(value))


def join_grid(after, before):
    return jnp.concatenate([after[:, :, : BAND // 2], before[:, :, BAND // 2 :]], 2)


def join_region(after, before):
    after, before = (x.reshape(x.shape[0], -1, 4, WIDTH) for x in (after, before))
    near = jnp.concatenate([after[:, :4], before[:, 4:8], after[:, 8:9], before[:, 9:]], 1)
    return near.reshape(near.shape[0], -1, WIDTH)


def join_inner(after, before):
    return jnp.concatenate([after[..., : WIDTH // 2], before[..., WIDTH // 2 :]], 2)


def exchange(value):
    return lax.all_to_all(value, "mem", split_axis=0, concat_axis=0, tiled=True)


def call(kernel, name, out_shape, *args, flops=0):
    spaces = [pltpu.SMEM if arg.shape == (1,) else pltpu.VMEM for arg in args]
    moved = sum(x.size * x.dtype.itemsize for x in [*args, *jax.tree.leaves(out_shape)])
    return pl.pallas_call(
        kernel,
        out_shape=out_shape,
        in_specs=[pl.BlockSpec(memory_space=space) for space in spaces],
        out_specs=jax.tree.map(lambda _: pl.BlockSpec(memory_space=pltpu.VMEM), out_shape),
        compiler_params=pltpu.CompilerParams(vmem_limit_bytes=16 * 2**20),
        cost_estimate=pl.CostEstimate(flops=flops, bytes_accessed=moved, transcendentals=0),
        name=name,
    )(*args)


def local(sample_collection, obs_values, obs_inverse_variance, obs_mask):
    count = lax.axis_size("mem")
    shape = sample_collection.shape
    assert shape == (LOCAL, FIELDS, BAND, WIDTH) and count * PATCH == WIDTH
    me = lax.axis_index("mem").astype(jnp.int32).reshape(1)
    near = near_rows(sample_collection, join_grid)
    rows = jnp.transpose(sample_collection.reshape(LOCAL, FIELDS * BAND, WIDTH), (1, 0, 2))
    region_shape = jax.ShapeDtypeStruct((count, 2 * LOCAL + 8, WIDTH), BF)
    inner_shape = jax.ShapeDtypeStruct((count, LOCAL, WIDTH), BF)
    observations = (obs_values, obs_inverse_variance, obs_mask)
    region = exchange(call(pack_kernel, "forecast_pack", region_shape, rows, near.reshape(-1, WIDTH), *observations))
    members, points = count * LOCAL, 2 * WIDTH
    own_shapes = [
        jax.ShapeDtypeStruct((members, WIDTH), BF),
        jax.ShapeDtypeStruct((members + 16, members), F32),
        jax.ShapeDtypeStruct((8, WIDTH), F32),
    ]
    flops = 2 * members * members * points
    region_near = near_rows(region, join_region)
    own = call(own_kernel, "own_half", own_shapes, me, region, flops=flops)
    inner = exchange(call(analysis_kernel, "analysis", inner_shape, me, region_near, *own, flops=8 * flops))
    inner_near = near_rows(inner, join_inner)
    rows_shape = jax.ShapeDtypeStruct((FIELDS * BAND, LOCAL, WIDTH), F32)
    inner = call(unpack_kernel, "unpack_own", rows_shape, inner)
    out_shape = jax.ShapeDtypeStruct((LOCAL * FIELDS * BAND, WIDTH), F32)
    cycled = call(forecast_kernel, "unpack_forecast", out_shape, inner, inner_near)
    return cycled.reshape(shape)


def solution(mesh):
    return jax.shard_map(
        local,
        mesh=mesh,
        in_specs=(
            P("mem", None, "rows", None),
            P(None, "rows", "mem"),
            P(None, "rows", "mem"),
            P(None, "rows", "mem"),
        ),
        out_specs=P("mem", None, "rows", None),
        check_vma=False,
    )
```

```python
import functools

import jax
import jax.numpy as jnp
from jax import lax
from jax.experimental import pallas as pl
from jax.experimental.pallas import tpu as pltpu
from jax.sharding import PartitionSpec as P

PATCH = 8
RADIUS = 4
FSTEPS = 4
CADV = 0.05

LOCAL = 16
FIELDS = 2
BAND = 8
WIDTH = 128
REGION = PATCH + 2 * RADIUS

BF = jnp.bfloat16
F32 = jnp.float32


def forecast_rows(u_rows, v_rows):
    for _ in range(FSTEPS):
        new_u, new_v = [], []
        for i in range(1, len(u_rows) - 1):
            cu, cv = CADV * u_rows[i], CADV * v_rows[i]
            for rows, new in ((u_rows, new_u), (v_rows, new_v)):
                along_x = pltpu.roll(rows[i], WIDTH - 1, 1) - pltpu.roll(rows[i], 1, 1)
                along_y = rows[i + 1] - rows[i - 1]
                new.append(rows[i] - (cu * along_x + cv * along_y))
        u_rows, v_rows = new_u, new_v
    return u_rows, v_rows


def swap_blocks(parts, size):
    count = len(parts)
    lane = lax.broadcasted_iota(jnp.int32, parts[0].shape, 1) // size
    stride = 1
    while stride < count:
        upper = (lane & stride) != 0
        new = list(parts)
        for j in range(count):
            if j & stride == 0:
                a, b = parts[j], parts[j + stride]
                new[j] = jnp.where(upper, pltpu.roll(b, stride * size, 1), a)
                new[j + stride] = jnp.where(upper, b, pltpu.roll(a, WIDTH - stride * size, 1))
        parts = new
        stride *= 2
    return parts


def observation_rows(values_ref, inverse_ref, mask_ref):
    points = FIELDS * BAND
    weight = (mask_ref[...].astype(F32) * inverse_ref[...]).astype(BF).astype(F32).reshape(points, PATCH)
    values = values_ref[...].reshape(points, PATCH)
    high = values.astype(BF).astype(F32)
    middle = (values - high).astype(BF).astype(F32)
    low = values - high - middle
    rows = jnp.concatenate([weight, high, middle, low], 0).astype(BF)
    source = lax.broadcasted_iota(jnp.int32, (PATCH, WIDTH), 0)
    lane = lax.broadcasted_iota(jnp.int32, (PATCH, WIDTH), 1)
    spread = (lane % PATCH == source).astype(F32).astype(BF)
    wide = jnp.dot(rows, spread, preferred_element_type=F32)
    row = lax.broadcasted_iota(jnp.int32, wide.shape, 0)
    lane = lax.broadcasted_iota(jnp.int32, wide.shape, 1)
    part, field, y = row // points, (row % points) // BAND, row % BAND
    place = (field * (BAND // 2) + y % (BAND // 2)) * 2 + part % 2
    wide = jnp.where(lane // PATCH == place, wide, 0.0).astype(BF)
    target = lax.broadcasted_iota(jnp.int32, (8, 4 * points), 0)
    row = lax.broadcasted_iota(jnp.int32, (8, 4 * points), 1)
    wanted = ((row % BAND) // (BAND // 2)) * 4 + 2 + row // (2 * points)
    gather = (target == wanted).astype(F32).astype(BF)
    return jnp.dot(gather, wide, preferred_element_type=F32)


def pack_kernel(rows_ref, near_ref, values_ref, inverse_ref, mask_ref, out_ref):
    points = FIELDS * BAND

    def near(field, index):
        return near_ref[pl.ds(field * BAND + index, LOCAL, stride=points), :]

    fields = []
    for field in range(FIELDS):
        before = [near(field, r) for r in range(BAND - FSTEPS, BAND)]
        own = [rows_ref[field * BAND + r] for r in range(BAND)]
        after = [near(field, r) for r in range(FSTEPS)]
        fields.append(before + own + after)
    done = forecast_rows(*fields)
    last = out_ref.shape[0] - 1
    half_rows = BAND // 2
    index = lax.broadcasted_iota(jnp.int32, (8, WIDTH), 0)
    values, means = [], [jnp.zeros((8, WIDTH), F32)] * (FIELDS * half_rows)
    for half in range(2):
        for j in range(FIELDS * half_rows):
            value = done[j // half_rows][half * half_rows + j % half_rows]
            mean = jnp.sum(value, 0, keepdims=True) * (1.0 / LOCAL)
            high = mean.astype(BF).astype(F32)
            means[j] = jnp.where(index == 4 * half, high, jnp.where(index == 4 * half + 1, mean - high, means[j]))
            values.append(value - mean)
    rows = jnp.concatenate(values + means, 0).astype(BF)
    column = lax.broadcasted_iota(jnp.int32, (WIDTH, 2 * WIDTH), 0)
    lane = lax.broadcasted_iota(jnp.int32, (WIDTH, 2 * WIDTH), 1)
    wanted = ((lane // REGION) * PATCH + lane % REGION + (WIDTH - RADIUS)) % WIDTH
    widen = (column == wanted).astype(F32).astype(BF)
    wide = jnp.dot(rows, widen, preferred_element_type=F32)
    obs = observation_rows(values_ref, inverse_ref, mask_ref)
    start = len(values) * LOCAL
    is_mean = index & 2 == 0
    means = []
    for j in range(8):
        part = wide[start + j * 8 : start + j * 8 + 8]
        means.append(jnp.where(is_mean, part[:, :WIDTH], pltpu.roll(part[:, WIDTH:], 2, 0)))
    means = swap_blocks(means, REGION)
    for side in range(2):
        for half in range(2):
            parts = [
                wide[(half * 8 + j) * LOCAL : (half * 8 + j + 1) * LOCAL, side * WIDTH : (side + 1) * WIDTH].astype(BF)
                for j in range(8)
            ]
            parts = swap_blocks(parts, REGION)
            for i in range(8):
                out_ref[last - side * 8 - i, half * LOCAL : (half + 1) * LOCAL] = parts[i]
        for i in range(8):
            mean = means[i] if side == 0 else pltpu.roll(means[i], 6, 0)
            out_ref[last - side * 8 - i, 2 * LOCAL :] = jnp.where(is_mean, mean, obs).astype(BF)


def halves_of(ref, me):
    count = ref.shape[0]
    tails = [ref[s, 2 * LOCAL :].astype(F32) for s in range(count)]

    def tail_of(device):
        return ref[count - 1 - device, 2 * LOCAL :].astype(F32)

    lane = lax.broadcasted_iota(jnp.int32, (8, WIDTH), 1) % REGION
    left = tail_of(lax.rem(me + count - 1, count))
    own = tail_of(me)
    right = tail_of(lax.rem(me + 1, count))

    def seen(offset):
        return jnp.where(
            lane < RADIUS,
            pltpu.roll(left, (WIDTH + RADIUS - PATCH - offset) % WIDTH, 1),
            jnp.where(
                lane < RADIUS + PATCH,
                pltpu.roll(own, (WIDTH + RADIUS - offset) % WIDTH, 1),
                pltpu.roll(right, (WIDTH + RADIUS + PATCH - offset) % WIDTH, 1),
            ),
        )

    first, second = seen(0), seen(PATCH)
    result = []
    for half in range(2):
        base = half * 4
        means = [t[base : base + 1] + t[base + 1 : base + 2] for t in tails]
        mean = functools.reduce(jnp.add, means) * (1.0 / count)
        deviation = []
        for s, own_mean in enumerate(means):
            value = ref[s, half * LOCAL : (half + 1) * LOCAL].astype(F32)
            deviation.append((value + (own_mean - mean)).astype(BF))
        weight = first[base + 2 : base + 3]
        obs = second[base + 2 : base + 3] + first[base + 3 : base + 4] + second[base + 3 : base + 4]
        innovation = (obs - mean).astype(BF).astype(F32)
        result.append((jnp.concatenate(deviation, 0), mean, weight, innovation))
    return result


def half_sums(halves, row_distances):
    lane = lax.broadcasted_iota(jnp.int32, (1, WIDTH), 1)
    region_column = lane % REGION
    half_row = (lane // REGION) % (BAND // 2)
    column_distance = jnp.maximum(
        jnp.maximum(RADIUS - region_column, region_column - (RADIUS + PATCH - 1)), 0
    )
    weighted, deviation, innovation = [], [], []
    for (dev, _, weight, inno), row_distance in zip(halves, row_distances):
        far = jnp.maximum(row_distance(half_row), column_distance).astype(F32)
        factor = weight * (1.0 - far / (RADIUS + 1.0))
        weighted.append((dev.astype(F32) * factor).astype(BF))
        deviation.append(dev)
        innovation.append(jnp.broadcast_to(inno, (16, WIDTH)).astype(BF))
    deviation = jnp.concatenate(deviation, 1)
    rows = jnp.concatenate([deviation, jnp.concatenate(innovation, 1)], 0)
    weighted = jnp.concatenate(weighted, 1)
    return deviation, lax.dot_general(rows, weighted, (((1,), (1,)), ((), ())), preferred_element_type=F32)


def own_kernel(me_ref, own_ref, inner_ref, sums_ref, mean_ref):
    halves = halves_of(own_ref, me_ref[0])
    deviation, sums_ref[...] = half_sums(halves, [jnp.zeros_like] * 2)
    lane = lax.broadcasted_iota(jnp.int32, (2 * WIDTH, WIDTH), 0)
    target = lax.broadcasted_iota(jnp.int32, (2 * WIDTH, WIDTH), 1)
    narrow = (lane == (target // PATCH) * REGION + RADIUS + target % PATCH).astype(F32).astype(BF)
    inner_ref[...] = jnp.dot(deviation, narrow, preferred_element_type=F32).astype(BF)
    mean = jnp.broadcast_to(jnp.concatenate([halves[0][1], halves[1][1]], 1), (16, 2 * WIDTH))
    high = mean.astype(BF)
    middle = (mean - high.astype(F32)).astype(BF)
    low = (mean - high.astype(F32) - middle.astype(F32)).astype(BF)
    parts = jnp.dot(jnp.concatenate([high, middle, low], 0), narrow, preferred_element_type=F32)
    mean_ref[...] = parts[:8] + (parts[16:24] + parts[32:40])


def analysis_kernel(me_ref, near_ref, inner_ref, sums_ref, mean_ref, out_ref):
    count = near_ref.shape[0]
    members = count * LOCAL
    halves = halves_of(near_ref, me_ref[0])
    both = sums_ref[...] + half_sums(halves, [lambda r: r + 1, lambda r: RADIUS - r])[1]
    row = lax.broadcasted_iota(jnp.int32, (members, members), 0)
    col = lax.broadcasted_iota(jnp.int32, (members, members), 1)
    system = both[:members] + jnp.where(row == col, members - 1.0, 0.0)
    def mul(a, b):
        return jnp.dot(a.astype(BF), b.astype(BF), preferred_element_type=F32)

    def with_line(a, line):
        return jnp.concatenate([a.astype(BF), line.astype(BF)], 0)

    inner, line = inner_ref[...], both[members:]
    system_b = system.astype(BF)
    first = mul(with_line(system_b, line), system_b)
    system_x = mul(system_b, inner)
    scale = jnp.sqrt(jnp.sum(system * system))
    inverse = 1.0 / scale
    x1 = 1.5 * inner.astype(F32) - (0.5 * inverse) * system_x
    line1 = 1.5 * line - (0.5 * inverse) * first[members:]
    y1 = inverse * (1.5 * system - (0.5 * inverse) * first[:members])
    p1 = 1.5 * y1 - (0.5 * inverse) * mul(y1, system_b)
    p1b = p1.astype(BF)
    second = mul(with_line(p1b, line1), p1b)
    x2 = 1.5 * x1 - 0.5 * mul(p1b, x1)
    line2 = 1.5 * line1 - 0.5 * second[members:]
    q1 = 1.5 * p1 - 0.5 * second[:members]
    p2 = 1.5 * q1 - 0.5 * mul(q1, p1b)
    p2b = p2.astype(BF)
    factor = 1.0 / jnp.sqrt(scale)
    x3 = (1.5 * x2 - 0.5 * mul(p2b, x2)) * factor
    line3 = (1.5 * line2 - 0.5 * mul(line2, p2b)) * factor
    line_b = line3.astype(BF)
    lines = with_line(line_b, line3 - line_b.astype(F32))
    shift = mul(lines, x3)
    shift = shift[:1] + shift[16:17]
    root = jnp.sqrt(jnp.full((1, 1), members - 1.0, F32))
    result = (root * x3 + (shift + mean_ref[:1])).astype(BF)
    for s in range(count):
        out_ref[s] = result[s * LOCAL : (s + 1) * LOCAL]


def unpacked(ref):
    return [row.astype(F32) for row in swap_blocks([ref[p] for p in reversed(range(ref.shape[0]))], PATCH)]


def unpack_kernel(in_ref, out_ref):
    for i, row in enumerate(unpacked(in_ref)):
        out_ref[i] = row


def forecast_kernel(own_ref, near_ref, out_ref):
    def by_field(rows):
        half = BAND // 2
        return [
            [rows[h * FIELDS * half + field * half + r] for h in range(2) for r in range(half)]
            for field in range(FIELDS)
        ]

    own, near = by_field(own_ref), by_field(unpacked(near_ref))
    fields = [n[BAND - FSTEPS :] + o + n[:FSTEPS] for o, n in zip(own, near)]
    done = forecast_rows(*fields)
    for field in range(FIELDS):
        for r in range(BAND):
            out_ref[pl.ds(field * BAND + r, LOCAL, stride=FIELDS * BAND), :] = done[field][r]


def from_next(value):
    count = lax.axis_size("rows")
    return lax.ppermute(value, "rows", [((i + 1) % count, i) for i in range(count)])


def from_previous(value):
    count = lax.axis_size("rows")
    return lax.ppermute(value, "rows", [(i, (i + 1) % count) for i in range(count)])


def near_rows(value, join):
    if lax.axis_size("rows") == 2:
        return from_next(value)
    return join(from_next(value), from_previous(value))


def join_grid(after, before):
    return jnp.concatenate([after[:, :, : BAND // 2], before[:, :, BAND // 2 :]], 2)


def join_region(after, before):
    after, before = (x.reshape(x.shape[0], -1, 4, WIDTH) for x in (after, before))
    near = jnp.concatenate([after[:, :4], before[:, 4:8], after[:, 8:9], before[:, 9:]], 1)
    return near.reshape(near.shape[0], -1, WIDTH)


def join_inner(after, before):
    return jnp.concatenate([after[..., : WIDTH // 2], before[..., WIDTH // 2 :]], 2)


def exchange(value):
    group = [list(reversed(range(lax.axis_size("mem"))))]
    return lax.all_to_all(value, "mem", split_axis=0, concat_axis=0, axis_index_groups=group, tiled=True)


def call(kernel, name, out_shape, *args, flops=0):
    spaces = [pltpu.SMEM if arg.shape == (1,) else pltpu.VMEM for arg in args]
    moved = sum(x.size * x.dtype.itemsize for x in [*args, *jax.tree.leaves(out_shape)])
    return pl.pallas_call(
        kernel,
        out_shape=out_shape,
        in_specs=[pl.BlockSpec(memory_space=space) for space in spaces],
        out_specs=jax.tree.map(lambda _: pl.BlockSpec(memory_space=pltpu.VMEM), out_shape),
        compiler_params=pltpu.CompilerParams(vmem_limit_bytes=16 * 2**20),
        cost_estimate=pl.CostEstimate(flops=flops, bytes_accessed=moved, transcendentals=0),
        name=name,
    )(*args)


def local(sample_collection, obs_values, obs_inverse_variance, obs_mask):
    count = lax.axis_size("mem")
    shape = sample_collection.shape
    assert shape == (LOCAL, FIELDS, BAND, WIDTH) and count * PATCH == WIDTH
    me = lax.axis_index("mem").astype(jnp.int32).reshape(1)
    near = near_rows(sample_collection, join_grid)
    rows = jnp.transpose(sample_collection.reshape(LOCAL, FIELDS * BAND, WIDTH), (1, 0, 2))
    region_shape = jax.ShapeDtypeStruct((count, 2 * LOCAL + 8, WIDTH), BF)
    inner_shape = jax.ShapeDtypeStruct((count, LOCAL, WIDTH), BF)
    observations = (obs_values, obs_inverse_variance, obs_mask)
    region = exchange(call(pack_kernel, "forecast_pack", region_shape, rows, near.reshape(-1, WIDTH), *observations))
    members, points = count * LOCAL, 2 * WIDTH
    own_shapes = [
        jax.ShapeDtypeStruct((members, WIDTH), BF),
        jax.ShapeDtypeStruct((members + 16, members), F32),
        jax.ShapeDtypeStruct((8, WIDTH), F32),
    ]
    flops = 2 * members * members * points
    region_near = near_rows(region, join_region)
    own = call(own_kernel, "own_half", own_shapes, me, region, flops=flops)
    inner = exchange(call(analysis_kernel, "analysis", inner_shape, me, region_near, *own, flops=8 * flops))
    inner_near = near_rows(inner, join_inner)
    rows_shape = jax.ShapeDtypeStruct((FIELDS * BAND, LOCAL, WIDTH), F32)
    inner = call(unpack_kernel, "unpack_own", rows_shape, inner)
    out_shape = jax.ShapeDtypeStruct((LOCAL * FIELDS * BAND, WIDTH), F32)
    cycled = call(forecast_kernel, "unpack_forecast", out_shape, inner, inner_near)
    return cycled.reshape(shape)


def solution(mesh):
    return jax.shard_map(
        local,
        mesh=mesh,
        in_specs=(
            P("mem", None, "rows", None),
            P(None, "rows", "mem"),
            P(None, "rows", "mem"),
            P(None, "rows", "mem"),
        ),
        out_specs=P("mem", None, "rows", None),
        check_vma=False,
    )
```

```python
import functools

import jax
import jax.numpy as jnp
from jax import lax
from jax.experimental import pallas as pl
from jax.experimental.pallas import tpu as pltpu
from jax.sharding import PartitionSpec as P

PATCH = 8
RADIUS = 4
FSTEPS = 4
CADV = 0.05

LOCAL = 16
FIELDS = 2
BAND = 8
WIDTH = 128
PLACES = WIDTH // PATCH
REGION = PATCH + 2 * RADIUS

BF = jnp.bfloat16
F32 = jnp.float32


def position(place):
    low, high = place & 3, place >> 2
    return PLACES - 1 - (low * 4 + (high & 1) * 2 + (high >> 1))


def forecast_rows(u_rows, v_rows):
    for _ in range(FSTEPS):
        new_u, new_v = [], []
        for i in range(1, len(u_rows) - 1):
            cu, cv = CADV * u_rows[i], CADV * v_rows[i]
            for rows, new in ((u_rows, new_u), (v_rows, new_v)):
                along_x = pltpu.roll(rows[i], WIDTH - 1, 1) - pltpu.roll(rows[i], 1, 1)
                along_y = rows[i + 1] - rows[i - 1]
                new.append(rows[i] - (cu * along_x + cv * along_y))
        u_rows, v_rows = new_u, new_v
    return u_rows, v_rows


def swap_blocks(parts, size):
    count = len(parts)
    lane = lax.broadcasted_iota(jnp.int32, parts[0].shape, 1) // size
    stride = 1
    while stride < count:
        upper = (lane & stride) != 0
        new = list(parts)
        for j in range(count):
            if j & stride == 0:
                a, b = parts[j], parts[j + stride]
                new[j] = jnp.where(upper, pltpu.roll(b, stride * size, 1), a)
                new[j + stride] = jnp.where(upper, b, pltpu.roll(a, WIDTH - stride * size, 1))
        parts = new
        stride *= 2
    return parts


def observation_rows(values_ref, inverse_ref, mask_ref):
    points = FIELDS * BAND
    weight = (mask_ref[...].astype(F32) * inverse_ref[...]).astype(BF).astype(F32).reshape(points, PATCH)
    values = values_ref[...].reshape(points, PATCH)
    high = values.astype(BF).astype(F32)
    middle = (values - high).astype(BF).astype(F32)
    low = values - high - middle
    rows = jnp.concatenate([weight, high, middle, low], 0).astype(BF)
    source = lax.broadcasted_iota(jnp.int32, (PATCH, WIDTH), 0)
    lane = lax.broadcasted_iota(jnp.int32, (PATCH, WIDTH), 1)
    spread = (lane % PATCH == source).astype(F32).astype(BF)
    wide = jnp.dot(rows, spread, preferred_element_type=F32)
    row = lax.broadcasted_iota(jnp.int32, wide.shape, 0)
    lane = lax.broadcasted_iota(jnp.int32, wide.shape, 1)
    part, field, y = row // points, (row % points) // BAND, row % BAND
    place = (field * (BAND // 2) + y % (BAND // 2)) * 2 + part % 2
    wide = jnp.where(lane // PATCH == place, wide, 0.0).astype(BF)
    target = lax.broadcasted_iota(jnp.int32, (8, 4 * points), 0)
    row = lax.broadcasted_iota(jnp.int32, (8, 4 * points), 1)
    wanted = ((row % BAND) // (BAND // 2)) * 4 + 2 + row // (2 * points)
    gather = (target == wanted).astype(F32).astype(BF)
    return jnp.dot(gather, wide, preferred_element_type=F32)


def pack_kernel(rows_ref, near_ref, values_ref, inverse_ref, mask_ref, out_ref):
    points = FIELDS * BAND

    def near(field, index):
        return near_ref[pl.ds(field * BAND + index, LOCAL, stride=points), :]

    fields = []
    for field in range(FIELDS):
        before = [near(field, r) for r in range(BAND - FSTEPS, BAND)]
        own = [rows_ref[field * BAND + r] for r in range(BAND)]
        after = [near(field, r) for r in range(FSTEPS)]
        fields.append(before + own + after)
    done = forecast_rows(*fields)
    half_rows = BAND // 2
    index = lax.broadcasted_iota(jnp.int32, (8, WIDTH), 0)
    values, means = [], [jnp.zeros((8, WIDTH), F32)] * (FIELDS * half_rows)
    for half in range(2):
        for j in range(FIELDS * half_rows):
            value = done[j // half_rows][half * half_rows + j % half_rows]
            mean = jnp.sum(value, 0, keepdims=True) * (1.0 / LOCAL)
            high = mean.astype(BF).astype(F32)
            means[j] = jnp.where(index == 4 * half, high, jnp.where(index == 4 * half + 1, mean - high, means[j]))
            values.append(value - mean)
    rows = jnp.concatenate(values + means, 0).astype(BF)
    column = lax.broadcasted_iota(jnp.int32, (WIDTH, 2 * WIDTH), 0)
    lane = lax.broadcasted_iota(jnp.int32, (WIDTH, 2 * WIDTH), 1)
    wanted = ((lane // REGION) * PATCH + lane % REGION + (WIDTH - RADIUS)) % WIDTH
    widen = (column == wanted).astype(F32).astype(BF)
    wide = jnp.dot(rows, widen, preferred_element_type=F32)
    obs = observation_rows(values_ref, inverse_ref, mask_ref)
    start = len(values) * LOCAL
    is_mean = index & 2 == 0
    means = []
    for j in range(8):
        part = wide[start + j * 8 : start + j * 8 + 8]
        means.append(jnp.where(is_mean, part[:, :WIDTH], pltpu.roll(part[:, WIDTH:], 2, 0)))
    means = swap_blocks(means, REGION)
    for side in range(2):
        for half in range(2):
            parts = [
                wide[(half * 8 + j) * LOCAL : (half * 8 + j + 1) * LOCAL, side * WIDTH : (side + 1) * WIDTH].astype(BF)
                for j in range(8)
            ]
            parts = swap_blocks(parts, REGION)
            for i in range(8):
                out_ref[position(side * 8 + i), half * LOCAL : (half + 1) * LOCAL] = parts[i]
        for i in range(8):
            mean = means[i] if side == 0 else pltpu.roll(means[i], 6, 0)
            out_ref[position(side * 8 + i), 2 * LOCAL :] = jnp.where(is_mean, mean, obs).astype(BF)


def halves_of(ref, me):
    count = ref.shape[0]
    tails = [ref[s, 2 * LOCAL :].astype(F32) for s in range(count)]

    def tail_of(device):
        return ref[position(device), 2 * LOCAL :].astype(F32)

    lane = lax.broadcasted_iota(jnp.int32, (8, WIDTH), 1) % REGION
    left = tail_of(lax.rem(me + count - 1, count))
    own = tail_of(me)
    right = tail_of(lax.rem(me + 1, count))

    def seen(offset):
        return jnp.where(
            lane < RADIUS,
            pltpu.roll(left, (WIDTH + RADIUS - PATCH - offset) % WIDTH, 1),
            jnp.where(
                lane < RADIUS + PATCH,
                pltpu.roll(own, (WIDTH + RADIUS - offset) % WIDTH, 1),
                pltpu.roll(right, (WIDTH + RADIUS + PATCH - offset) % WIDTH, 1),
            ),
        )

    first, second = seen(0), seen(PATCH)
    result = []
    for half in range(2):
        base = half * 4
        means = [t[base : base + 1] + t[base + 1 : base + 2] for t in tails]
        mean = functools.reduce(jnp.add, means) * (1.0 / count)
        deviation = []
        for s, own_mean in enumerate(means):
            value = ref[s, half * LOCAL : (half + 1) * LOCAL].astype(F32)
            deviation.append((value + (own_mean - mean)).astype(BF))
        weight = first[base + 2 : base + 3]
        obs = second[base + 2 : base + 3] + first[base + 3 : base + 4] + second[base + 3 : base + 4]
        innovation = (obs - mean).astype(BF).astype(F32)
        result.append((jnp.concatenate(deviation, 0), mean, weight, innovation))
    return result


def half_sums(halves, row_distances):
    lane = lax.broadcasted_iota(jnp.int32, (1, WIDTH), 1)
    region_column = lane % REGION
    half_row = (lane // REGION) % (BAND // 2)
    column_distance = jnp.maximum(
        jnp.maximum(RADIUS - region_column, region_column - (RADIUS + PATCH - 1)), 0
    )
    weighted, deviation, innovation = [], [], []
    for (dev, _, weight, inno), row_distance in zip(halves, row_distances):
        far = jnp.maximum(row_distance(half_row), column_distance).astype(F32)
        factor = weight * (1.0 - far / (RADIUS + 1.0))
        weighted.append((dev.astype(F32) * factor).astype(BF))
        deviation.append(dev)
        innovation.append(jnp.broadcast_to(inno, (16, WIDTH)).astype(BF))
    deviation = jnp.concatenate(deviation, 1)
    rows = jnp.concatenate([deviation, jnp.concatenate(innovation, 1)], 0)
    weighted = jnp.concatenate(weighted, 1)
    return deviation, lax.dot_general(rows, weighted, (((1,), (1,)), ((), ())), preferred_element_type=F32)


def own_kernel(me_ref, own_ref, inner_ref, sums_ref, mean_ref):
    halves = halves_of(own_ref, me_ref[0])
    deviation, sums_ref[...] = half_sums(halves, [jnp.zeros_like] * 2)
    lane = lax.broadcasted_iota(jnp.int32, (2 * WIDTH, WIDTH), 0)
    target = lax.broadcasted_iota(jnp.int32, (2 * WIDTH, WIDTH), 1)
    narrow = (lane == (target // PATCH) * REGION + RADIUS + target % PATCH).astype(F32).astype(BF)
    inner_ref[...] = jnp.dot(deviation, narrow, preferred_element_type=F32).astype(BF)
    mean = jnp.broadcast_to(jnp.concatenate([halves[0][1], halves[1][1]], 1), (16, 2 * WIDTH))
    high = mean.astype(BF)
    middle = (mean - high.astype(F32)).astype(BF)
    low = (mean - high.astype(F32) - middle.astype(F32)).astype(BF)
    parts = jnp.dot(jnp.concatenate([high, middle, low], 0), narrow, preferred_element_type=F32)
    mean_ref[...] = parts[:8] + (parts[16:24] + parts[32:40])


def analysis_kernel(me_ref, near_ref, inner_ref, sums_ref, mean_ref, out_ref):
    count = near_ref.shape[0]
    members = count * LOCAL
    halves = halves_of(near_ref, me_ref[0])
    both = sums_ref[...] + half_sums(halves, [lambda r: r + 1, lambda r: RADIUS - r])[1]
    row = lax.broadcasted_iota(jnp.int32, (members, members), 0)
    col = lax.broadcasted_iota(jnp.int32, (members, members), 1)
    system = both[:members] + jnp.where(row == col, members - 1.0, 0.0)
    def mul(a, b):
        return jnp.dot(a.astype(BF), b.astype(BF), preferred_element_type=F32)

    def with_line(a, line):
        return jnp.concatenate([a.astype(BF), line.astype(BF)], 0)

    inner, line = inner_ref[...], both[members:]
    system_b = system.astype(BF)
    first = mul(with_line(system_b, line), system_b)
    system_x = mul(system_b, inner)
    scale = jnp.sqrt(jnp.sum(system * system))
    inverse = 1.0 / scale
    x1 = 1.5 * inner.astype(F32) - (0.5 * inverse) * system_x
    line1 = 1.5 * line - (0.5 * inverse) * first[members:]
    y1 = inverse * (1.5 * system - (0.5 * inverse) * first[:members])
    p1 = 1.5 * y1 - (0.5 * inverse) * mul(y1, system_b)
    p1b = p1.astype(BF)
    second = mul(with_line(p1b, line1), p1b)
    x2 = 1.5 * x1 - 0.5 * mul(p1b, x1)
    line2 = 1.5 * line1 - 0.5 * second[members:]
    q1 = 1.5 * p1 - 0.5 * second[:members]
    p2 = 1.5 * q1 - 0.5 * mul(q1, p1b)
    p2b = p2.astype(BF)
    factor = 1.0 / jnp.sqrt(scale)
    x3 = (1.5 * x2 - 0.5 * mul(p2b, x2)) * factor
    line3 = (1.5 * line2 - 0.5 * mul(line2, p2b)) * factor
    line_b = line3.astype(BF)
    lines = with_line(line_b, line3 - line_b.astype(F32))
    shift = mul(lines, x3)
    shift = shift[:1] + shift[16:17]
    root = jnp.sqrt(jnp.full((1, 1), members - 1.0, F32))
    result = (root * x3 + (shift + mean_ref[:1])).astype(BF)
    for s in range(count):
        out_ref[s] = result[s * LOCAL : (s + 1) * LOCAL]


def unpacked(ref):
    return [row.astype(F32) for row in swap_blocks([ref[position(p)] for p in range(ref.shape[0])], PATCH)]


def unpack_kernel(in_ref, out_ref):
    for i, row in enumerate(unpacked(in_ref)):
        out_ref[i] = row


def forecast_kernel(own_ref, near_ref, out_ref):
    def by_field(rows):
        half = BAND // 2
        return [
            [rows[h * FIELDS * half + field * half + r] for h in range(2) for r in range(half)]
            for field in range(FIELDS)
        ]

    own, near = by_field(own_ref), by_field(unpacked(near_ref))
    fields = [n[BAND - FSTEPS :] + o + n[:FSTEPS] for o, n in zip(own, near)]
    done = forecast_rows(*fields)
    for field in range(FIELDS):
        for r in range(BAND):
            out_ref[pl.ds(field * BAND + r, LOCAL, stride=FIELDS * BAND), :] = done[field][r]


def from_next(value):
    count = lax.axis_size("rows")
    return lax.ppermute(value, "rows", [((i + 1) % count, i) for i in range(count)])


def from_previous(value):
    count = lax.axis_size("rows")
    return lax.ppermute(value, "rows", [(i, (i + 1) % count) for i in range(count)])


def near_rows(value, join):
    if lax.axis_size("rows") == 2:
        return from_next(value)
    return join(from_next(value), from_previous(value))


def join_grid(after, before):
    return jnp.concatenate([after[:, :, : BAND // 2], before[:, :, BAND // 2 :]], 2)


def join_region(after, before):
    after, before = (x.reshape(x.shape[0], -1, 4, WIDTH) for x in (after, before))
    near = jnp.concatenate([after[:, :4], before[:, 4:8], after[:, 8:9], before[:, 9:]], 1)
    return near.reshape(near.shape[0], -1, WIDTH)


def join_inner(after, before):
    return jnp.concatenate([after[..., : WIDTH // 2], before[..., WIDTH // 2 :]], 2)


def exchange(value):
    group = [sorted(range(lax.axis_size("mem")), key=position)]
    return lax.all_to_all(value, "mem", split_axis=0, concat_axis=0, axis_index_groups=group, tiled=True)


def call(kernel, name, out_shape, *args, flops=0):
    spaces = [pltpu.SMEM if arg.shape == (1,) else pltpu.VMEM for arg in args]
    moved = sum(x.size * x.dtype.itemsize for x in [*args, *jax.tree.leaves(out_shape)])
    return pl.pallas_call(
        kernel,
        out_shape=out_shape,
        in_specs=[pl.BlockSpec(memory_space=space) for space in spaces],
        out_specs=jax.tree.map(lambda _: pl.BlockSpec(memory_space=pltpu.VMEM), out_shape),
        compiler_params=pltpu.CompilerParams(vmem_limit_bytes=16 * 2**20),
        cost_estimate=pl.CostEstimate(flops=flops, bytes_accessed=moved, transcendentals=0),
        name=name,
    )(*args)


def local(sample_collection, obs_values, obs_inverse_variance, obs_mask):
    count = lax.axis_size("mem")
    shape = sample_collection.shape
    assert shape == (LOCAL, FIELDS, BAND, WIDTH) and count == PLACES
    me = lax.axis_index("mem").astype(jnp.int32).reshape(1)
    near = near_rows(sample_collection, join_grid)
    rows = jnp.transpose(sample_collection.reshape(LOCAL, FIELDS * BAND, WIDTH), (1, 0, 2))
    region_shape = jax.ShapeDtypeStruct((count, 2 * LOCAL + 8, WIDTH), BF)
    inner_shape = jax.ShapeDtypeStruct((count, LOCAL, WIDTH), BF)
    observations = (obs_values, obs_inverse_variance, obs_mask)
    region = exchange(call(pack_kernel, "forecast_pack", region_shape, rows, near.reshape(-1, WIDTH), *observations))
    members, points = count * LOCAL, 2 * WIDTH
    own_shapes = [
        jax.ShapeDtypeStruct((members, WIDTH), BF),
        jax.ShapeDtypeStruct((members + 16, members), F32),
        jax.ShapeDtypeStruct((8, WIDTH), F32),
    ]
    flops = 2 * members * members * points
    region_near = near_rows(region, join_region)
    own = call(own_kernel, "own_half", own_shapes, me, region, flops=flops)
    inner = exchange(call(analysis_kernel, "analysis", inner_shape, me, region_near, *own, flops=8 * flops))
    inner_near = near_rows(inner, join_inner)
    rows_shape = jax.ShapeDtypeStruct((FIELDS * BAND, LOCAL, WIDTH), F32)
    inner = call(unpack_kernel, "unpack_own", rows_shape, inner)
    out_shape = jax.ShapeDtypeStruct((LOCAL * FIELDS * BAND, WIDTH), F32)
    cycled = call(forecast_kernel, "unpack_forecast", out_shape, inner, inner_near)
    return cycled.reshape(shape)


def solution(mesh):
    return jax.shard_map(
        local,
        mesh=mesh,
        in_specs=(
            P("mem", None, "rows", None),
            P(None, "rows", "mem"),
            P(None, "rows", "mem"),
            P(None, "rows", "mem"),
        ),
        out_specs=P("mem", None, "rows", None),
        check_vma=False,
    )
```

```python
import functools

import jax
import jax.numpy as jnp
from jax import lax
from jax.experimental import pallas as pl
from jax.experimental.pallas import tpu as pltpu
from jax.sharding import PartitionSpec as P

PATCH = 8
RADIUS = 4
FSTEPS = 4
CADV = 0.05

LOCAL = 16
FIELDS = 2
BAND = 8
WIDTH = 128
PLACES = WIDTH // PATCH
REGION = PATCH + 2 * RADIUS

BF = jnp.bfloat16
F32 = jnp.float32


def position(place):
    low, high = place & 3, place >> 2
    return PLACES - 1 - (low * 4 + (high & 1) * 2 + (high >> 1))


def forecast_rows(u_rows, v_rows):
    for _ in range(FSTEPS):
        new_u, new_v = [], []
        for i in range(1, len(u_rows) - 1):
            cu, cv = CADV * u_rows[i], CADV * v_rows[i]
            for rows, new in ((u_rows, new_u), (v_rows, new_v)):
                along_x = pltpu.roll(rows[i], WIDTH - 1, 1) - pltpu.roll(rows[i], 1, 1)
                along_y = rows[i + 1] - rows[i - 1]
                new.append(rows[i] - (cu * along_x + cv * along_y))
        u_rows, v_rows = new_u, new_v
    return u_rows, v_rows


def swap_blocks(parts, size):
    count = len(parts)
    lane = lax.broadcasted_iota(jnp.int32, parts[0].shape, 1) // size
    stride = 1
    while stride < count:
        upper = (lane & stride) != 0
        new = list(parts)
        for j in range(count):
            if j & stride == 0:
                a, b = parts[j], parts[j + stride]
                new[j] = jnp.where(upper, pltpu.roll(b, stride * size, 1), a)
                new[j + stride] = jnp.where(upper, b, pltpu.roll(a, WIDTH - stride * size, 1))
        parts = new
        stride *= 2
    return parts


def observation_rows(values_ref, inverse_ref, mask_ref):
    points = FIELDS * BAND
    weight = (mask_ref[...].astype(F32) * inverse_ref[...]).astype(BF).astype(F32).reshape(points, PATCH)
    values = values_ref[...].reshape(points, PATCH)
    high = values.astype(BF).astype(F32)
    middle = (values - high).astype(BF).astype(F32)
    low = values - high - middle
    rows = jnp.concatenate([weight, high, middle, low], 0).astype(BF)
    source = lax.broadcasted_iota(jnp.int32, (PATCH, WIDTH), 0)
    lane = lax.broadcasted_iota(jnp.int32, (PATCH, WIDTH), 1)
    spread = (lane % PATCH == source).astype(F32).astype(BF)
    wide = jnp.dot(rows, spread, preferred_element_type=F32)
    row = lax.broadcasted_iota(jnp.int32, wide.shape, 0)
    lane = lax.broadcasted_iota(jnp.int32, wide.shape, 1)
    part, field, y = row // points, (row % points) // BAND, row % BAND
    place = (field * (BAND // 2) + y % (BAND // 2)) * 2 + part % 2
    wide = jnp.where(lane // PATCH == place, wide, 0.0).astype(BF)
    target = lax.broadcasted_iota(jnp.int32, (8, 4 * points), 0)
    row = lax.broadcasted_iota(jnp.int32, (8, 4 * points), 1)
    wanted = ((row % BAND) // (BAND // 2)) * 4 + 2 + row // (2 * points)
    gather = (target == wanted).astype(F32).astype(BF)
    return jnp.dot(gather, wide, preferred_element_type=F32)


def pack_kernel(rows_ref, near_ref, values_ref, inverse_ref, mask_ref, out_ref):
    points = FIELDS * BAND

    def near(field, index):
        return near_ref[pl.ds(field * BAND + index, LOCAL, stride=points), :]

    fields = []
    for field in range(FIELDS):
        before = [near(field, r) for r in range(BAND - FSTEPS, BAND)]
        own = [rows_ref[field * BAND + r] for r in range(BAND)]
        after = [near(field, r) for r in range(FSTEPS)]
        fields.append(before + own + after)
    done = forecast_rows(*fields)
    half_rows = BAND // 2
    index = lax.broadcasted_iota(jnp.int32, (8, WIDTH), 0)
    values, means = [], [jnp.zeros((8, WIDTH), F32)] * (FIELDS * half_rows)
    for half in range(2):
        for j in range(FIELDS * half_rows):
            value = done[j // half_rows][half * half_rows + j % half_rows]
            mean = jnp.sum(value, 0, keepdims=True) * (1.0 / LOCAL)
            high = mean.astype(BF).astype(F32)
            means[j] = jnp.where(index == 4 * half, high, jnp.where(index == 4 * half + 1, mean - high, means[j]))
            values.append(value - mean)
    rows = jnp.concatenate(values + means, 0).astype(BF)
    column = lax.broadcasted_iota(jnp.int32, (WIDTH, 2 * WIDTH), 0)
    lane = lax.broadcasted_iota(jnp.int32, (WIDTH, 2 * WIDTH), 1)
    wanted = ((lane // REGION) * PATCH + lane % REGION + (WIDTH - RADIUS)) % WIDTH
    widen = (column == wanted).astype(F32).astype(BF)
    wide = jnp.dot(rows, widen, preferred_element_type=F32)
    obs = observation_rows(values_ref, inverse_ref, mask_ref)
    start = len(values) * LOCAL
    is_mean = index & 2 == 0
    means = []
    for j in range(8):
        part = wide[start + j * 8 : start + j * 8 + 8]
        means.append(jnp.where(is_mean, part[:, :WIDTH], pltpu.roll(part[:, WIDTH:], 2, 0)))
    means = swap_blocks(means, REGION)
    for side in range(2):
        for half in range(2):
            parts = [
                wide[(half * 8 + j) * LOCAL : (half * 8 + j + 1) * LOCAL, side * WIDTH : (side + 1) * WIDTH].astype(BF)
                for j in range(8)
            ]
            parts = swap_blocks(parts, REGION)
            for i in range(8):
                out_ref[position(side * 8 + i), half * LOCAL : (half + 1) * LOCAL] = parts[i]
        for i in range(8):
            mean = means[i] if side == 0 else pltpu.roll(means[i], 6, 0)
            out_ref[position(side * 8 + i), 2 * LOCAL :] = jnp.where(is_mean, mean, obs).astype(BF)


def halves_of(ref, me):
    count = ref.shape[0]
    tails = [ref[s, 2 * LOCAL :].astype(F32) for s in range(count)]

    def tail_of(device):
        return ref[position(device), 2 * LOCAL :].astype(F32)

    lane = lax.broadcasted_iota(jnp.int32, (8, WIDTH), 1) % REGION
    left = tail_of(lax.rem(me + count - 1, count))
    own = tail_of(me)
    right = tail_of(lax.rem(me + 1, count))

    def seen(offset):
        return jnp.where(
            lane < RADIUS,
            pltpu.roll(left, (WIDTH + RADIUS - PATCH - offset) % WIDTH, 1),
            jnp.where(
                lane < RADIUS + PATCH,
                pltpu.roll(own, (WIDTH + RADIUS - offset) % WIDTH, 1),
                pltpu.roll(right, (WIDTH + RADIUS + PATCH - offset) % WIDTH, 1),
            ),
        )

    first, second = seen(0), seen(PATCH)
    result = []
    for half in range(2):
        base = half * 4
        means = [t[base : base + 1] + t[base + 1 : base + 2] for t in tails]
        mean = functools.reduce(jnp.add, means) * (1.0 / count)
        deviation = []
        for s, own_mean in enumerate(means):
            value = ref[s, half * LOCAL : (half + 1) * LOCAL].astype(F32)
            deviation.append((value + (own_mean - mean)).astype(BF))
        weight = first[base + 2 : base + 3]
        obs = second[base + 2 : base + 3] + first[base + 3 : base + 4] + second[base + 3 : base + 4]
        innovation = (obs - mean).astype(BF).astype(F32)
        result.append((jnp.concatenate(deviation, 0), mean, weight, innovation))
    return result


def half_sums(halves, row_distances):
    lane = lax.broadcasted_iota(jnp.int32, (1, WIDTH), 1)
    region_column = lane % REGION
    half_row = (lane // REGION) % (BAND // 2)
    column_distance = jnp.maximum(
        jnp.maximum(RADIUS - region_column, region_column - (RADIUS + PATCH - 1)), 0
    )
    weighted, deviation, innovation = [], [], []
    for (dev, _, weight, inno), row_distance in zip(halves, row_distances):
        far = jnp.maximum(row_distance(half_row), column_distance).astype(F32)
        factor = weight * (1.0 - far / (RADIUS + 1.0))
        weighted.append((dev.astype(F32) * factor).astype(BF))
        deviation.append(dev)
        innovation.append(jnp.broadcast_to(inno, (16, WIDTH)).astype(BF))
    deviation = jnp.concatenate(deviation, 1)
    rows = jnp.concatenate([deviation, jnp.concatenate(innovation, 1)], 0)
    weighted = jnp.concatenate(weighted, 1)
    return deviation, lax.dot_general(rows, weighted, (((1,), (1,)), ((), ())), preferred_element_type=F32)


def own_kernel(me_ref, own_ref, inner_ref, sums_ref, mean_ref):
    halves = halves_of(own_ref, me_ref[0])
    deviation, sums_ref[...] = half_sums(halves, [jnp.zeros_like] * 2)
    lane = lax.broadcasted_iota(jnp.int32, (2 * WIDTH, WIDTH), 0)
    target = lax.broadcasted_iota(jnp.int32, (2 * WIDTH, WIDTH), 1)
    narrow = (lane == (target // PATCH) * REGION + RADIUS + target % PATCH).astype(F32).astype(BF)
    inner_ref[...] = jnp.dot(deviation, narrow, preferred_element_type=F32).astype(BF)
    mean = jnp.broadcast_to(jnp.concatenate([halves[0][1], halves[1][1]], 1), (16, 2 * WIDTH))
    high = mean.astype(BF)
    middle = (mean - high.astype(F32)).astype(BF)
    low = (mean - high.astype(F32) - middle.astype(F32)).astype(BF)
    parts = jnp.dot(jnp.concatenate([high, middle, low], 0), narrow, preferred_element_type=F32)
    mean_ref[...] = parts[:8] + (parts[16:24] + parts[32:40])


def analysis_kernel(me_ref, near_ref, inner_ref, sums_ref, mean_ref, out_ref):
    count = near_ref.shape[0]
    members = count * LOCAL
    halves = halves_of(near_ref, me_ref[0])
    both = sums_ref[...] + half_sums(halves, [lambda r: r + 1, lambda r: RADIUS - r])[1]
    row = lax.broadcasted_iota(jnp.int32, (members, members), 0)
    col = lax.broadcasted_iota(jnp.int32, (members, members), 1)
    system = both[:members] + jnp.where(row == col, members - 1.0, 0.0)
    def mul(a, b):
        return jnp.dot(a.astype(BF), b.astype(BF), preferred_element_type=F32)

    def with_line(a, line):
        return jnp.concatenate([a.astype(BF), line.astype(BF)], 0)

    inner, line = inner_ref[...], both[members:]
    system_b = system.astype(BF)
    first = mul(with_line(system_b, line), system_b)
    system_x = mul(system_b, inner)
    scale = jnp.sqrt(jnp.sum(system * system))
    inverse = 1.0 / scale
    x1 = 1.5 * inner.astype(F32) - (0.5 * inverse) * system_x
    line1 = 1.5 * line - (0.5 * inverse) * first[members:]
    y1 = inverse * (1.5 * system - (0.5 * inverse) * first[:members])
    p1 = 1.5 * y1 - (0.5 * inverse) * mul(y1, system_b)
    p1b = p1.astype(BF)
    second = mul(with_line(p1b, line1), p1b)
    x2 = 1.5 * x1 - 0.5 * mul(p1b, x1)
    line2 = 1.5 * line1 - 0.5 * second[members:]
    q1 = 1.5 * p1 - 0.5 * second[:members]
    p2 = 1.5 * q1 - 0.5 * mul(q1, p1b)
    p2b = p2.astype(BF)
    factor = 1.0 / jnp.sqrt(scale)
    x3 = (1.5 * x2 - 0.5 * mul(p2b, x2)) * factor
    line3 = (1.5 * line2 - 0.5 * mul(line2, p2b)) * factor
    line_b = line3.astype(BF)
    lines = with_line(line_b, line3 - line_b.astype(F32))
    shift = mul(lines, x3)
    shift = shift[:1] + shift[16:17]
    root = jnp.sqrt(jnp.full((1, 1), members - 1.0, F32))
    result = (root * x3 + (shift + mean_ref[:1])).astype(BF)
    for s in range(count):
        out_ref[s] = result[s * LOCAL : (s + 1) * LOCAL]


def unpacked(ref):
    return [row.astype(F32) for row in swap_blocks([ref[position(p)] for p in range(ref.shape[0])], PATCH)]


def unpack_kernel(in_ref, out_ref):
    for i, row in enumerate(unpacked(in_ref)):
        out_ref[i] = row


def forecast_kernel(own_ref, near_ref, out_ref):
    def by_field(rows):
        half = BAND // 2
        return [
            [rows[h * FIELDS * half + field * half + r] for h in range(2) for r in range(half)]
            for field in range(FIELDS)
        ]

    own, near = by_field(own_ref), by_field(unpacked(near_ref))
    fields = [n[BAND - FSTEPS :] + o + n[:FSTEPS] for o, n in zip(own, near)]
    done = forecast_rows(*fields)
    for field in range(FIELDS):
        for r in range(BAND):
            out_ref[pl.ds(field * BAND + r, LOCAL, stride=FIELDS * BAND), :] = done[field][r]


def from_next(value):
    count = lax.axis_size("rows")
    return lax.ppermute(value, "rows", [((i + 1) % count, i) for i in range(count)])


def from_previous(value):
    count = lax.axis_size("rows")
    return lax.ppermute(value, "rows", [(i, (i + 1) % count) for i in range(count)])


def near_rows(value, join):
    if lax.axis_size("rows") == 2:
        return from_next(value)
    return join(from_next(value), from_previous(value))


def join_grid(after, before):
    return jnp.concatenate([after[:, :, : BAND // 2], before[:, :, BAND // 2 :]], 2)


def join_region(after, before):
    after, before = (x.reshape(x.shape[0], -1, 4, WIDTH) for x in (after, before))
    near = jnp.concatenate([after[:, :4], before[:, 4:8], after[:, 8:9], before[:, 9:]], 1)
    return near.reshape(near.shape[0], -1, WIDTH)


def join_inner(after, before):
    return jnp.concatenate([after[..., : WIDTH // 2], before[..., WIDTH // 2 :]], 2)


def exchange(value):
    bands = lax.axis_size("rows")
    places = sorted(range(lax.axis_size("mem")), key=position)
    groups = [[place * bands + band for place in places] for band in reversed(range(bands))]
    return lax.all_to_all(value, ("mem", "rows"), split_axis=0, concat_axis=0, axis_index_groups=groups, tiled=True)


def call(kernel, name, out_shape, *args, flops=0):
    spaces = [pltpu.SMEM if arg.shape == (1,) else pltpu.VMEM for arg in args]
    moved = sum(x.size * x.dtype.itemsize for x in [*args, *jax.tree.leaves(out_shape)])
    return pl.pallas_call(
        kernel,
        out_shape=out_shape,
        in_specs=[pl.BlockSpec(memory_space=space) for space in spaces],
        out_specs=jax.tree.map(lambda _: pl.BlockSpec(memory_space=pltpu.VMEM), out_shape),
        compiler_params=pltpu.CompilerParams(vmem_limit_bytes=16 * 2**20),
        cost_estimate=pl.CostEstimate(flops=flops, bytes_accessed=moved, transcendentals=0),
        name=name,
    )(*args)


def local(sample_collection, obs_values, obs_inverse_variance, obs_mask):
    count = lax.axis_size("mem")
    shape = sample_collection.shape
    assert shape == (LOCAL, FIELDS, BAND, WIDTH) and count == PLACES
    me = lax.axis_index("mem").astype(jnp.int32).reshape(1)
    near = near_rows(sample_collection, join_grid)
    rows = jnp.transpose(sample_collection.reshape(LOCAL, FIELDS * BAND, WIDTH), (1, 0, 2))
    region_shape = jax.ShapeDtypeStruct((count, 2 * LOCAL + 8, WIDTH), BF)
    inner_shape = jax.ShapeDtypeStruct((count, LOCAL, WIDTH), BF)
    observations = (obs_values, obs_inverse_variance, obs_mask)
    region = exchange(call(pack_kernel, "forecast_pack", region_shape, rows, near.reshape(-1, WIDTH), *observations))
    members, points = count * LOCAL, 2 * WIDTH
    own_shapes = [
        jax.ShapeDtypeStruct((members, WIDTH), BF),
        jax.ShapeDtypeStruct((members + 16, members), F32),
        jax.ShapeDtypeStruct((8, WIDTH), F32),
    ]
    flops = 2 * members * members * points
    region_near = near_rows(region, join_region)
    own = call(own_kernel, "own_half", own_shapes, me, region, flops=flops)
    inner = exchange(call(analysis_kernel, "analysis", inner_shape, me, region_near, *own, flops=8 * flops))
    inner_near = near_rows(inner, join_inner)
    rows_shape = jax.ShapeDtypeStruct((FIELDS * BAND, LOCAL, WIDTH), F32)
    inner = call(unpack_kernel, "unpack_own", rows_shape, inner)
    out_shape = jax.ShapeDtypeStruct((LOCAL * FIELDS * BAND, WIDTH), F32)
    cycled = call(forecast_kernel, "unpack_forecast", out_shape, inner, inner_near)
    return cycled.reshape(shape)


def solution(mesh):
    return jax.shard_map(
        local,
        mesh=mesh,
        in_specs=(
            P("mem", None, "rows", None),
            P(None, "rows", "mem"),
            P(None, "rows", "mem"),
            P(None, "rows", "mem"),
        ),
        out_specs=P("mem", None, "rows", None),
        check_vma=False,
    )
```

```python
import functools

import jax
import jax.numpy as jnp
from jax import lax
from jax.experimental import pallas as pl
from jax.experimental.pallas import tpu as pltpu
from jax.sharding import PartitionSpec as P

PATCH = 8
RADIUS = 4
FSTEPS = 4
CADV = 0.05

LOCAL = 16
FIELDS = 2
BAND = 8
WIDTH = 128
PLACES = WIDTH // PATCH
REGION = PATCH + 2 * RADIUS

BF = jnp.bfloat16
F32 = jnp.float32


def position(place):
    low, high = place & 3, place >> 2
    return PLACES - 1 - (low * 4 + (high & 1) * 2 + (high >> 1))


def forecast_rows(u_rows, v_rows):
    for _ in range(FSTEPS):
        new_u, new_v = [], []
        for i in range(1, len(u_rows) - 1):
            cu, cv = CADV * u_rows[i], CADV * v_rows[i]
            for rows, new in ((u_rows, new_u), (v_rows, new_v)):
                along_x = pltpu.roll(rows[i], WIDTH - 1, 1) - pltpu.roll(rows[i], 1, 1)
                along_y = rows[i + 1] - rows[i - 1]
                new.append(rows[i] - (cu * along_x + cv * along_y))
        u_rows, v_rows = new_u, new_v
    return u_rows, v_rows


def swap_blocks(parts, size):
    count = len(parts)
    lane = lax.broadcasted_iota(jnp.int32, parts[0].shape, 1) // size
    stride = 1
    while stride < count:
        upper = (lane & stride) != 0
        new = list(parts)
        for j in range(count):
            if j & stride == 0:
                a, b = parts[j], parts[j + stride]
                new[j] = jnp.where(upper, pltpu.roll(b, stride * size, 1), a)
                new[j + stride] = jnp.where(upper, b, pltpu.roll(a, WIDTH - stride * size, 1))
        parts = new
        stride *= 2
    return parts


def observation_rows(values_ref, inverse_ref, mask_ref):
    points = FIELDS * BAND
    weight = (mask_ref[...].astype(F32) * inverse_ref[...]).astype(BF).astype(F32).reshape(points, PATCH)
    values = values_ref[...].reshape(points, PATCH)
    high = values.astype(BF).astype(F32)
    middle = (values - high).astype(BF).astype(F32)
    low = values - high - middle
    rows = jnp.concatenate([weight, high, middle, low], 0).astype(BF)
    source = lax.broadcasted_iota(jnp.int32, (PATCH, WIDTH), 0)
    lane = lax.broadcasted_iota(jnp.int32, (PATCH, WIDTH), 1)
    spread = (lane % PATCH == source).astype(F32).astype(BF)
    wide = jnp.dot(rows, spread, preferred_element_type=F32)
    row = lax.broadcasted_iota(jnp.int32, wide.shape, 0)
    lane = lax.broadcasted_iota(jnp.int32, wide.shape, 1)
    part, field, y = row // points, (row % points) // BAND, row % BAND
    place = (field * (BAND // 2) + y % (BAND // 2)) * 2 + part % 2
    wide = jnp.where(lane // PATCH == place, wide, 0.0).astype(BF)
    target = lax.broadcasted_iota(jnp.int32, (8, 4 * points), 0)
    row = lax.broadcasted_iota(jnp.int32, (8, 4 * points), 1)
    wanted = ((row % BAND) // (BAND // 2)) * 4 + 2 + row // (2 * points)
    gather = (target == wanted).astype(F32).astype(BF)
    return jnp.dot(gather, wide, preferred_element_type=F32)


def pack_kernel(rows_ref, near_ref, values_ref, inverse_ref, mask_ref, out_ref):
    points = FIELDS * BAND

    def near(field, index):
        return near_ref[pl.ds(field * BAND + index, LOCAL, stride=points), :]

    fields = []
    for field in range(FIELDS):
        before = [near(field, r) for r in range(BAND - FSTEPS, BAND)]
        own = [rows_ref[field * BAND + r] for r in range(BAND)]
        after = [near(field, r) for r in range(FSTEPS)]
        fields.append(before + own + after)
    done = forecast_rows(*fields)
    half_rows = BAND // 2
    index = lax.broadcasted_iota(jnp.int32, (8, WIDTH), 0)
    values, means = [], [jnp.zeros((8, WIDTH), F32)] * (FIELDS * half_rows)
    for half in range(2):
        for j in range(FIELDS * half_rows):
            value = done[j // half_rows][half * half_rows + j % half_rows]
            mean = jnp.sum(value, 0, keepdims=True) * (1.0 / LOCAL)
            high = mean.astype(BF).astype(F32)
            means[j] = jnp.where(index == 4 * half, high, jnp.where(index == 4 * half + 1, mean - high, means[j]))
            values.append(value - mean)
    rows = jnp.concatenate(values + means, 0).astype(BF)
    column = lax.broadcasted_iota(jnp.int32, (WIDTH, 2 * WIDTH), 0)
    lane = lax.broadcasted_iota(jnp.int32, (WIDTH, 2 * WIDTH), 1)
    wanted = ((lane // REGION) * PATCH + lane % REGION + (WIDTH - RADIUS)) % WIDTH
    widen = (column == wanted).astype(F32).astype(BF)
    wide = jnp.dot(rows, widen, preferred_element_type=F32)
    obs = observation_rows(values_ref, inverse_ref, mask_ref)
    start = len(values) * LOCAL
    is_mean = index & 2 == 0
    means = []
    for j in range(8):
        part = wide[start + j * 8 : start + j * 8 + 8]
        means.append(jnp.where(is_mean, part[:, :WIDTH], pltpu.roll(part[:, WIDTH:], 2, 0)))
    means = swap_blocks(means, REGION)
    for side in range(2):
        for half in range(2):
            parts = [
                wide[(half * 8 + j) * LOCAL : (half * 8 + j + 1) * LOCAL, side * WIDTH : (side + 1) * WIDTH].astype(BF)
                for j in range(8)
            ]
            parts = swap_blocks(parts, REGION)
            for i in range(8):
                out_ref[position(side * 8 + i), half * LOCAL : (half + 1) * LOCAL] = parts[i]
        for i in range(8):
            mean = means[i] if side == 0 else pltpu.roll(means[i], 6, 0)
            out_ref[position(side * 8 + i), 2 * LOCAL :] = jnp.where(is_mean, mean, obs).astype(BF)


def halves_of(ref, me):
    count = ref.shape[0]
    tails = [ref[s, 2 * LOCAL :].astype(F32) for s in range(count)]

    def tail_of(device):
        return ref[position(device), 2 * LOCAL :].astype(F32)

    lane = lax.broadcasted_iota(jnp.int32, (8, WIDTH), 1) % REGION
    left = tail_of(lax.rem(me + count - 1, count))
    own = tail_of(me)
    right = tail_of(lax.rem(me + 1, count))

    def seen(offset):
        return jnp.where(
            lane < RADIUS,
            pltpu.roll(left, (WIDTH + RADIUS - PATCH - offset) % WIDTH, 1),
            jnp.where(
                lane < RADIUS + PATCH,
                pltpu.roll(own, (WIDTH + RADIUS - offset) % WIDTH, 1),
                pltpu.roll(right, (WIDTH + RADIUS + PATCH - offset) % WIDTH, 1),
            ),
        )

    first, second = seen(0), seen(PATCH)
    result = []
    for half in range(2):
        base = half * 4
        means = [t[base : base + 1] + t[base + 1 : base + 2] for t in tails]
        mean = functools.reduce(jnp.add, means) * (1.0 / count)
        deviation = []
        for s, own_mean in enumerate(means):
            value = ref[s, half * LOCAL : (half + 1) * LOCAL].astype(F32)
            deviation.append((value + (own_mean - mean)).astype(BF))
        weight = first[base + 2 : base + 3]
        obs = second[base + 2 : base + 3] + first[base + 3 : base + 4] + second[base + 3 : base + 4]
        innovation = (obs - mean).astype(BF).astype(F32)
        result.append((jnp.concatenate(deviation, 0), mean, weight, innovation))
    return result


def half_sums(halves, distances):
    lane = lax.broadcasted_iota(jnp.int32, (1, WIDTH), 1)
    region_column = lane % REGION
    half_row = (lane // REGION) % (BAND // 2)
    column_distance = jnp.maximum(
        jnp.maximum(RADIUS - region_column, region_column - (RADIUS + PATCH - 1)), 0
    )
    deviation = jnp.concatenate([dev for dev, _, _, _ in halves], 1)
    innovation = jnp.concatenate([jnp.broadcast_to(inno, (16, WIDTH)) for _, _, _, inno in halves], 1)
    rows = jnp.concatenate([deviation, innovation.astype(BF)], 0)
    weighted = []
    for row_distances in distances:
        parts = []
        for (dev, _, weight, _), row_distance in zip(halves, row_distances):
            far = jnp.maximum(row_distance(half_row), column_distance).astype(F32)
            factor = weight * (1.0 - far / (RADIUS + 1.0))
            parts.append((dev.astype(F32) * factor).astype(BF))
        weighted.append(jnp.concatenate(parts, 1))
    weighted = jnp.concatenate(weighted, 0)
    return deviation, lax.dot_general(rows, weighted, (((1,), (1,)), ((), ())), preferred_element_type=F32)


INSIDE = (jnp.zeros_like, jnp.zeros_like)
OUTSIDE = (lambda r: r + 1, lambda r: RADIUS - r)


def interior(halves, deviation):
    lane = lax.broadcasted_iota(jnp.int32, (2 * WIDTH, WIDTH), 0)
    target = lax.broadcasted_iota(jnp.int32, (2 * WIDTH, WIDTH), 1)
    narrow = (lane == (target // PATCH) * REGION + RADIUS + target % PATCH).astype(F32).astype(BF)
    inner = jnp.dot(deviation, narrow, preferred_element_type=F32).astype(BF)
    mean = jnp.broadcast_to(jnp.concatenate([halves[0][1], halves[1][1]], 1), (16, 2 * WIDTH))
    high = mean.astype(BF)
    middle = (mean - high.astype(F32)).astype(BF)
    low = (mean - high.astype(F32) - middle.astype(F32)).astype(BF)
    parts = jnp.dot(jnp.concatenate([high, middle, low], 0), narrow, preferred_element_type=F32)
    return inner, parts[:8] + (parts[16:24] + parts[32:40])


def own_kernel(patches, me_ref, own_ref, inner_ref, sums_ref, mean_ref):
    halves = halves_of(own_ref, me_ref[0])
    deviation, sums_ref[...] = half_sums(halves, (INSIDE, OUTSIDE)[:patches])
    inner_ref[...], mean_ref[...] = interior(halves, deviation)


def analysis_kernel(patches, me_ref, near_ref, inner_ref, sums_ref, mean_ref, out_ref):
    count = near_ref.shape[0]
    members = count * LOCAL
    halves = halves_of(near_ref, me_ref[0])
    deviation, sums = half_sums(halves, (OUTSIDE, INSIDE)[:patches])
    both = sums_ref[...] + sums
    each = range(patches)
    inner, mean = [inner_ref[...]], [mean_ref[...]]
    if patches == 2:
        near_inner, near_mean = interior(halves, deviation)
        inner.append(near_inner)
        mean.append(near_mean)
    row = lax.broadcasted_iota(jnp.int32, (members, members), 0)
    col = lax.broadcasted_iota(jnp.int32, (members, members), 1)
    diagonal = jnp.where(row == col, members - 1.0, 0.0)

    def mul(a, b):
        return jnp.dot(a.astype(BF), b.astype(BF), preferred_element_type=F32)

    def with_line(a, line):
        return jnp.concatenate([a.astype(BF), line.astype(BF)], 0)

    system = [both[:members, i * members : (i + 1) * members] + diagonal for i in each]
    line = [both[members:, i * members : (i + 1) * members] for i in each]
    system_b = [system[i].astype(BF) for i in each]
    first = [mul(with_line(system_b[i], line[i]), system_b[i]) for i in each]
    system_x = [mul(system_b[i], inner[i]) for i in each]
    scale = [jnp.sqrt(jnp.sum(system[i] * system[i])) for i in each]
    inverse = [1.0 / scale[i] for i in each]
    x1 = [1.5 * inner[i].astype(F32) - (0.5 * inverse[i]) * system_x[i] for i in each]
    line1 = [1.5 * line[i] - (0.5 * inverse[i]) * first[i][members:] for i in each]
    y1 = [inverse[i] * (1.5 * system[i] - (0.5 * inverse[i]) * first[i][:members]) for i in each]
    p1 = [1.5 * y1[i] - (0.5 * inverse[i]) * mul(y1[i], system_b[i]) for i in each]
    p1b = [p1[i].astype(BF) for i in each]
    second = [mul(with_line(p1b[i], line1[i]), p1b[i]) for i in each]
    x2 = [1.5 * x1[i] - 0.5 * mul(p1b[i], x1[i]) for i in each]
    line2 = [1.5 * line1[i] - 0.5 * second[i][members:] for i in each]
    q1 = [1.5 * p1[i] - 0.5 * second[i][:members] for i in each]
    p2b = [(1.5 * q1[i] - 0.5 * mul(q1[i], p1b[i])).astype(BF) for i in each]
    factor = [1.0 / jnp.sqrt(scale[i]) for i in each]
    x3 = [(1.5 * x2[i] - 0.5 * mul(p2b[i], x2[i])) * factor[i] for i in each]
    line3 = [(1.5 * line2[i] - 0.5 * mul(line2[i], p2b[i])) * factor[i] for i in each]
    line_b = [line3[i].astype(BF) for i in each]
    shift = [mul(with_line(line_b[i], line3[i] - line_b[i].astype(F32)), x3[i]) for i in each]
    root = jnp.sqrt(jnp.full((1, 1), members - 1.0, F32))
    for i in each:
        total = shift[i][:1] + shift[i][16:17] + mean[i][:1]
        result = (root * x3[i] + total).astype(BF)
        for s in range(count):
            out_ref[s, i * LOCAL : (i + 1) * LOCAL] = result[s * LOCAL : (s + 1) * LOCAL]


def forecast_kernel(in_ref, out_ref):
    def unpacked(start):
        blocks = [in_ref[position(p), start : start + LOCAL] for p in range(in_ref.shape[0])]
        return [row.astype(F32) for row in swap_blocks(blocks, PATCH)]

    def by_field(rows):
        half = BAND // 2
        return [
            [rows[h * FIELDS * half + field * half + r] for h in range(2) for r in range(half)]
            for field in range(FIELDS)
        ]

    own, near = by_field(unpacked(0)), by_field(unpacked(LOCAL))
    fields = [n[BAND - FSTEPS :] + o + n[:FSTEPS] for o, n in zip(own, near)]
    done = forecast_rows(*fields)
    for field in range(FIELDS):
        for r in range(BAND):
            out_ref[pl.ds(field * BAND + r, LOCAL, stride=FIELDS * BAND), :] = done[field][r]


def from_next(value):
    count = lax.axis_size("rows")
    return lax.ppermute(value, "rows", [((i + 1) % count, i) for i in range(count)])


def from_previous(value):
    count = lax.axis_size("rows")
    return lax.ppermute(value, "rows", [(i, (i + 1) % count) for i in range(count)])


def near_rows(value, join):
    if lax.axis_size("rows") == 2:
        return from_next(value)
    return join(from_next(value), from_previous(value))


def join_grid(after, before):
    return jnp.concatenate([after[:, :, : BAND // 2], before[:, :, BAND // 2 :]], 2)


def join_region(after, before):
    after, before = (x.reshape(x.shape[0], -1, 4, WIDTH) for x in (after, before))
    near = jnp.concatenate([after[:, :4], before[:, 4:8], after[:, 8:9], before[:, 9:]], 1)
    return near.reshape(near.shape[0], -1, WIDTH)


def join_inner(after, before):
    return jnp.concatenate([after[..., : WIDTH // 2], before[..., WIDTH // 2 :]], 2)


def exchange(value):
    group = [sorted(range(lax.axis_size("mem")), key=position)]
    return lax.all_to_all(value, "mem", split_axis=0, concat_axis=0, axis_index_groups=group, tiled=True)


def call(kernel, name, out_shape, *args, flops=0):
    spaces = [pltpu.SMEM if arg.shape == (1,) else pltpu.VMEM for arg in args]
    moved = sum(x.size * x.dtype.itemsize for x in [*args, *jax.tree.leaves(out_shape)])
    return pl.pallas_call(
        kernel,
        out_shape=out_shape,
        in_specs=[pl.BlockSpec(memory_space=space) for space in spaces],
        out_specs=jax.tree.map(lambda _: pl.BlockSpec(memory_space=pltpu.VMEM), out_shape),
        compiler_params=pltpu.CompilerParams(vmem_limit_bytes=16 * 2**20),
        cost_estimate=pl.CostEstimate(flops=flops, bytes_accessed=moved, transcendentals=0),
        name=name,
    )(*args)


def local(sample_collection, obs_values, obs_inverse_variance, obs_mask):
    count = lax.axis_size("mem")
    shape = sample_collection.shape
    assert shape == (LOCAL, FIELDS, BAND, WIDTH) and count == PLACES
    me = lax.axis_index("mem").astype(jnp.int32).reshape(1)
    near = near_rows(sample_collection, join_grid)
    rows = jnp.transpose(sample_collection.reshape(LOCAL, FIELDS * BAND, WIDTH), (1, 0, 2))
    region_shape = jax.ShapeDtypeStruct((count, 2 * LOCAL + 8, WIDTH), BF)
    observations = (obs_values, obs_inverse_variance, obs_mask)
    region = exchange(call(pack_kernel, "forecast_pack", region_shape, rows, near.reshape(-1, WIDTH), *observations))
    members, points = count * LOCAL, 2 * WIDTH
    patches = 2 if lax.axis_size("rows") == 2 else 1
    own_shapes = [
        jax.ShapeDtypeStruct((members, WIDTH), BF),
        jax.ShapeDtypeStruct((members + 16, patches * members), F32),
        jax.ShapeDtypeStruct((8, WIDTH), F32),
    ]
    flops = 2 * members * members * points
    region_near = near_rows(region, join_region)
    own = call(functools.partial(own_kernel, patches), "own_half", own_shapes, me, region, flops=flops)
    analysed_shape = jax.ShapeDtypeStruct((count, patches * LOCAL, WIDTH), BF)
    kernel = functools.partial(analysis_kernel, patches)
    inner = exchange(call(kernel, "analysis", analysed_shape, me, region_near, *own, flops=8 * flops))
    if patches == 1:
        inner = jnp.concatenate([inner, near_rows(inner, join_inner)], 1)
    out_shape = jax.ShapeDtypeStruct((LOCAL * FIELDS * BAND, WIDTH), F32)
    cycled = call(forecast_kernel, "unpack_forecast", out_shape, inner)
    return cycled.reshape(shape)


def solution(mesh):
    return jax.shard_map(
        local,
        mesh=mesh,
        in_specs=(
            P("mem", None, "rows", None),
            P(None, "rows", "mem"),
            P(None, "rows", "mem"),
            P(None, "rows", "mem"),
        ),
        out_specs=P("mem", None, "rows", None),
        check_vma=False,
    )
```

```python
import functools

import jax
import jax.numpy as jnp
from jax import lax
from jax.experimental import pallas as pl
from jax.experimental.pallas import tpu as pltpu
from jax.sharding import PartitionSpec as P

PATCH = 8
RADIUS = 4
FSTEPS = 4
CADV = 0.05

LOCAL = 16
FIELDS = 2
BAND = 8
WIDTH = 128
PLACES = WIDTH // PATCH
REGION = PATCH + 2 * RADIUS

BF = jnp.bfloat16
F32 = jnp.float32


def position(place):
    low, high = place & 3, place >> 2
    return PLACES - 1 - (low * 4 + (high & 1) * 2 + (high >> 1))


def back_position(place):
    return PLACES - 1 - place


def group(rule):
    return sorted(range(PLACES), key=rule)


def forecast_rows(u_rows, v_rows):
    for _ in range(FSTEPS):
        new_u, new_v = [], []
        for i in range(1, len(u_rows) - 1):
            cu, cv = CADV * u_rows[i], CADV * v_rows[i]
            for rows, new in ((u_rows, new_u), (v_rows, new_v)):
                along_x = pltpu.roll(rows[i], WIDTH - 1, 1) - pltpu.roll(rows[i], 1, 1)
                along_y = rows[i + 1] - rows[i - 1]
                new.append(rows[i] - (cu * along_x + cv * along_y))
        u_rows, v_rows = new_u, new_v
    return u_rows, v_rows


def swap_blocks(parts, size):
    count = len(parts)
    lane = lax.broadcasted_iota(jnp.int32, parts[0].shape, 1) // size
    stride = 1
    while stride < count:
        upper = (lane & stride) != 0
        new = list(parts)
        for j in range(count):
            if j & stride == 0:
                a, b = parts[j], parts[j + stride]
                new[j] = jnp.where(upper, pltpu.roll(b, stride * size, 1), a)
                new[j + stride] = jnp.where(upper, b, pltpu.roll(a, WIDTH - stride * size, 1))
        parts = new
        stride *= 2
    return parts


def observation_rows(values_ref, inverse_ref, mask_ref):
    points = FIELDS * BAND
    weight = (mask_ref[...].astype(F32) * inverse_ref[...]).astype(BF).astype(F32).reshape(points, PATCH)
    values = values_ref[...].reshape(points, PATCH)
    high = values.astype(BF).astype(F32)
    middle = (values - high).astype(BF).astype(F32)
    low = values - high - middle
    rows = jnp.concatenate([weight, high, middle, low], 0).astype(BF)
    source = lax.broadcasted_iota(jnp.int32, (PATCH, WIDTH), 0)
    lane = lax.broadcasted_iota(jnp.int32, (PATCH, WIDTH), 1)
    spread = (lane % PATCH == source).astype(F32).astype(BF)
    wide = jnp.dot(rows, spread, preferred_element_type=F32)
    row = lax.broadcasted_iota(jnp.int32, wide.shape, 0)
    lane = lax.broadcasted_iota(jnp.int32, wide.shape, 1)
    part, field, y = row // points, (row % points) // BAND, row % BAND
    place = (field * (BAND // 2) + y % (BAND // 2)) * 2 + part % 2
    wide = jnp.where(lane // PATCH == place, wide, 0.0).astype(BF)
    target = lax.broadcasted_iota(jnp.int32, (8, 4 * points), 0)
    row = lax.broadcasted_iota(jnp.int32, (8, 4 * points), 1)
    wanted = ((row % BAND) // (BAND // 2)) * 4 + 2 + row // (2 * points)
    gather = (target == wanted).astype(F32).astype(BF)
    return jnp.dot(gather, wide, preferred_element_type=F32)


def pack_kernel(rows_ref, near_ref, values_ref, inverse_ref, mask_ref, out_ref):
    points = FIELDS * BAND

    def near(field, index):
        return near_ref[pl.ds(field * BAND + index, LOCAL, stride=points), :]

    fields = []
    for field in range(FIELDS):
        before = [near(field, r) for r in range(BAND - FSTEPS, BAND)]
        own = [rows_ref[field * BAND + r] for r in range(BAND)]
        after = [near(field, r) for r in range(FSTEPS)]
        fields.append(before + own + after)
    done = forecast_rows(*fields)
    half_rows = BAND // 2
    index = lax.broadcasted_iota(jnp.int32, (8, WIDTH), 0)
    values, means = [], [jnp.zeros((8, WIDTH), F32)] * (FIELDS * half_rows)
    for half in range(2):
        for j in range(FIELDS * half_rows):
            value = done[j // half_rows][half * half_rows + j % half_rows]
            mean = jnp.sum(value, 0, keepdims=True) * (1.0 / LOCAL)
            high = mean.astype(BF).astype(F32)
            means[j] = jnp.where(index == 4 * half, high, jnp.where(index == 4 * half + 1, mean - high, means[j]))
            values.append(value - mean)
    rows = jnp.concatenate(values + means, 0).astype(BF)
    column = lax.broadcasted_iota(jnp.int32, (WIDTH, 2 * WIDTH), 0)
    lane = lax.broadcasted_iota(jnp.int32, (WIDTH, 2 * WIDTH), 1)
    wanted = ((lane // REGION) * PATCH + lane % REGION + (WIDTH - RADIUS)) % WIDTH
    widen = (column == wanted).astype(F32).astype(BF)
    wide = jnp.dot(rows, widen, preferred_element_type=F32)
    obs = observation_rows(values_ref, inverse_ref, mask_ref)
    start = len(values) * LOCAL
    is_mean = index & 2 == 0
    means = []
    for j in range(8):
        part = wide[start + j * 8 : start + j * 8 + 8]
        means.append(jnp.where(is_mean, part[:, :WIDTH], pltpu.roll(part[:, WIDTH:], 2, 0)))
    means = swap_blocks(means, REGION)
    for side in range(2):
        for half in range(2):
            parts = [
                wide[(half * 8 + j) * LOCAL : (half * 8 + j + 1) * LOCAL, side * WIDTH : (side + 1) * WIDTH].astype(BF)
                for j in range(8)
            ]
            parts = swap_blocks(parts, REGION)
            for i in range(8):
                out_ref[position(side * 8 + i), half * LOCAL : (half + 1) * LOCAL] = parts[i]
        for i in range(8):
            mean = means[i] if side == 0 else pltpu.roll(means[i], 6, 0)
            out_ref[position(side * 8 + i), 2 * LOCAL :] = jnp.where(is_mean, mean, obs).astype(BF)


def halves_of(ref, me):
    count = ref.shape[0]
    tails = [ref[s, 2 * LOCAL :].astype(F32) for s in range(count)]

    def tail_of(device):
        return ref[position(device), 2 * LOCAL :].astype(F32)

    lane = lax.broadcasted_iota(jnp.int32, (8, WIDTH), 1) % REGION
    left = tail_of(lax.rem(me + count - 1, count))
    own = tail_of(me)
    right = tail_of(lax.rem(me + 1, count))

    def seen(offset):
        return jnp.where(
            lane < RADIUS,
            pltpu.roll(left, (WIDTH + RADIUS - PATCH - offset) % WIDTH, 1),
            jnp.where(
                lane < RADIUS + PATCH,
                pltpu.roll(own, (WIDTH + RADIUS - offset) % WIDTH, 1),
                pltpu.roll(right, (WIDTH + RADIUS + PATCH - offset) % WIDTH, 1),
            ),
        )

    first, second = seen(0), seen(PATCH)
    result = []
    for half in range(2):
        base = half * 4
        means = [t[base : base + 1] + t[base + 1 : base + 2] for t in tails]
        mean = functools.reduce(jnp.add, means) * (1.0 / count)
        deviation = []
        for s, own_mean in enumerate(means):
            value = ref[s, half * LOCAL : (half + 1) * LOCAL].astype(F32)
            deviation.append((value + (own_mean - mean)).astype(BF))
        weight = first[base + 2 : base + 3]
        obs = second[base + 2 : base + 3] + first[base + 3 : base + 4] + second[base + 3 : base + 4]
        innovation = (obs - mean).astype(BF).astype(F32)
        result.append((jnp.concatenate(deviation, 0), mean, weight, innovation))
    return result


def half_sums(halves, distances):
    lane = lax.broadcasted_iota(jnp.int32, (1, WIDTH), 1)
    region_column = lane % REGION
    half_row = (lane // REGION) % (BAND // 2)
    column_distance = jnp.maximum(
        jnp.maximum(RADIUS - region_column, region_column - (RADIUS + PATCH - 1)), 0
    )
    deviation = jnp.concatenate([dev for dev, _, _, _ in halves], 1)
    innovation = jnp.concatenate([jnp.broadcast_to(inno, (16, WIDTH)) for _, _, _, inno in halves], 1)
    rows = jnp.concatenate([deviation, innovation.astype(BF)], 0)
    weighted = []
    for row_distances in distances:
        parts = []
        for (dev, _, weight, _), row_distance in zip(halves, row_distances):
            far = jnp.maximum(row_distance(half_row), column_distance).astype(F32)
            factor = weight * (1.0 - far / (RADIUS + 1.0))
            parts.append((dev.astype(F32) * factor).astype(BF))
        weighted.append(jnp.concatenate(parts, 1))
    weighted = jnp.concatenate(weighted, 0)
    return deviation, lax.dot_general(rows, weighted, (((1,), (1,)), ((), ())), preferred_element_type=F32)


INSIDE = (jnp.zeros_like, jnp.zeros_like)
OUTSIDE = (lambda r: r + 1, lambda r: RADIUS - r)


def interior(halves, deviation):
    lane = lax.broadcasted_iota(jnp.int32, (2 * WIDTH, WIDTH), 0)
    target = lax.broadcasted_iota(jnp.int32, (2 * WIDTH, WIDTH), 1)
    narrow = (lane == (target // PATCH) * REGION + RADIUS + target % PATCH).astype(F32).astype(BF)
    inner = jnp.dot(deviation, narrow, preferred_element_type=F32).astype(BF)
    mean = jnp.broadcast_to(jnp.concatenate([halves[0][1], halves[1][1]], 1), (16, 2 * WIDTH))
    high = mean.astype(BF)
    middle = (mean - high.astype(F32)).astype(BF)
    low = (mean - high.astype(F32) - middle.astype(F32)).astype(BF)
    parts = jnp.dot(jnp.concatenate([high, middle, low], 0), narrow, preferred_element_type=F32)
    return inner, parts[:8] + (parts[16:24] + parts[32:40])


def own_kernel(patches, me_ref, own_ref, inner_ref, sums_ref, mean_ref):
    halves = halves_of(own_ref, me_ref[0])
    deviation, sums_ref[...] = half_sums(halves, (INSIDE, OUTSIDE)[:patches])
    inner_ref[...], mean_ref[...] = interior(halves, deviation)


def analysis_kernel(patches, me_ref, near_ref, inner_ref, sums_ref, mean_ref, out_ref):
    count = near_ref.shape[0]
    members = count * LOCAL
    halves = halves_of(near_ref, me_ref[0])
    deviation, sums = half_sums(halves, (OUTSIDE, INSIDE)[:patches])
    both = sums_ref[...] + sums
    each = range(patches)
    inner, mean = [inner_ref[...]], [mean_ref[...]]
    if patches == 2:
        near_inner, near_mean = interior(halves, deviation)
        inner.append(near_inner)
        mean.append(near_mean)
    row = lax.broadcasted_iota(jnp.int32, (members, members), 0)
    col = lax.broadcasted_iota(jnp.int32, (members, members), 1)
    diagonal = jnp.where(row == col, members - 1.0, 0.0)

    def mul(a, b):
        return jnp.dot(a.astype(BF), b.astype(BF), preferred_element_type=F32)

    def with_line(a, line):
        return jnp.concatenate([a.astype(BF), line.astype(BF)], 0)

    system = [both[:members, i * members : (i + 1) * members] + diagonal for i in each]
    line = [both[members:, i * members : (i + 1) * members] for i in each]
    system_b = [system[i].astype(BF) for i in each]
    first = [mul(with_line(system_b[i], line[i]), system_b[i]) for i in each]
    system_x = [mul(system_b[i], inner[i]) for i in each]
    scale = [jnp.sqrt(jnp.sum(system[i] * system[i])) for i in each]
    inverse = [1.0 / scale[i] for i in each]
    x1 = [1.5 * inner[i].astype(F32) - (0.5 * inverse[i]) * system_x[i] for i in each]
    line1 = [1.5 * line[i] - (0.5 * inverse[i]) * first[i][members:] for i in each]
    y1 = [inverse[i] * (1.5 * system[i] - (0.5 * inverse[i]) * first[i][:members]) for i in each]
    p1 = [1.5 * y1[i] - (0.5 * inverse[i]) * mul(y1[i], system_b[i]) for i in each]
    p1b = [p1[i].astype(BF) for i in each]
    second = [mul(with_line(p1b[i], line1[i]), p1b[i]) for i in each]
    x2 = [1.5 * x1[i] - 0.5 * mul(p1b[i], x1[i]) for i in each]
    line2 = [1.5 * line1[i] - 0.5 * second[i][members:] for i in each]
    q1 = [1.5 * p1[i] - 0.5 * second[i][:members] for i in each]
    p2b = [(1.5 * q1[i] - 0.5 * mul(q1[i], p1b[i])).astype(BF) for i in each]
    factor = [1.0 / jnp.sqrt(scale[i]) for i in each]
    x3 = [(1.5 * x2[i] - 0.5 * mul(p2b[i], x2[i])) * factor[i] for i in each]
    line3 = [(1.5 * line2[i] - 0.5 * mul(line2[i], p2b[i])) * factor[i] for i in each]
    line_b = [line3[i].astype(BF) for i in each]
    shift = [mul(with_line(line_b[i], line3[i] - line_b[i].astype(F32)), x3[i]) for i in each]
    root = jnp.sqrt(jnp.full((1, 1), members - 1.0, F32))
    for i in each:
        total = shift[i][:1] + shift[i][16:17] + mean[i][:1]
        result = (root * x3[i] + total).astype(BF)
        for s, place in enumerate(group(position)):
            out_ref[back_position(place), i * LOCAL : (i + 1) * LOCAL] = result[s * LOCAL : (s + 1) * LOCAL]


def forecast_kernel(in_ref, out_ref):
    def unpacked(start):
        blocks = [in_ref[back_position(p), start : start + LOCAL] for p in range(in_ref.shape[0])]
        return [row.astype(F32) for row in swap_blocks(blocks, PATCH)]

    def by_field(rows):
        half = BAND // 2
        return [
            [rows[h * FIELDS * half + field * half + r] for h in range(2) for r in range(half)]
            for field in range(FIELDS)
        ]

    own, near = by_field(unpacked(0)), by_field(unpacked(LOCAL))
    fields = [n[BAND - FSTEPS :] + o + n[:FSTEPS] for o, n in zip(own, near)]
    done = forecast_rows(*fields)
    for field in range(FIELDS):
        for r in range(BAND):
            out_ref[pl.ds(field * BAND + r, LOCAL, stride=FIELDS * BAND), :] = done[field][r]


def from_next(value):
    count = lax.axis_size("rows")
    return lax.ppermute(value, "rows", [((i + 1) % count, i) for i in range(count)])


def from_previous(value):
    count = lax.axis_size("rows")
    return lax.ppermute(value, "rows", [(i, (i + 1) % count) for i in range(count)])


def near_rows(value, join):
    if lax.axis_size("rows") == 2:
        return from_next(value)
    return join(from_next(value), from_previous(value))


def join_grid(after, before):
    return jnp.concatenate([after[:, :, : BAND // 2], before[:, :, BAND // 2 :]], 2)


def join_region(after, before):
    after, before = (x.reshape(x.shape[0], -1, 4, WIDTH) for x in (after, before))
    near = jnp.concatenate([after[:, :4], before[:, 4:8], after[:, 8:9], before[:, 9:]], 1)
    return near.reshape(near.shape[0], -1, WIDTH)


def join_inner(after, before):
    return jnp.concatenate([after[..., : WIDTH // 2], before[..., WIDTH // 2 :]], 2)


def exchange(value, rule):
    return lax.all_to_all(value, "mem", split_axis=0, concat_axis=0, axis_index_groups=[group(rule)], tiled=True)


def call(kernel, name, out_shape, *args, flops=0):
    spaces = [pltpu.SMEM if arg.shape == (1,) else pltpu.VMEM for arg in args]
    moved = sum(x.size * x.dtype.itemsize for x in [*args, *jax.tree.leaves(out_shape)])
    return pl.pallas_call(
        kernel,
        out_shape=out_shape,
        in_specs=[pl.BlockSpec(memory_space=space) for space in spaces],
        out_specs=jax.tree.map(lambda _: pl.BlockSpec(memory_space=pltpu.VMEM), out_shape),
        compiler_params=pltpu.CompilerParams(vmem_limit_bytes=16 * 2**20),
        cost_estimate=pl.CostEstimate(flops=flops, bytes_accessed=moved, transcendentals=0),
        name=name,
    )(*args)


def local(sample_collection, obs_values, obs_inverse_variance, obs_mask):
    count = lax.axis_size("mem")
    shape = sample_collection.shape
    assert shape == (LOCAL, FIELDS, BAND, WIDTH) and count == PLACES
    me = lax.axis_index("mem").astype(jnp.int32).reshape(1)
    near = near_rows(sample_collection, join_grid)
    rows = jnp.transpose(sample_collection.reshape(LOCAL, FIELDS * BAND, WIDTH), (1, 0, 2))
    region_shape = jax.ShapeDtypeStruct((count, 2 * LOCAL + 8, WIDTH), BF)
    observations = (obs_values, obs_inverse_variance, obs_mask)
    sending = call(pack_kernel, "forecast_pack", region_shape, rows, near.reshape(-1, WIDTH), *observations)
    region = exchange(sending, position)
    members, points = count * LOCAL, 2 * WIDTH
    patches = 2 if lax.axis_size("rows") == 2 else 1
    own_shapes = [
        jax.ShapeDtypeStruct((members, WIDTH), BF),
        jax.ShapeDtypeStruct((members + 16, patches * members), F32),
        jax.ShapeDtypeStruct((8, WIDTH), F32),
    ]
    flops = 2 * members * members * points
    region_near = near_rows(region, join_region)
    own = call(functools.partial(own_kernel, patches), "own_half", own_shapes, me, region, flops=flops)
    analysed_shape = jax.ShapeDtypeStruct((count, patches * LOCAL, WIDTH), BF)
    kernel = functools.partial(analysis_kernel, patches)
    analysed = call(kernel, "analysis", analysed_shape, me, region_near, *own, flops=8 * flops)
    inner = exchange(analysed, back_position)
    if patches == 1:
        inner = jnp.concatenate([inner, near_rows(inner, join_inner)], 1)
    out_shape = jax.ShapeDtypeStruct((LOCAL * FIELDS * BAND, WIDTH), F32)
    cycled = call(forecast_kernel, "unpack_forecast", out_shape, inner)
    return cycled.reshape(shape)


def solution(mesh):
    return jax.shard_map(
        local,
        mesh=mesh,
        in_specs=(
            P("mem", None, "rows", None),
            P(None, "rows", "mem"),
            P(None, "rows", "mem"),
            P(None, "rows", "mem"),
        ),
        out_specs=P("mem", None, "rows", None),
        check_vma=False,
    )
```

```python
import functools

import jax
import jax.numpy as jnp
from jax import lax
from jax.experimental import pallas as pl
from jax.experimental.pallas import tpu as pltpu
from jax.sharding import PartitionSpec as P

PATCH = 8
RADIUS = 4
FSTEPS = 4
CADV = 0.05

LOCAL = 16
FIELDS = 2
BAND = 8
WIDTH = 128
PLACES = WIDTH // PATCH
REGION = PATCH + 2 * RADIUS

BF = jnp.bfloat16
F32 = jnp.float32


def position(place):
    low, high = place & 3, place >> 2
    return PLACES - 1 - (low * 4 + (high & 1) * 2 + (high >> 1))


def forecast_rows(u_rows, v_rows):
    for _ in range(FSTEPS):
        new_u, new_v = [], []
        for i in range(1, len(u_rows) - 1):
            cu, cv = CADV * u_rows[i], CADV * v_rows[i]
            for rows, new in ((u_rows, new_u), (v_rows, new_v)):
                along_x = pltpu.roll(rows[i], WIDTH - 1, 1) - pltpu.roll(rows[i], 1, 1)
                along_y = rows[i + 1] - rows[i - 1]
                new.append(rows[i] - (cu * along_x + cv * along_y))
        u_rows, v_rows = new_u, new_v
    return u_rows, v_rows


def swap_blocks(parts, size, most):
    count = len(parts)
    block = lax.broadcasted_iota(jnp.int32, parts[0].shape, 1) // size
    stride = 1
    while stride < count:
        base = min(most, count // stride)
        here = [(block // stride) % base == digit for digit in range(base)]
        new = []
        for j in range(count):
            own = (j // stride) % base
            value = parts[j]
            for digit in range(base):
                if digit != own:
                    move = (digit - own) * stride
                    value = jnp.where(here[digit], pltpu.roll(parts[j + move], (move * size) % WIDTH, 1), value)
            new.append(value)
        parts = new
        stride *= base
    return parts


def observation_rows(values_ref, inverse_ref, mask_ref):
    points = FIELDS * BAND
    weight = (mask_ref[...].astype(F32) * inverse_ref[...]).astype(BF).astype(F32).reshape(points, PATCH)
    values = values_ref[...].reshape(points, PATCH)
    high = values.astype(BF).astype(F32)
    middle = (values - high).astype(BF).astype(F32)
    low = values - high - middle
    rows = jnp.concatenate([weight, high, middle, low], 0).astype(BF)
    source = lax.broadcasted_iota(jnp.int32, (PATCH, WIDTH), 0)
    lane = lax.broadcasted_iota(jnp.int32, (PATCH, WIDTH), 1)
    spread = (lane % PATCH == source).astype(F32).astype(BF)
    wide = jnp.dot(rows, spread, preferred_element_type=F32)
    row = lax.broadcasted_iota(jnp.int32, wide.shape, 0)
    lane = lax.broadcasted_iota(jnp.int32, wide.shape, 1)
    part, field, y = row // points, (row % points) // BAND, row % BAND
    place = (field * (BAND // 2) + y % (BAND // 2)) * 2 + part % 2
    wide = jnp.where(lane // PATCH == place, wide, 0.0).astype(BF)
    target = lax.broadcasted_iota(jnp.int32, (8, 4 * points), 0)
    row = lax.broadcasted_iota(jnp.int32, (8, 4 * points), 1)
    wanted = ((row % BAND) // (BAND // 2)) * 4 + 2 + row // (2 * points)
    gather = (target == wanted).astype(F32).astype(BF)
    return jnp.dot(gather, wide, preferred_element_type=F32)


def pack_kernel(rows_ref, near_ref, values_ref, inverse_ref, mask_ref, out_ref):
    points = FIELDS * BAND

    def near(field, index):
        return near_ref[pl.ds(field * BAND + index, LOCAL, stride=points), :]

    fields = []
    for field in range(FIELDS):
        before = [near(field, r) for r in range(BAND - FSTEPS, BAND)]
        own = [rows_ref[field * BAND + r] for r in range(BAND)]
        after = [near(field, r) for r in range(FSTEPS)]
        fields.append(before + own + after)
    done = forecast_rows(*fields)
    half_rows = BAND // 2
    index = lax.broadcasted_iota(jnp.int32, (8, WIDTH), 0)
    values, means = [], [jnp.zeros((8, WIDTH), F32)] * (FIELDS * half_rows)
    for half in range(2):
        for j in range(FIELDS * half_rows):
            value = done[j // half_rows][half * half_rows + j % half_rows]
            mean = jnp.sum(value, 0, keepdims=True) * (1.0 / LOCAL)
            high = mean.astype(BF).astype(F32)
            means[j] = jnp.where(index == 4 * half, high, jnp.where(index == 4 * half + 1, mean - high, means[j]))
            values.append(value - mean)
    rows = jnp.concatenate(values + means, 0).astype(BF)
    column = lax.broadcasted_iota(jnp.int32, (WIDTH, 2 * WIDTH), 0)
    lane = lax.broadcasted_iota(jnp.int32, (WIDTH, 2 * WIDTH), 1)
    wanted = ((lane // REGION) * PATCH + lane % REGION + (WIDTH - RADIUS)) % WIDTH
    widen = (column == wanted).astype(F32).astype(BF)
    wide = jnp.dot(rows, widen, preferred_element_type=F32)
    obs = observation_rows(values_ref, inverse_ref, mask_ref)
    start = len(values) * LOCAL
    is_mean = index & 2 == 0
    means = []
    for j in range(8):
        part = wide[start + j * 8 : start + j * 8 + 8]
        means.append(jnp.where(is_mean, part[:, :WIDTH], pltpu.roll(part[:, WIDTH:], 2, 0)))
    means = swap_blocks(means, REGION, 2)
    for side in range(2):
        for half in range(2):
            parts = [
                wide[(half * 8 + j) * LOCAL : (half * 8 + j + 1) * LOCAL, side * WIDTH : (side + 1) * WIDTH].astype(BF)
                for j in range(8)
            ]
            parts = swap_blocks(parts, REGION, 2)
            for i in range(8):
                out_ref[position(side * 8 + i), half * LOCAL : (half + 1) * LOCAL] = parts[i]
        for i in range(8):
            mean = means[i] if side == 0 else pltpu.roll(means[i], 6, 0)
            out_ref[position(side * 8 + i), 2 * LOCAL :] = jnp.where(is_mean, mean, obs).astype(BF)


def halves_of(ref, me):
    count = ref.shape[0]
    tails = [ref[s, 2 * LOCAL :].astype(F32) for s in range(count)]

    def tail_of(device):
        return ref[position(device), 2 * LOCAL :].astype(F32)

    lane = lax.broadcasted_iota(jnp.int32, (8, WIDTH), 1) % REGION
    left = tail_of(lax.rem(me + count - 1, count))
    own = tail_of(me)
    right = tail_of(lax.rem(me + 1, count))

    def seen(offset):
        return jnp.where(
            lane < RADIUS,
            pltpu.roll(left, (WIDTH + RADIUS - PATCH - offset) % WIDTH, 1),
            jnp.where(
                lane < RADIUS + PATCH,
                pltpu.roll(own, (WIDTH + RADIUS - offset) % WIDTH, 1),
                pltpu.roll(right, (WIDTH + RADIUS + PATCH - offset) % WIDTH, 1),
            ),
        )

    first, second = seen(0), seen(PATCH)
    result = []
    for half in range(2):
        base = half * 4
        means = [t[base : base + 1] + t[base + 1 : base + 2] for t in tails]
        mean = functools.reduce(jnp.add, means) * (1.0 / count)
        deviation = []
        for s, own_mean in enumerate(means):
            value = ref[s, half * LOCAL : (half + 1) * LOCAL].astype(F32)
            deviation.append((value + (own_mean - mean)).astype(BF))
        weight = first[base + 2 : base + 3]
        obs = second[base + 2 : base + 3] + first[base + 3 : base + 4] + second[base + 3 : base + 4]
        innovation = (obs - mean).astype(BF).astype(F32)
        result.append((jnp.concatenate(deviation, 0), mean, weight, innovation))
    return result


def half_sums(halves, distances):
    lane = lax.broadcasted_iota(jnp.int32, (1, WIDTH), 1)
    region_column = lane % REGION
    half_row = (lane // REGION) % (BAND // 2)
    column_distance = jnp.maximum(
        jnp.maximum(RADIUS - region_column, region_column - (RADIUS + PATCH - 1)), 0
    )
    deviation = jnp.concatenate([dev for dev, _, _, _ in halves], 1)
    innovation = jnp.concatenate([jnp.broadcast_to(inno, (16, WIDTH)) for _, _, _, inno in halves], 1)
    rows = jnp.concatenate([deviation, innovation.astype(BF)], 0)
    weighted = []
    for row_distances in distances:
        parts = []
        for (dev, _, weight, _), row_distance in zip(halves, row_distances):
            far = jnp.maximum(row_distance(half_row), column_distance).astype(F32)
            factor = weight * (1.0 - far / (RADIUS + 1.0))
            parts.append((dev.astype(F32) * factor).astype(BF))
        weighted.append(jnp.concatenate(parts, 1))
    weighted = jnp.concatenate(weighted, 0)
    return deviation, lax.dot_general(rows, weighted, (((1,), (1,)), ((), ())), preferred_element_type=F32)


INSIDE = (jnp.zeros_like, jnp.zeros_like)
OUTSIDE = (lambda r: r + 1, lambda r: RADIUS - r)


def interior(halves, deviation):
    lane = lax.broadcasted_iota(jnp.int32, (2 * WIDTH, WIDTH), 0)
    target = lax.broadcasted_iota(jnp.int32, (2 * WIDTH, WIDTH), 1)
    narrow = (lane == (target // PATCH) * REGION + RADIUS + target % PATCH).astype(F32).astype(BF)
    inner = jnp.dot(deviation, narrow, preferred_element_type=F32).astype(BF)
    mean = jnp.broadcast_to(jnp.concatenate([halves[0][1], halves[1][1]], 1), (16, 2 * WIDTH))
    high = mean.astype(BF)
    middle = (mean - high.astype(F32)).astype(BF)
    low = (mean - high.astype(F32) - middle.astype(F32)).astype(BF)
    parts = jnp.dot(jnp.concatenate([high, middle, low], 0), narrow, preferred_element_type=F32)
    return inner, parts[:8] + (parts[16:24] + parts[32:40])


def own_kernel(patches, me_ref, own_ref, inner_ref, sums_ref, mean_ref):
    halves = halves_of(own_ref, me_ref[0])
    deviation, sums_ref[...] = half_sums(halves, (INSIDE, OUTSIDE)[:patches])
    inner_ref[...], mean_ref[...] = interior(halves, deviation)


def analysis_kernel(patches, me_ref, near_ref, inner_ref, sums_ref, mean_ref, out_ref):
    count = near_ref.shape[0]
    members = count * LOCAL
    halves = halves_of(near_ref, me_ref[0])
    deviation, sums = half_sums(halves, (OUTSIDE, INSIDE)[:patches])
    both = sums_ref[...] + sums
    each = range(patches)
    inner, mean = [inner_ref[...]], [mean_ref[...]]
    if patches == 2:
        near_inner, near_mean = interior(halves, deviation)
        inner.append(near_inner)
        mean.append(near_mean)
    row = lax.broadcasted_iota(jnp.int32, (members, members), 0)
    col = lax.broadcasted_iota(jnp.int32, (members, members), 1)
    diagonal = jnp.where(row == col, members - 1.0, 0.0)

    def mul(a, b):
        return jnp.dot(a.astype(BF), b.astype(BF), preferred_element_type=F32)

    def with_line(a, line):
        return jnp.concatenate([a.astype(BF), line.astype(BF)], 0)

    system = [both[:members, i * members : (i + 1) * members] + diagonal for i in each]
    line = [both[members:, i * members : (i + 1) * members] for i in each]
    system_b = [system[i].astype(BF) for i in each]
    first = [mul(with_line(system_b[i], line[i]), system_b[i]) for i in each]
    system_x = [mul(system_b[i], inner[i]) for i in each]
    scale = [jnp.sqrt(jnp.sum(system[i] * system[i])) for i in each]
    inverse = [1.0 / scale[i] for i in each]
    x1 = [1.5 * inner[i].astype(F32) - (0.5 * inverse[i]) * system_x[i] for i in each]
    line1 = [1.5 * line[i] - (0.5 * inverse[i]) * first[i][members:] for i in each]
    y1 = [inverse[i] * (1.5 * system[i] - (0.5 * inverse[i]) * first[i][:members]) for i in each]
    p1 = [1.5 * y1[i] - (0.5 * inverse[i]) * mul(y1[i], system_b[i]) for i in each]
    p1b = [p1[i].astype(BF) for i in each]
    second = [mul(with_line(p1b[i], line1[i]), p1b[i]) for i in each]
    x2 = [1.5 * x1[i] - 0.5 * mul(p1b[i], x1[i]) for i in each]
    line2 = [1.5 * line1[i] - 0.5 * second[i][members:] for i in each]
    q1 = [1.5 * p1[i] - 0.5 * second[i][:members] for i in each]
    p2b = [(1.5 * q1[i] - 0.5 * mul(q1[i], p1b[i])).astype(BF) for i in each]
    factor = [1.0 / jnp.sqrt(scale[i]) for i in each]
    x3 = [(1.5 * x2[i] - 0.5 * mul(p2b[i], x2[i])) * factor[i] for i in each]
    line3 = [(1.5 * line2[i] - 0.5 * mul(line2[i], p2b[i])) * factor[i] for i in each]
    line_b = [line3[i].astype(BF) for i in each]
    shift = [mul(with_line(line_b[i], line3[i] - line_b[i].astype(F32)), x3[i]) for i in each]
    root = jnp.sqrt(jnp.full((1, 1), members - 1.0, F32))
    for i in each:
        total = shift[i][:1] + shift[i][16:17] + mean[i][:1]
        result = (root * x3[i] + total).astype(BF)
        for s in range(count):
            out_ref[s, i * LOCAL : (i + 1) * LOCAL] = result[s * LOCAL : (s + 1) * LOCAL]


def forecast_kernel(in_ref, out_ref):
    def unpacked(start):
        blocks = [in_ref[position(p), start : start + LOCAL] for p in range(in_ref.shape[0])]
        return [row.astype(F32) for row in swap_blocks(blocks, PATCH, 4)]

    def by_field(rows):
        half = BAND // 2
        return [
            [rows[h * FIELDS * half + field * half + r] for h in range(2) for r in range(half)]
            for field in range(FIELDS)
        ]

    own, near = by_field(unpacked(0)), by_field(unpacked(LOCAL))
    fields = [n[BAND - FSTEPS :] + o + n[:FSTEPS] for o, n in zip(own, near)]
    done = forecast_rows(*fields)
    for field in range(FIELDS):
        for r in range(BAND):
            out_ref[pl.ds(field * BAND + r, LOCAL, stride=FIELDS * BAND), :] = done[field][r]


def from_next(value):
    count = lax.axis_size("rows")
    return lax.ppermute(value, "rows", [((i + 1) % count, i) for i in range(count)])


def from_previous(value):
    count = lax.axis_size("rows")
    return lax.ppermute(value, "rows", [(i, (i + 1) % count) for i in range(count)])


def near_rows(value, join):
    if lax.axis_size("rows") == 2:
        return from_next(value)
    return join(from_next(value), from_previous(value))


def join_grid(after, before):
    return jnp.concatenate([after[:, :, : BAND // 2], before[:, :, BAND // 2 :]], 2)


def join_region(after, before):
    after, before = (x.reshape(x.shape[0], -1, 4, WIDTH) for x in (after, before))
    near = jnp.concatenate([after[:, :4], before[:, 4:8], after[:, 8:9], before[:, 9:]], 1)
    return near.reshape(near.shape[0], -1, WIDTH)


def join_inner(after, before):
    return jnp.concatenate([after[..., : WIDTH // 2], before[..., WIDTH // 2 :]], 2)


def exchange(value):
    group = [sorted(range(lax.axis_size("mem")), key=position)]
    return lax.all_to_all(value, "mem", split_axis=0, concat_axis=0, axis_index_groups=group, tiled=True)


def call(kernel, name, out_shape, *args, flops=0):
    spaces = [pltpu.SMEM if arg.shape == (1,) else pltpu.VMEM for arg in args]
    moved = sum(x.size * x.dtype.itemsize for x in [*args, *jax.tree.leaves(out_shape)])
    return pl.pallas_call(
        kernel,
        out_shape=out_shape,
        in_specs=[pl.BlockSpec(memory_space=space) for space in spaces],
        out_specs=jax.tree.map(lambda _: pl.BlockSpec(memory_space=pltpu.VMEM), out_shape),
        compiler_params=pltpu.CompilerParams(vmem_limit_bytes=16 * 2**20),
        cost_estimate=pl.CostEstimate(flops=flops, bytes_accessed=moved, transcendentals=0),
        name=name,
    )(*args)


def local(sample_collection, obs_values, obs_inverse_variance, obs_mask):
    count = lax.axis_size("mem")
    shape = sample_collection.shape
    assert shape == (LOCAL, FIELDS, BAND, WIDTH) and count == PLACES
    me = lax.axis_index("mem").astype(jnp.int32).reshape(1)
    near = near_rows(sample_collection, join_grid)
    rows = jnp.transpose(sample_collection.reshape(LOCAL, FIELDS * BAND, WIDTH), (1, 0, 2))
    region_shape = jax.ShapeDtypeStruct((count, 2 * LOCAL + 8, WIDTH), BF)
    observations = (obs_values, obs_inverse_variance, obs_mask)
    region = exchange(call(pack_kernel, "forecast_pack", region_shape, rows, near.reshape(-1, WIDTH), *observations))
    members, points = count * LOCAL, 2 * WIDTH
    patches = 2 if lax.axis_size("rows") == 2 else 1
    own_shapes = [
        jax.ShapeDtypeStruct((members, WIDTH), BF),
        jax.ShapeDtypeStruct((members + 16, patches * members), F32),
        jax.ShapeDtypeStruct((8, WIDTH), F32),
    ]
    flops = 2 * members * members * points
    region_near = near_rows(region, join_region)
    own = call(functools.partial(own_kernel, patches), "own_half", own_shapes, me, region, flops=flops)
    analysed_shape = jax.ShapeDtypeStruct((count, patches * LOCAL, WIDTH), BF)
    kernel = functools.partial(analysis_kernel, patches)
    inner = exchange(call(kernel, "analysis", analysed_shape, me, region_near, *own, flops=8 * flops))
    if patches == 1:
        inner = jnp.concatenate([inner, near_rows(inner, join_inner)], 1)
    out_shape = jax.ShapeDtypeStruct((LOCAL * FIELDS * BAND, WIDTH), F32)
    cycled = call(forecast_kernel, "unpack_forecast", out_shape, inner)
    return cycled.reshape(shape)


def solution(mesh):
    return jax.shard_map(
        local,
        mesh=mesh,
        in_specs=(
            P("mem", None, "rows", None),
            P(None, "rows", "mem"),
            P(None, "rows", "mem"),
            P(None, "rows", "mem"),
        ),
        out_specs=P("mem", None, "rows", None),
        check_vma=False,
    )
```

```python
import functools

import jax
import jax.numpy as jnp
from jax import lax
from jax.experimental import pallas as pl
from jax.experimental.pallas import tpu as pltpu
from jax.sharding import PartitionSpec as P

PATCH = 8
RADIUS = 4
FSTEPS = 4
CADV = 0.05

LOCAL = 16
FIELDS = 2
BAND = 8
WIDTH = 128
PLACES = WIDTH // PATCH
REGION = PATCH + 2 * RADIUS

BF = jnp.bfloat16
F32 = jnp.float32


GOING = (15, 7, 11, 6, 10, 5, 9, 4, 8, 3, 2, 1, 14, 13, 12, 0)
BACK = (15, 7, 11, 3, 14, 6, 10, 2, 13, 5, 9, 1, 12, 4, 8, 0)


def position(place, order=GOING):
    if isinstance(place, int):
        return order.index(place)
    return functools.reduce(lambda kept, k: jnp.where(place == order[k], k, kept), range(1, PLACES), 0)


def forecast_rows(u_rows, v_rows):
    for _ in range(FSTEPS):
        new_u, new_v = [], []
        for i in range(1, len(u_rows) - 1):
            cu, cv = CADV * u_rows[i], CADV * v_rows[i]
            for rows, new in ((u_rows, new_u), (v_rows, new_v)):
                along_x = pltpu.roll(rows[i], WIDTH - 1, 1) - pltpu.roll(rows[i], 1, 1)
                along_y = rows[i + 1] - rows[i - 1]
                new.append(rows[i] - (cu * along_x + cv * along_y))
        u_rows, v_rows = new_u, new_v
    return u_rows, v_rows


def swap_blocks(parts, size):
    count = len(parts)
    lane = lax.broadcasted_iota(jnp.int32, parts[0].shape, 1) // size
    stride = 1
    while stride < count:
        upper = (lane & stride) != 0
        new = list(parts)
        for j in range(count):
            if j & stride == 0:
                a, b = parts[j], parts[j + stride]
                new[j] = jnp.where(upper, pltpu.roll(b, stride * size, 1), a)
                new[j + stride] = jnp.where(upper, b, pltpu.roll(a, WIDTH - stride * size, 1))
        parts = new
        stride *= 2
    return parts


def observation_rows(values_ref, inverse_ref, mask_ref):
    points = FIELDS * BAND
    weight = (mask_ref[...].astype(F32) * inverse_ref[...]).astype(BF).astype(F32).reshape(points, PATCH)
    values = values_ref[...].reshape(points, PATCH)
    high = values.astype(BF).astype(F32)
    middle = (values - high).astype(BF).astype(F32)
    low = values - high - middle
    rows = jnp.concatenate([weight, high, middle, low], 0).astype(BF)
    source = lax.broadcasted_iota(jnp.int32, (PATCH, WIDTH), 0)
    lane = lax.broadcasted_iota(jnp.int32, (PATCH, WIDTH), 1)
    spread = (lane % PATCH == source).astype(F32).astype(BF)
    wide = jnp.dot(rows, spread, preferred_element_type=F32)
    row = lax.broadcasted_iota(jnp.int32, wide.shape, 0)
    lane = lax.broadcasted_iota(jnp.int32, wide.shape, 1)
    part, field, y = row // points, (row % points) // BAND, row % BAND
    place = (field * (BAND // 2) + y % (BAND // 2)) * 2 + part % 2
    wide = jnp.where(lane // PATCH == place, wide, 0.0).astype(BF)
    target = lax.broadcasted_iota(jnp.int32, (8, 4 * points), 0)
    row = lax.broadcasted_iota(jnp.int32, (8, 4 * points), 1)
    wanted = ((row % BAND) // (BAND // 2)) * 4 + 2 + row // (2 * points)
    gather = (target == wanted).astype(F32).astype(BF)
    return jnp.dot(gather, wide, preferred_element_type=F32)


def pack_kernel(rows_ref, near_ref, values_ref, inverse_ref, mask_ref, out_ref):
    points = FIELDS * BAND

    def near(field, index):
        return near_ref[pl.ds(field * BAND + index, LOCAL, stride=points), :]

    fields = []
    for field in range(FIELDS):
        before = [near(field, r) for r in range(BAND - FSTEPS, BAND)]
        own = [rows_ref[field * BAND + r] for r in range(BAND)]
        after = [near(field, r) for r in range(FSTEPS)]
        fields.append(before + own + after)
    done = forecast_rows(*fields)
    half_rows = BAND // 2
    index = lax.broadcasted_iota(jnp.int32, (8, WIDTH), 0)
    values, means = [], [jnp.zeros((8, WIDTH), F32)] * (FIELDS * half_rows)
    for half in range(2):
        for j in range(FIELDS * half_rows):
            value = done[j // half_rows][half * half_rows + j % half_rows]
            mean = jnp.sum(value, 0, keepdims=True) * (1.0 / LOCAL)
            high = mean.astype(BF).astype(F32)
            means[j] = jnp.where(index == 4 * half, high, jnp.where(index == 4 * half + 1, mean - high, means[j]))
            values.append(value - mean)
    rows = jnp.concatenate(values + means, 0).astype(BF)
    column = lax.broadcasted_iota(jnp.int32, (WIDTH, 2 * WIDTH), 0)
    lane = lax.broadcasted_iota(jnp.int32, (WIDTH, 2 * WIDTH), 1)
    wanted = ((lane // REGION) * PATCH + lane % REGION + (WIDTH - RADIUS)) % WIDTH
    widen = (column == wanted).astype(F32).astype(BF)
    wide = jnp.dot(rows, widen, preferred_element_type=F32)
    obs = observation_rows(values_ref, inverse_ref, mask_ref)
    start = len(values) * LOCAL
    is_mean = index & 2 == 0
    means = []
    for j in range(8):
        part = wide[start + j * 8 : start + j * 8 + 8]
        means.append(jnp.where(is_mean, part[:, :WIDTH], pltpu.roll(part[:, WIDTH:], 2, 0)))
    means = swap_blocks(means, REGION)
    for side in range(2):
        for half in range(2):
            parts = [
                wide[(half * 8 + j) * LOCAL : (half * 8 + j + 1) * LOCAL, side * WIDTH : (side + 1) * WIDTH].astype(BF)
                for j in range(8)
            ]
            parts = swap_blocks(parts, REGION)
            for i in range(8):
                out_ref[position(side * 8 + i), half * LOCAL : (half + 1) * LOCAL] = parts[i]
        for i in range(8):
            mean = means[i] if side == 0 else pltpu.roll(means[i], 6, 0)
            out_ref[position(side * 8 + i), 2 * LOCAL :] = jnp.where(is_mean, mean, obs).astype(BF)


def halves_of(ref, me):
    count = ref.shape[0]
    tails = [ref[s, 2 * LOCAL :].astype(F32) for s in range(count)]

    def tail_of(device):
        return ref[position(device), 2 * LOCAL :].astype(F32)

    lane = lax.broadcasted_iota(jnp.int32, (8, WIDTH), 1) % REGION
    left = tail_of(lax.rem(me + count - 1, count))
    own = tail_of(me)
    right = tail_of(lax.rem(me + 1, count))

    def seen(offset):
        return jnp.where(
            lane < RADIUS,
            pltpu.roll(left, (WIDTH + RADIUS - PATCH - offset) % WIDTH, 1),
            jnp.where(
                lane < RADIUS + PATCH,
                pltpu.roll(own, (WIDTH + RADIUS - offset) % WIDTH, 1),
                pltpu.roll(right, (WIDTH + RADIUS + PATCH - offset) % WIDTH, 1),
            ),
        )

    first, second = seen(0), seen(PATCH)
    result = []
    for half in range(2):
        base = half * 4
        means = [t[base : base + 1] + t[base + 1 : base + 2] for t in tails]
        mean = functools.reduce(jnp.add, means) * (1.0 / count)
        deviation = []
        for s, own_mean in enumerate(means):
            value = ref[s, half * LOCAL : (half + 1) * LOCAL].astype(F32)
            deviation.append((value + (own_mean - mean)).astype(BF))
        weight = first[base + 2 : base + 3]
        obs = second[base + 2 : base + 3] + first[base + 3 : base + 4] + second[base + 3 : base + 4]
        innovation = (obs - mean).astype(BF).astype(F32)
        result.append((jnp.concatenate(deviation, 0), mean, weight, innovation))
    return result


def half_sums(halves, distances):
    lane = lax.broadcasted_iota(jnp.int32, (1, WIDTH), 1)
    region_column = lane % REGION
    half_row = (lane // REGION) % (BAND // 2)
    column_distance = jnp.maximum(
        jnp.maximum(RADIUS - region_column, region_column - (RADIUS + PATCH - 1)), 0
    )
    deviation = jnp.concatenate([dev for dev, _, _, _ in halves], 1)
    innovation = jnp.concatenate([jnp.broadcast_to(inno, (16, WIDTH)) for _, _, _, inno in halves], 1)
    rows = jnp.concatenate([deviation, innovation.astype(BF)], 0)
    weighted = []
    for row_distances in distances:
        parts = []
        for (dev, _, weight, _), row_distance in zip(halves, row_distances):
            far = jnp.maximum(row_distance(half_row), column_distance).astype(F32)
            factor = weight * (1.0 - far / (RADIUS + 1.0))
            parts.append((dev.astype(F32) * factor).astype(BF))
        weighted.append(jnp.concatenate(parts, 1))
    weighted = jnp.concatenate(weighted, 0)
    return deviation, lax.dot_general(rows, weighted, (((1,), (1,)), ((), ())), preferred_element_type=F32)


INSIDE = (jnp.zeros_like, jnp.zeros_like)
OUTSIDE = (lambda r: r + 1, lambda r: RADIUS - r)


def interior(halves, deviation):
    lane = lax.broadcasted_iota(jnp.int32, (2 * WIDTH, WIDTH), 0)
    target = lax.broadcasted_iota(jnp.int32, (2 * WIDTH, WIDTH), 1)
    narrow = (lane == (target // PATCH) * REGION + RADIUS + target % PATCH).astype(F32).astype(BF)
    inner = jnp.dot(deviation, narrow, preferred_element_type=F32).astype(BF)
    mean = jnp.broadcast_to(jnp.concatenate([halves[0][1], halves[1][1]], 1), (16, 2 * WIDTH))
    high = mean.astype(BF)
    middle = (mean - high.astype(F32)).astype(BF)
    low = (mean - high.astype(F32) - middle.astype(F32)).astype(BF)
    parts = jnp.dot(jnp.concatenate([high, middle, low], 0), narrow, preferred_element_type=F32)
    return inner, parts[:8] + (parts[16:24] + parts[32:40])


def own_kernel(patches, me_ref, own_ref, inner_ref, sums_ref, mean_ref):
    halves = halves_of(own_ref, me_ref[0])
    deviation, sums_ref[...] = half_sums(halves, (INSIDE, OUTSIDE)[:patches])
    inner_ref[...], mean_ref[...] = interior(halves, deviation)


def analysis_kernel(patches, me_ref, near_ref, inner_ref, sums_ref, mean_ref, out_ref):
    count = near_ref.shape[0]
    members = count * LOCAL
    halves = halves_of(near_ref, me_ref[0])
    deviation, sums = half_sums(halves, (OUTSIDE, INSIDE)[:patches])
    both = sums_ref[...] + sums
    each = range(patches)
    inner, mean = [inner_ref[...]], [mean_ref[...]]
    if patches == 2:
        near_inner, near_mean = interior(halves, deviation)
        inner.append(near_inner)
        mean.append(near_mean)
    row = lax.broadcasted_iota(jnp.int32, (members, members), 0)
    col = lax.broadcasted_iota(jnp.int32, (members, members), 1)
    diagonal = jnp.where(row == col, members - 1.0, 0.0)

    def mul(a, b):
        return jnp.dot(a.astype(BF), b.astype(BF), preferred_element_type=F32)

    def with_line(a, line):
        return jnp.concatenate([a.astype(BF), line.astype(BF)], 0)

    system = [both[:members, i * members : (i + 1) * members] + diagonal for i in each]
    line = [both[members:, i * members : (i + 1) * members] for i in each]
    system_b = [system[i].astype(BF) for i in each]
    first = [mul(with_line(system_b[i], line[i]), system_b[i]) for i in each]
    system_x = [mul(system_b[i], inner[i]) for i in each]
    scale = [jnp.sqrt(jnp.sum(system[i] * system[i])) for i in each]
    inverse = [1.0 / scale[i] for i in each]
    x1 = [1.5 * inner[i].astype(F32) - (0.5 * inverse[i]) * system_x[i] for i in each]
    line1 = [1.5 * line[i] - (0.5 * inverse[i]) * first[i][members:] for i in each]
    y1 = [inverse[i] * (1.5 * system[i] - (0.5 * inverse[i]) * first[i][:members]) for i in each]
    p1 = [1.5 * y1[i] - (0.5 * inverse[i]) * mul(y1[i], system_b[i]) for i in each]
    p1b = [p1[i].astype(BF) for i in each]
    second = [mul(with_line(p1b[i], line1[i]), p1b[i]) for i in each]
    x2 = [1.5 * x1[i] - 0.5 * mul(p1b[i], x1[i]) for i in each]
    line2 = [1.5 * line1[i] - 0.5 * second[i][members:] for i in each]
    q1 = [1.5 * p1[i] - 0.5 * second[i][:members] for i in each]
    p2b = [(1.5 * q1[i] - 0.5 * mul(q1[i], p1b[i])).astype(BF) for i in each]
    factor = [1.0 / jnp.sqrt(scale[i]) for i in each]
    x3 = [(1.5 * x2[i] - 0.5 * mul(p2b[i], x2[i])) * factor[i] for i in each]
    line3 = [(1.5 * line2[i] - 0.5 * mul(line2[i], p2b[i])) * factor[i] for i in each]
    line_b = [line3[i].astype(BF) for i in each]
    shift = [mul(with_line(line_b[i], line3[i] - line_b[i].astype(F32)), x3[i]) for i in each]
    root = jnp.sqrt(jnp.full((1, 1), members - 1.0, F32))
    for i in each:
        total = shift[i][:1] + shift[i][16:17] + mean[i][:1]
        result = (root * x3[i] + total).astype(BF)
        for s, place in enumerate(GOING):
            out_ref[position(place, BACK), i * LOCAL : (i + 1) * LOCAL] = result[s * LOCAL : (s + 1) * LOCAL]


def forecast_kernel(in_ref, out_ref):
    def unpacked(start):
        blocks = [in_ref[position(p, BACK), start : start + LOCAL] for p in range(in_ref.shape[0])]
        return [row.astype(F32) for row in swap_blocks(blocks, PATCH)]

    def by_field(rows):
        half = BAND // 2
        return [
            [rows[h * FIELDS * half + field * half + r] for h in range(2) for r in range(half)]
            for field in range(FIELDS)
        ]

    own, near = by_field(unpacked(0)), by_field(unpacked(LOCAL))
    fields = [n[BAND - FSTEPS :] + o + n[:FSTEPS] for o, n in zip(own, near)]
    done = forecast_rows(*fields)
    for field in range(FIELDS):
        for r in range(BAND):
            out_ref[pl.ds(field * BAND + r, LOCAL, stride=FIELDS * BAND), :] = done[field][r]


def from_next(value):
    count = lax.axis_size("rows")
    return lax.ppermute(value, "rows", [((i + 1) % count, i) for i in range(count)])


def from_previous(value):
    count = lax.axis_size("rows")
    return lax.ppermute(value, "rows", [(i, (i + 1) % count) for i in range(count)])


def near_rows(value, join):
    if lax.axis_size("rows") == 2:
        return from_next(value)
    return join(from_next(value), from_previous(value))


def join_grid(after, before):
    return jnp.concatenate([after[:, :, : BAND // 2], before[:, :, BAND // 2 :]], 2)


def join_region(after, before):
    after, before = (x.reshape(x.shape[0], -1, 4, WIDTH) for x in (after, before))
    near = jnp.concatenate([after[:, :4], before[:, 4:8], after[:, 8:9], before[:, 9:]], 1)
    return near.reshape(near.shape[0], -1, WIDTH)


def join_inner(after, before):
    return jnp.concatenate([after[..., : WIDTH // 2], before[..., WIDTH // 2 :]], 2)


def exchange(value, order):
    return lax.all_to_all(value, "mem", split_axis=0, concat_axis=0, axis_index_groups=[list(order)], tiled=True)


def call(kernel, name, out_shape, *args, flops=0):
    spaces = [pltpu.SMEM if arg.shape == (1,) else pltpu.VMEM for arg in args]
    moved = sum(x.size * x.dtype.itemsize for x in [*args, *jax.tree.leaves(out_shape)])
    return pl.pallas_call(
        kernel,
        out_shape=out_shape,
        in_specs=[pl.BlockSpec(memory_space=space) for space in spaces],
        out_specs=jax.tree.map(lambda _: pl.BlockSpec(memory_space=pltpu.VMEM), out_shape),
        compiler_params=pltpu.CompilerParams(vmem_limit_bytes=16 * 2**20),
        cost_estimate=pl.CostEstimate(flops=flops, bytes_accessed=moved, transcendentals=0),
        name=name,
    )(*args)


def local(sample_collection, obs_values, obs_inverse_variance, obs_mask):
    count = lax.axis_size("mem")
    shape = sample_collection.shape
    assert shape == (LOCAL, FIELDS, BAND, WIDTH) and count == PLACES
    me = lax.axis_index("mem").astype(jnp.int32).reshape(1)
    near = near_rows(sample_collection, join_grid)
    rows = jnp.transpose(sample_collection.reshape(LOCAL, FIELDS * BAND, WIDTH), (1, 0, 2))
    region_shape = jax.ShapeDtypeStruct((count, 2 * LOCAL + 8, WIDTH), BF)
    observations = (obs_values, obs_inverse_variance, obs_mask)
    sending = call(pack_kernel, "forecast_pack", region_shape, rows, near.reshape(-1, WIDTH), *observations)
    region = exchange(sending, GOING)
    members, points = count * LOCAL, 2 * WIDTH
    patches = 2 if lax.axis_size("rows") == 2 else 1
    own_shapes = [
        jax.ShapeDtypeStruct((members, WIDTH), BF),
        jax.ShapeDtypeStruct((members + 16, patches * members), F32),
        jax.ShapeDtypeStruct((8, WIDTH), F32),
    ]
    flops = 2 * members * members * points
    region_near = near_rows(region, join_region)
    own = call(functools.partial(own_kernel, patches), "own_half", own_shapes, me, region, flops=flops)
    analysed_shape = jax.ShapeDtypeStruct((count, patches * LOCAL, WIDTH), BF)
    kernel = functools.partial(analysis_kernel, patches)
    analysed = call(kernel, "analysis", analysed_shape, me, region_near, *own, flops=8 * flops)
    inner = exchange(analysed, BACK)
    if patches == 1:
        inner = jnp.concatenate([inner, near_rows(inner, join_inner)], 1)
    out_shape = jax.ShapeDtypeStruct((LOCAL * FIELDS * BAND, WIDTH), F32)
    cycled = call(forecast_kernel, "unpack_forecast", out_shape, inner)
    return cycled.reshape(shape)


def solution(mesh):
    return jax.shard_map(
        local,
        mesh=mesh,
        in_specs=(
            P("mem", None, "rows", None),
            P(None, "rows", "mem"),
            P(None, "rows", "mem"),
            P(None, "rows", "mem"),
        ),
        out_specs=P("mem", None, "rows", None),
        check_vma=False,
    )
```

```python
import functools

import jax
import jax.numpy as jnp
from jax import lax
from jax.experimental import pallas as pl
from jax.experimental.pallas import tpu as pltpu
from jax.sharding import PartitionSpec as P

PATCH = 8
RADIUS = 4
FSTEPS = 4
CADV = 0.05

LOCAL = 16
FIELDS = 2
BAND = 8
WIDTH = 128
PLACES = WIDTH // PATCH
REGION = PATCH + 2 * RADIUS

BF = jnp.bfloat16
F32 = jnp.float32


GOING = (15, 7, 11, 3, 14, 6, 10, 2, 13, 5, 9, 1, 12, 4, 8, 0)
BACK = (1, 2, 3, 4, 5, 6, 7, 8, 9, 10, 11, 12, 13, 14, 15, 0)


def position(place, order=GOING):
    if isinstance(place, int):
        return order.index(place)
    return functools.reduce(lambda kept, k: jnp.where(place == order[k], k, kept), range(1, PLACES), 0)


def forecast_rows(u_rows, v_rows):
    for _ in range(FSTEPS):
        new_u, new_v = [], []
        for i in range(1, len(u_rows) - 1):
            cu, cv = CADV * u_rows[i], CADV * v_rows[i]
            for rows, new in ((u_rows, new_u), (v_rows, new_v)):
                along_x = pltpu.roll(rows[i], WIDTH - 1, 1) - pltpu.roll(rows[i], 1, 1)
                along_y = rows[i + 1] - rows[i - 1]
                new.append(rows[i] - (cu * along_x + cv * along_y))
        u_rows, v_rows = new_u, new_v
    return u_rows, v_rows


def swap_blocks(parts, size):
    count = len(parts)
    lane = lax.broadcasted_iota(jnp.int32, parts[0].shape, 1) // size
    stride = 1
    while stride < count:
        upper = (lane & stride) != 0
        new = list(parts)
        for j in range(count):
            if j & stride == 0:
                a, b = parts[j], parts[j + stride]
                new[j] = jnp.where(upper, pltpu.roll(b, stride * size, 1), a)
                new[j + stride] = jnp.where(upper, b, pltpu.roll(a, WIDTH - stride * size, 1))
        parts = new
        stride *= 2
    return parts


def observation_rows(values_ref, inverse_ref, mask_ref):
    points = FIELDS * BAND
    weight = (mask_ref[...].astype(F32) * inverse_ref[...]).astype(BF).astype(F32).reshape(points, PATCH)
    values = values_ref[...].reshape(points, PATCH)
    high = values.astype(BF).astype(F32)
    middle = (values - high).astype(BF).astype(F32)
    low = values - high - middle
    rows = jnp.concatenate([weight, high, middle, low], 0).astype(BF)
    source = lax.broadcasted_iota(jnp.int32, (PATCH, WIDTH), 0)
    lane = lax.broadcasted_iota(jnp.int32, (PATCH, WIDTH), 1)
    spread = (lane % PATCH == source).astype(F32).astype(BF)
    wide = jnp.dot(rows, spread, preferred_element_type=F32)
    row = lax.broadcasted_iota(jnp.int32, wide.shape, 0)
    lane = lax.broadcasted_iota(jnp.int32, wide.shape, 1)
    part, field, y = row // points, (row % points) // BAND, row % BAND
    place = (field * (BAND // 2) + y % (BAND // 2)) * 2 + part % 2
    wide = jnp.where(lane // PATCH == place, wide, 0.0).astype(BF)
    target = lax.broadcasted_iota(jnp.int32, (8, 4 * points), 0)
    row = lax.broadcasted_iota(jnp.int32, (8, 4 * points), 1)
    wanted = ((row % BAND) // (BAND // 2)) * 4 + 2 + row // (2 * points)
    gather = (target == wanted).astype(F32).astype(BF)
    return jnp.dot(gather, wide, preferred_element_type=F32)


def pack_kernel(rows_ref, near_ref, values_ref, inverse_ref, mask_ref, out_ref):
    points = FIELDS * BAND

    def near(field, index):
        return near_ref[pl.ds(field * BAND + index, LOCAL, stride=points), :]

    fields = []
    for field in range(FIELDS):
        before = [near(field, r) for r in range(BAND - FSTEPS, BAND)]
        own = [rows_ref[field * BAND + r] for r in range(BAND)]
        after = [near(field, r) for r in range(FSTEPS)]
        fields.append(before + own + after)
    done = forecast_rows(*fields)
    half_rows = BAND // 2
    index = lax.broadcasted_iota(jnp.int32, (8, WIDTH), 0)
    values, means = [], [jnp.zeros((8, WIDTH), F32)] * (FIELDS * half_rows)
    for half in range(2):
        for j in range(FIELDS * half_rows):
            value = done[j // half_rows][half * half_rows + j % half_rows]
            mean = jnp.sum(value, 0, keepdims=True) * (1.0 / LOCAL)
            high = mean.astype(BF).astype(F32)
            means[j] = jnp.where(index == 4 * half, high, jnp.where(index == 4 * half + 1, mean - high, means[j]))
            values.append(value - mean)
    rows = jnp.concatenate(values + means, 0).astype(BF)
    column = lax.broadcasted_iota(jnp.int32, (WIDTH, 2 * WIDTH), 0)
    lane = lax.broadcasted_iota(jnp.int32, (WIDTH, 2 * WIDTH), 1)
    wanted = ((lane // REGION) * PATCH + lane % REGION + (WIDTH - RADIUS)) % WIDTH
    widen = (column == wanted).astype(F32).astype(BF)
    wide = jnp.dot(rows, widen, preferred_element_type=F32)
    obs = observation_rows(values_ref, inverse_ref, mask_ref)
    start = len(values) * LOCAL
    is_mean = index & 2 == 0
    means = []
    for j in range(8):
        part = wide[start + j * 8 : start + j * 8 + 8]
        means.append(jnp.where(is_mean, part[:, :WIDTH], pltpu.roll(part[:, WIDTH:], 2, 0)))
    means = swap_blocks(means, REGION)
    for side in range(2):
        for half in range(2):
            parts = [
                wide[(half * 8 + j) * LOCAL : (half * 8 + j + 1) * LOCAL, side * WIDTH : (side + 1) * WIDTH].astype(BF)
                for j in range(8)
            ]
            parts = swap_blocks(parts, REGION)
            for i in range(8):
                out_ref[position(side * 8 + i), half * LOCAL : (half + 1) * LOCAL] = parts[i]
        for i in range(8):
            mean = means[i] if side == 0 else pltpu.roll(means[i], 6, 0)
            out_ref[position(side * 8 + i), 2 * LOCAL :] = jnp.where(is_mean, mean, obs).astype(BF)


def halves_of(ref, me):
    count = ref.shape[0]
    tails = [ref[s, 2 * LOCAL :].astype(F32) for s in range(count)]

    def tail_of(device):
        return ref[position(device), 2 * LOCAL :].astype(F32)

    lane = lax.broadcasted_iota(jnp.int32, (8, WIDTH), 1) % REGION
    left = tail_of(lax.rem(me + count - 1, count))
    own = tail_of(me)
    right = tail_of(lax.rem(me + 1, count))

    def seen(offset):
        return jnp.where(
            lane < RADIUS,
            pltpu.roll(left, (WIDTH + RADIUS - PATCH - offset) % WIDTH, 1),
            jnp.where(
                lane < RADIUS + PATCH,
                pltpu.roll(own, (WIDTH + RADIUS - offset) % WIDTH, 1),
                pltpu.roll(right, (WIDTH + RADIUS + PATCH - offset) % WIDTH, 1),
            ),
        )

    first, second = seen(0), seen(PATCH)
    result = []
    for half in range(2):
        base = half * 4
        means = [t[base : base + 1] + t[base + 1 : base + 2] for t in tails]
        mean = functools.reduce(jnp.add, means) * (1.0 / count)
        deviation = []
        for s, own_mean in enumerate(means):
            value = ref[s, half * LOCAL : (half + 1) * LOCAL].astype(F32)
            deviation.append((value + (own_mean - mean)).astype(BF))
        weight = first[base + 2 : base + 3]
        obs = second[base + 2 : base + 3] + first[base + 3 : base + 4] + second[base + 3 : base + 4]
        innovation = (obs - mean).astype(BF).astype(F32)
        result.append((jnp.concatenate(deviation, 0), mean, weight, innovation))
    return result


def half_sums(halves, distances):
    lane = lax.broadcasted_iota(jnp.int32, (1, WIDTH), 1)
    region_column = lane % REGION
    half_row = (lane // REGION) % (BAND // 2)
    column_distance = jnp.maximum(
        jnp.maximum(RADIUS - region_column, region_column - (RADIUS + PATCH - 1)), 0
    )
    deviation = jnp.concatenate([dev for dev, _, _, _ in halves], 1)
    innovation = jnp.concatenate([jnp.broadcast_to(inno, (16, WIDTH)) for _, _, _, inno in halves], 1)
    rows = jnp.concatenate([deviation, innovation.astype(BF)], 0)
    weighted = []
    for row_distances in distances:
        parts = []
        for (dev, _, weight, _), row_distance in zip(halves, row_distances):
            far = jnp.maximum(row_distance(half_row), column_distance).astype(F32)
            factor = weight * (1.0 - far / (RADIUS + 1.0))
            parts.append((dev.astype(F32) * factor).astype(BF))
        weighted.append(jnp.concatenate(parts, 1))
    weighted = jnp.concatenate(weighted, 0)
    return deviation, lax.dot_general(rows, weighted, (((1,), (1,)), ((), ())), preferred_element_type=F32)


INSIDE = (jnp.zeros_like, jnp.zeros_like)
OUTSIDE = (lambda r: r + 1, lambda r: RADIUS - r)


def interior(halves, deviation):
    lane = lax.broadcasted_iota(jnp.int32, (2 * WIDTH, WIDTH), 0)
    target = lax.broadcasted_iota(jnp.int32, (2 * WIDTH, WIDTH), 1)
    narrow = (lane == (target // PATCH) * REGION + RADIUS + target % PATCH).astype(F32).astype(BF)
    inner = jnp.dot(deviation, narrow, preferred_element_type=F32).astype(BF)
    mean = jnp.broadcast_to(jnp.concatenate([halves[0][1], halves[1][1]], 1), (16, 2 * WIDTH))
    high = mean.astype(BF)
    middle = (mean - high.astype(F32)).astype(BF)
    low = (mean - high.astype(F32) - middle.astype(F32)).astype(BF)
    parts = jnp.dot(jnp.concatenate([high, middle, low], 0), narrow, preferred_element_type=F32)
    return inner, parts[:8] + (parts[16:24] + parts[32:40])


def own_kernel(patches, me_ref, own_ref, inner_ref, sums_ref, mean_ref):
    halves = halves_of(own_ref, me_ref[0])
    deviation, sums_ref[...] = half_sums(halves, (INSIDE, OUTSIDE)[:patches])
    inner_ref[...], mean_ref[...] = interior(halves, deviation)


def analysis_kernel(patches, me_ref, near_ref, inner_ref, sums_ref, mean_ref, out_ref):
    count = near_ref.shape[0]
    members = count * LOCAL
    halves = halves_of(near_ref, me_ref[0])
    deviation, sums = half_sums(halves, (OUTSIDE, INSIDE)[:patches])
    both = sums_ref[...] + sums
    each = range(patches)
    inner, mean = [inner_ref[...]], [mean_ref[...]]
    if patches == 2:
        near_inner, near_mean = interior(halves, deviation)
        inner.append(near_inner)
        mean.append(near_mean)
    row = lax.broadcasted_iota(jnp.int32, (members, members), 0)
    col = lax.broadcasted_iota(jnp.int32, (members, members), 1)
    diagonal = jnp.where(row == col, members - 1.0, 0.0)

    def mul(a, b):
        return jnp.dot(a.astype(BF), b.astype(BF), preferred_element_type=F32)

    def with_line(a, line):
        return jnp.concatenate([a.astype(BF), line.astype(BF)], 0)

    system = [both[:members, i * members : (i + 1) * members] + diagonal for i in each]
    line = [both[members:, i * members : (i + 1) * members] for i in each]
    system_b = [system[i].astype(BF) for i in each]
    first = [mul(with_line(system_b[i], line[i]), system_b[i]) for i in each]
    system_x = [mul(system_b[i], inner[i]) for i in each]
    scale = [jnp.sqrt(jnp.sum(system[i] * system[i])) for i in each]
    inverse = [1.0 / scale[i] for i in each]
    x1 = [1.5 * inner[i].astype(F32) - (0.5 * inverse[i]) * system_x[i] for i in each]
    line1 = [1.5 * line[i] - (0.5 * inverse[i]) * first[i][members:] for i in each]
    y1 = [inverse[i] * (1.5 * system[i] - (0.5 * inverse[i]) * first[i][:members]) for i in each]
    p1 = [1.5 * y1[i] - (0.5 * inverse[i]) * mul(y1[i], system_b[i]) for i in each]
    p1b = [p1[i].astype(BF) for i in each]
    second = [mul(with_line(p1b[i], line1[i]), p1b[i]) for i in each]
    x2 = [1.5 * x1[i] - 0.5 * mul(p1b[i], x1[i]) for i in each]
    line2 = [1.5 * line1[i] - 0.5 * second[i][members:] for i in each]
    q1 = [1.5 * p1[i] - 0.5 * second[i][:members] for i in each]
    p2b = [(1.5 * q1[i] - 0.5 * mul(q1[i], p1b[i])).astype(BF) for i in each]
    factor = [1.0 / jnp.sqrt(scale[i]) for i in each]
    x3 = [(1.5 * x2[i] - 0.5 * mul(p2b[i], x2[i])) * factor[i] for i in each]
    line3 = [(1.5 * line2[i] - 0.5 * mul(line2[i], p2b[i])) * factor[i] for i in each]
    line_b = [line3[i].astype(BF) for i in each]
    shift = [mul(with_line(line_b[i], line3[i] - line_b[i].astype(F32)), x3[i]) for i in each]
    root = jnp.sqrt(jnp.full((1, 1), members - 1.0, F32))
    for i in each:
        total = shift[i][:1] + shift[i][16:17] + mean[i][:1]
        result = (root * x3[i] + total).astype(BF)
        for s, place in enumerate(GOING):
            out_ref[position(place, BACK), i * LOCAL : (i + 1) * LOCAL] = result[s * LOCAL : (s + 1) * LOCAL]


def forecast_kernel(in_ref, out_ref):
    def unpacked(start):
        blocks = [in_ref[position(p, BACK), start : start + LOCAL] for p in range(in_ref.shape[0])]
        return [row.astype(F32) for row in swap_blocks(blocks, PATCH)]

    def by_field(rows):
        half = BAND // 2
        return [
            [rows[h * FIELDS * half + field * half + r] for h in range(2) for r in range(half)]
            for field in range(FIELDS)
        ]

    own, near = by_field(unpacked(0)), by_field(unpacked(LOCAL))
    fields = [n[BAND - FSTEPS :] + o + n[:FSTEPS] for o, n in zip(own, near)]
    done = forecast_rows(*fields)
    for field in range(FIELDS):
        for r in range(BAND):
            out_ref[pl.ds(field * BAND + r, LOCAL, stride=FIELDS * BAND), :] = done[field][r]


def from_next(value):
    count = lax.axis_size("rows")
    return lax.ppermute(value, "rows", [((i + 1) % count, i) for i in range(count)])


def from_previous(value):
    count = lax.axis_size("rows")
    return lax.ppermute(value, "rows", [(i, (i + 1) % count) for i in range(count)])


def near_rows(value, join):
    if lax.axis_size("rows") == 2:
        return from_next(value)
    return join(from_next(value), from_previous(value))


def join_grid(after, before):
    return jnp.concatenate([after[:, :, : BAND // 2], before[:, :, BAND // 2 :]], 2)


def join_region(after, before):
    after, before = (x.reshape(x.shape[0], -1, 4, WIDTH) for x in (after, before))
    near = jnp.concatenate([after[:, :4], before[:, 4:8], after[:, 8:9], before[:, 9:]], 1)
    return near.reshape(near.shape[0], -1, WIDTH)


def join_inner(after, before):
    return jnp.concatenate([after[..., : WIDTH // 2], before[..., WIDTH // 2 :]], 2)


def exchange(value, order):
    return lax.all_to_all(value, "mem", split_axis=0, concat_axis=0, axis_index_groups=[list(order)], tiled=True)


def call(kernel, name, out_shape, *args, flops=0):
    spaces = [pltpu.SMEM if arg.shape == (1,) else pltpu.VMEM for arg in args]
    moved = sum(x.size * x.dtype.itemsize for x in [*args, *jax.tree.leaves(out_shape)])
    return pl.pallas_call(
        kernel,
        out_shape=out_shape,
        in_specs=[pl.BlockSpec(memory_space=space) for space in spaces],
        out_specs=jax.tree.map(lambda _: pl.BlockSpec(memory_space=pltpu.VMEM), out_shape),
        compiler_params=pltpu.CompilerParams(vmem_limit_bytes=16 * 2**20),
        cost_estimate=pl.CostEstimate(flops=flops, bytes_accessed=moved, transcendentals=0),
        name=name,
    )(*args)


def local(sample_collection, obs_values, obs_inverse_variance, obs_mask):
    count = lax.axis_size("mem")
    shape = sample_collection.shape
    assert shape == (LOCAL, FIELDS, BAND, WIDTH) and count == PLACES
    me = lax.axis_index("mem").astype(jnp.int32).reshape(1)
    near = near_rows(sample_collection, join_grid)
    rows = jnp.transpose(sample_collection.reshape(LOCAL, FIELDS * BAND, WIDTH), (1, 0, 2))
    region_shape = jax.ShapeDtypeStruct((count, 2 * LOCAL + 8, WIDTH), BF)
    observations = (obs_values, obs_inverse_variance, obs_mask)
    sending = call(pack_kernel, "forecast_pack", region_shape, rows, near.reshape(-1, WIDTH), *observations)
    region = exchange(sending, GOING)
    members, points = count * LOCAL, 2 * WIDTH
    patches = 2 if lax.axis_size("rows") == 2 else 1
    own_shapes = [
        jax.ShapeDtypeStruct((members, WIDTH), BF),
        jax.ShapeDtypeStruct((members + 16, patches * members), F32),
        jax.ShapeDtypeStruct((8, WIDTH), F32),
    ]
    flops = 2 * members * members * points
    region_near = near_rows(region, join_region)
    own = call(functools.partial(own_kernel, patches), "own_half", own_shapes, me, region, flops=flops)
    analysed_shape = jax.ShapeDtypeStruct((count, patches * LOCAL, WIDTH), BF)
    kernel = functools.partial(analysis_kernel, patches)
    analysed = call(kernel, "analysis", analysed_shape, me, region_near, *own, flops=8 * flops)
    inner = exchange(analysed, BACK)
    if patches == 1:
        inner = jnp.concatenate([inner, near_rows(inner, join_inner)], 1)
    out_shape = jax.ShapeDtypeStruct((LOCAL * FIELDS * BAND, WIDTH), F32)
    cycled = call(forecast_kernel, "unpack_forecast", out_shape, inner)
    return cycled.reshape(shape)


def solution(mesh):
    return jax.shard_map(
        local,
        mesh=mesh,
        in_specs=(
            P("mem", None, "rows", None),
            P(None, "rows", "mem"),
            P(None, "rows", "mem"),
            P(None, "rows", "mem"),
        ),
        out_specs=P("mem", None, "rows", None),
        check_vma=False,
    )
```

```python
import functools

import jax
import jax.numpy as jnp
from jax import lax
from jax.experimental import pallas as pl
from jax.experimental.pallas import tpu as pltpu
from jax.sharding import PartitionSpec as P

PATCH = 8
RADIUS = 4
FSTEPS = 4
CADV = 0.05

LOCAL = 16
FIELDS = 2
BAND = 8
WIDTH = 128
PLACES = WIDTH // PATCH
REGION = PATCH + 2 * RADIUS

BF = jnp.bfloat16
F32 = jnp.float32


def position(place):
    low, high = place & 3, place >> 2
    return PLACES - 1 - (low * 4 + (high & 1) * 2 + (high >> 1))


def advance(u_rows, v_rows, i):
    cu, cv = CADV * u_rows[i], CADV * v_rows[i]
    stepped = []
    for rows in (u_rows, v_rows):
        along_x = pltpu.roll(rows[i], WIDTH - 1, 1) - pltpu.roll(rows[i], 1, 1)
        along_y = rows[i + 1] - rows[i - 1]
        stepped.append(rows[i] - (cu * along_x + cv * along_y))
    return stepped


def forecast_rows(u_rows, v_rows, known=None):
    for step in range(1, FSTEPS + 1):
        stepped = []
        for i in range(1, len(u_rows) - 1):
            row = i - 1 + step - FSTEPS
            given = known(step, row) if known is not None and step <= row < BAND - step else None
            stepped.append(given if given is not None else advance(u_rows, v_rows, i))
        u_rows, v_rows = [u for u, _ in stepped], [v for _, v in stepped]
    return u_rows, v_rows


def inner_steps():
    return [(step, row) for step in range(1, FSTEPS) for row in range(step, BAND - step)]


def swap_blocks(parts, size):
    count = len(parts)
    lane = lax.broadcasted_iota(jnp.int32, parts[0].shape, 1) // size
    stride = 1
    while stride < count:
        upper = (lane & stride) != 0
        new = list(parts)
        for j in range(count):
            if j & stride == 0:
                a, b = parts[j], parts[j + stride]
                new[j] = jnp.where(upper, pltpu.roll(b, stride * size, 1), a)
                new[j + stride] = jnp.where(upper, b, pltpu.roll(a, WIDTH - stride * size, 1))
        parts = new
        stride *= 2
    return parts


def observation_rows(values_ref, inverse_ref, mask_ref):
    points = FIELDS * BAND
    weight = (mask_ref[...].astype(F32) * inverse_ref[...]).astype(BF).astype(F32).reshape(points, PATCH)
    values = values_ref[...].reshape(points, PATCH)
    high = values.astype(BF).astype(F32)
    middle = (values - high).astype(BF).astype(F32)
    low = values - high - middle
    rows = jnp.concatenate([weight, high, middle, low], 0).astype(BF)
    source = lax.broadcasted_iota(jnp.int32, (PATCH, WIDTH), 0)
    lane = lax.broadcasted_iota(jnp.int32, (PATCH, WIDTH), 1)
    spread = (lane % PATCH == source).astype(F32).astype(BF)
    wide = jnp.dot(rows, spread, preferred_element_type=F32)
    row = lax.broadcasted_iota(jnp.int32, wide.shape, 0)
    lane = lax.broadcasted_iota(jnp.int32, wide.shape, 1)
    part, field, y = row // points, (row % points) // BAND, row % BAND
    place = (field * (BAND // 2) + y % (BAND // 2)) * 2 + part % 2
    wide = jnp.where(lane // PATCH == place, wide, 0.0).astype(BF)
    target = lax.broadcasted_iota(jnp.int32, (8, 4 * points), 0)
    row = lax.broadcasted_iota(jnp.int32, (8, 4 * points), 1)
    wanted = ((row % BAND) // (BAND // 2)) * 4 + 2 + row // (2 * points)
    gather = (target == wanted).astype(F32).astype(BF)
    return jnp.dot(gather, wide, preferred_element_type=F32)


def inner_kernel(rows_ref, values_ref, inverse_ref, mask_ref, out_ref, obs_ref):
    obs_ref[...] = observation_rows(values_ref, inverse_ref, mask_ref)
    u_rows, v_rows = ([rows_ref[field * BAND + r] for r in range(BAND)] for field in range(FIELDS))
    kept = 0
    for _ in range(1, FSTEPS):
        stepped = [advance(u_rows, v_rows, i) for i in range(1, len(u_rows) - 1)]
        u_rows, v_rows = [u for u, _ in stepped], [v for _, v in stepped]
        for row in stepped:
            for value in row:
                out_ref[kept] = value
                kept += 1


def pack_kernel(rows_ref, inner_ref, obs_ref, near_ref, out_ref):
    points = FIELDS * BAND
    places = inner_steps()

    def known(step, row):
        first = FIELDS * places.index((step, row))
        return [inner_ref[first + field] for field in range(FIELDS)]

    def near(field, index):
        return near_ref[pl.ds(field * BAND + index, LOCAL, stride=points), :]

    fields = []
    for field in range(FIELDS):
        before = [near(field, r) for r in range(BAND - FSTEPS, BAND)]
        own = [rows_ref[field * BAND + r] for r in range(BAND)]
        after = [near(field, r) for r in range(FSTEPS)]
        fields.append(before + own + after)
    done = forecast_rows(*fields, known)
    half_rows = BAND // 2
    index = lax.broadcasted_iota(jnp.int32, (8, WIDTH), 0)
    values, means = [], [jnp.zeros((8, WIDTH), F32)] * (FIELDS * half_rows)
    for half in range(2):
        for j in range(FIELDS * half_rows):
            value = done[j // half_rows][half * half_rows + j % half_rows]
            mean = jnp.sum(value, 0, keepdims=True) * (1.0 / LOCAL)
            high = mean.astype(BF).astype(F32)
            means[j] = jnp.where(index == 4 * half, high, jnp.where(index == 4 * half + 1, mean - high, means[j]))
            values.append(value - mean)
    rows = jnp.concatenate(values + means, 0).astype(BF)
    column = lax.broadcasted_iota(jnp.int32, (WIDTH, 2 * WIDTH), 0)
    lane = lax.broadcasted_iota(jnp.int32, (WIDTH, 2 * WIDTH), 1)
    wanted = ((lane // REGION) * PATCH + lane % REGION + (WIDTH - RADIUS)) % WIDTH
    widen = (column == wanted).astype(F32).astype(BF)
    wide = jnp.dot(rows, widen, preferred_element_type=F32)
    obs = obs_ref[...]
    start = len(values) * LOCAL
    is_mean = index & 2 == 0
    means = []
    for j in range(8):
        part = wide[start + j * 8 : start + j * 8 + 8]
        means.append(jnp.where(is_mean, part[:, :WIDTH], pltpu.roll(part[:, WIDTH:], 2, 0)))
    means = swap_blocks(means, REGION)
    for side in range(2):
        for half in range(2):
            parts = [
                wide[(half * 8 + j) * LOCAL : (half * 8 + j + 1) * LOCAL, side * WIDTH : (side + 1) * WIDTH].astype(BF)
                for j in range(8)
            ]
            parts = swap_blocks(parts, REGION)
            for i in range(8):
                out_ref[position(side * 8 + i), half * LOCAL : (half + 1) * LOCAL] = parts[i]
        for i in range(8):
            mean = means[i] if side == 0 else pltpu.roll(means[i], 6, 0)
            out_ref[position(side * 8 + i), 2 * LOCAL :] = jnp.where(is_mean, mean, obs).astype(BF)


def halves_of(ref, me):
    count = ref.shape[0]
    tails = [ref[s, 2 * LOCAL :].astype(F32) for s in range(count)]

    def tail_of(device):
        return ref[position(device), 2 * LOCAL :].astype(F32)

    lane = lax.broadcasted_iota(jnp.int32, (8, WIDTH), 1) % REGION
    left = tail_of(lax.rem(me + count - 1, count))
    own = tail_of(me)
    right = tail_of(lax.rem(me + 1, count))

    def seen(offset):
        return jnp.where(
            lane < RADIUS,
            pltpu.roll(left, (WIDTH + RADIUS - PATCH - offset) % WIDTH, 1),
            jnp.where(
                lane < RADIUS + PATCH,
                pltpu.roll(own, (WIDTH + RADIUS - offset) % WIDTH, 1),
                pltpu.roll(right, (WIDTH + RADIUS + PATCH - offset) % WIDTH, 1),
            ),
        )

    first, second = seen(0), seen(PATCH)
    result = []
    for half in range(2):
        base = half * 4
        means = [t[base : base + 1] + t[base + 1 : base + 2] for t in tails]
        mean = functools.reduce(jnp.add, means) * (1.0 / count)
        deviation = []
        for s, own_mean in enumerate(means):
            value = ref[s, half * LOCAL : (half + 1) * LOCAL].astype(F32)
            deviation.append((value + (own_mean - mean)).astype(BF))
        weight = first[base + 2 : base + 3]
        obs = second[base + 2 : base + 3] + first[base + 3 : base + 4] + second[base + 3 : base + 4]
        innovation = (obs - mean).astype(BF).astype(F32)
        result.append((jnp.concatenate(deviation, 0), mean, weight, innovation))
    return result


def half_sums(halves, distances):
    lane = lax.broadcasted_iota(jnp.int32, (1, WIDTH), 1)
    region_column = lane % REGION
    half_row = (lane // REGION) % (BAND // 2)
    column_distance = jnp.maximum(
        jnp.maximum(RADIUS - region_column, region_column - (RADIUS + PATCH - 1)), 0
    )
    deviation = jnp.concatenate([dev for dev, _, _, _ in halves], 1)
    innovation = jnp.concatenate([jnp.broadcast_to(inno, (16, WIDTH)) for _, _, _, inno in halves], 1)
    rows = jnp.concatenate([deviation, innovation.astype(BF)], 0)
    weighted = []
    for row_distances in distances:
        parts = []
        for (dev, _, weight, _), row_distance in zip(halves, row_distances):
            far = jnp.maximum(row_distance(half_row), column_distance).astype(F32)
            factor = weight * (1.0 - far / (RADIUS + 1.0))
            parts.append((dev.astype(F32) * factor).astype(BF))
        weighted.append(jnp.concatenate(parts, 1))
    weighted = jnp.concatenate(weighted, 0)
    return deviation, lax.dot_general(rows, weighted, (((1,), (1,)), ((), ())), preferred_element_type=F32)


INSIDE = (jnp.zeros_like, jnp.zeros_like)
OUTSIDE = (lambda r: r + 1, lambda r: RADIUS - r)


def interior(halves, deviation):
    lane = lax.broadcasted_iota(jnp.int32, (2 * WIDTH, WIDTH), 0)
    target = lax.broadcasted_iota(jnp.int32, (2 * WIDTH, WIDTH), 1)
    narrow = (lane == (target // PATCH) * REGION + RADIUS + target % PATCH).astype(F32).astype(BF)
    inner = jnp.dot(deviation, narrow, preferred_element_type=F32).astype(BF)
    mean = jnp.broadcast_to(jnp.concatenate([halves[0][1], halves[1][1]], 1), (16, 2 * WIDTH))
    high = mean.astype(BF)
    middle = (mean - high.astype(F32)).astype(BF)
    low = (mean - high.astype(F32) - middle.astype(F32)).astype(BF)
    parts = jnp.dot(jnp.concatenate([high, middle, low], 0), narrow, preferred_element_type=F32)
    return inner, parts[:8] + (parts[16:24] + parts[32:40])


def own_kernel(patches, me_ref, own_ref, inner_ref, sums_ref, mean_ref):
    halves = halves_of(own_ref, me_ref[0])
    deviation, sums_ref[...] = half_sums(halves, (INSIDE, OUTSIDE)[:patches])
    inner_ref[...], mean_ref[...] = interior(halves, deviation)


def analysis_kernel(patches, me_ref, near_ref, inner_ref, sums_ref, mean_ref, out_ref):
    count = near_ref.shape[0]
    members = count * LOCAL
    halves = halves_of(near_ref, me_ref[0])
    deviation, sums = half_sums(halves, (OUTSIDE, INSIDE)[:patches])
    both = sums_ref[...] + sums
    each = range(patches)
    inner, mean = [inner_ref[...]], [mean_ref[...]]
    if patches == 2:
        near_inner, near_mean = interior(halves, deviation)
        inner.append(near_inner)
        mean.append(near_mean)
    row = lax.broadcasted_iota(jnp.int32, (members, members), 0)
    col = lax.broadcasted_iota(jnp.int32, (members, members), 1)
    diagonal = jnp.where(row == col, members - 1.0, 0.0)

    def mul(a, b):
        return jnp.dot(a.astype(BF), b.astype(BF), preferred_element_type=F32)

    def with_line(a, line):
        return jnp.concatenate([a.astype(BF), line.astype(BF)], 0)

    system = [both[:members, i * members : (i + 1) * members] + diagonal for i in each]
    line = [both[members:, i * members : (i + 1) * members] for i in each]
    system_b = [system[i].astype(BF) for i in each]
    first = [mul(with_line(system_b[i], line[i]), system_b[i]) for i in each]
    system_x = [mul(system_b[i], inner[i]) for i in each]
    scale = [jnp.sqrt(jnp.sum(system[i] * system[i])) for i in each]
    inverse = [1.0 / scale[i] for i in each]
    x1 = [1.5 * inner[i].astype(F32) - (0.5 * inverse[i]) * system_x[i] for i in each]
    line1 = [1.5 * line[i] - (0.5 * inverse[i]) * first[i][members:] for i in each]
    y1 = [inverse[i] * (1.5 * system[i] - (0.5 * inverse[i]) * first[i][:members]) for i in each]
    p1 = [1.5 * y1[i] - (0.5 * inverse[i]) * mul(y1[i], system_b[i]) for i in each]
    p1b = [p1[i].astype(BF) for i in each]
    second = [mul(with_line(p1b[i], line1[i]), p1b[i]) for i in each]
    x2 = [1.5 * x1[i] - 0.5 * mul(p1b[i], x1[i]) for i in each]
    line2 = [1.5 * line1[i] - 0.5 * second[i][members:] for i in each]
    q1 = [1.5 * p1[i] - 0.5 * second[i][:members] for i in each]
    p2b = [(1.5 * q1[i] - 0.5 * mul(q1[i], p1b[i])).astype(BF) for i in each]
    factor = [1.0 / jnp.sqrt(scale[i]) for i in each]
    x3 = [(1.5 * x2[i] - 0.5 * mul(p2b[i], x2[i])) * factor[i] for i in each]
    line3 = [(1.5 * line2[i] - 0.5 * mul(line2[i], p2b[i])) * factor[i] for i in each]
    line_b = [line3[i].astype(BF) for i in each]
    shift = [mul(with_line(line_b[i], line3[i] - line_b[i].astype(F32)), x3[i]) for i in each]
    root = jnp.sqrt(jnp.full((1, 1), members - 1.0, F32))
    for i in each:
        total = shift[i][:1] + shift[i][16:17] + mean[i][:1]
        result = (root * x3[i] + total).astype(BF)
        for s in range(count):
            out_ref[s, i * LOCAL : (i + 1) * LOCAL] = result[s * LOCAL : (s + 1) * LOCAL]


def forecast_kernel(in_ref, out_ref):
    def unpacked(start):
        blocks = [in_ref[position(p), start : start + LOCAL] for p in range(in_ref.shape[0])]
        return [row.astype(F32) for row in swap_blocks(blocks, PATCH)]

    def by_field(rows):
        half = BAND // 2
        return [
            [rows[h * FIELDS * half + field * half + r] for h in range(2) for r in range(half)]
            for field in range(FIELDS)
        ]

    own, near = by_field(unpacked(0)), by_field(unpacked(LOCAL))
    fields = [n[BAND - FSTEPS :] + o + n[:FSTEPS] for o, n in zip(own, near)]
    done = forecast_rows(*fields)
    for field in range(FIELDS):
        for r in range(BAND):
            out_ref[pl.ds(field * BAND + r, LOCAL, stride=FIELDS * BAND), :] = done[field][r]


def from_next(value):
    count = lax.axis_size("rows")
    return lax.ppermute(value, "rows", [((i + 1) % count, i) for i in range(count)])


def from_previous(value):
    count = lax.axis_size("rows")
    return lax.ppermute(value, "rows", [(i, (i + 1) % count) for i in range(count)])


def near_rows(value, join):
    if lax.axis_size("rows") == 2:
        return from_next(value)
    return join(from_next(value), from_previous(value))


def join_grid(after, before):
    return jnp.concatenate([after[:, :, : BAND // 2], before[:, :, BAND // 2 :]], 2)


def join_region(after, before):
    after, before = (x.reshape(x.shape[0], -1, 4, WIDTH) for x in (after, before))
    near = jnp.concatenate([after[:, :4], before[:, 4:8], after[:, 8:9], before[:, 9:]], 1)
    return near.reshape(near.shape[0], -1, WIDTH)


def join_inner(after, before):
    return jnp.concatenate([after[..., : WIDTH // 2], before[..., WIDTH // 2 :]], 2)


def exchange(value):
    group = [sorted(range(lax.axis_size("mem")), key=position)]
    return lax.all_to_all(value, "mem", split_axis=0, concat_axis=0, axis_index_groups=group, tiled=True)


def call(kernel, name, out_shape, *args, flops=0):
    spaces = [pltpu.SMEM if arg.shape == (1,) else pltpu.VMEM for arg in args]
    moved = sum(x.size * x.dtype.itemsize for x in [*args, *jax.tree.leaves(out_shape)])
    return pl.pallas_call(
        kernel,
        out_shape=out_shape,
        in_specs=[pl.BlockSpec(memory_space=space) for space in spaces],
        out_specs=jax.tree.map(lambda _: pl.BlockSpec(memory_space=pltpu.VMEM), out_shape),
        compiler_params=pltpu.CompilerParams(vmem_limit_bytes=16 * 2**20),
        cost_estimate=pl.CostEstimate(flops=flops, bytes_accessed=moved, transcendentals=0),
        name=name,
    )(*args)


def local(sample_collection, obs_values, obs_inverse_variance, obs_mask):
    count = lax.axis_size("mem")
    shape = sample_collection.shape
    assert shape == (LOCAL, FIELDS, BAND, WIDTH) and count == PLACES
    me = lax.axis_index("mem").astype(jnp.int32).reshape(1)
    near = near_rows(sample_collection, join_grid)
    rows = jnp.transpose(sample_collection.reshape(LOCAL, FIELDS * BAND, WIDTH), (1, 0, 2))
    region_shape = jax.ShapeDtypeStruct((count, 2 * LOCAL + 8, WIDTH), BF)
    kept = FIELDS * len(inner_steps())
    inner_shapes = [jax.ShapeDtypeStruct((kept, LOCAL, WIDTH), F32), jax.ShapeDtypeStruct((8, WIDTH), F32)]
    inner = call(inner_kernel, "inner_rows", inner_shapes, rows, obs_values, obs_inverse_variance, obs_mask)
    region = exchange(call(pack_kernel, "forecast_pack", region_shape, rows, *inner, near.reshape(-1, WIDTH)))
    members, points = count * LOCAL, 2 * WIDTH
    patches = 2 if lax.axis_size("rows") == 2 else 1
    own_shapes = [
        jax.ShapeDtypeStruct((members, WIDTH), BF),
        jax.ShapeDtypeStruct((members + 16, patches * members), F32),
        jax.ShapeDtypeStruct((8, WIDTH), F32),
    ]
    flops = 2 * members * members * points
    region_near = near_rows(region, join_region)
    own = call(functools.partial(own_kernel, patches), "own_half", own_shapes, me, region, flops=flops)
    analysed_shape = jax.ShapeDtypeStruct((count, patches * LOCAL, WIDTH), BF)
    kernel = functools.partial(analysis_kernel, patches)
    inner = exchange(call(kernel, "analysis", analysed_shape, me, region_near, *own, flops=8 * flops))
    if patches == 1:
        inner = jnp.concatenate([inner, near_rows(inner, join_inner)], 1)
    out_shape = jax.ShapeDtypeStruct((LOCAL * FIELDS * BAND, WIDTH), F32)
    cycled = call(forecast_kernel, "unpack_forecast", out_shape, inner)
    return cycled.reshape(shape)


def solution(mesh):
    return jax.shard_map(
        local,
        mesh=mesh,
        in_specs=(
            P("mem", None, "rows", None),
            P(None, "rows", "mem"),
            P(None, "rows", "mem"),
            P(None, "rows", "mem"),
        ),
        out_specs=P("mem", None, "rows", None),
        check_vma=False,
    )
```

```python
import functools

import jax
import jax.numpy as jnp
from jax import lax
from jax.experimental import pallas as pl
from jax.experimental.pallas import tpu as pltpu
from jax.sharding import PartitionSpec as P

PATCH = 8
RADIUS = 4
FSTEPS = 4
CADV = 0.05

LOCAL = 16
FIELDS = 2
BAND = 8
WIDTH = 128
PLACES = WIDTH // PATCH
REGION = PATCH + 2 * RADIUS

BF = jnp.bfloat16
F32 = jnp.float32


def position(place):
    low, high = place & 3, place >> 2
    return PLACES - 1 - (low * 4 + (high & 1) * 2 + (high >> 1))


def advance(u_rows, v_rows, i):
    cu, cv = CADV * u_rows[i], CADV * v_rows[i]
    stepped = []
    for rows in (u_rows, v_rows):
        along_x = pltpu.roll(rows[i], WIDTH - 1, 1) - pltpu.roll(rows[i], 1, 1)
        along_y = rows[i + 1] - rows[i - 1]
        stepped.append(rows[i] - (cu * along_x + cv * along_y))
    return stepped


def forecast_rows(u_rows, v_rows, known=None):
    for step in range(1, FSTEPS + 1):
        stepped = []
        for i in range(1, len(u_rows) - 1):
            row = i - 1 + step - FSTEPS
            given = known(step, row) if known is not None and step <= row < BAND - step else None
            stepped.append(given if given is not None else advance(u_rows, v_rows, i))
        u_rows, v_rows = [u for u, _ in stepped], [v for _, v in stepped]
    return u_rows, v_rows


def inner_steps():
    return [(step, row) for step in range(1, FSTEPS) for row in range(step, BAND - step)]


def swap_blocks(parts, size):
    count = len(parts)
    lane = lax.broadcasted_iota(jnp.int32, parts[0].shape, 1) // size
    stride = 1
    while stride < count:
        upper = (lane & stride) != 0
        new = list(parts)
        for j in range(count):
            if j & stride == 0:
                a, b = parts[j], parts[j + stride]
                new[j] = jnp.where(upper, pltpu.roll(b, stride * size, 1), a)
                new[j + stride] = jnp.where(upper, b, pltpu.roll(a, WIDTH - stride * size, 1))
        parts = new
        stride *= 2
    return parts


def observation_rows(values_ref, inverse_ref, mask_ref):
    points = FIELDS * BAND
    weight = (mask_ref[...].astype(F32) * inverse_ref[...]).astype(BF).astype(F32).reshape(points, PATCH)
    values = values_ref[...].reshape(points, PATCH)
    high = values.astype(BF).astype(F32)
    middle = (values - high).astype(BF).astype(F32)
    low = values - high - middle
    rows = jnp.concatenate([weight, high, middle, low], 0).astype(BF)
    source = lax.broadcasted_iota(jnp.int32, (PATCH, WIDTH), 0)
    lane = lax.broadcasted_iota(jnp.int32, (PATCH, WIDTH), 1)
    spread = (lane % PATCH == source).astype(F32).astype(BF)
    wide = jnp.dot(rows, spread, preferred_element_type=F32)
    row = lax.broadcasted_iota(jnp.int32, wide.shape, 0)
    lane = lax.broadcasted_iota(jnp.int32, wide.shape, 1)
    part, field, y = row // points, (row % points) // BAND, row % BAND
    place = (field * (BAND // 2) + y % (BAND // 2)) * 2 + part % 2
    wide = jnp.where(lane // PATCH == place, wide, 0.0).astype(BF)
    target = lax.broadcasted_iota(jnp.int32, (8, 4 * points), 0)
    row = lax.broadcasted_iota(jnp.int32, (8, 4 * points), 1)
    wanted = ((row % BAND) // (BAND // 2)) * 4 + 2 + row // (2 * points)
    gather = (target == wanted).astype(F32).astype(BF)
    return jnp.dot(gather, wide, preferred_element_type=F32)


def advance_inner(u_rows, v_rows, out_ref):
    kept = 0
    for _ in range(1, FSTEPS):
        stepped = [advance(u_rows, v_rows, i) for i in range(1, len(u_rows) - 1)]
        u_rows, v_rows = [u for u, _ in stepped], [v for _, v in stepped]
        for row in stepped:
            for value in row:
                out_ref[kept] = value
                kept += 1


def kept_rows(inner_ref):
    places = inner_steps()

    def known(step, row):
        first = FIELDS * places.index((step, row))
        return [inner_ref[first + field] for field in range(FIELDS)]

    return known


def inner_kernel(rows_ref, values_ref, inverse_ref, mask_ref, out_ref, obs_ref):
    obs_ref[...] = observation_rows(values_ref, inverse_ref, mask_ref)
    advance_inner(*([rows_ref[field * BAND + r] for r in range(BAND)] for field in range(FIELDS)), out_ref)


def pack_kernel(rows_ref, inner_ref, obs_ref, near_ref, out_ref):
    points = FIELDS * BAND

    def near(field, index):
        return near_ref[pl.ds(field * BAND + index, LOCAL, stride=points), :]

    fields = []
    for field in range(FIELDS):
        before = [near(field, r) for r in range(BAND - FSTEPS, BAND)]
        own = [rows_ref[field * BAND + r] for r in range(BAND)]
        after = [near(field, r) for r in range(FSTEPS)]
        fields.append(before + own + after)
    done = forecast_rows(*fields, kept_rows(inner_ref))
    half_rows = BAND // 2
    index = lax.broadcasted_iota(jnp.int32, (8, WIDTH), 0)
    values, means = [], [jnp.zeros((8, WIDTH), F32)] * (FIELDS * half_rows)
    for half in range(2):
        for j in range(FIELDS * half_rows):
            value = done[j // half_rows][half * half_rows + j % half_rows]
            mean = jnp.sum(value, 0, keepdims=True) * (1.0 / LOCAL)
            high = mean.astype(BF).astype(F32)
            means[j] = jnp.where(index == 4 * half, high, jnp.where(index == 4 * half + 1, mean - high, means[j]))
            values.append(value - mean)
    rows = jnp.concatenate(values + means, 0).astype(BF)
    column = lax.broadcasted_iota(jnp.int32, (WIDTH, 2 * WIDTH), 0)
    lane = lax.broadcasted_iota(jnp.int32, (WIDTH, 2 * WIDTH), 1)
    wanted = ((lane // REGION) * PATCH + lane % REGION + (WIDTH - RADIUS)) % WIDTH
    widen = (column == wanted).astype(F32).astype(BF)
    wide = jnp.dot(rows, widen, preferred_element_type=F32)
    obs = obs_ref[...]
    start = len(values) * LOCAL
    is_mean = index & 2 == 0
    means = []
    for j in range(8):
        part = wide[start + j * 8 : start + j * 8 + 8]
        means.append(jnp.where(is_mean, part[:, :WIDTH], pltpu.roll(part[:, WIDTH:], 2, 0)))
    means = swap_blocks(means, REGION)
    for side in range(2):
        for half in range(2):
            parts = [
                wide[(half * 8 + j) * LOCAL : (half * 8 + j + 1) * LOCAL, side * WIDTH : (side + 1) * WIDTH].astype(BF)
                for j in range(8)
            ]
            parts = swap_blocks(parts, REGION)
            for i in range(8):
                out_ref[position(side * 8 + i), half * LOCAL : (half + 1) * LOCAL] = parts[i]
        for i in range(8):
            mean = means[i] if side == 0 else pltpu.roll(means[i], 6, 0)
            out_ref[position(side * 8 + i), 2 * LOCAL :] = jnp.where(is_mean, mean, obs).astype(BF)


def halves_of(ref, me):
    count = ref.shape[0]
    tails = [ref[s, 2 * LOCAL :].astype(F32) for s in range(count)]

    def tail_of(device):
        return ref[position(device), 2 * LOCAL :].astype(F32)

    lane = lax.broadcasted_iota(jnp.int32, (8, WIDTH), 1) % REGION
    left = tail_of(lax.rem(me + count - 1, count))
    own = tail_of(me)
    right = tail_of(lax.rem(me + 1, count))

    def seen(offset):
        return jnp.where(
            lane < RADIUS,
            pltpu.roll(left, (WIDTH + RADIUS - PATCH - offset) % WIDTH, 1),
            jnp.where(
                lane < RADIUS + PATCH,
                pltpu.roll(own, (WIDTH + RADIUS - offset) % WIDTH, 1),
                pltpu.roll(right, (WIDTH + RADIUS + PATCH - offset) % WIDTH, 1),
            ),
        )

    first, second = seen(0), seen(PATCH)
    result = []
    for half in range(2):
        base = half * 4
        means = [t[base : base + 1] + t[base + 1 : base + 2] for t in tails]
        mean = functools.reduce(jnp.add, means) * (1.0 / count)
        deviation = []
        for s, own_mean in enumerate(means):
            value = ref[s, half * LOCAL : (half + 1) * LOCAL].astype(F32)
            deviation.append((value + (own_mean - mean)).astype(BF))
        weight = first[base + 2 : base + 3]
        obs = second[base + 2 : base + 3] + first[base + 3 : base + 4] + second[base + 3 : base + 4]
        innovation = (obs - mean).astype(BF).astype(F32)
        result.append((jnp.concatenate(deviation, 0), mean, weight, innovation))
    return result


def half_sums(halves, row_distances):
    lane = lax.broadcasted_iota(jnp.int32, (1, WIDTH), 1)
    region_column = lane % REGION
    half_row = (lane // REGION) % (BAND // 2)
    column_distance = jnp.maximum(
        jnp.maximum(RADIUS - region_column, region_column - (RADIUS + PATCH - 1)), 0
    )
    weighted, deviation, innovation = [], [], []
    for (dev, _, weight, inno), row_distance in zip(halves, row_distances):
        far = jnp.maximum(row_distance(half_row), column_distance).astype(F32)
        factor = weight * (1.0 - far / (RADIUS + 1.0))
        weighted.append((dev.astype(F32) * factor).astype(BF))
        deviation.append(dev)
        innovation.append(jnp.broadcast_to(inno, (16, WIDTH)).astype(BF))
    deviation = jnp.concatenate(deviation, 1)
    rows = jnp.concatenate([deviation, jnp.concatenate(innovation, 1)], 0)
    weighted = jnp.concatenate(weighted, 1)
    return deviation, lax.dot_general(rows, weighted, (((1,), (1,)), ((), ())), preferred_element_type=F32)


def own_kernel(me_ref, own_ref, inner_ref, sums_ref, mean_ref):
    halves = halves_of(own_ref, me_ref[0])
    deviation, sums_ref[...] = half_sums(halves, [jnp.zeros_like] * 2)
    lane = lax.broadcasted_iota(jnp.int32, (2 * WIDTH, WIDTH), 0)
    target = lax.broadcasted_iota(jnp.int32, (2 * WIDTH, WIDTH), 1)
    narrow = (lane == (target // PATCH) * REGION + RADIUS + target % PATCH).astype(F32).astype(BF)
    inner_ref[...] = jnp.dot(deviation, narrow, preferred_element_type=F32).astype(BF)
    mean = jnp.broadcast_to(jnp.concatenate([halves[0][1], halves[1][1]], 1), (16, 2 * WIDTH))
    high = mean.astype(BF)
    middle = (mean - high.astype(F32)).astype(BF)
    low = (mean - high.astype(F32) - middle.astype(F32)).astype(BF)
    parts = jnp.dot(jnp.concatenate([high, middle, low], 0), narrow, preferred_element_type=F32)
    mean_ref[...] = parts[:8] + (parts[16:24] + parts[32:40])


def analysis_kernel(me_ref, near_ref, inner_ref, sums_ref, mean_ref, out_ref):
    count = near_ref.shape[0]
    members = count * LOCAL
    halves = halves_of(near_ref, me_ref[0])
    both = sums_ref[...] + half_sums(halves, [lambda r: r + 1, lambda r: RADIUS - r])[1]
    row = lax.broadcasted_iota(jnp.int32, (members, members), 0)
    col = lax.broadcasted_iota(jnp.int32, (members, members), 1)
    system = both[:members] + jnp.where(row == col, members - 1.0, 0.0)
    def mul(a, b):
        return jnp.dot(a.astype(BF), b.astype(BF), preferred_element_type=F32)

    def with_line(a, line):
        return jnp.concatenate([a.astype(BF), line.astype(BF)], 0)

    inner, line = inner_ref[...], both[members:]
    system_b = system.astype(BF)
    first = mul(with_line(system_b, line), system_b)
    system_x = mul(system_b, inner)
    scale = jnp.sqrt(jnp.sum(system * system))
    inverse = 1.0 / scale
    x1 = 1.5 * inner.astype(F32) - (0.5 * inverse) * system_x
    line1 = 1.5 * line - (0.5 * inverse) * first[members:]
    y1 = inverse * (1.5 * system - (0.5 * inverse) * first[:members])
    p1 = 1.5 * y1 - (0.5 * inverse) * mul(y1, system_b)
    p1b = p1.astype(BF)
    second = mul(with_line(p1b, line1), p1b)
    x2 = 1.5 * x1 - 0.5 * mul(p1b, x1)
    line2 = 1.5 * line1 - 0.5 * second[members:]
    q1 = 1.5 * p1 - 0.5 * second[:members]
    p2 = 1.5 * q1 - 0.5 * mul(q1, p1b)
    p2b = p2.astype(BF)
    factor = 1.0 / jnp.sqrt(scale)
    x3 = (1.5 * x2 - 0.5 * mul(p2b, x2)) * factor
    line3 = (1.5 * line2 - 0.5 * mul(line2, p2b)) * factor
    line_b = line3.astype(BF)
    lines = with_line(line_b, line3 - line_b.astype(F32))
    shift = mul(lines, x3)
    shift = shift[:1] + shift[16:17]
    root = jnp.sqrt(jnp.full((1, 1), members - 1.0, F32))
    result = (root * x3 + (shift + mean_ref[:1])).astype(BF)
    for s in range(count):
        out_ref[s] = result[s * LOCAL : (s + 1) * LOCAL]


def unpacked(ref):
    return [row.astype(F32) for row in swap_blocks([ref[position(p)] for p in range(ref.shape[0])], PATCH)]


def by_field(rows):
    half = BAND // 2
    return [[rows[h * FIELDS * half + field * half + r] for h in range(2) for r in range(half)] for field in range(FIELDS)]


def unpack_kernel(in_ref, rows_ref, inner_ref):
    rows = unpacked(in_ref)
    for i, row in enumerate(rows):
        rows_ref[i] = row
    advance_inner(*by_field(rows), inner_ref)


def forecast_kernel(own_ref, inner_ref, near_ref, out_ref):
    own, near = by_field(own_ref), by_field(unpacked(near_ref))
    fields = [n[BAND - FSTEPS :] + o + n[:FSTEPS] for o, n in zip(own, near)]
    done = forecast_rows(*fields, kept_rows(inner_ref))
    for field in range(FIELDS):
        for r in range(BAND):
            out_ref[pl.ds(field * BAND + r, LOCAL, stride=FIELDS * BAND), :] = done[field][r]


def from_next(value):
    count = lax.axis_size("rows")
    return lax.ppermute(value, "rows", [((i + 1) % count, i) for i in range(count)])


def from_previous(value):
    count = lax.axis_size("rows")
    return lax.ppermute(value, "rows", [(i, (i + 1) % count) for i in range(count)])


def near_rows(value, join):
    if lax.axis_size("rows") == 2:
        return from_next(value)
    return join(from_next(value), from_previous(value))


def join_grid(after, before):
    return jnp.concatenate([after[:, :, : BAND // 2], before[:, :, BAND // 2 :]], 2)


def join_region(after, before):
    after, before = (x.reshape(x.shape[0], -1, 4, WIDTH) for x in (after, before))
    near = jnp.concatenate([after[:, :4], before[:, 4:8], after[:, 8:9], before[:, 9:]], 1)
    return near.reshape(near.shape[0], -1, WIDTH)


def join_inner(after, before):
    return jnp.concatenate([after[..., : WIDTH // 2], before[..., WIDTH // 2 :]], 2)


def exchange(value):
    bands = lax.axis_size("rows")
    places = sorted(range(lax.axis_size("mem")), key=position)
    groups = [[place * bands + band for place in places] for band in reversed(range(bands))]
    return lax.all_to_all(value, ("mem", "rows"), split_axis=0, concat_axis=0, axis_index_groups=groups, tiled=True)


def call(kernel, name, out_shape, *args, flops=0):
    spaces = [pltpu.SMEM if arg.shape == (1,) else pltpu.VMEM for arg in args]
    moved = sum(x.size * x.dtype.itemsize for x in [*args, *jax.tree.leaves(out_shape)])
    return pl.pallas_call(
        kernel,
        out_shape=out_shape,
        in_specs=[pl.BlockSpec(memory_space=space) for space in spaces],
        out_specs=jax.tree.map(lambda _: pl.BlockSpec(memory_space=pltpu.VMEM), out_shape),
        compiler_params=pltpu.CompilerParams(vmem_limit_bytes=16 * 2**20),
        cost_estimate=pl.CostEstimate(flops=flops, bytes_accessed=moved, transcendentals=0),
        name=name,
    )(*args)


def local(sample_collection, obs_values, obs_inverse_variance, obs_mask):
    count = lax.axis_size("mem")
    shape = sample_collection.shape
    assert shape == (LOCAL, FIELDS, BAND, WIDTH) and count == PLACES
    me = lax.axis_index("mem").astype(jnp.int32).reshape(1)
    near = near_rows(sample_collection, join_grid)
    rows = jnp.transpose(sample_collection.reshape(LOCAL, FIELDS * BAND, WIDTH), (1, 0, 2))
    region_shape = jax.ShapeDtypeStruct((count, 2 * LOCAL + 8, WIDTH), BF)
    inner_shape = jax.ShapeDtypeStruct((count, LOCAL, WIDTH), BF)
    rows_shape = jax.ShapeDtypeStruct((FIELDS * BAND, LOCAL, WIDTH), F32)
    kept_shape = jax.ShapeDtypeStruct((FIELDS * len(inner_steps()), LOCAL, WIDTH), F32)
    first = [kept_shape, jax.ShapeDtypeStruct((8, WIDTH), F32)]
    kept = call(inner_kernel, "inner_rows", first, rows, obs_values, obs_inverse_variance, obs_mask)
    region = exchange(call(pack_kernel, "forecast_pack", region_shape, rows, *kept, near.reshape(-1, WIDTH)))
    members, points = count * LOCAL, 2 * WIDTH
    own_shapes = [
        jax.ShapeDtypeStruct((members, WIDTH), BF),
        jax.ShapeDtypeStruct((members + 16, members), F32),
        jax.ShapeDtypeStruct((8, WIDTH), F32),
    ]
    flops = 2 * members * members * points
    region_near = near_rows(region, join_region)
    own = call(own_kernel, "own_half", own_shapes, me, region, flops=flops)
    inner = exchange(call(analysis_kernel, "analysis", inner_shape, me, region_near, *own, flops=8 * flops))
    inner_near = near_rows(inner, join_inner)
    own_rows = call(unpack_kernel, "unpack_own", [rows_shape, kept_shape], inner)
    out_shape = jax.ShapeDtypeStruct((LOCAL * FIELDS * BAND, WIDTH), F32)
    cycled = call(forecast_kernel, "unpack_forecast", out_shape, *own_rows, inner_near)
    return cycled.reshape(shape)


def solution(mesh):
    return jax.shard_map(
        local,
        mesh=mesh,
        in_specs=(
            P("mem", None, "rows", None),
            P(None, "rows", "mem"),
            P(None, "rows", "mem"),
            P(None, "rows", "mem"),
        ),
        out_specs=P("mem", None, "rows", None),
        check_vma=False,
    )
```

```python
import functools

import jax
import jax.numpy as jnp
from jax import lax
from jax.experimental import pallas as pl
from jax.experimental.pallas import tpu as pltpu
from jax.sharding import PartitionSpec as P

PATCH = 8
RADIUS = 4
FSTEPS = 4
CADV = 0.05

LOCAL = 16
FIELDS = 2
BAND = 8
WIDTH = 128
PLACES = WIDTH // PATCH
REGION = PATCH + 2 * RADIUS

BF = jnp.bfloat16
F32 = jnp.float32


ORDER = (15, 7, 3, 10, 14, 6, 2, 9, 13, 5, 1, 8, 12, 4, 0, 11)


def position(place):
    if isinstance(place, int):
        return ORDER.index(place)
    return functools.reduce(lambda kept, k: jnp.where(place == ORDER[k], k, kept), range(1, PLACES), 0)


def advance(u_rows, v_rows, i):
    cu, cv = CADV * u_rows[i], CADV * v_rows[i]
    stepped = []
    for rows in (u_rows, v_rows):
        along_x = pltpu.roll(rows[i], WIDTH - 1, 1) - pltpu.roll(rows[i], 1, 1)
        along_y = rows[i + 1] - rows[i - 1]
        stepped.append(rows[i] - (cu * along_x + cv * along_y))
    return stepped


def forecast_rows(u_rows, v_rows, known=None):
    for step in range(1, FSTEPS + 1):
        stepped = []
        for i in range(1, len(u_rows) - 1):
            row = i - 1 + step - FSTEPS
            given = known(step, row) if known is not None and step <= row < BAND - step else None
            stepped.append(given if given is not None else advance(u_rows, v_rows, i))
        u_rows, v_rows = [u for u, _ in stepped], [v for _, v in stepped]
    return u_rows, v_rows


def inner_steps():
    return [(step, row) for step in range(1, FSTEPS) for row in range(step, BAND - step)]


def swap_blocks(parts, size):
    count = len(parts)
    lane = lax.broadcasted_iota(jnp.int32, parts[0].shape, 1) // size
    stride = 1
    while stride < count:
        upper = (lane & stride) != 0
        new = list(parts)
        for j in range(count):
            if j & stride == 0:
                a, b = parts[j], parts[j + stride]
                new[j] = jnp.where(upper, pltpu.roll(b, stride * size, 1), a)
                new[j + stride] = jnp.where(upper, b, pltpu.roll(a, WIDTH - stride * size, 1))
        parts = new
        stride *= 2
    return parts


def observation_rows(values_ref, inverse_ref, mask_ref):
    points = FIELDS * BAND
    weight = (mask_ref[...].astype(F32) * inverse_ref[...]).astype(BF).astype(F32).reshape(points, PATCH)
    values = values_ref[...].reshape(points, PATCH)
    high = values.astype(BF).astype(F32)
    middle = (values - high).astype(BF).astype(F32)
    low = values - high - middle
    rows = jnp.concatenate([weight, high, middle, low], 0).astype(BF)
    source = lax.broadcasted_iota(jnp.int32, (PATCH, WIDTH), 0)
    lane = lax.broadcasted_iota(jnp.int32, (PATCH, WIDTH), 1)
    spread = (lane % PATCH == source).astype(F32).astype(BF)
    wide = jnp.dot(rows, spread, preferred_element_type=F32)
    row = lax.broadcasted_iota(jnp.int32, wide.shape, 0)
    lane = lax.broadcasted_iota(jnp.int32, wide.shape, 1)
    part, field, y = row // points, (row % points) // BAND, row % BAND
    place = (field * (BAND // 2) + y % (BAND // 2)) * 2 + part % 2
    wide = jnp.where(lane // PATCH == place, wide, 0.0).astype(BF)
    target = lax.broadcasted_iota(jnp.int32, (8, 4 * points), 0)
    row = lax.broadcasted_iota(jnp.int32, (8, 4 * points), 1)
    wanted = ((row % BAND) // (BAND // 2)) * 4 + 2 + row // (2 * points)
    gather = (target == wanted).astype(F32).astype(BF)
    return jnp.dot(gather, wide, preferred_element_type=F32)


def advance_inner(u_rows, v_rows, out_ref):
    kept = 0
    for _ in range(1, FSTEPS):
        stepped = [advance(u_rows, v_rows, i) for i in range(1, len(u_rows) - 1)]
        u_rows, v_rows = [u for u, _ in stepped], [v for _, v in stepped]
        for row in stepped:
            for value in row:
                out_ref[kept] = value
                kept += 1


def kept_rows(inner_ref):
    places = inner_steps()

    def known(step, row):
        first = FIELDS * places.index((step, row))
        return [inner_ref[first + field] for field in range(FIELDS)]

    return known


def inner_kernel(rows_ref, values_ref, inverse_ref, mask_ref, out_ref, obs_ref):
    obs_ref[...] = observation_rows(values_ref, inverse_ref, mask_ref)
    advance_inner(*([rows_ref[field * BAND + r] for r in range(BAND)] for field in range(FIELDS)), out_ref)


def pack_kernel(rows_ref, inner_ref, obs_ref, near_ref, out_ref):
    points = FIELDS * BAND

    def near(field, index):
        return near_ref[pl.ds(field * BAND + index, LOCAL, stride=points), :]

    fields = []
    for field in range(FIELDS):
        before = [near(field, r) for r in range(BAND - FSTEPS, BAND)]
        own = [rows_ref[field * BAND + r] for r in range(BAND)]
        after = [near(field, r) for r in range(FSTEPS)]
        fields.append(before + own + after)
    done = forecast_rows(*fields, kept_rows(inner_ref))
    half_rows = BAND // 2
    index = lax.broadcasted_iota(jnp.int32, (8, WIDTH), 0)
    values, means = [], [jnp.zeros((8, WIDTH), F32)] * (FIELDS * half_rows)
    for half in range(2):
        for j in range(FIELDS * half_rows):
            value = done[j // half_rows][half * half_rows + j % half_rows]
            mean = jnp.sum(value, 0, keepdims=True) * (1.0 / LOCAL)
            high = mean.astype(BF).astype(F32)
            means[j] = jnp.where(index == 4 * half, high, jnp.where(index == 4 * half + 1, mean - high, means[j]))
            values.append(value - mean)
    rows = jnp.concatenate(values + means, 0).astype(BF)
    column = lax.broadcasted_iota(jnp.int32, (WIDTH, 2 * WIDTH), 0)
    lane = lax.broadcasted_iota(jnp.int32, (WIDTH, 2 * WIDTH), 1)
    wanted = ((lane // REGION) * PATCH + lane % REGION + (WIDTH - RADIUS)) % WIDTH
    widen = (column == wanted).astype(F32).astype(BF)
    wide = jnp.dot(rows, widen, preferred_element_type=F32)
    obs = obs_ref[...]
    start = len(values) * LOCAL
    is_mean = index & 2 == 0
    means = []
    for j in range(8):
        part = wide[start + j * 8 : start + j * 8 + 8]
        means.append(jnp.where(is_mean, part[:, :WIDTH], pltpu.roll(part[:, WIDTH:], 2, 0)))
    means = swap_blocks(means, REGION)
    for side in range(2):
        for half in range(2):
            parts = [
                wide[(half * 8 + j) * LOCAL : (half * 8 + j + 1) * LOCAL, side * WIDTH : (side + 1) * WIDTH].astype(BF)
                for j in range(8)
            ]
            parts = swap_blocks(parts, REGION)
            for i in range(8):
                out_ref[position(side * 8 + i), half * LOCAL : (half + 1) * LOCAL] = parts[i]
        for i in range(8):
            mean = means[i] if side == 0 else pltpu.roll(means[i], 6, 0)
            out_ref[position(side * 8 + i), 2 * LOCAL :] = jnp.where(is_mean, mean, obs).astype(BF)


def halves_of(ref, me):
    count = ref.shape[0]
    tails = [ref[s, 2 * LOCAL :].astype(F32) for s in range(count)]

    def tail_of(device):
        return ref[position(device), 2 * LOCAL :].astype(F32)

    lane = lax.broadcasted_iota(jnp.int32, (8, WIDTH), 1) % REGION
    left = tail_of(lax.rem(me + count - 1, count))
    own = tail_of(me)
    right = tail_of(lax.rem(me + 1, count))

    def seen(offset):
        return jnp.where(
            lane < RADIUS,
            pltpu.roll(left, (WIDTH + RADIUS - PATCH - offset) % WIDTH, 1),
            jnp.where(
                lane < RADIUS + PATCH,
                pltpu.roll(own, (WIDTH + RADIUS - offset) % WIDTH, 1),
                pltpu.roll(right, (WIDTH + RADIUS + PATCH - offset) % WIDTH, 1),
            ),
        )

    first, second = seen(0), seen(PATCH)
    result = []
    for half in range(2):
        base = half * 4
        means = [t[base : base + 1] + t[base + 1 : base + 2] for t in tails]
        mean = functools.reduce(jnp.add, means) * (1.0 / count)
        deviation = []
        for s, own_mean in enumerate(means):
            value = ref[s, half * LOCAL : (half + 1) * LOCAL].astype(F32)
            deviation.append((value + (own_mean - mean)).astype(BF))
        weight = first[base + 2 : base + 3]
        obs = second[base + 2 : base + 3] + first[base + 3 : base + 4] + second[base + 3 : base + 4]
        innovation = (obs - mean).astype(BF).astype(F32)
        result.append((jnp.concatenate(deviation, 0), mean, weight, innovation))
    return result


def half_sums(halves, row_distances):
    lane = lax.broadcasted_iota(jnp.int32, (1, WIDTH), 1)
    region_column = lane % REGION
    half_row = (lane // REGION) % (BAND // 2)
    column_distance = jnp.maximum(
        jnp.maximum(RADIUS - region_column, region_column - (RADIUS + PATCH - 1)), 0
    )
    weighted, deviation, innovation = [], [], []
    for (dev, _, weight, inno), row_distance in zip(halves, row_distances):
        far = jnp.maximum(row_distance(half_row), column_distance).astype(F32)
        factor = weight * (1.0 - far / (RADIUS + 1.0))
        weighted.append((dev.astype(F32) * factor).astype(BF))
        deviation.append(dev)
        innovation.append(jnp.broadcast_to(inno, (16, WIDTH)).astype(BF))
    deviation = jnp.concatenate(deviation, 1)
    rows = jnp.concatenate([deviation, jnp.concatenate(innovation, 1)], 0)
    weighted = jnp.concatenate(weighted, 1)
    return deviation, lax.dot_general(rows, weighted, (((1,), (1,)), ((), ())), preferred_element_type=F32)


def own_kernel(me_ref, own_ref, inner_ref, sums_ref, mean_ref):
    halves = halves_of(own_ref, me_ref[0])
    deviation, sums_ref[...] = half_sums(halves, [jnp.zeros_like] * 2)
    lane = lax.broadcasted_iota(jnp.int32, (2 * WIDTH, WIDTH), 0)
    target = lax.broadcasted_iota(jnp.int32, (2 * WIDTH, WIDTH), 1)
    narrow = (lane == (target // PATCH) * REGION + RADIUS + target % PATCH).astype(F32).astype(BF)
    inner_ref[...] = jnp.dot(deviation, narrow, preferred_element_type=F32).astype(BF)
    mean = jnp.broadcast_to(jnp.concatenate([halves[0][1], halves[1][1]], 1), (16, 2 * WIDTH))
    high = mean.astype(BF)
    middle = (mean - high.astype(F32)).astype(BF)
    low = (mean - high.astype(F32) - middle.astype(F32)).astype(BF)
    parts = jnp.dot(jnp.concatenate([high, middle, low], 0), narrow, preferred_element_type=F32)
    mean_ref[...] = parts[:8] + (parts[16:24] + parts[32:40])


def analysis_kernel(me_ref, near_ref, inner_ref, sums_ref, mean_ref, out_ref):
    count = near_ref.shape[0]
    members = count * LOCAL
    halves = halves_of(near_ref, me_ref[0])
    both = sums_ref[...] + half_sums(halves, [lambda r: r + 1, lambda r: RADIUS - r])[1]
    row = lax.broadcasted_iota(jnp.int32, (members, members), 0)
    col = lax.broadcasted_iota(jnp.int32, (members, members), 1)
    system = both[:members] + jnp.where(row == col, members - 1.0, 0.0)
    def mul(a, b):
        return jnp.dot(a.astype(BF), b.astype(BF), preferred_element_type=F32)

    def with_line(a, line):
        return jnp.concatenate([a.astype(BF), line.astype(BF)], 0)

    inner, line = inner_ref[...], both[members:]
    system_b = system.astype(BF)
    first = mul(with_line(system_b, line), system_b)
    system_x = mul(system_b, inner)
    scale = jnp.sqrt(jnp.sum(system * system))
    inverse = 1.0 / scale
    x1 = 1.5 * inner.astype(F32) - (0.5 * inverse) * system_x
    line1 = 1.5 * line - (0.5 * inverse) * first[members:]
    y1 = inverse * (1.5 * system - (0.5 * inverse) * first[:members])
    p1 = 1.5 * y1 - (0.5 * inverse) * mul(y1, system_b)
    p1b = p1.astype(BF)
    second = mul(with_line(p1b, line1), p1b)
    x2 = 1.5 * x1 - 0.5 * mul(p1b, x1)
    line2 = 1.5 * line1 - 0.5 * second[members:]
    q1 = 1.5 * p1 - 0.5 * second[:members]
    p2 = 1.5 * q1 - 0.5 * mul(q1, p1b)
    p2b = p2.astype(BF)
    factor = 1.0 / jnp.sqrt(scale)
    x3 = (1.5 * x2 - 0.5 * mul(p2b, x2)) * factor
    line3 = (1.5 * line2 - 0.5 * mul(line2, p2b)) * factor
    line_b = line3.astype(BF)
    lines = with_line(line_b, line3 - line_b.astype(F32))
    shift = mul(lines, x3)
    shift = shift[:1] + shift[16:17]
    root = jnp.sqrt(jnp.full((1, 1), members - 1.0, F32))
    result = (root * x3 + (shift + mean_ref[:1])).astype(BF)
    for s in range(count):
        out_ref[s] = result[s * LOCAL : (s + 1) * LOCAL]


def unpacked(ref):
    return [row.astype(F32) for row in swap_blocks([ref[position(p)] for p in range(ref.shape[0])], PATCH)]


def by_field(rows):
    half = BAND // 2
    return [[rows[h * FIELDS * half + field * half + r] for h in range(2) for r in range(half)] for field in range(FIELDS)]


def unpack_kernel(in_ref, rows_ref, inner_ref):
    rows = unpacked(in_ref)
    for i, row in enumerate(rows):
        rows_ref[i] = row
    advance_inner(*by_field(rows), inner_ref)


def forecast_kernel(own_ref, inner_ref, near_ref, out_ref):
    own, near = by_field(own_ref), by_field(unpacked(near_ref))
    fields = [n[BAND - FSTEPS :] + o + n[:FSTEPS] for o, n in zip(own, near)]
    done = forecast_rows(*fields, kept_rows(inner_ref))
    for field in range(FIELDS):
        for r in range(BAND):
            out_ref[pl.ds(field * BAND + r, LOCAL, stride=FIELDS * BAND), :] = done[field][r]


def from_next(value):
    count = lax.axis_size("rows")
    return lax.ppermute(value, "rows", [((i + 1) % count, i) for i in range(count)])


def from_previous(value):
    count = lax.axis_size("rows")
    return lax.ppermute(value, "rows", [(i, (i + 1) % count) for i in range(count)])


def near_rows(value, join):
    if lax.axis_size("rows") == 2:
        return from_next(value)
    return join(from_next(value), from_previous(value))


def join_grid(after, before):
    return jnp.concatenate([after[:, :, : BAND // 2], before[:, :, BAND // 2 :]], 2)


def join_region(after, before):
    after, before = (x.reshape(x.shape[0], -1, 4, WIDTH) for x in (after, before))
    near = jnp.concatenate([after[:, :4], before[:, 4:8], after[:, 8:9], before[:, 9:]], 1)
    return near.reshape(near.shape[0], -1, WIDTH)


def join_inner(after, before):
    return jnp.concatenate([after[..., : WIDTH // 2], before[..., WIDTH // 2 :]], 2)


def exchange(value):
    return lax.all_to_all(value, "mem", split_axis=0, concat_axis=0, axis_index_groups=[list(ORDER)], tiled=True)


def call(kernel, name, out_shape, *args, flops=0):
    spaces = [pltpu.SMEM if arg.shape == (1,) else pltpu.VMEM for arg in args]
    moved = sum(x.size * x.dtype.itemsize for x in [*args, *jax.tree.leaves(out_shape)])
    return pl.pallas_call(
        kernel,
        out_shape=out_shape,
        in_specs=[pl.BlockSpec(memory_space=space) for space in spaces],
        out_specs=jax.tree.map(lambda _: pl.BlockSpec(memory_space=pltpu.VMEM), out_shape),
        compiler_params=pltpu.CompilerParams(vmem_limit_bytes=16 * 2**20),
        cost_estimate=pl.CostEstimate(flops=flops, bytes_accessed=moved, transcendentals=0),
        name=name,
    )(*args)


def local(sample_collection, obs_values, obs_inverse_variance, obs_mask):
    count = lax.axis_size("mem")
    shape = sample_collection.shape
    assert shape == (LOCAL, FIELDS, BAND, WIDTH) and count == PLACES
    me = lax.axis_index("mem").astype(jnp.int32).reshape(1)
    near = near_rows(sample_collection, join_grid)
    rows = jnp.transpose(sample_collection.reshape(LOCAL, FIELDS * BAND, WIDTH), (1, 0, 2))
    region_shape = jax.ShapeDtypeStruct((count, 2 * LOCAL + 8, WIDTH), BF)
    inner_shape = jax.ShapeDtypeStruct((count, LOCAL, WIDTH), BF)
    rows_shape = jax.ShapeDtypeStruct((FIELDS * BAND, LOCAL, WIDTH), F32)
    kept_shape = jax.ShapeDtypeStruct((FIELDS * len(inner_steps()), LOCAL, WIDTH), F32)
    first = [kept_shape, jax.ShapeDtypeStruct((8, WIDTH), F32)]
    kept = call(inner_kernel, "inner_rows", first, rows, obs_values, obs_inverse_variance, obs_mask)
    region = exchange(call(pack_kernel, "forecast_pack", region_shape, rows, *kept, near.reshape(-1, WIDTH)))
    members, points = count * LOCAL, 2 * WIDTH
    own_shapes = [
        jax.ShapeDtypeStruct((members, WIDTH), BF),
        jax.ShapeDtypeStruct((members + 16, members), F32),
        jax.ShapeDtypeStruct((8, WIDTH), F32),
    ]
    flops = 2 * members * members * points
    region_near = near_rows(region, join_region)
    own = call(own_kernel, "own_half", own_shapes, me, region, flops=flops)
    inner = exchange(call(analysis_kernel, "analysis", inner_shape, me, region_near, *own, flops=8 * flops))
    inner_near = near_rows(inner, join_inner)
    own_rows = call(unpack_kernel, "unpack_own", [rows_shape, kept_shape], inner)
    out_shape = jax.ShapeDtypeStruct((LOCAL * FIELDS * BAND, WIDTH), F32)
    cycled = call(forecast_kernel, "unpack_forecast", out_shape, *own_rows, inner_near)
    return cycled.reshape(shape)


def solution(mesh):
    return jax.shard_map(
        local,
        mesh=mesh,
        in_specs=(
            P("mem", None, "rows", None),
            P(None, "rows", "mem"),
            P(None, "rows", "mem"),
            P(None, "rows", "mem"),
        ),
        out_specs=P("mem", None, "rows", None),
        check_vma=False,
    )
```

```python
import functools

import jax
import jax.numpy as jnp
from jax import lax
from jax.experimental import pallas as pl
from jax.experimental.pallas import tpu as pltpu
from jax.sharding import PartitionSpec as P

PATCH = 8
RADIUS = 4
FSTEPS = 4
CADV = 0.05

LOCAL = 16
FIELDS = 2
BAND = 8
WIDTH = 128
PLACES = WIDTH // PATCH
REGION = PATCH + 2 * RADIUS

BF = jnp.bfloat16
F32 = jnp.float32


ORDER = (15, 11, 7, 3, 14, 10, 6, 2, 13, 9, 5, 1, 12, 8, 4, 0)


def position(place):
    if isinstance(place, int):
        return ORDER.index(place)
    return functools.reduce(lambda kept, k: jnp.where(place == ORDER[k], k, kept), range(1, PLACES), 0)


def advance(u_rows, v_rows, i):
    cu, cv = CADV * u_rows[i], CADV * v_rows[i]
    stepped = []
    for rows in (u_rows, v_rows):
        along_x = pltpu.roll(rows[i], WIDTH - 1, 1) - pltpu.roll(rows[i], 1, 1)
        along_y = rows[i + 1] - rows[i - 1]
        stepped.append(rows[i] - (cu * along_x + cv * along_y))
    return stepped


def forecast_rows(u_rows, v_rows, known=None):
    for step in range(1, FSTEPS + 1):
        stepped = []
        for i in range(1, len(u_rows) - 1):
            row = i - 1 + step - FSTEPS
            given = known(step, row) if known is not None and step <= row < BAND - step else None
            stepped.append(given if given is not None else advance(u_rows, v_rows, i))
        u_rows, v_rows = [u for u, _ in stepped], [v for _, v in stepped]
    return u_rows, v_rows


def inner_steps():
    return [(step, row) for step in range(1, FSTEPS) for row in range(step, BAND - step)]


def swap_blocks(parts, size):
    count = len(parts)
    lane = lax.broadcasted_iota(jnp.int32, parts[0].shape, 1) // size
    stride = 1
    while stride < count:
        upper = (lane & stride) != 0
        new = list(parts)
        for j in range(count):
            if j & stride == 0:
                a, b = parts[j], parts[j + stride]
                new[j] = jnp.where(upper, pltpu.roll(b, stride * size, 1), a)
                new[j + stride] = jnp.where(upper, b, pltpu.roll(a, WIDTH - stride * size, 1))
        parts = new
        stride *= 2
    return parts


def observation_rows(values_ref, inverse_ref, mask_ref):
    points = FIELDS * BAND
    weight = (mask_ref[...].astype(F32) * inverse_ref[...]).astype(BF).astype(F32).reshape(points, PATCH)
    values = values_ref[...].reshape(points, PATCH)
    high = values.astype(BF).astype(F32)
    middle = (values - high).astype(BF).astype(F32)
    low = values - high - middle
    rows = jnp.concatenate([weight, high, middle, low], 0).astype(BF)
    source = lax.broadcasted_iota(jnp.int32, (PATCH, WIDTH), 0)
    lane = lax.broadcasted_iota(jnp.int32, (PATCH, WIDTH), 1)
    spread = (lane % PATCH == source).astype(F32).astype(BF)
    wide = jnp.dot(rows, spread, preferred_element_type=F32)
    row = lax.broadcasted_iota(jnp.int32, wide.shape, 0)
    lane = lax.broadcasted_iota(jnp.int32, wide.shape, 1)
    part, field, y = row // points, (row % points) // BAND, row % BAND
    place = (field * (BAND // 2) + y % (BAND // 2)) * 2 + part % 2
    wide = jnp.where(lane // PATCH == place, wide, 0.0).astype(BF)
    target = lax.broadcasted_iota(jnp.int32, (8, 4 * points), 0)
    row = lax.broadcasted_iota(jnp.int32, (8, 4 * points), 1)
    wanted = ((row % BAND) // (BAND // 2)) * 4 + 2 + row // (2 * points)
    gather = (target == wanted).astype(F32).astype(BF)
    return jnp.dot(gather, wide, preferred_element_type=F32)


def advance_inner(u_rows, v_rows, out_ref):
    kept = 0
    for _ in range(1, FSTEPS):
        stepped = [advance(u_rows, v_rows, i) for i in range(1, len(u_rows) - 1)]
        u_rows, v_rows = [u for u, _ in stepped], [v for _, v in stepped]
        for row in stepped:
            for value in row:
                out_ref[kept] = value
                kept += 1


def kept_rows(inner_ref):
    places = inner_steps()

    def known(step, row):
        first = FIELDS * places.index((step, row))
        return [inner_ref[first + field] for field in range(FIELDS)]

    return known


def inner_kernel(rows_ref, values_ref, inverse_ref, mask_ref, out_ref, obs_ref):
    obs_ref[...] = observation_rows(values_ref, inverse_ref, mask_ref)
    advance_inner(*([rows_ref[field * BAND + r] for r in range(BAND)] for field in range(FIELDS)), out_ref)


def pack_kernel(rows_ref, inner_ref, obs_ref, near_ref, out_ref):
    points = FIELDS * BAND

    def near(field, index):
        return near_ref[pl.ds(field * BAND + index, LOCAL, stride=points), :]

    fields = []
    for field in range(FIELDS):
        before = [near(field, r) for r in range(BAND - FSTEPS, BAND)]
        own = [rows_ref[field * BAND + r] for r in range(BAND)]
        after = [near(field, r) for r in range(FSTEPS)]
        fields.append(before + own + after)
    done = forecast_rows(*fields, kept_rows(inner_ref))
    half_rows = BAND // 2
    index = lax.broadcasted_iota(jnp.int32, (8, WIDTH), 0)
    values, means = [], [jnp.zeros((8, WIDTH), F32)] * (FIELDS * half_rows)
    for half in range(2):
        for j in range(FIELDS * half_rows):
            value = done[j // half_rows][half * half_rows + j % half_rows]
            mean = jnp.sum(value, 0, keepdims=True) * (1.0 / LOCAL)
            high = mean.astype(BF).astype(F32)
            means[j] = jnp.where(index == 4 * half, high, jnp.where(index == 4 * half + 1, mean - high, means[j]))
            values.append(value - mean)
    rows = jnp.concatenate(values + means, 0).astype(BF)
    column = lax.broadcasted_iota(jnp.int32, (WIDTH, 2 * WIDTH), 0)
    lane = lax.broadcasted_iota(jnp.int32, (WIDTH, 2 * WIDTH), 1)
    wanted = ((lane // REGION) * PATCH + lane % REGION + (WIDTH - RADIUS)) % WIDTH
    widen = (column == wanted).astype(F32).astype(BF)
    wide = jnp.dot(rows, widen, preferred_element_type=F32)
    obs = obs_ref[...]
    start = len(values) * LOCAL
    is_mean = index & 2 == 0
    means = []
    for j in range(8):
        part = wide[start + j * 8 : start + j * 8 + 8]
        means.append(jnp.where(is_mean, part[:, :WIDTH], pltpu.roll(part[:, WIDTH:], 2, 0)))
    means = swap_blocks(means, REGION)
    for side in range(2):
        for half in range(2):
            parts = [
                wide[(half * 8 + j) * LOCAL : (half * 8 + j + 1) * LOCAL, side * WIDTH : (side + 1) * WIDTH].astype(BF)
                for j in range(8)
            ]
            parts = swap_blocks(parts, REGION)
            for i in range(8):
                out_ref[position(side * 8 + i), half * LOCAL : (half + 1) * LOCAL] = parts[i]
        for i in range(8):
            mean = means[i] if side == 0 else pltpu.roll(means[i], 6, 0)
            out_ref[position(side * 8 + i), 2 * LOCAL :] = jnp.where(is_mean, mean, obs).astype(BF)


def halves_of(ref, me):
    count = ref.shape[0]
    tails = [ref[s, 2 * LOCAL :].astype(F32) for s in range(count)]

    def tail_of(device):
        return ref[position(device), 2 * LOCAL :].astype(F32)

    lane = lax.broadcasted_iota(jnp.int32, (8, WIDTH), 1) % REGION
    left = tail_of(lax.rem(me + count - 1, count))
    own = tail_of(me)
    right = tail_of(lax.rem(me + 1, count))

    def seen(offset):
        return jnp.where(
            lane < RADIUS,
            pltpu.roll(left, (WIDTH + RADIUS - PATCH - offset) % WIDTH, 1),
            jnp.where(
                lane < RADIUS + PATCH,
                pltpu.roll(own, (WIDTH + RADIUS - offset) % WIDTH, 1),
                pltpu.roll(right, (WIDTH + RADIUS + PATCH - offset) % WIDTH, 1),
            ),
        )

    first, second = seen(0), seen(PATCH)
    result = []
    for half in range(2):
        base = half * 4
        means = [t[base : base + 1] + t[base + 1 : base + 2] for t in tails]
        mean = functools.reduce(jnp.add, means) * (1.0 / count)
        deviation = []
        for s, own_mean in enumerate(means):
            value = ref[s, half * LOCAL : (half + 1) * LOCAL].astype(F32)
            deviation.append((value + (own_mean - mean)).astype(BF))
        weight = first[base + 2 : base + 3]
        obs = second[base + 2 : base + 3] + first[base + 3 : base + 4] + second[base + 3 : base + 4]
        innovation = (obs - mean).astype(BF).astype(F32)
        result.append((jnp.concatenate(deviation, 0), mean, weight, innovation))
    return result


def half_sums(halves, row_distances):
    lane = lax.broadcasted_iota(jnp.int32, (1, WIDTH), 1)
    region_column = lane % REGION
    half_row = (lane // REGION) % (BAND // 2)
    column_distance = jnp.maximum(
        jnp.maximum(RADIUS - region_column, region_column - (RADIUS + PATCH - 1)), 0
    )
    weighted, deviation, innovation = [], [], []
    for (dev, _, weight, inno), row_distance in zip(halves, row_distances):
        far = jnp.maximum(row_distance(half_row), column_distance).astype(F32)
        factor = weight * (1.0 - far / (RADIUS + 1.0))
        weighted.append((dev.astype(F32) * factor).astype(BF))
        deviation.append(dev)
        innovation.append(jnp.broadcast_to(inno, (16, WIDTH)).astype(BF))
    deviation = jnp.concatenate(deviation, 1)
    rows = jnp.concatenate([deviation, jnp.concatenate(innovation, 1)], 0)
    weighted = jnp.concatenate(weighted, 1)
    return deviation, lax.dot_general(rows, weighted, (((1,), (1,)), ((), ())), preferred_element_type=F32)


def own_kernel(me_ref, own_ref, inner_ref, sums_ref, mean_ref):
    halves = halves_of(own_ref, me_ref[0])
    deviation, sums_ref[...] = half_sums(halves, [jnp.zeros_like] * 2)
    lane = lax.broadcasted_iota(jnp.int32, (2 * WIDTH, WIDTH), 0)
    target = lax.broadcasted_iota(jnp.int32, (2 * WIDTH, WIDTH), 1)
    narrow = (lane == (target // PATCH) * REGION + RADIUS + target % PATCH).astype(F32).astype(BF)
    inner_ref[...] = jnp.dot(deviation, narrow, preferred_element_type=F32).astype(BF)
    mean = jnp.broadcast_to(jnp.concatenate([halves[0][1], halves[1][1]], 1), (16, 2 * WIDTH))
    high = mean.astype(BF)
    middle = (mean - high.astype(F32)).astype(BF)
    low = (mean - high.astype(F32) - middle.astype(F32)).astype(BF)
    parts = jnp.dot(jnp.concatenate([high, middle, low], 0), narrow, preferred_element_type=F32)
    mean_ref[...] = parts[:8] + (parts[16:24] + parts[32:40])


def analysis_kernel(me_ref, near_ref, inner_ref, sums_ref, mean_ref, out_ref):
    count = near_ref.shape[0]
    members = count * LOCAL
    halves = halves_of(near_ref, me_ref[0])
    both = sums_ref[...] + half_sums(halves, [lambda r: r + 1, lambda r: RADIUS - r])[1]
    row = lax.broadcasted_iota(jnp.int32, (members, members), 0)
    col = lax.broadcasted_iota(jnp.int32, (members, members), 1)
    system = both[:members] + jnp.where(row == col, members - 1.0, 0.0)
    def mul(a, b):
        return jnp.dot(a.astype(BF), b.astype(BF), preferred_element_type=F32)

    def with_line(a, line):
        return jnp.concatenate([a.astype(BF), line.astype(BF)], 0)

    inner, line = inner_ref[...], both[members:]
    system_b = system.astype(BF)
    first = mul(with_line(system_b, line), system_b)
    system_x = mul(system_b, inner)
    scale = jnp.sqrt(jnp.sum(system * system))
    inverse = 1.0 / scale
    x1 = 1.5 * inner.astype(F32) - (0.5 * inverse) * system_x
    line1 = 1.5 * line - (0.5 * inverse) * first[members:]
    y1 = inverse * (1.5 * system - (0.5 * inverse) * first[:members])
    p1 = 1.5 * y1 - (0.5 * inverse) * mul(y1, system_b)
    p1b = p1.astype(BF)
    second = mul(with_line(p1b, line1), p1b)
    x2 = 1.5 * x1 - 0.5 * mul(p1b, x1)
    line2 = 1.5 * line1 - 0.5 * second[members:]
    q1 = 1.5 * p1 - 0.5 * second[:members]
    p2 = 1.5 * q1 - 0.5 * mul(q1, p1b)
    p2b = p2.astype(BF)
    factor = 1.0 / jnp.sqrt(scale)
    x3 = (1.5 * x2 - 0.5 * mul(p2b, x2)) * factor
    line3 = (1.5 * line2 - 0.5 * mul(line2, p2b)) * factor
    line_b = line3.astype(BF)
    lines = with_line(line_b, line3 - line_b.astype(F32))
    shift = mul(lines, x3)
    shift = shift[:1] + shift[16:17]
    root = jnp.sqrt(jnp.full((1, 1), members - 1.0, F32))
    result = (root * x3 + (shift + mean_ref[:1])).astype(BF)
    for s in range(count):
        out_ref[s] = result[s * LOCAL : (s + 1) * LOCAL]


def unpacked(ref):
    return [row.astype(F32) for row in swap_blocks([ref[position(p)] for p in range(ref.shape[0])], PATCH)]


def by_field(rows):
    half = BAND // 2
    return [[rows[h * FIELDS * half + field * half + r] for h in range(2) for r in range(half)] for field in range(FIELDS)]


def unpack_kernel(in_ref, rows_ref, inner_ref):
    rows = unpacked(in_ref)
    for i, row in enumerate(rows):
        rows_ref[i] = row
    advance_inner(*by_field(rows), inner_ref)


def forecast_kernel(own_ref, inner_ref, near_ref, out_ref):
    own, near = by_field(own_ref), by_field(unpacked(near_ref))
    fields = [n[BAND - FSTEPS :] + o + n[:FSTEPS] for o, n in zip(own, near)]
    done = forecast_rows(*fields, kept_rows(inner_ref))
    for field in range(FIELDS):
        for r in range(BAND):
            out_ref[pl.ds(field * BAND + r, LOCAL, stride=FIELDS * BAND), :] = done[field][r]


def from_next(value):
    count = lax.axis_size("rows")
    return lax.ppermute(value, "rows", [((i + 1) % count, i) for i in range(count)])


def from_previous(value):
    count = lax.axis_size("rows")
    return lax.ppermute(value, "rows", [(i, (i + 1) % count) for i in range(count)])


def near_rows(value, join):
    if lax.axis_size("rows") == 2:
        return from_next(value)
    return join(from_next(value), from_previous(value))


def join_grid(after, before):
    return jnp.concatenate([after[:, :, : BAND // 2], before[:, :, BAND // 2 :]], 2)


def join_region(after, before):
    after, before = (x.reshape(x.shape[0], -1, 4, WIDTH) for x in (after, before))
    near = jnp.concatenate([after[:, :4], before[:, 4:8], after[:, 8:9], before[:, 9:]], 1)
    return near.reshape(near.shape[0], -1, WIDTH)


def join_inner(after, before):
    return jnp.concatenate([after[..., : WIDTH // 2], before[..., WIDTH // 2 :]], 2)


def exchange(value):
    return lax.all_to_all(value, "mem", split_axis=0, concat_axis=0, axis_index_groups=[list(ORDER)], tiled=True)


def call(kernel, name, out_shape, *args, flops=0):
    spaces = [pltpu.SMEM if arg.shape == (1,) else pltpu.VMEM for arg in args]
    moved = sum(x.size * x.dtype.itemsize for x in [*args, *jax.tree.leaves(out_shape)])
    return pl.pallas_call(
        kernel,
        out_shape=out_shape,
        in_specs=[pl.BlockSpec(memory_space=space) for space in spaces],
        out_specs=jax.tree.map(lambda _: pl.BlockSpec(memory_space=pltpu.VMEM), out_shape),
        compiler_params=pltpu.CompilerParams(vmem_limit_bytes=16 * 2**20),
        cost_estimate=pl.CostEstimate(flops=flops, bytes_accessed=moved, transcendentals=0),
        name=name,
    )(*args)


def local(sample_collection, obs_values, obs_inverse_variance, obs_mask):
    count = lax.axis_size("mem")
    shape = sample_collection.shape
    assert shape == (LOCAL, FIELDS, BAND, WIDTH) and count == PLACES
    me = lax.axis_index("mem").astype(jnp.int32).reshape(1)
    near = near_rows(sample_collection, join_grid)
    rows = jnp.transpose(sample_collection.reshape(LOCAL, FIELDS * BAND, WIDTH), (1, 0, 2))
    region_shape = jax.ShapeDtypeStruct((count, 2 * LOCAL + 8, WIDTH), BF)
    inner_shape = jax.ShapeDtypeStruct((count, LOCAL, WIDTH), BF)
    rows_shape = jax.ShapeDtypeStruct((FIELDS * BAND, LOCAL, WIDTH), F32)
    kept_shape = jax.ShapeDtypeStruct((FIELDS * len(inner_steps()), LOCAL, WIDTH), F32)
    first = [kept_shape, jax.ShapeDtypeStruct((8, WIDTH), F32)]
    kept = call(inner_kernel, "inner_rows", first, rows, obs_values, obs_inverse_variance, obs_mask)
    region = exchange(call(pack_kernel, "forecast_pack", region_shape, rows, *kept, near.reshape(-1, WIDTH)))
    members, points = count * LOCAL, 2 * WIDTH
    own_shapes = [
        jax.ShapeDtypeStruct((members, WIDTH), BF),
        jax.ShapeDtypeStruct((members + 16, members), F32),
        jax.ShapeDtypeStruct((8, WIDTH), F32),
    ]
    flops = 2 * members * members * points
    region_near = near_rows(region, join_region)
    own = call(own_kernel, "own_half", own_shapes, me, region, flops=flops)
    inner = exchange(call(analysis_kernel, "analysis", inner_shape, me, region_near, *own, flops=8 * flops))
    inner_near = near_rows(inner, join_inner)
    own_rows = call(unpack_kernel, "unpack_own", [rows_shape, kept_shape], inner)
    out_shape = jax.ShapeDtypeStruct((LOCAL * FIELDS * BAND, WIDTH), F32)
    cycled = call(forecast_kernel, "unpack_forecast", out_shape, *own_rows, inner_near)
    return cycled.reshape(shape)


def solution(mesh):
    return jax.shard_map(
        local,
        mesh=mesh,
        in_specs=(
            P("mem", None, "rows", None),
            P(None, "rows", "mem"),
            P(None, "rows", "mem"),
            P(None, "rows", "mem"),
        ),
        out_specs=P("mem", None, "rows", None),
        check_vma=False,
    )
```

```python
import functools

import jax
import jax.numpy as jnp
from jax import lax
from jax.experimental import pallas as pl
from jax.experimental.pallas import tpu as pltpu
from jax.sharding import PartitionSpec as P

PATCH = 8
RADIUS = 4
FSTEPS = 4
CADV = 0.05

LOCAL = 16
FIELDS = 2
BAND = 8
WIDTH = 128
PLACES = WIDTH // PATCH
REGION = PATCH + 2 * RADIUS

BF = jnp.bfloat16
F32 = jnp.float32


def position(place):
    low, high = place & 3, place >> 2
    return PLACES - 1 - (low * 4 + (high & 1) * 2 + (high >> 1))


def advance(u_rows, v_rows, i):
    cu, cv = CADV * u_rows[i], CADV * v_rows[i]
    stepped = []
    for rows in (u_rows, v_rows):
        along_x = pltpu.roll(rows[i], WIDTH - 1, 1) - pltpu.roll(rows[i], 1, 1)
        along_y = rows[i + 1] - rows[i - 1]
        stepped.append(rows[i] - (cu * along_x + cv * along_y))
    return stepped


def forecast_rows(u_rows, v_rows, known=None):
    for step in range(1, FSTEPS + 1):
        stepped = []
        for i in range(1, len(u_rows) - 1):
            row = i - 1 + step - FSTEPS
            given = known(step, row) if known is not None and step <= row < BAND - step else None
            stepped.append(given if given is not None else advance(u_rows, v_rows, i))
        u_rows, v_rows = [u for u, _ in stepped], [v for _, v in stepped]
    return u_rows, v_rows


def inner_steps():
    return [(step, row) for step in range(1, FSTEPS) for row in range(step, BAND - step)]


def swap_blocks(parts, size, most):
    count = len(parts)
    block = lax.broadcasted_iota(jnp.int32, parts[0].shape, 1) // size
    stride = 1
    while stride < count:
        base = min(most, count // stride)
        here = [(block // stride) % base == digit for digit in range(base)]
        new = []
        for j in range(count):
            own = (j // stride) % base
            value = parts[j]
            for digit in range(base):
                if digit != own:
                    move = (digit - own) * stride
                    value = jnp.where(here[digit], pltpu.roll(parts[j + move], (move * size) % WIDTH, 1), value)
            new.append(value)
        parts = new
        stride *= base
    return parts


def observation_rows(values_ref, inverse_ref, mask_ref):
    points = FIELDS * BAND
    weight = (mask_ref[...].astype(F32) * inverse_ref[...]).astype(BF).astype(F32).reshape(points, PATCH)
    values = values_ref[...].reshape(points, PATCH)
    high = values.astype(BF).astype(F32)
    middle = (values - high).astype(BF).astype(F32)
    low = values - high - middle
    rows = jnp.concatenate([weight, high, middle, low], 0).astype(BF)
    source = lax.broadcasted_iota(jnp.int32, (PATCH, WIDTH), 0)
    lane = lax.broadcasted_iota(jnp.int32, (PATCH, WIDTH), 1)
    spread = (lane % PATCH == source).astype(F32).astype(BF)
    wide = jnp.dot(rows, spread, preferred_element_type=F32)
    row = lax.broadcasted_iota(jnp.int32, wide.shape, 0)
    lane = lax.broadcasted_iota(jnp.int32, wide.shape, 1)
    part, field, y = row // points, (row % points) // BAND, row % BAND
    place = (field * (BAND // 2) + y % (BAND // 2)) * 2 + part % 2
    wide = jnp.where(lane // PATCH == place, wide, 0.0).astype(BF)
    target = lax.broadcasted_iota(jnp.int32, (8, 4 * points), 0)
    row = lax.broadcasted_iota(jnp.int32, (8, 4 * points), 1)
    wanted = ((row % BAND) // (BAND // 2)) * 4 + 2 + row // (2 * points)
    gather = (target == wanted).astype(F32).astype(BF)
    return jnp.dot(gather, wide, preferred_element_type=F32)


def advance_inner(u_rows, v_rows, out_ref):
    kept = 0
    for _ in range(1, FSTEPS):
        stepped = [advance(u_rows, v_rows, i) for i in range(1, len(u_rows) - 1)]
        u_rows, v_rows = [u for u, _ in stepped], [v for _, v in stepped]
        for row in stepped:
            for value in row:
                out_ref[kept] = value
                kept += 1


def kept_rows(inner_ref):
    places = inner_steps()

    def known(step, row):
        first = FIELDS * places.index((step, row))
        return [inner_ref[first + field] for field in range(FIELDS)]

    return known


def inner_kernel(rows_ref, values_ref, inverse_ref, mask_ref, out_ref, obs_ref):
    obs_ref[...] = observation_rows(values_ref, inverse_ref, mask_ref)
    advance_inner(*([rows_ref[field * BAND + r] for r in range(BAND)] for field in range(FIELDS)), out_ref)


def pack_kernel(rows_ref, inner_ref, obs_ref, near_ref, out_ref):
    points = FIELDS * BAND

    def near(field, index):
        return near_ref[pl.ds(field * BAND + index, LOCAL, stride=points), :]

    fields = []
    for field in range(FIELDS):
        before = [near(field, r) for r in range(BAND - FSTEPS, BAND)]
        own = [rows_ref[field * BAND + r] for r in range(BAND)]
        after = [near(field, r) for r in range(FSTEPS)]
        fields.append(before + own + after)
    done = forecast_rows(*fields, kept_rows(inner_ref))
    half_rows = BAND // 2
    index = lax.broadcasted_iota(jnp.int32, (8, WIDTH), 0)
    values, means = [], [jnp.zeros((8, WIDTH), F32)] * (FIELDS * half_rows)
    for half in range(2):
        for j in range(FIELDS * half_rows):
            value = done[j // half_rows][half * half_rows + j % half_rows]
            mean = jnp.sum(value, 0, keepdims=True) * (1.0 / LOCAL)
            high = mean.astype(BF).astype(F32)
            means[j] = jnp.where(index == 4 * half, high, jnp.where(index == 4 * half + 1, mean - high, means[j]))
            values.append(value - mean)
    rows = jnp.concatenate(values + means, 0).astype(BF)
    column = lax.broadcasted_iota(jnp.int32, (WIDTH, 2 * WIDTH), 0)
    lane = lax.broadcasted_iota(jnp.int32, (WIDTH, 2 * WIDTH), 1)
    wanted = ((lane // REGION) * PATCH + lane % REGION + (WIDTH - RADIUS)) % WIDTH
    widen = (column == wanted).astype(F32).astype(BF)
    wide = jnp.dot(rows, widen, preferred_element_type=F32)
    obs = obs_ref[...]
    start = len(values) * LOCAL
    is_mean = index & 2 == 0
    means = []
    for j in range(8):
        part = wide[start + j * 8 : start + j * 8 + 8]
        means.append(jnp.where(is_mean, part[:, :WIDTH], pltpu.roll(part[:, WIDTH:], 2, 0)))
    means = swap_blocks(means, REGION, 2)
    for side in range(2):
        for half in range(2):
            parts = [
                wide[(half * 8 + j) * LOCAL : (half * 8 + j + 1) * LOCAL, side * WIDTH : (side + 1) * WIDTH].astype(BF)
                for j in range(8)
            ]
            parts = swap_blocks(parts, REGION, 2)
            for i in range(8):
                out_ref[position(side * 8 + i), half * LOCAL : (half + 1) * LOCAL] = parts[i]
        for i in range(8):
            mean = means[i] if side == 0 else pltpu.roll(means[i], 6, 0)
            out_ref[position(side * 8 + i), 2 * LOCAL :] = jnp.where(is_mean, mean, obs).astype(BF)


def halves_of(ref, me):
    count = ref.shape[0]
    tails = [ref[s, 2 * LOCAL :].astype(F32) for s in range(count)]

    def tail_of(device):
        return ref[position(device), 2 * LOCAL :].astype(F32)

    lane = lax.broadcasted_iota(jnp.int32, (8, WIDTH), 1) % REGION
    left = tail_of(lax.rem(me + count - 1, count))
    own = tail_of(me)
    right = tail_of(lax.rem(me + 1, count))

    def seen(offset):
        return jnp.where(
            lane < RADIUS,
            pltpu.roll(left, (WIDTH + RADIUS - PATCH - offset) % WIDTH, 1),
            jnp.where(
                lane < RADIUS + PATCH,
                pltpu.roll(own, (WIDTH + RADIUS - offset) % WIDTH, 1),
                pltpu.roll(right, (WIDTH + RADIUS + PATCH - offset) % WIDTH, 1),
            ),
        )

    first, second = seen(0), seen(PATCH)
    result = []
    for half in range(2):
        base = half * 4
        means = [t[base : base + 1] + t[base + 1 : base + 2] for t in tails]
        mean = functools.reduce(jnp.add, means) * (1.0 / count)
        deviation = []
        for s, own_mean in enumerate(means):
            value = ref[s, half * LOCAL : (half + 1) * LOCAL].astype(F32)
            deviation.append((value + (own_mean - mean)).astype(BF))
        weight = first[base + 2 : base + 3]
        obs = second[base + 2 : base + 3] + first[base + 3 : base + 4] + second[base + 3 : base + 4]
        innovation = (obs - mean).astype(BF).astype(F32)
        result.append((jnp.concatenate(deviation, 0), mean, weight, innovation))
    return result


def half_sums(halves, row_distances):
    lane = lax.broadcasted_iota(jnp.int32, (1, WIDTH), 1)
    region_column = lane % REGION
    half_row = (lane // REGION) % (BAND // 2)
    column_distance = jnp.maximum(
        jnp.maximum(RADIUS - region_column, region_column - (RADIUS + PATCH - 1)), 0
    )
    weighted, deviation, innovation = [], [], []
    for (dev, _, weight, inno), row_distance in zip(halves, row_distances):
        far = jnp.maximum(row_distance(half_row), column_distance).astype(F32)
        factor = weight * (1.0 - far / (RADIUS + 1.0))
        weighted.append((dev.astype(F32) * factor).astype(BF))
        deviation.append(dev)
        innovation.append(jnp.broadcast_to(inno, (16, WIDTH)).astype(BF))
    deviation = jnp.concatenate(deviation, 1)
    rows = jnp.concatenate([deviation, jnp.concatenate(innovation, 1)], 0)
    weighted = jnp.concatenate(weighted, 1)
    return deviation, lax.dot_general(rows, weighted, (((1,), (1,)), ((), ())), preferred_element_type=F32)


def own_kernel(me_ref, own_ref, inner_ref, sums_ref, mean_ref):
    halves = halves_of(own_ref, me_ref[0])
    deviation, sums_ref[...] = half_sums(halves, [jnp.zeros_like] * 2)
    lane = lax.broadcasted_iota(jnp.int32, (2 * WIDTH, WIDTH), 0)
    target = lax.broadcasted_iota(jnp.int32, (2 * WIDTH, WIDTH), 1)
    narrow = (lane == (target // PATCH) * REGION + RADIUS + target % PATCH).astype(F32).astype(BF)
    inner_ref[...] = jnp.dot(deviation, narrow, preferred_element_type=F32).astype(BF)
    mean = jnp.broadcast_to(jnp.concatenate([halves[0][1], halves[1][1]], 1), (16, 2 * WIDTH))
    high = mean.astype(BF)
    middle = (mean - high.astype(F32)).astype(BF)
    low = (mean - high.astype(F32) - middle.astype(F32)).astype(BF)
    parts = jnp.dot(jnp.concatenate([high, middle, low], 0), narrow, preferred_element_type=F32)
    mean_ref[...] = parts[:8] + (parts[16:24] + parts[32:40])


def analysis_kernel(me_ref, near_ref, inner_ref, sums_ref, mean_ref, out_ref):
    count = near_ref.shape[0]
    members = count * LOCAL
    halves = halves_of(near_ref, me_ref[0])
    both = sums_ref[...] + half_sums(halves, [lambda r: r + 1, lambda r: RADIUS - r])[1]
    row = lax.broadcasted_iota(jnp.int32, (members, members), 0)
    col = lax.broadcasted_iota(jnp.int32, (members, members), 1)
    system = both[:members] + jnp.where(row == col, members - 1.0, 0.0)
    def mul(a, b):
        return jnp.dot(a.astype(BF), b.astype(BF), preferred_element_type=F32)

    def with_line(a, line):
        return jnp.concatenate([a.astype(BF), line.astype(BF)], 0)

    inner, line = inner_ref[...], both[members:]
    system_b = system.astype(BF)
    first = mul(with_line(system_b, line), system_b)
    system_x = mul(system_b, inner)
    scale = jnp.sqrt(jnp.sum(system * system))
    inverse = 1.0 / scale
    x1 = 1.5 * inner.astype(F32) - (0.5 * inverse) * system_x
    line1 = 1.5 * line - (0.5 * inverse) * first[members:]
    y1 = inverse * (1.5 * system - (0.5 * inverse) * first[:members])
    p1 = 1.5 * y1 - (0.5 * inverse) * mul(y1, system_b)
    p1b = p1.astype(BF)
    second = mul(with_line(p1b, line1), p1b)
    x2 = 1.5 * x1 - 0.5 * mul(p1b, x1)
    line2 = 1.5 * line1 - 0.5 * second[members:]
    q1 = 1.5 * p1 - 0.5 * second[:members]
    p2 = 1.5 * q1 - 0.5 * mul(q1, p1b)
    p2b = p2.astype(BF)
    factor = 1.0 / jnp.sqrt(scale)
    x3 = (1.5 * x2 - 0.5 * mul(p2b, x2)) * factor
    line3 = (1.5 * line2 - 0.5 * mul(line2, p2b)) * factor
    line_b = line3.astype(BF)
    lines = with_line(line_b, line3 - line_b.astype(F32))
    shift = mul(lines, x3)
    shift = shift[:1] + shift[16:17]
    root = jnp.sqrt(jnp.full((1, 1), members - 1.0, F32))
    result = (root * x3 + (shift + mean_ref[:1])).astype(BF)
    for s in range(count):
        out_ref[s] = result[s * LOCAL : (s + 1) * LOCAL]


def by_field(rows):
    half = BAND // 2
    return [[rows[h * FIELDS * half + field * half + r] for h in range(2) for r in range(half)] for field in range(FIELDS)]


def unpack_kernel(in_ref, rows_ref):
    blocks = [in_ref[position(p)] for p in range(in_ref.shape[0])]
    for i, row in enumerate(swap_blocks(blocks, PATCH, 4)):
        rows_ref[i] = row


def read_rows(ref):
    return by_field([ref[i].astype(F32) for i in range(ref.shape[0])])


def inner_again_kernel(rows_ref, inner_ref):
    advance_inner(*read_rows(rows_ref), inner_ref)


def forecast_kernel(own_ref, inner_ref, near_ref, out_ref):
    own, near = read_rows(own_ref), read_rows(near_ref)
    fields = [n[BAND - FSTEPS :] + o + n[:FSTEPS] for o, n in zip(own, near)]
    done = forecast_rows(*fields, kept_rows(inner_ref))
    for field in range(FIELDS):
        for r in range(BAND):
            out_ref[pl.ds(field * BAND + r, LOCAL, stride=FIELDS * BAND), :] = done[field][r]


def from_next(value):
    count = lax.axis_size("rows")
    return lax.ppermute(value, "rows", [((i + 1) % count, i) for i in range(count)])


def from_previous(value):
    count = lax.axis_size("rows")
    return lax.ppermute(value, "rows", [(i, (i + 1) % count) for i in range(count)])


def near_rows(value, join):
    if lax.axis_size("rows") == 2:
        return from_next(value)
    return join(from_next(value), from_previous(value))


def join_grid(after, before):
    return jnp.concatenate([after[:, :, : BAND // 2], before[:, :, BAND // 2 :]], 2)


def join_region(after, before):
    after, before = (x.reshape(x.shape[0], -1, 4, WIDTH) for x in (after, before))
    near = jnp.concatenate([after[:, :4], before[:, 4:8], after[:, 8:9], before[:, 9:]], 1)
    return near.reshape(near.shape[0], -1, WIDTH)


def join_inner(after, before):
    return jnp.concatenate([after[: FIELDS * BAND // 2], before[FIELDS * BAND // 2 :]], 0)


def exchange(value):
    bands = lax.axis_size("rows")
    places = sorted(range(lax.axis_size("mem")), key=position)
    groups = [[place * bands + band for place in places] for band in reversed(range(bands))]
    return lax.all_to_all(value, ("mem", "rows"), split_axis=0, concat_axis=0, axis_index_groups=groups, tiled=True)


def call(kernel, name, out_shape, *args, flops=0):
    spaces = [pltpu.SMEM if arg.shape == (1,) else pltpu.VMEM for arg in args]
    moved = sum(x.size * x.dtype.itemsize for x in [*args, *jax.tree.leaves(out_shape)])
    return pl.pallas_call(
        kernel,
        out_shape=out_shape,
        in_specs=[pl.BlockSpec(memory_space=space) for space in spaces],
        out_specs=jax.tree.map(lambda _: pl.BlockSpec(memory_space=pltpu.VMEM), out_shape),
        compiler_params=pltpu.CompilerParams(vmem_limit_bytes=16 * 2**20),
        cost_estimate=pl.CostEstimate(flops=flops, bytes_accessed=moved, transcendentals=0),
        name=name,
    )(*args)


def local(sample_collection, obs_values, obs_inverse_variance, obs_mask):
    count = lax.axis_size("mem")
    shape = sample_collection.shape
    assert shape == (LOCAL, FIELDS, BAND, WIDTH) and count == PLACES
    me = lax.axis_index("mem").astype(jnp.int32).reshape(1)
    near = near_rows(sample_collection, join_grid)
    rows = jnp.transpose(sample_collection.reshape(LOCAL, FIELDS * BAND, WIDTH), (1, 0, 2))
    region_shape = jax.ShapeDtypeStruct((count, 2 * LOCAL + 8, WIDTH), BF)
    inner_shape = jax.ShapeDtypeStruct((count, LOCAL, WIDTH), BF)
    rows_shape = jax.ShapeDtypeStruct((FIELDS * BAND, LOCAL, WIDTH), F32)
    kept_shape = jax.ShapeDtypeStruct((FIELDS * len(inner_steps()), LOCAL, WIDTH), F32)
    first = [kept_shape, jax.ShapeDtypeStruct((8, WIDTH), F32)]
    kept = call(inner_kernel, "inner_rows", first, rows, obs_values, obs_inverse_variance, obs_mask)
    region = exchange(call(pack_kernel, "forecast_pack", region_shape, rows, *kept, near.reshape(-1, WIDTH)))
    members, points = count * LOCAL, 2 * WIDTH
    own_shapes = [
        jax.ShapeDtypeStruct((members, WIDTH), BF),
        jax.ShapeDtypeStruct((members + 16, members), F32),
        jax.ShapeDtypeStruct((8, WIDTH), F32),
    ]
    flops = 2 * members * members * points
    region_near = near_rows(region, join_region)
    own = call(own_kernel, "own_half", own_shapes, me, region, flops=flops)
    inner = exchange(call(analysis_kernel, "analysis", inner_shape, me, region_near, *own, flops=8 * flops))
    own_rows = call(unpack_kernel, "unpack_own", jax.ShapeDtypeStruct(rows_shape.shape, BF), inner)
    rows_near = near_rows(own_rows, join_inner)
    kept = call(inner_again_kernel, "inner_rows_again", kept_shape, own_rows)
    out_shape = jax.ShapeDtypeStruct((LOCAL * FIELDS * BAND, WIDTH), F32)
    cycled = call(forecast_kernel, "unpack_forecast", out_shape, own_rows, kept, rows_near)
    return cycled.reshape(shape)


def solution(mesh):
    return jax.shard_map(
        local,
        mesh=mesh,
        in_specs=(
            P("mem", None, "rows", None),
            P(None, "rows", "mem"),
            P(None, "rows", "mem"),
            P(None, "rows", "mem"),
        ),
        out_specs=P("mem", None, "rows", None),
        check_vma=False,
    )
```

```python
import functools

import jax
import jax.numpy as jnp
from jax import lax
from jax.experimental import pallas as pl
from jax.experimental.pallas import tpu as pltpu
from jax.sharding import PartitionSpec as P

PATCH = 8
RADIUS = 4
FSTEPS = 4
CADV = 0.05

LOCAL = 16
FIELDS = 2
BAND = 8
WIDTH = 128
PLACES = WIDTH // PATCH
REGION = PATCH + 2 * RADIUS

BF = jnp.bfloat16
F32 = jnp.float32


def position(place):
    low, high = place & 3, place >> 2
    return PLACES - 1 - (low * 4 + (high & 1) * 2 + (high >> 1))


def advance(u_rows, v_rows, i):
    cu, cv = CADV * u_rows[i], CADV * v_rows[i]
    stepped = []
    for rows in (u_rows, v_rows):
        along_x = pltpu.roll(rows[i], WIDTH - 1, 1) - pltpu.roll(rows[i], 1, 1)
        along_y = rows[i + 1] - rows[i - 1]
        stepped.append(rows[i] - (cu * along_x + cv * along_y))
    return stepped


def forecast_rows(u_rows, v_rows, known=None):
    for step in range(1, FSTEPS + 1):
        stepped = []
        for i in range(1, len(u_rows) - 1):
            row = i - 1 + step - FSTEPS
            given = known(step, row) if known is not None and step <= row < BAND - step else None
            stepped.append(given if given is not None else advance(u_rows, v_rows, i))
        u_rows, v_rows = [u for u, _ in stepped], [v for _, v in stepped]
    return u_rows, v_rows


def inner_steps():
    return [(step, row) for step in range(1, FSTEPS) for row in range(step, BAND - step)]


def swap_blocks(parts, size, most):
    count = len(parts)
    block = lax.broadcasted_iota(jnp.int32, parts[0].shape, 1) // size
    stride = 1
    while stride < count:
        base = min(most, count // stride)
        here = [(block // stride) % base == digit for digit in range(base)]
        new = []
        for j in range(count):
            own = (j // stride) % base
            value = parts[j]
            for digit in range(base):
                if digit != own:
                    move = (digit - own) * stride
                    value = jnp.where(here[digit], pltpu.roll(parts[j + move], (move * size) % WIDTH, 1), value)
            new.append(value)
        parts = new
        stride *= base
    return parts


def observation_rows(values_ref, inverse_ref, mask_ref):
    points = FIELDS * BAND
    weight = (mask_ref[...].astype(F32) * inverse_ref[...]).astype(BF).astype(F32).reshape(points, PATCH)
    values = values_ref[...].reshape(points, PATCH)
    high = values.astype(BF).astype(F32)
    middle = (values - high).astype(BF).astype(F32)
    low = values - high - middle
    rows = jnp.concatenate([weight, high, middle, low], 0).astype(BF)
    source = lax.broadcasted_iota(jnp.int32, (PATCH, WIDTH), 0)
    lane = lax.broadcasted_iota(jnp.int32, (PATCH, WIDTH), 1)
    spread = (lane % PATCH == source).astype(F32).astype(BF)
    wide = jnp.dot(rows, spread, preferred_element_type=F32)
    row = lax.broadcasted_iota(jnp.int32, wide.shape, 0)
    lane = lax.broadcasted_iota(jnp.int32, wide.shape, 1)
    part, field, y = row // points, (row % points) // BAND, row % BAND
    place = (field * (BAND // 2) + y % (BAND // 2)) * 2 + part % 2
    wide = jnp.where(lane // PATCH == place, wide, 0.0).astype(BF)
    target = lax.broadcasted_iota(jnp.int32, (8, 4 * points), 0)
    row = lax.broadcasted_iota(jnp.int32, (8, 4 * points), 1)
    wanted = ((row % BAND) // (BAND // 2)) * 4 + 2 + row // (2 * points)
    gather = (target == wanted).astype(F32).astype(BF)
    return jnp.dot(gather, wide, preferred_element_type=F32)


def advance_inner(u_rows, v_rows, out_ref):
    kept = 0
    for _ in range(1, FSTEPS):
        stepped = [advance(u_rows, v_rows, i) for i in range(1, len(u_rows) - 1)]
        u_rows, v_rows = [u for u, _ in stepped], [v for _, v in stepped]
        for row in stepped:
            for value in row:
                out_ref[kept] = value
                kept += 1


def kept_rows(inner_ref):
    places = inner_steps()

    def known(step, row):
        first = FIELDS * places.index((step, row))
        return [inner_ref[first + field] for field in range(FIELDS)]

    return known


def inner_kernel(rows_ref, values_ref, inverse_ref, mask_ref, out_ref, obs_ref):
    obs_ref[...] = observation_rows(values_ref, inverse_ref, mask_ref)
    advance_inner(*([rows_ref[field * BAND + r] for r in range(BAND)] for field in range(FIELDS)), out_ref)


def pack_kernel(rows_ref, inner_ref, obs_ref, near_ref, out_ref):
    points = FIELDS * BAND

    def near(field, index):
        return near_ref[pl.ds(field * BAND + index, LOCAL, stride=points), :]

    fields = []
    for field in range(FIELDS):
        before = [near(field, r) for r in range(BAND - FSTEPS, BAND)]
        own = [rows_ref[field * BAND + r] for r in range(BAND)]
        after = [near(field, r) for r in range(FSTEPS)]
        fields.append(before + own + after)
    done = forecast_rows(*fields, kept_rows(inner_ref))
    half_rows = BAND // 2
    index = lax.broadcasted_iota(jnp.int32, (8, WIDTH), 0)
    values, means = [], [jnp.zeros((8, WIDTH), F32)] * (FIELDS * half_rows)
    for half in range(2):
        for j in range(FIELDS * half_rows):
            value = done[j // half_rows][half * half_rows + j % half_rows]
            mean = jnp.sum(value, 0, keepdims=True) * (1.0 / LOCAL)
            high = mean.astype(BF).astype(F32)
            means[j] = jnp.where(index == 4 * half, high, jnp.where(index == 4 * half + 1, mean - high, means[j]))
            values.append(value - mean)
    rows = jnp.concatenate(values + means, 0).astype(BF)
    column = lax.broadcasted_iota(jnp.int32, (WIDTH, 2 * WIDTH), 0)
    lane = lax.broadcasted_iota(jnp.int32, (WIDTH, 2 * WIDTH), 1)
    wanted = ((lane // REGION) * PATCH + lane % REGION + (WIDTH - RADIUS)) % WIDTH
    widen = (column == wanted).astype(F32).astype(BF)
    wide = jnp.dot(rows, widen, preferred_element_type=F32)
    obs = obs_ref[...]
    start = len(values) * LOCAL
    is_mean = index & 2 == 0
    means = []
    for j in range(8):
        part = wide[start + j * 8 : start + j * 8 + 8]
        means.append(jnp.where(is_mean, part[:, :WIDTH], pltpu.roll(part[:, WIDTH:], 2, 0)))
    means = swap_blocks(means, REGION, 2)
    for side in range(2):
        for half in range(2):
            parts = [
                wide[(half * 8 + j) * LOCAL : (half * 8 + j + 1) * LOCAL, side * WIDTH : (side + 1) * WIDTH].astype(BF)
                for j in range(8)
            ]
            parts = swap_blocks(parts, REGION, 2)
            for i in range(8):
                out_ref[position(side * 8 + i), half * LOCAL : (half + 1) * LOCAL] = parts[i]
        for i in range(8):
            mean = means[i] if side == 0 else pltpu.roll(means[i], 6, 0)
            out_ref[position(side * 8 + i), 2 * LOCAL :] = jnp.where(is_mean, mean, obs).astype(BF)


def halves_of(ref, me):
    count = ref.shape[0]
    tails = [ref[s, 2 * LOCAL :].astype(F32) for s in range(count)]

    def tail_of(device):
        return ref[position(device), 2 * LOCAL :].astype(F32)

    lane = lax.broadcasted_iota(jnp.int32, (8, WIDTH), 1) % REGION
    left = tail_of(lax.rem(me + count - 1, count))
    own = tail_of(me)
    right = tail_of(lax.rem(me + 1, count))

    def seen(offset):
        return jnp.where(
            lane < RADIUS,
            pltpu.roll(left, (WIDTH + RADIUS - PATCH - offset) % WIDTH, 1),
            jnp.where(
                lane < RADIUS + PATCH,
                pltpu.roll(own, (WIDTH + RADIUS - offset) % WIDTH, 1),
                pltpu.roll(right, (WIDTH + RADIUS + PATCH - offset) % WIDTH, 1),
            ),
        )

    first, second = seen(0), seen(PATCH)
    result = []
    for half in range(2):
        base = half * 4
        means = [t[base : base + 1] + t[base + 1 : base + 2] for t in tails]
        level = means
        while len(level) > 1:
            level = [a + b for a, b in zip(level[::2], level[1::2])]
        mean = level[0] * (1.0 / count)
        deviation = []
        for s, own_mean in enumerate(means):
            value = ref[s, half * LOCAL : (half + 1) * LOCAL].astype(F32)
            deviation.append((value + (own_mean - mean)).astype(BF))
        weight = first[base + 2 : base + 3]
        obs = second[base + 2 : base + 3] + first[base + 3 : base + 4] + second[base + 3 : base + 4]
        innovation = (obs - mean).astype(BF).astype(F32)
        result.append((jnp.concatenate(deviation, 0), mean, weight, innovation))
    return result


def half_sums(halves, row_distances):
    lane = lax.broadcasted_iota(jnp.int32, (1, WIDTH), 1)
    region_column = lane % REGION
    half_row = (lane // REGION) % (BAND // 2)
    column_distance = jnp.maximum(
        jnp.maximum(RADIUS - region_column, region_column - (RADIUS + PATCH - 1)), 0
    )
    weighted, deviation, innovation = [], [], []
    for (dev, _, weight, inno), row_distance in zip(halves, row_distances):
        far = jnp.maximum(row_distance(half_row), column_distance).astype(F32)
        factor = weight * (1.0 - far / (RADIUS + 1.0))
        weighted.append((dev.astype(F32) * factor).astype(BF))
        deviation.append(dev)
        innovation.append(jnp.broadcast_to(inno, (16, WIDTH)).astype(BF))
    deviation = jnp.concatenate(deviation, 1)
    rows = jnp.concatenate([deviation, jnp.concatenate(innovation, 1)], 0)
    weighted = jnp.concatenate(weighted, 1)
    return deviation, lax.dot_general(rows, weighted, (((1,), (1,)), ((), ())), preferred_element_type=F32)


def own_kernel(me_ref, own_ref, inner_ref, sums_ref, mean_ref):
    halves = halves_of(own_ref, me_ref[0])
    deviation, sums = half_sums(halves, [jnp.zeros_like] * 2)
    row = lax.broadcasted_iota(jnp.int32, sums.shape, 0)
    col = lax.broadcasted_iota(jnp.int32, sums.shape, 1)
    sums_ref[...] = sums + jnp.where(row == col, sums.shape[1] - 1.0, 0.0)
    lane = lax.broadcasted_iota(jnp.int32, (2 * WIDTH, WIDTH), 0)
    target = lax.broadcasted_iota(jnp.int32, (2 * WIDTH, WIDTH), 1)
    narrow = (lane == (target // PATCH) * REGION + RADIUS + target % PATCH).astype(F32).astype(BF)
    inner_ref[...] = jnp.dot(deviation, narrow, preferred_element_type=F32).astype(BF)
    mean = jnp.broadcast_to(jnp.concatenate([halves[0][1], halves[1][1]], 1), (16, 2 * WIDTH))
    high = mean.astype(BF)
    middle = (mean - high.astype(F32)).astype(BF)
    low = (mean - high.astype(F32) - middle.astype(F32)).astype(BF)
    parts = jnp.dot(jnp.concatenate([high, middle, low], 0), narrow, preferred_element_type=F32)
    mean_ref[...] = parts[:8] + (parts[16:24] + parts[32:40])


def analysis_kernel(me_ref, near_ref, inner_ref, sums_ref, mean_ref, out_ref):
    count = near_ref.shape[0]
    members = count * LOCAL
    halves = halves_of(near_ref, me_ref[0])
    both = sums_ref[...] + half_sums(halves, [lambda r: r + 1, lambda r: RADIUS - r])[1]
    system = both[:members]

    def mul(a, b):
        return jnp.dot(a.astype(BF), b.astype(BF), preferred_element_type=F32)

    def with_line(a, line):
        return jnp.concatenate([a.astype(BF), line.astype(BF)], 0)

    inner, line = inner_ref[...], both[members:]
    system_b = system.astype(BF)
    first = mul(with_line(system_b, line), system_b)
    system_x = mul(system_b, inner)
    scale = jnp.sqrt(jnp.sum(system * system))
    inverse = 1.0 / scale
    x1 = 1.5 * inner.astype(F32) - (0.5 * inverse) * system_x
    line1 = 1.5 * line - (0.5 * inverse) * first[members:]
    y1 = inverse * (1.5 * system - (0.5 * inverse) * first[:members])
    p1 = 1.5 * y1 - (0.5 * inverse) * mul(y1, system_b)
    p1b = p1.astype(BF)
    second = mul(with_line(p1b, line1), p1b)
    x2 = 1.5 * x1 - 0.5 * mul(p1b, x1)
    line2 = 1.5 * line1 - 0.5 * second[members:]
    q1 = 1.5 * p1 - 0.5 * second[:members]
    p2 = 1.5 * q1 - 0.5 * mul(q1, p1b)
    p2b = p2.astype(BF)
    factor = 1.0 / jnp.sqrt(scale)
    x3 = (1.5 * x2 - 0.5 * mul(p2b, x2)) * factor
    line3 = (1.5 * line2 - 0.5 * mul(line2, p2b)) * factor
    line_b = line3.astype(BF)
    lines = with_line(line_b, line3 - line_b.astype(F32))
    shift = mul(lines, x3)
    shift = shift[:1] + shift[16:17]
    root = jnp.sqrt(jnp.full((1, 1), members - 1.0, F32))
    result = (root * x3 + (shift + mean_ref[:1])).astype(BF)
    for s in range(count):
        out_ref[s] = result[s * LOCAL : (s + 1) * LOCAL]


def by_field(rows):
    half = BAND // 2
    return [[rows[h * FIELDS * half + field * half + r] for h in range(2) for r in range(half)] for field in range(FIELDS)]


def unpack_kernel(in_ref, rows_ref):
    blocks = [in_ref[position(p)] for p in range(in_ref.shape[0])]
    for i, row in enumerate(swap_blocks(blocks, PATCH, 4)):
        rows_ref[i] = row


def read_rows(ref):
    return by_field([ref[i].astype(F32) for i in range(ref.shape[0])])


def inner_again_kernel(rows_ref, inner_ref):
    advance_inner(*read_rows(rows_ref), inner_ref)


def forecast_kernel(own_ref, inner_ref, near_ref, out_ref):
    own, near = read_rows(own_ref), read_rows(near_ref)
    fields = [n[BAND - FSTEPS :] + o + n[:FSTEPS] for o, n in zip(own, near)]
    done = forecast_rows(*fields, kept_rows(inner_ref))
    for field in range(FIELDS):
        for r in range(BAND):
            out_ref[pl.ds(field * BAND + r, LOCAL, stride=FIELDS * BAND), :] = done[field][r]


def from_next(value):
    count = lax.axis_size("rows")
    return lax.ppermute(value, "rows", [((i + 1) % count, i) for i in range(count)])


def from_previous(value):
    count = lax.axis_size("rows")
    return lax.ppermute(value, "rows", [(i, (i + 1) % count) for i in range(count)])


def near_rows(value, join):
    if lax.axis_size("rows") == 2:
        return from_next(value)
    return join(from_next(value), from_previous(value))


def join_grid(after, before):
    return jnp.concatenate([after[:, :, : BAND // 2], before[:, :, BAND // 2 :]], 2)


def join_region(after, before):
    after, before = (x.reshape(x.shape[0], -1, 4, WIDTH) for x in (after, before))
    near = jnp.concatenate([after[:, :4], before[:, 4:8], after[:, 8:9], before[:, 9:]], 1)
    return near.reshape(near.shape[0], -1, WIDTH)


def join_inner(after, before):
    return jnp.concatenate([after[: FIELDS * BAND // 2], before[FIELDS * BAND // 2 :]], 0)


def exchange(value):
    bands = lax.axis_size("rows")
    places = sorted(range(lax.axis_size("mem")), key=position)
    groups = [[place * bands + band for place in places] for band in reversed(range(bands))]
    return lax.all_to_all(value, ("mem", "rows"), split_axis=0, concat_axis=0, axis_index_groups=groups, tiled=True)


def call(kernel, name, out_shape, *args, flops=0):
    spaces = [pltpu.SMEM if arg.shape == (1,) else pltpu.VMEM for arg in args]
    moved = sum(x.size * x.dtype.itemsize for x in [*args, *jax.tree.leaves(out_shape)])
    return pl.pallas_call(
        kernel,
        out_shape=out_shape,
        in_specs=[pl.BlockSpec(memory_space=space) for space in spaces],
        out_specs=jax.tree.map(lambda _: pl.BlockSpec(memory_space=pltpu.VMEM), out_shape),
        compiler_params=pltpu.CompilerParams(vmem_limit_bytes=16 * 2**20),
        cost_estimate=pl.CostEstimate(flops=flops, bytes_accessed=moved, transcendentals=0),
        name=name,
    )(*args)


def local(sample_collection, obs_values, obs_inverse_variance, obs_mask):
    count = lax.axis_size("mem")
    shape = sample_collection.shape
    assert shape == (LOCAL, FIELDS, BAND, WIDTH) and count == PLACES
    me = lax.axis_index("mem").astype(jnp.int32).reshape(1)
    near = near_rows(sample_collection, join_grid)
    rows = jnp.transpose(sample_collection.reshape(LOCAL, FIELDS * BAND, WIDTH), (1, 0, 2))
    region_shape = jax.ShapeDtypeStruct((count, 2 * LOCAL + 8, WIDTH), BF)
    inner_shape = jax.ShapeDtypeStruct((count, LOCAL, WIDTH), BF)
    rows_shape = jax.ShapeDtypeStruct((FIELDS * BAND, LOCAL, WIDTH), F32)
    kept_shape = jax.ShapeDtypeStruct((FIELDS * len(inner_steps()), LOCAL, WIDTH), F32)
    first = [kept_shape, jax.ShapeDtypeStruct((8, WIDTH), F32)]
    kept = call(inner_kernel, "inner_rows", first, rows, obs_values, obs_inverse_variance, obs_mask)
    region = exchange(call(pack_kernel, "forecast_pack", region_shape, rows, *kept, near.reshape(-1, WIDTH)))
    members, points = count * LOCAL, 2 * WIDTH
    own_shapes = [
        jax.ShapeDtypeStruct((members, WIDTH), BF),
        jax.ShapeDtypeStruct((members + 16, members), F32),
        jax.ShapeDtypeStruct((8, WIDTH), F32),
    ]
    flops = 2 * members * members * points
    region_near = near_rows(region, join_region)
    own = call(own_kernel, "own_half", own_shapes, me, region, flops=flops)
    inner = exchange(call(analysis_kernel, "analysis", inner_shape, me, region_near, *own, flops=8 * flops))
    own_rows = call(unpack_kernel, "unpack_own", jax.ShapeDtypeStruct(rows_shape.shape, BF), inner)
    rows_near = near_rows(own_rows, join_inner)
    kept = call(inner_again_kernel, "inner_rows_again", kept_shape, own_rows)
    out_shape = jax.ShapeDtypeStruct((LOCAL * FIELDS * BAND, WIDTH), F32)
    cycled = call(forecast_kernel, "unpack_forecast", out_shape, own_rows, kept, rows_near)
    return cycled.reshape(shape)


def solution(mesh):
    return jax.shard_map(
        local,
        mesh=mesh,
        in_specs=(
            P("mem", None, "rows", None),
            P(None, "rows", "mem"),
            P(None, "rows", "mem"),
            P(None, "rows", "mem"),
        ),
        out_specs=P("mem", None, "rows", None),
        check_vma=False,
    )
```
